32 devices in a mesh: parts: 2 (over y), dp: 2 (over core), tensor: 8 (over z, x).
Axes of the slice: x: 2, y: 2, z: 4, core: 2. Of those that a mesh axis runs over, the one named last changes fastest.
Arguments:
- tokens: bfloat16 [4096, 5120], P(('parts', 'dp', 'tensor')), parts along dimension 0, may hold values from -6 to 6
- cotangent: bfloat16 [4096, 1024], P(('parts', 'dp', 'tensor')), parts along dimension 0, may hold values from -0.119628906 to 0.119628906
- frozen_value: bfloat16 [5120, 1024], P('tensor', 'dp'), may hold values from -0.078125 to 0.078125
- down_store: bfloat16 [512, 327680], P('parts', 'tensor'), parts along dimension 0, may hold values from -0.078125 to 0.078125
- up_store: bfloat16 [512, 65536], P('parts', 'tensor'), parts along dimension 0, may hold values from -0.75 to 0.75
- block_adapter: int32 [32], P(('parts', 'dp', 'tensor')), parts along dimension 0, may hold values from 0 to 255
- adapter_slot: int32 [512], P('parts'), parts along dimension 0, may hold values from 0 to 255, each once
Outputs:
- mixed: bfloat16 [4096, 1024], P(('parts', 'dp', 'tensor')), parts along dimension 0
- grad_down: float32 [512, 327680], P(('parts', 'dp'), 'tensor'), parts along dimension 0
- grad_up: float32 [512, 65536], P(('parts', 'dp'), 'tensor'), parts along dimension 0
The draws below stay inside these ranges and needn't reach their ends.
There are 2 independent parts, one for each index of `parts`. The reference program is written for one: setup_inputs(seed, part) draws one part's arguments, and reference() takes and returns one part's arrays. A program takes and returns all parts, laid end to end along the dimension named above; an argument that names none is the same for every part. Nothing has to cross between parts.
Inputs may be any that keep to these rules, and one draw needn't show every extreme that they name: `adapter_slot`: each store row holds exactly one adapter.
All inputs are finite; a program needn't handle non-finite values.
Results may differ from the reference program's by a relative error of at most 0.0046.
Values may be sent and summed in bfloat16 or wider, within the bound.
No kernel may reach another device: no remote copies, remote signals or barrier semaphores. Data moves between devices by JAX's collectives and lax.ppermute only.
A program may use at most 256 MiB of HBM per device.

```python
import math
import jax
import jax.numpy as jnp
import numpy as np
from jax import lax

D = 5120
VALUE_OUTPUTS = 1024
R = 64
ADAPTERS = 256
BLOCK = 128
TOKEN_TOTAL = 2048
BLOCKS = 16


def place_ends(result, rng, smallest, largest):
    dims = result.shape
    place = [jax.random.randint(jax.random.fold_in(rng, axis), (), 0, dims[axis]) for axis in range(len(dims))]
    result = result.at[tuple(place)].set(smallest)
    longest = dims.index(max(dims))
    place[longest] = (place[longest] + 1) % dims[longest]
    return result.at[tuple(place)].set(largest)


def shard_levels(own_key, shape, shards, least, largest):
    gain, own = 1.0, jax.random.fold_in(own_key, 6)
    for position, shards_of in shards:
        heights = jnp.exp(jax.random.uniform(jax.random.fold_in(own, position), (shards_of,), jnp.float32, least / len(shards), largest / len(shards)))
        gain = gain * jnp.repeat(heights, shape[position] // shards_of).reshape([-1 if axis == position else 1 for axis in range(len(shape))])
    return gain


def rank_bounds(amount, lean):
    weights = [(1 << 20) // math.isqrt(standing ** lean) + 1 for standing in range(1, amount + 1)]
    scale = 1 + sum(weights) // (1 << 30)
    return np.cumsum(np.array([max(1, weight // scale) for weight in weights]))


def ranked_ids(key, extent, amount, skew):
    grid = rank_bounds(amount, skew)
    pick = jax.random.randint(jax.random.fold_in(key, 1), extent, 0, int(grid[amount - 1]))
    rank = jnp.searchsorted(jnp.asarray(grid, jnp.int32), pick, side="right")
    return jax.random.permutation(jax.random.fold_in(key, 2), amount)[rank].astype(jnp.int32)


def noise(rng, dims, spread, most, shards=(), dtype=jnp.bfloat16):
    factor_of = shard_levels(rng, dims, shards, -0.22, 0.18) if shards else 1.0
    array = jax.random.normal(rng, dims, jnp.float32) * spread * factor_of
    return jnp.minimum(jnp.maximum(array, -most), most).astype(dtype)


def setup_inputs(seed: int = 0, part: int = 0) -> dict:
    seeds = jax.random.split(jax.random.key(seed), 8)
    own_keys = jax.random.split(jax.random.fold_in(seeds[7], part), 8)
    return {
        "tokens": noise(own_keys[0], (TOKEN_TOTAL, D), 1.0, 6.0, ((0, 16),)),
        "cotangent": noise(own_keys[1], (TOKEN_TOTAL, VALUE_OUTPUTS), 0.02, 0.119628906, ((0, 16),)),
        "frozen_value": noise(seeds[2], (D, VALUE_OUTPUTS), D ** -0.5, 0.078125, ((0, 8), (1, 2))),
        "down_store": noise(own_keys[3], (ADAPTERS, D * R), D ** -0.5, 0.078125, ((1, 8),)),
        "up_store": noise(own_keys[4], (ADAPTERS, R * VALUE_OUTPUTS), R ** -0.5, 0.75, ((1, 8),)),
        "block_adapter": place_ends(ranked_ids(own_keys[5], (BLOCKS,), ADAPTERS, 2), jax.random.fold_in(own_keys[5], 3), 0, ADAPTERS - 1).astype(jnp.int32),
        "adapter_slot": jax.random.permutation(own_keys[6], ADAPTERS).astype(jnp.int32),
    }


adapter_scale = 2.0


def reference(tokens, cotangent, frozen_value, down_store, up_store, block_adapter, adapter_slot):
    frozen_output = jnp.dot(tokens, frozen_value, preferred_element_type=jnp.float32)
    stored = jnp.take(adapter_slot, block_adapter).astype(jnp.int32)
    token_blocks = tokens.reshape(BLOCKS, BLOCK, D)
    grad_blocks = cotangent.reshape(BLOCKS, BLOCK, VALUE_OUTPUTS)

    def one_block(items):
        block_x, block_gradient, row = items
        down = lax.dynamic_index_in_dim(down_store, row, 0, False).reshape(D, R)
        adapter_output = lax.dynamic_index_in_dim(up_store, row, 0, False).reshape(R, VALUE_OUTPUTS)
        down_projected = jnp.dot(block_x, down, preferred_element_type=jnp.float32).astype(jnp.bfloat16)
        up_projected = jnp.dot(down_projected, adapter_output, preferred_element_type=jnp.float32)
        down_projected_gradient = (adapter_scale * jnp.dot(block_gradient, adapter_output.T, preferred_element_type=jnp.float32)).astype(jnp.bfloat16)
        down_term = jnp.dot(block_x.T, down_projected_gradient, preferred_element_type=jnp.float32)
        up_weight_gradient = adapter_scale * jnp.dot(down_projected.T, block_gradient, preferred_element_type=jnp.float32)
        return up_projected, down_term.reshape(-1), up_weight_gradient.reshape(-1)

    up_projected, down_terms, up_terms = lax.map(one_block, (token_blocks, grad_blocks, stored))
    mixed = (frozen_output + adapter_scale * up_projected.reshape(TOKEN_TOTAL, VALUE_OUTPUTS)).astype(jnp.bfloat16)
    grad_down = jax.ops.segment_sum(down_terms, stored, num_segments=ADAPTERS)
    grad_up = jax.ops.segment_sum(up_terms, stored, num_segments=ADAPTERS)
    return mixed, grad_down, grad_up
```

```python
import functools

import jax
import jax.numpy as jnp
from jax import lax
from jax.experimental import pallas as pl
from jax.experimental.pallas import tpu as pltpu
from jax.sharding import PartitionSpec as P

D = 5120
VALUE_OUTPUTS = 1024
R = 64
ADAPTERS = 256
LANES = 128
GROUP_ROWS = 16

adapter_scale = 2.0
VMEM = pl.BlockSpec(memory_space=pltpu.VMEM)
SMEM = pl.BlockSpec(memory_space=pltpu.SMEM)
ANY = pl.BlockSpec(memory_space=pl.ANY)
LIMIT = pltpu.CompilerParams(vmem_limit_bytes=40 * 1024 * 1024)


def dot(a, b):
    return jnp.dot(a, b, preferred_element_type=jnp.float32)


def dot_t(a, b):
    return lax.dot_general(a, b, (((1,), (1,)), ((), ())), preferred_element_type=jnp.float32)


def t_dot(a, b):
    return lax.dot_general(a, b, (((0,), (0,)), ((), ())), preferred_element_type=jnp.float32)


def fold_rows(left, piece):
    return jnp.dot(left, piece, preferred_element_type=jnp.float32)


def store_rows(requests, adapter_slot):
    table = jnp.arange(adapter_slot.shape[0], dtype=jnp.int32)
    return jnp.sum(jnp.where(requests[:, None] == table[None, :], adapter_slot[None, :], 0), axis=1)


def plain_body(tokens, cotangent, frozen_value, down_store, up_store, block_adapter, adapter_slot):
    token_rows = tokens.shape[0]
    blocks_here = block_adapter.shape[0]
    block_rows = token_rows // blocks_here
    group = lax.axis_size("tensor")
    columns = lax.all_gather(frozen_value, "dp", axis=1, tiled=True)
    frozen_output = fold_rows(tokens, lax.all_gather(columns, "tensor", axis=0, tiled=True))
    requests = lax.all_gather(block_adapter, "tensor", axis=0, tiled=True)
    stored = store_rows(requests, adapter_slot)
    order = stored.reshape(group, blocks_here).T.reshape(-1)
    down_send = jnp.take(down_store, order, axis=0).reshape(blocks_here, group, -1)
    up_send = jnp.take(up_store, order, axis=0).reshape(blocks_here, group, -1)
    down_got = lax.all_to_all(down_send, "tensor", split_axis=1, concat_axis=1, tiled=True)
    up_got = lax.all_to_all(up_send, "tensor", split_axis=1, concat_axis=1, tiled=True)
    down_panel = down_got.reshape(blocks_here, D, R)
    up_panel = up_got.reshape(blocks_here, R, VALUE_OUTPUTS)
    token_blocks = tokens.reshape(blocks_here, block_rows, D)
    grad_blocks = cotangent.reshape(blocks_here, block_rows, VALUE_OUTPUTS)
    down_projected = jnp.einsum(
        "jtd,jdr->jtr", token_blocks, down_panel, preferred_element_type=jnp.float32
    ).astype(jnp.bfloat16)
    up_projected = jnp.einsum(
        "jtr,jrk->jtk", down_projected, up_panel, preferred_element_type=jnp.float32
    )
    mixed = (
        frozen_output + adapter_scale * up_projected.reshape(token_rows, VALUE_OUTPUTS)
    ).astype(jnp.bfloat16)
    down_projected_gradient = (
        adapter_scale
        * jnp.einsum("jtk,jrk->jtr", grad_blocks, up_panel, preferred_element_type=jnp.float32)
    ).astype(jnp.bfloat16)
    down_term = jnp.einsum(
        "jtd,jtr->jdr", token_blocks, down_projected_gradient, preferred_element_type=jnp.float32
    )
    up_weight_gradient = adapter_scale * jnp.einsum(
        "jtr,jtk->jrk", down_projected, grad_blocks, preferred_element_type=jnp.float32
    )
    down_back = lax.all_to_all(
        down_term.reshape(blocks_here, group, -1), "tensor", split_axis=1, concat_axis=1, tiled=True
    )
    up_back = lax.all_to_all(
        up_weight_gradient.reshape(blocks_here, group, -1), "tensor", split_axis=1, concat_axis=1, tiled=True
    )
    down_flat = down_back.reshape(blocks_here * group, -1)
    up_flat = up_back.reshape(blocks_here * group, -1)
    down_table = jax.ops.segment_sum(down_flat, order, num_segments=ADAPTERS)
    up_table = jax.ops.segment_sum(up_flat, order, num_segments=ADAPTERS)
    grad_down = lax.psum_scatter(down_table, "dp", scatter_dimension=0, tiled=True)
    grad_up = lax.psum_scatter(up_table, "dp", scatter_dimension=0, tiled=True)
    return mixed, grad_down, grad_up


def split_kernel(where, x_ref, mine_ref, theirs_ref):
    inner = where[0]
    outer, rows, width = mine_ref.shape
    for k in range(outer):
        own = pl.multiple_of((2 * k + inner) * width, LANES)
        other = pl.multiple_of((2 * k + 1 - inner) * width, LANES)
        mine_ref[k] = x_ref[:, pl.ds(own, width)]
        theirs_ref[k] = x_ref[:, pl.ds(other, width)]


def interleave_kernel(x_ref, xs_ref):
    group, rows2, half = xs_ref.shape
    rows, width = rows2 // 2, 2 * half
    source = lax.broadcasted_iota(jnp.int32, (width, half), 0)
    target = lax.broadcasted_iota(jnp.int32, (width, half), 1)
    even = (source == 2 * target).astype(jnp.bfloat16)
    odd = (source == 2 * target + 1).astype(jnp.bfloat16)
    for k in range(group):
        x = x_ref[:, k * width:(k + 1) * width]
        xs_ref[k, :rows] = dot(x, even).astype(jnp.bfloat16)
        xs_ref[k, rows:] = dot(x, odd).astype(jnp.bfloat16)


def gather_kernel(count, down_chunks, up_chunks, rows, down_ref, up_ref, *rest):
    outs, (down_buf, up_buf, flat, sems) = rest[:count], rest[count:]
    copies = []
    for s in range(count):
        start = pl.multiple_of((rows[s] // GROUP_ROWS) * GROUP_ROWS, GROUP_ROWS)
        a = pltpu.make_async_copy(down_ref.at[pl.ds(start, GROUP_ROWS)], down_buf.at[s], sems.at[2 * s])
        b = pltpu.make_async_copy(up_ref.at[pl.ds(start, GROUP_ROWS)], up_buf.at[s], sems.at[2 * s + 1])
        a.start()
        b.start()
        copies.append((a, b))
    step = 8
    for s in range(count):
        row = rows[s] % GROUP_ROWS
        upper = row >= 8
        sub = row % 8
        copies[s][0].wait()
        copies[s][1].wait()

        def pick(buf, lane):
            tile = buf[s, :, pl.ds(pl.multiple_of(lane, LANES), LANES)].astype(jnp.float32)
            return jnp.where(upper, tile[8:], tile[:8])

        def some(i, carry):
            for u in range(step):
                j = i * step + u
                flat[pl.ds(pl.multiple_of(j * 8, 8), 8), :] = pick(down_buf, j * LANES)
            return carry

        lax.fori_loop(0, down_chunks // step, some, 0)
        outs[s][:down_chunks] = flat[pl.ds(sub, down_chunks, stride=8), :].astype(jnp.bfloat16)
        across = up_chunks // 8
        for j in range(up_chunks):
            place = (j % across) * 8 + j // across
            flat[place * 8:place * 8 + 8, :] = pick(up_buf, j * LANES)
        outs[s][down_chunks:] = flat[pl.ds(sub, up_chunks, stride=8), :].astype(jnp.bfloat16)


def zero_kernel(after_ref, down_ref, up_ref, zeros, sems):
    del after_ref
    zeros[...] = jnp.zeros_like(zeros)
    part = zeros.shape[0]
    copies = []
    for ref, sem in ((down_ref, sems.at[0]), (up_ref, sems.at[1])):
        for g in range(ref.shape[0]):
            for c in range(ref.shape[1] // part):
                copies.append(pltpu.make_async_copy(zeros, ref.at[g, pl.ds(c * part, part)], sem))
    for c in copies:
        c.start()
    for c in copies:
        c.wait()


def adapter_kernel(count, down_chunks, where, xs_ref, g_ref, *rest):
    pieces, outs, (lifted_ref, up_panel) = rest[:count], rest[count:2 * count], rest[2 * count:]
    me = where[0]
    rows = g_ref.shape[0]
    across = g_ref.shape[1] // LANES
    total = jnp.zeros((2 * rows, LANES), jnp.float32)
    for s in range(count):
        owner = me ^ s
        total += dot(xs_ref[owner], pieces[s][:down_chunks])
        at = pl.multiple_of(owner * 8, 8)
        for c in range(across):
            block = pieces[s][down_chunks + 8 * c:down_chunks + 8 * c + 8, :].astype(jnp.float32)
            up_panel[pl.ds(at, 8), c * LANES:(c + 1) * LANES] = block
            up_panel[pl.ds(R + at, 8), c * LANES:(c + 1) * LANES] = block
    panel = up_panel[...].astype(jnp.bfloat16)
    left = lax.broadcasted_iota(jnp.int32, (rows, LANES), 1) < R
    inner = total[:rows] + pltpu.roll(total[rows:], R, 1)
    inner = jnp.where(left, inner, 0.0).astype(jnp.bfloat16)
    g = g_ref[...]
    lifted_ref[...] = adapter_scale * dot(inner, panel)
    inner_grad = adapter_scale * dot_t(g, panel)
    diagonal = jnp.concatenate(
        [jnp.where(left, inner_grad, 0.0), jnp.where(left, 0.0, inner_grad)], axis=0
    ).astype(jnp.bfloat16)
    up_term = adapter_scale * t_dot(inner, g)
    up_panel[...] = up_term
    for s in range(count):
        owner = me ^ s
        outs[s][:down_chunks] = t_dot(xs_ref[owner], diagonal).astype(jnp.bfloat16)
        at = pl.multiple_of(owner * 8, 8)
        rows_here = up_panel[pl.ds(at, 8), :]
        up_part = jnp.concatenate(
            [rows_here[:, c * LANES:(c + 1) * LANES] for c in range(across)], axis=0
        )
        outs[s][down_chunks:] = up_part.astype(jnp.bfloat16)


def scatter_kernel(count, down_chunks, up_chunks, first_row, rows, *rest):
    pieces = rest[:count]
    down_out, up_out = rest[count + 2:count + 4]
    down_sum, up_sum, ordered, sem = rest[count + 4:]
    owned_rows = down_out.shape[0] * 8
    across = up_chunks // 8
    slots = []
    for b in range(count):
        slot = jnp.int32(b)
        for e in range(b - 1, -1, -1):
            slot = jnp.where(rows[e] == rows[b], e, slot)
        slots.append(slot)
        down = pieces[b][:down_chunks].astype(jnp.float32).reshape(down_chunks, 1, LANES)
        for c in range(across):
            ordered[pl.ds(c, 8, stride=across), :] = pieces[b][
                down_chunks + 8 * c:down_chunks + 8 * c + 8
            ].astype(jnp.float32)
        up = ordered[...].reshape(up_chunks, 1, LANES)

        @pl.when(slot == b)
        def _():
            down_sum[b] = down
            up_sum[b] = up

        @pl.when(slot != b)
        def _():
            down_sum[slot] += down
            up_sum[slot] += up

    def copies(b):
        local = rows[b] - first_row[0]
        return (
            pltpu.make_async_copy(down_sum.at[b], down_out.at[local // 8, :, local % 8], sem),
            pltpu.make_async_copy(up_sum.at[b], up_out.at[local // 8, :, local % 8], sem),
        )

    def mine(b):
        local = rows[b] - first_row[0]
        return (slots[b] == b) & (local >= 0) & (local < owned_rows)

    for b in range(count):
        @pl.when(mine(b))
        def _():
            for copy in copies(b):
                copy.start()
    for b in range(count):
        @pl.when(mine(b))
        def _():
            for copy in copies(b):
                copy.wait()


def base_kernel(outer, where, x_refs, w_ref, arrivals, own_ref, other_ref, acc):
    z, half = where[0], where[1]
    width = arrivals[0][3].shape[1]

    def left(block):
        return jnp.concatenate([ref[block] for ref in x_refs], axis=0)

    acc[...] = dot(left(z), w_ref[...])
    for direction, distance, crossed, ref in arrivals:
        source = z - direction * distance

        @pl.when((source >= 0) & (source < outer))
        def _():
            at = pl.multiple_of((half if not crossed else 1 - half) * width, LANES)
            acc[:, pl.ds(at, width)] += dot(left(source), ref[...])

    rows = own_ref.shape[0]
    own_ref[...] = acc[:rows]
    other_ref[...] = acc[rows:]


def fast_body(tokens, cotangent, frozen_value, down_store, up_store, block_adapter, adapter_slot):
    group, parts = lax.axis_size("tensor"), lax.axis_size("parts")
    outer = group // 2
    token_rows = tokens.shape[0]
    slice_width = D // group
    down_chunks = down_store.shape[1] // LANES
    up_chunks = up_store.shape[1] // LANES
    piece = jax.ShapeDtypeStruct((down_chunks + up_chunks, LANES), jnp.bfloat16)
    me, part, core = lax.axis_index("tensor"), lax.axis_index("parts"), lax.axis_index("dp")
    z, x = me // 2, me % 2
    here = jnp.stack([me, x, z, part])

    def exchange(value, s):
        return lax.ppermute(value, "tensor", [(t, t ^ s) for t in range(group)])

    def other_core(value):
        return lax.ppermute(value, "dp", [(0, 1), (1, 0)])

    row = store_rows(block_adapter, adapter_slot)
    rows = jnp.concatenate([row] + [exchange(row, s) for s in range(1, group)])
    rows_core = other_core(rows)

    width = frozen_value.shape[1] // parts
    half = lax.dynamic_slice_in_dim(frozen_value, part * width, width, axis=1)
    arrivals = []
    for direction in (1, -1):
        moving = half
        for distance in range(1, outer):
            steps = [
                (t, t + 2 * direction)
                for t in range(group)
                if 0 <= t // 2 + direction < outer and 0 <= t // 2 - direction * (distance - 1) < outer
            ]
            moving = lax.ppermute(moving, "tensor", steps)
            arrivals.append((direction, distance, False, moving))
            crossing = [
                (a * group + t, (1 - a) * group + t)
                for a in range(parts)
                for t in range(group)
                if 0 <= t // 2 - direction * distance < outer
            ]
            arrivals.append(
                (direction, distance, True, lax.ppermute(moving, ("parts", "tensor"), crossing))
            )

    block = jax.ShapeDtypeStruct((outer, token_rows, slice_width), jnp.bfloat16)
    x_mine, x_theirs = pl.pallas_call(
        split_kernel, out_shape=(block, block), in_specs=[SMEM, VMEM], out_specs=(VMEM, VMEM),
        name="split_tokens",
    )(x[None], tokens)
    x_far = exchange(x_theirs, 1)
    x_blocks = (x_mine, other_core(x_mine), x_far, other_core(x_far))

    xs = pl.pallas_call(
        interleave_kernel,
        out_shape=jax.ShapeDtypeStruct((group, 2 * token_rows, slice_width // 2), jnp.bfloat16),
        in_specs=[VMEM], out_specs=VMEM, name="pair_columns", compiler_params=LIMIT,
    )(tokens)

    sent = pl.pallas_call(
        functools.partial(gather_kernel, group, down_chunks, up_chunks),
        out_shape=[piece] * group,
        in_specs=[SMEM, ANY, ANY],
        out_specs=[VMEM] * group,
        scratch_shapes=[
            pltpu.VMEM((group, GROUP_ROWS, down_store.shape[1]), jnp.bfloat16),
            pltpu.VMEM((group, GROUP_ROWS, up_store.shape[1]), jnp.bfloat16),
            pltpu.VMEM((down_chunks * 8, LANES), jnp.float32),
            pltpu.SemaphoreType.DMA((2 * group,)),
        ],
        compiler_params=LIMIT,
        name="pick_panels",
    )(rows, down_store, up_store)
    panels = [sent[0]] + [exchange(sent[s], s) for s in range(1, group)]

    owned_groups = ADAPTERS // lax.axis_size("dp") // 8
    down_shape = jax.ShapeDtypeStruct((owned_groups, down_chunks, 8, 1, LANES), jnp.float32)
    up_shape = jax.ShapeDtypeStruct((owned_groups, up_chunks, 8, 1, LANES), jnp.float32)
    down_zero, up_zero = pl.pallas_call(
        zero_kernel, out_shape=(down_shape, up_shape), in_specs=[ANY], out_specs=(ANY, ANY),
        scratch_shapes=[pltpu.VMEM((up_chunks, 8, 1, LANES), jnp.float32), pltpu.SemaphoreType.DMA((2,))],
        compiler_params=LIMIT, name="clear_rows",
    )(sent[0])

    results = pl.pallas_call(
        functools.partial(adapter_kernel, group, down_chunks),
        out_shape=[piece] * group + [jax.ShapeDtypeStruct((token_rows, VALUE_OUTPUTS), jnp.float32)],
        in_specs=[SMEM] + [VMEM] * (2 + group),
        out_specs=[VMEM] * (group + 1),
        scratch_shapes=[pltpu.VMEM((2 * R, VALUE_OUTPUTS), jnp.float32)],
        compiler_params=LIMIT,
        name="adapter",
    )(here, xs, cotangent, *panels)
    terms, lifted = results[:group], results[group]
    back = [terms[0]] + [exchange(terms[s], s) for s in range(1, group)]
    back_core = [other_core(term) for term in back]

    grad_down, grad_up = pl.pallas_call(
        functools.partial(scatter_kernel, 2 * group, down_chunks, up_chunks),
        out_shape=(down_shape, up_shape),
        in_specs=[SMEM, SMEM] + [VMEM] * (2 * group) + [ANY, ANY],
        out_specs=(ANY, ANY),
        input_output_aliases={2 + 2 * group: 0, 3 + 2 * group: 1},
        scratch_shapes=[
            pltpu.VMEM((2 * group, down_chunks, 1, LANES), jnp.float32),
            pltpu.VMEM((2 * group, up_chunks, 1, LANES), jnp.float32),
            pltpu.VMEM((up_chunks, LANES), jnp.float32),
            pltpu.SemaphoreType.DMA(()),
        ],
        compiler_params=LIMIT,
        name="place_rows",
    )((core * (ADAPTERS // lax.axis_size("dp")))[None], jnp.concatenate([rows, rows_core]), *back, *back_core,
      down_zero, up_zero)
    grad_down = grad_down.reshape(owned_groups, down_chunks, 8, LANES).transpose(0, 2, 1, 3)
    grad_up = grad_up.reshape(owned_groups, up_chunks, 8, LANES).transpose(0, 2, 1, 3)

    def base(where, *refs):
        x_refs, w_ref, got = refs[:4], refs[4], refs[5:5 + len(arrivals)]
        tagged = [a[:3] + (ref,) for a, ref in zip(arrivals, got)]
        base_kernel(outer, where, x_refs, w_ref, tagged, *refs[5 + len(arrivals):])

    sums = jax.ShapeDtypeStruct((2 * token_rows, frozen_value.shape[1]), jnp.float32)
    own, other = pl.pallas_call(
        base,
        out_shape=(sums, sums),
        in_specs=[SMEM] + [VMEM] * (5 + len(arrivals)),
        out_specs=(VMEM, VMEM),
        scratch_shapes=[pltpu.VMEM((4 * token_rows, frozen_value.shape[1]), jnp.float32)],
        compiler_params=LIMIT,
        name="frozen_part",
    )(jnp.stack([z, part]), *x_blocks, frozen_value, *[a[3] for a in arrivals])
    columns = own + exchange(other, 1)
    kept, gone = columns[:token_rows], columns[token_rows:]
    got = other_core(gone)
    frozen_output = jnp.where(
        core == 0, jnp.concatenate([kept, got], axis=1), jnp.concatenate([got, kept], axis=1)
    )
    mixed = (frozen_output + lifted).astype(jnp.bfloat16)
    return mixed, grad_down.reshape(owned_groups * 8, -1), grad_up.reshape(owned_groups * 8, -1)


def fits(mesh):
    group, cores, parts = mesh.shape["tensor"], mesh.shape["dp"], mesh.shape["parts"]
    return cores == 2 and parts == 2 and group <= 8 and group & (group - 1) == 0 and R == 8 * group


def body(mesh, tokens, *rest):
    block_adapter = rest[4]
    one_block = block_adapter.shape[0] == 1
    return (fast_body if fits(mesh) and one_block else plain_body)(tokens, *rest)


def solution(mesh):
    placed = (
        P(("parts", "dp", "tensor"), None),
        P(("parts", "dp", "tensor"), None),
        P("tensor", "dp"),
        P("parts", "tensor"),
        P("parts", "tensor"),
        P(("parts", "dp", "tensor")),
        P("parts"),
    )
    return jax.shard_map(
        functools.partial(body, mesh),
        mesh=mesh,
        in_specs=placed,
        out_specs=(
            P(("parts", "dp", "tensor"), None),
            P(("parts", "dp"), "tensor"),
            P(("parts", "dp"), "tensor"),
        ),
        check_vma=False,
    )
```

```python
import functools

import jax
import jax.numpy as jnp
from jax import lax
from jax.experimental import pallas as pl
from jax.experimental.pallas import tpu as pltpu
from jax.sharding import PartitionSpec as P

D = 5120
VALUE_OUTPUTS = 1024
R = 64
ADAPTERS = 256
LANES = 128
GROUP_ROWS = 16

adapter_scale = 2.0
VMEM = pl.BlockSpec(memory_space=pltpu.VMEM)
SMEM = pl.BlockSpec(memory_space=pltpu.SMEM)
ANY = pl.BlockSpec(memory_space=pl.ANY)
LIMIT = pltpu.CompilerParams(vmem_limit_bytes=40 * 1024 * 1024)


def dot(a, b):
    return jnp.dot(a, b, preferred_element_type=jnp.float32)


def dot_t(a, b):
    return lax.dot_general(a, b, (((1,), (1,)), ((), ())), preferred_element_type=jnp.float32)


def t_dot(a, b):
    return lax.dot_general(a, b, (((0,), (0,)), ((), ())), preferred_element_type=jnp.float32)


def fold_rows(left, piece):
    return jnp.dot(left, piece, preferred_element_type=jnp.float32)


def store_rows(requests, adapter_slot):
    table = jnp.arange(adapter_slot.shape[0], dtype=jnp.int32)
    return jnp.sum(jnp.where(requests[:, None] == table[None, :], adapter_slot[None, :], 0), axis=1)


def plain_body(tokens, cotangent, frozen_value, down_store, up_store, block_adapter, adapter_slot):
    token_rows = tokens.shape[0]
    blocks_here = block_adapter.shape[0]
    block_rows = token_rows // blocks_here
    group = lax.axis_size("tensor")
    columns = lax.all_gather(frozen_value, "dp", axis=1, tiled=True)
    frozen_output = fold_rows(tokens, lax.all_gather(columns, "tensor", axis=0, tiled=True))
    requests = lax.all_gather(block_adapter, "tensor", axis=0, tiled=True)
    stored = store_rows(requests, adapter_slot)
    order = stored.reshape(group, blocks_here).T.reshape(-1)
    down_send = jnp.take(down_store, order, axis=0).reshape(blocks_here, group, -1)
    up_send = jnp.take(up_store, order, axis=0).reshape(blocks_here, group, -1)
    down_got = lax.all_to_all(down_send, "tensor", split_axis=1, concat_axis=1, tiled=True)
    up_got = lax.all_to_all(up_send, "tensor", split_axis=1, concat_axis=1, tiled=True)
    down_panel = down_got.reshape(blocks_here, D, R)
    up_panel = up_got.reshape(blocks_here, R, VALUE_OUTPUTS)
    token_blocks = tokens.reshape(blocks_here, block_rows, D)
    grad_blocks = cotangent.reshape(blocks_here, block_rows, VALUE_OUTPUTS)
    down_projected = jnp.einsum(
        "jtd,jdr->jtr", token_blocks, down_panel, preferred_element_type=jnp.float32
    ).astype(jnp.bfloat16)
    up_projected = jnp.einsum(
        "jtr,jrk->jtk", down_projected, up_panel, preferred_element_type=jnp.float32
    )
    mixed = (
        frozen_output + adapter_scale * up_projected.reshape(token_rows, VALUE_OUTPUTS)
    ).astype(jnp.bfloat16)
    down_projected_gradient = (
        adapter_scale
        * jnp.einsum("jtk,jrk->jtr", grad_blocks, up_panel, preferred_element_type=jnp.float32)
    ).astype(jnp.bfloat16)
    down_term = jnp.einsum(
        "jtd,jtr->jdr", token_blocks, down_projected_gradient, preferred_element_type=jnp.float32
    )
    up_weight_gradient = adapter_scale * jnp.einsum(
        "jtr,jtk->jrk", down_projected, grad_blocks, preferred_element_type=jnp.float32
    )
    down_back = lax.all_to_all(
        down_term.reshape(blocks_here, group, -1), "tensor", split_axis=1, concat_axis=1, tiled=True
    )
    up_back = lax.all_to_all(
        up_weight_gradient.reshape(blocks_here, group, -1), "tensor", split_axis=1, concat_axis=1, tiled=True
    )
    down_flat = down_back.reshape(blocks_here * group, -1)
    up_flat = up_back.reshape(blocks_here * group, -1)
    down_table = jax.ops.segment_sum(down_flat, order, num_segments=ADAPTERS)
    up_table = jax.ops.segment_sum(up_flat, order, num_segments=ADAPTERS)
    grad_down = lax.psum_scatter(down_table, "dp", scatter_dimension=0, tiled=True)
    grad_up = lax.psum_scatter(up_table, "dp", scatter_dimension=0, tiled=True)
    return mixed, grad_down, grad_up


def split_kernel(where, x_ref, mine_ref, theirs_ref):
    inner = where[0]
    outer, rows, width = mine_ref.shape
    for k in range(outer):
        own = pl.multiple_of((2 * k + inner) * width, LANES)
        other = pl.multiple_of((2 * k + 1 - inner) * width, LANES)
        mine_ref[k] = x_ref[:, pl.ds(own, width)]
        theirs_ref[k] = x_ref[:, pl.ds(other, width)]


def interleave_kernel(x_ref, xs_ref):
    group, rows2, half = xs_ref.shape
    rows, width = rows2 // 2, 2 * half
    source = lax.broadcasted_iota(jnp.int32, (width, half), 0)
    target = lax.broadcasted_iota(jnp.int32, (width, half), 1)
    even = (source == 2 * target).astype(jnp.bfloat16)
    odd = (source == 2 * target + 1).astype(jnp.bfloat16)
    for k in range(group):
        x = x_ref[:, k * width:(k + 1) * width]
        xs_ref[k, :rows] = dot(x, even).astype(jnp.bfloat16)
        xs_ref[k, rows:] = dot(x, odd).astype(jnp.bfloat16)


def gather_kernel(first, count, down_chunks, up_chunks, rows, down_ref, up_ref, _, *rest):
    outs, (down_buf, up_buf, flat, sems) = rest[:count], rest[count:]
    copies = []
    for s in range(count):
        start = pl.multiple_of((rows[first + s] // GROUP_ROWS) * GROUP_ROWS, GROUP_ROWS)
        a = pltpu.make_async_copy(down_ref.at[pl.ds(start, GROUP_ROWS)], down_buf.at[s], sems.at[2 * s])
        b = pltpu.make_async_copy(up_ref.at[pl.ds(start, GROUP_ROWS)], up_buf.at[s], sems.at[2 * s + 1])
        a.start()
        b.start()
        copies.append((a, b))
    step = 8
    for s in range(count):
        row = rows[first + s] % GROUP_ROWS
        upper = row >= 8
        sub = row % 8
        copies[s][0].wait()
        copies[s][1].wait()

        def pick(buf, lane):
            tile = buf[s, :, pl.ds(pl.multiple_of(lane, LANES), LANES)].astype(jnp.float32)
            return jnp.where(upper, tile[8:], tile[:8])

        def some(i, carry):
            for u in range(step):
                j = i * step + u
                flat[pl.ds(pl.multiple_of(j * 8, 8), 8), :] = pick(down_buf, j * LANES)
            return carry

        lax.fori_loop(0, down_chunks // step, some, 0)
        outs[s][:down_chunks] = flat[pl.ds(sub, down_chunks, stride=8), :].astype(jnp.bfloat16)
        across = up_chunks // 8
        for j in range(up_chunks):
            place = (j % across) * 8 + j // across
            flat[place * 8:place * 8 + 8, :] = pick(up_buf, j * LANES)
        outs[s][down_chunks:] = flat[pl.ds(sub, up_chunks, stride=8), :].astype(jnp.bfloat16)


def zero_kernel(after_ref, down_ref, up_ref, zeros, sems):
    del after_ref
    zeros[...] = jnp.zeros_like(zeros)
    part = zeros.shape[0]
    copies = []
    for ref, sem in ((down_ref, sems.at[0]), (up_ref, sems.at[1])):
        for g in range(ref.shape[0]):
            for c in range(ref.shape[1] // part):
                copies.append(pltpu.make_async_copy(zeros, ref.at[g, pl.ds(c * part, part)], sem))
    for c in copies:
        c.start()
    for c in copies:
        c.wait()


def adapter_kernel(count, down_chunks, where, xs_ref, g_ref, *rest):
    pieces, outs, (lifted_ref, up_panel) = rest[:count], rest[count + 1:2 * count + 1], rest[2 * count + 1:]
    me = where[0]
    rows = g_ref.shape[0]
    across = g_ref.shape[1] // LANES
    total = jnp.zeros((2 * rows, LANES), jnp.float32)
    for s in range(count):
        owner = me ^ s
        total += dot(xs_ref[owner], pieces[s][:down_chunks])
        at = pl.multiple_of(owner * 8, 8)
        for c in range(across):
            block = pieces[s][down_chunks + 8 * c:down_chunks + 8 * c + 8, :].astype(jnp.float32)
            up_panel[pl.ds(at, 8), c * LANES:(c + 1) * LANES] = block
            up_panel[pl.ds(R + at, 8), c * LANES:(c + 1) * LANES] = block
    panel = up_panel[...].astype(jnp.bfloat16)
    left = lax.broadcasted_iota(jnp.int32, (rows, LANES), 1) < R
    inner = total[:rows] + pltpu.roll(total[rows:], R, 1)
    inner = jnp.where(left, inner, 0.0).astype(jnp.bfloat16)
    g = g_ref[...]
    lifted_ref[...] = adapter_scale * dot(inner, panel)
    inner_grad = adapter_scale * dot_t(g, panel)
    diagonal = jnp.concatenate(
        [jnp.where(left, inner_grad, 0.0), jnp.where(left, 0.0, inner_grad)], axis=0
    ).astype(jnp.bfloat16)
    up_term = adapter_scale * t_dot(inner, g)
    up_panel[...] = up_term
    for s in range(count):
        owner = me ^ s
        outs[s][:down_chunks] = t_dot(xs_ref[owner], diagonal).astype(jnp.bfloat16)
        at = pl.multiple_of(owner * 8, 8)
        rows_here = up_panel[pl.ds(at, 8), :]
        up_part = jnp.concatenate(
            [rows_here[:, c * LANES:(c + 1) * LANES] for c in range(across)], axis=0
        )
        outs[s][down_chunks:] = up_part.astype(jnp.bfloat16)


def scatter_kernel(count, down_chunks, up_chunks, first_row, rows, *rest):
    pieces = rest[:count]
    down_out, up_out = rest[count + 2:count + 4]
    down_sum, up_sum, ordered, sem = rest[count + 4:]
    owned_rows = down_out.shape[0] * 8
    across = up_chunks // 8
    slots = []
    for b in range(count):
        slot = jnp.int32(b)
        for e in range(b - 1, -1, -1):
            slot = jnp.where(rows[e] == rows[b], e, slot)
        slots.append(slot)
        down = pieces[b][:down_chunks].astype(jnp.float32).reshape(down_chunks, 1, LANES)
        for c in range(across):
            ordered[pl.ds(c, 8, stride=across), :] = pieces[b][
                down_chunks + 8 * c:down_chunks + 8 * c + 8
            ].astype(jnp.float32)
        up = ordered[...].reshape(up_chunks, 1, LANES)

        @pl.when(slot == b)
        def _():
            down_sum[b] = down
            up_sum[b] = up

        @pl.when(slot != b)
        def _():
            down_sum[slot] += down
            up_sum[slot] += up

    def copies(b):
        local = rows[b] - first_row[0]
        return (
            pltpu.make_async_copy(down_sum.at[b], down_out.at[local // 8, :, local % 8], sem),
            pltpu.make_async_copy(up_sum.at[b], up_out.at[local // 8, :, local % 8], sem),
        )

    def mine(b):
        local = rows[b] - first_row[0]
        return (slots[b] == b) & (local >= 0) & (local < owned_rows)

    for b in range(count):
        @pl.when(mine(b))
        def _():
            for copy in copies(b):
                copy.start()
    for b in range(count):
        @pl.when(mine(b))
        def _():
            for copy in copies(b):
                copy.wait()


def base_kernel(*refs):
    x_refs, w_ref, own_ref, other_ref = refs[:4], refs[4], refs[-2], refs[-1]
    halves, _, width = w_ref.shape
    outer, _, depth = x_refs[0].shape
    rows = own_ref.shape[0]
    total = [0.0] * halves
    for k in range(outer):
        left = jnp.concatenate([ref[k] for ref in x_refs], axis=0)
        for h in range(halves):
            total[h] += dot(left, w_ref[h, k * depth:(k + 1) * depth, :])
    for h in range(halves):
        own_ref[:, h * width:(h + 1) * width] = total[h][:rows]
        other_ref[:, h * width:(h + 1) * width] = total[h][rows:]


def fast_body(tokens, cotangent, frozen_value, down_store, up_store, block_adapter, adapter_slot):
    group, parts = lax.axis_size("tensor"), lax.axis_size("parts")
    outer = group // 2
    token_rows = tokens.shape[0]
    slice_width = D // group
    down_chunks = down_store.shape[1] // LANES
    up_chunks = up_store.shape[1] // LANES
    piece = jax.ShapeDtypeStruct((down_chunks + up_chunks, LANES), jnp.bfloat16)
    me, part, core = lax.axis_index("tensor"), lax.axis_index("parts"), lax.axis_index("dp")
    z, x = me // 2, me % 2
    here = jnp.stack([me, x, z, part])

    def exchange(value, s):
        return lax.ppermute(value, "tensor", [(t, t ^ s) for t in range(group)])

    def other_core(value):
        return lax.ppermute(value, "dp", [(0, 1), (1, 0)])

    row = store_rows(block_adapter, adapter_slot)
    asked = [row] + [exchange(row, s) for s in range(1, group)]
    place = jnp.arange(2 * group, dtype=jnp.int32)
    rows = sum(jnp.where(place[:group] == s, asked[s], 0) for s in range(group))
    rows_core = other_core(rows)

    width = frozen_value.shape[1] // parts
    half = lax.dynamic_slice_in_dim(frozen_value, part * width, width, axis=1)
    lines = [list(range(0, group, 2)), list(range(1, group, 2))]
    half = lax.all_gather(half, "tensor", axis_index_groups=lines, axis=0, tiled=True)
    block = jax.ShapeDtypeStruct((outer, token_rows, slice_width), jnp.bfloat16)
    x_mine, x_theirs = pl.pallas_call(
        split_kernel, out_shape=(block, block), in_specs=[SMEM, VMEM], out_specs=(VMEM, VMEM),
        name="split_tokens",
    )(x[None], tokens)
    x_far = exchange(x_theirs, 1)
    x_blocks = (x_mine, other_core(x_mine), x_far, other_core(x_far))

    xs = pl.pallas_call(
        interleave_kernel,
        out_shape=jax.ShapeDtypeStruct((group, 2 * token_rows, slice_width // 2), jnp.bfloat16),
        in_specs=[VMEM], out_specs=VMEM, name="pair_columns", compiler_params=LIMIT,
    )(tokens)

    def pick(first, count, after):
        return pl.pallas_call(
            functools.partial(gather_kernel, first, count, down_chunks, up_chunks),
            out_shape=[piece] * count,
            in_specs=[SMEM, ANY, ANY, ANY],
            out_specs=[VMEM] * count,
            scratch_shapes=[
                pltpu.VMEM((count, GROUP_ROWS, down_store.shape[1]), jnp.bfloat16),
                pltpu.VMEM((count, GROUP_ROWS, up_store.shape[1]), jnp.bfloat16),
                pltpu.VMEM((down_chunks * 8, LANES), jnp.float32),
                pltpu.SemaphoreType.DMA((2 * count,)),
            ],
            compiler_params=LIMIT,
            name="pick_panels",
        )(rows, down_store, up_store, after)

    sent = pick(0, group // 2, rows)
    sent += pick(group // 2, group // 2, sent[0])
    panels = [sent[0]] + [exchange(sent[s], s) for s in range(1, group)]

    half, _ = lax.optimization_barrier((half, sent[-1]))
    projection = lax.all_gather(half, "parts", axis=0)

    owned_groups = ADAPTERS // lax.axis_size("dp") // 8
    down_shape = jax.ShapeDtypeStruct((owned_groups, down_chunks, 8, 1, LANES), jnp.float32)
    up_shape = jax.ShapeDtypeStruct((owned_groups, up_chunks, 8, 1, LANES), jnp.float32)
    down_zero, up_zero = pl.pallas_call(
        zero_kernel, out_shape=(down_shape, up_shape), in_specs=[ANY], out_specs=(ANY, ANY),
        scratch_shapes=[pltpu.VMEM((up_chunks, 8, 1, LANES), jnp.float32), pltpu.SemaphoreType.DMA((2,))],
        compiler_params=LIMIT, name="clear_rows",
    )(sent[-1])

    results = pl.pallas_call(
        functools.partial(adapter_kernel, group, down_chunks),
        out_shape=[piece] * group + [jax.ShapeDtypeStruct((token_rows, VALUE_OUTPUTS), jnp.float32)],
        in_specs=[SMEM] + [VMEM] * (2 + group) + [ANY],
        out_specs=[VMEM] * (group + 1),
        scratch_shapes=[pltpu.VMEM((2 * R, VALUE_OUTPUTS), jnp.float32)],
        compiler_params=LIMIT,
        name="adapter",
    )(here, xs, cotangent, *panels, down_zero)
    terms, lifted = results[:group], results[group]
    back = [terms[0]] + [exchange(terms[s], s) for s in range(1, group)]
    back_core = [other_core(term) for term in back]

    grad_down, grad_up = pl.pallas_call(
        functools.partial(scatter_kernel, 2 * group, down_chunks, up_chunks),
        out_shape=(down_shape, up_shape),
        in_specs=[SMEM, SMEM] + [VMEM] * (2 * group) + [ANY, ANY],
        out_specs=(ANY, ANY),
        input_output_aliases={2 + 2 * group: 0, 3 + 2 * group: 1},
        scratch_shapes=[
            pltpu.VMEM((2 * group, down_chunks, 1, LANES), jnp.float32),
            pltpu.VMEM((2 * group, up_chunks, 1, LANES), jnp.float32),
            pltpu.VMEM((up_chunks, LANES), jnp.float32),
            pltpu.SemaphoreType.DMA(()),
        ],
        compiler_params=LIMIT,
        name="place_rows",
    )((core * (ADAPTERS // lax.axis_size("dp")))[None], jnp.concatenate([rows, rows_core]), *back, *back_core,
      down_zero, up_zero)
    grad_down = grad_down.reshape(owned_groups, down_chunks, 8, LANES).transpose(0, 2, 1, 3)
    grad_up = grad_up.reshape(owned_groups, up_chunks, 8, LANES).transpose(0, 2, 1, 3)

    sums = jax.ShapeDtypeStruct((2 * token_rows, frozen_value.shape[1]), jnp.float32)
    own, other = pl.pallas_call(
        base_kernel,
        out_shape=(sums, sums),
        in_specs=[VMEM] * 5 + [ANY],
        out_specs=(VMEM, VMEM),
        compiler_params=LIMIT,
        name="frozen_part",
    )(*x_blocks, projection, terms[0])
    columns = own + exchange(other, 1)
    kept, gone = columns[:token_rows], columns[token_rows:]
    got = other_core(gone)
    frozen_output = jnp.where(
        core == 0, jnp.concatenate([kept, got], axis=1), jnp.concatenate([got, kept], axis=1)
    )
    mixed = (frozen_output + lifted).astype(jnp.bfloat16)
    return mixed, grad_down.reshape(owned_groups * 8, -1), grad_up.reshape(owned_groups * 8, -1)


def fits(mesh):
    group, cores, parts = mesh.shape["tensor"], mesh.shape["dp"], mesh.shape["parts"]
    return cores == 2 and parts == 2 and group <= 8 and group & (group - 1) == 0 and R == 8 * group


def body(mesh, tokens, *rest):
    block_adapter = rest[4]
    one_block = block_adapter.shape[0] == 1
    return (fast_body if fits(mesh) and one_block else plain_body)(tokens, *rest)


def solution(mesh):
    placed = (
        P(("parts", "dp", "tensor"), None),
        P(("parts", "dp", "tensor"), None),
        P("tensor", "dp"),
        P("parts", "tensor"),
        P("parts", "tensor"),
        P(("parts", "dp", "tensor")),
        P("parts"),
    )
    return jax.shard_map(
        functools.partial(body, mesh),
        mesh=mesh,
        in_specs=placed,
        out_specs=(
            P(("parts", "dp", "tensor"), None),
            P(("parts", "dp"), "tensor"),
            P(("parts", "dp"), "tensor"),
        ),
        check_vma=False,
    )
```

```python
import functools

import jax
import jax.numpy as jnp
from jax import lax
from jax.experimental import pallas as pl
from jax.experimental.pallas import tpu as pltpu
from jax.sharding import PartitionSpec as P

D = 5120
VALUE_OUTPUTS = 1024
R = 64
ADAPTERS = 256
LANES = 128
GROUP_ROWS = 16

adapter_scale = 2.0
VMEM = pl.BlockSpec(memory_space=pltpu.VMEM)
SMEM = pl.BlockSpec(memory_space=pltpu.SMEM)
ANY = pl.BlockSpec(memory_space=pl.ANY)
LIMIT = pltpu.CompilerParams(vmem_limit_bytes=16 * 1024 * 1024)
WIDE = pltpu.CompilerParams(vmem_limit_bytes=60 * 1024 * 1024)


def dot(a, b):
    return jnp.dot(a, b, preferred_element_type=jnp.float32)


def dot_t(a, b):
    return lax.dot_general(a, b, (((1,), (1,)), ((), ())), preferred_element_type=jnp.float32)


def t_dot(a, b):
    return lax.dot_general(a, b, (((0,), (0,)), ((), ())), preferred_element_type=jnp.float32)


def fold_rows(left, piece):
    return jnp.dot(left, piece, preferred_element_type=jnp.float32)


def store_rows(requests, adapter_slot):
    table = jnp.arange(adapter_slot.shape[0], dtype=jnp.int32)
    return jnp.sum(jnp.where(requests[:, None] == table[None, :], adapter_slot[None, :], 0), axis=1)


def plain_body(tokens, cotangent, frozen_value, down_store, up_store, block_adapter, adapter_slot):
    token_rows = tokens.shape[0]
    blocks_here = block_adapter.shape[0]
    block_rows = token_rows // blocks_here
    group = lax.axis_size("tensor")
    columns = lax.all_gather(frozen_value, "dp", axis=1, tiled=True)
    frozen_output = fold_rows(tokens, lax.all_gather(columns, "tensor", axis=0, tiled=True))
    requests = lax.all_gather(block_adapter, "tensor", axis=0, tiled=True)
    stored = store_rows(requests, adapter_slot)
    order = stored.reshape(group, blocks_here).T.reshape(-1)
    down_send = jnp.take(down_store, order, axis=0).reshape(blocks_here, group, -1)
    up_send = jnp.take(up_store, order, axis=0).reshape(blocks_here, group, -1)
    down_got = lax.all_to_all(down_send, "tensor", split_axis=1, concat_axis=1, tiled=True)
    up_got = lax.all_to_all(up_send, "tensor", split_axis=1, concat_axis=1, tiled=True)
    down_panel = down_got.reshape(blocks_here, D, R)
    up_panel = up_got.reshape(blocks_here, R, VALUE_OUTPUTS)
    token_blocks = tokens.reshape(blocks_here, block_rows, D)
    grad_blocks = cotangent.reshape(blocks_here, block_rows, VALUE_OUTPUTS)
    down_projected = jnp.einsum(
        "jtd,jdr->jtr", token_blocks, down_panel, preferred_element_type=jnp.float32
    ).astype(jnp.bfloat16)
    up_projected = jnp.einsum(
        "jtr,jrk->jtk", down_projected, up_panel, preferred_element_type=jnp.float32
    )
    mixed = (
        frozen_output + adapter_scale * up_projected.reshape(token_rows, VALUE_OUTPUTS)
    ).astype(jnp.bfloat16)
    down_projected_gradient = (
        adapter_scale
        * jnp.einsum("jtk,jrk->jtr", grad_blocks, up_panel, preferred_element_type=jnp.float32)
    ).astype(jnp.bfloat16)
    down_term = jnp.einsum(
        "jtd,jtr->jdr", token_blocks, down_projected_gradient, preferred_element_type=jnp.float32
    )
    up_weight_gradient = adapter_scale * jnp.einsum(
        "jtr,jtk->jrk", down_projected, grad_blocks, preferred_element_type=jnp.float32
    )
    down_back = lax.all_to_all(
        down_term.reshape(blocks_here, group, -1), "tensor", split_axis=1, concat_axis=1, tiled=True
    )
    up_back = lax.all_to_all(
        up_weight_gradient.reshape(blocks_here, group, -1), "tensor", split_axis=1, concat_axis=1, tiled=True
    )
    down_flat = down_back.reshape(blocks_here * group, -1)
    up_flat = up_back.reshape(blocks_here * group, -1)
    down_table = jax.ops.segment_sum(down_flat, order, num_segments=ADAPTERS)
    up_table = jax.ops.segment_sum(up_flat, order, num_segments=ADAPTERS)
    grad_down = lax.psum_scatter(down_table, "dp", scatter_dimension=0, tiled=True)
    grad_up = lax.psum_scatter(up_table, "dp", scatter_dimension=0, tiled=True)
    return mixed, grad_down, grad_up


def split_kernel(where, x_ref, mine_ref, theirs_ref):
    inner = where[0]
    outer, rows, width = mine_ref.shape
    for k in range(outer):
        own = pl.multiple_of((2 * k + inner) * width, LANES)
        other = pl.multiple_of((2 * k + 1 - inner) * width, LANES)
        mine_ref[k] = x_ref[:, pl.ds(own, width)]
        theirs_ref[k] = x_ref[:, pl.ds(other, width)]


def interleave_kernel(x_ref, xs_ref):
    group, rows2, half = xs_ref.shape
    rows, width = rows2 // 2, 2 * half
    source = lax.broadcasted_iota(jnp.int32, (width, half), 0)
    target = lax.broadcasted_iota(jnp.int32, (width, half), 1)
    even = (source == 2 * target).astype(jnp.bfloat16)
    odd = (source == 2 * target + 1).astype(jnp.bfloat16)
    for k in range(group):
        x = x_ref[:, k * width:(k + 1) * width]
        xs_ref[k, :rows] = dot(x, even).astype(jnp.bfloat16)
        xs_ref[k, rows:] = dot(x, odd).astype(jnp.bfloat16)


def gather_kernel(first, count, down_chunks, up_chunks, *refs):
    asked, (down_ref, up_ref, _) = refs[:first + count], refs[first + count:first + count + 3]
    outs, rows_ref = refs[first + count + 3:-8], refs[-8]
    down_buf, up_buf, flat, built, rows, sems, row_sem = refs[-7:]
    for s in range(first + count):
        pltpu.make_async_copy(asked[s], rows.at[s], row_sem).start()
    for s in range(first + count):
        pltpu.make_async_copy(asked[s], rows.at[s], row_sem).wait()
    copies = []
    for s in range(count):
        start = pl.multiple_of((rows[first + s, 0] // GROUP_ROWS) * GROUP_ROWS, GROUP_ROWS)
        a = pltpu.make_async_copy(down_ref.at[pl.ds(start, GROUP_ROWS)], down_buf.at[s], sems.at[3 * s])
        b = pltpu.make_async_copy(up_ref.at[pl.ds(start, GROUP_ROWS)], up_buf.at[s], sems.at[3 * s + 1])
        a.start()
        b.start()
        copies.append((a, b, pltpu.make_async_copy(built.at[s], outs[s], sems.at[3 * s + 2])))
    for s in range(first + count):
        rows_ref[s] = rows[s, 0]
    step = 16
    for s in range(count):
        row = rows[first + s, 0] % GROUP_ROWS
        upper = row >= 8
        sub = row % 8

        def pick(buf, lane):
            tile = buf[s, :, pl.ds(pl.multiple_of(lane, LANES), LANES)].astype(jnp.float32)
            return jnp.where(upper, tile[8:], tile[:8])

        def some(i, carry):
            for u in range(step):
                j = i * step + u
                flat[pl.ds(pl.multiple_of(j * 8, 8), 8), :] = pick(down_buf, j * LANES)
            return carry

        copies[s][0].wait()
        lax.fori_loop(0, down_chunks // step, some, 0)
        built[s, :down_chunks] = flat[pl.ds(sub, down_chunks, stride=8), :].astype(jnp.bfloat16)
        across = up_chunks // 8
        copies[s][1].wait()
        for j in range(up_chunks):
            place = (j % across) * 8 + j // across
            flat[place * 8:place * 8 + 8, :] = pick(up_buf, j * LANES)
        built[s, down_chunks:] = flat[pl.ds(sub, up_chunks, stride=8), :].astype(jnp.bfloat16)
        copies[s][2].start()
    for s in range(count):
        copies[s][2].wait()


def zero_kernel(after_ref, down_ref, up_ref, zeros, sems):
    del after_ref
    zeros[...] = jnp.zeros_like(zeros)
    part = zeros.shape[0]
    copies = []
    for ref, sem in ((down_ref, sems.at[0]), (up_ref, sems.at[1])):
        for g in range(ref.shape[0]):
            for c in range(ref.shape[1] // part):
                copies.append(pltpu.make_async_copy(zeros, ref.at[g, pl.ds(c * part, part)], sem))
    for c in copies:
        c.start()
    for c in copies:
        c.wait()


def adapter_kernel(count, down_chunks, where, xs_ref, g_ref, *rest):
    sources, targets = rest[:count], rest[count + 1:2 * count + 1]
    lifted_ref, up_panel, pieces, outs, sems = rest[2 * count + 1:]
    arriving = [pltpu.make_async_copy(sources[s], pieces.at[s], sems.at[0, s]) for s in range(count)]
    leaving = [pltpu.make_async_copy(outs.at[s], targets[s], sems.at[1, s]) for s in range(count)]
    for copy in arriving:
        copy.start()
    me = where[0]
    rows = g_ref.shape[0]
    across = g_ref.shape[1] // LANES
    total = jnp.zeros((2 * rows, LANES), jnp.float32)
    for s in range(count):
        owner = me ^ s
        arriving[s].wait()
        total += dot(xs_ref[owner], pieces[s, :down_chunks])
        at = pl.multiple_of(owner * 8, 8)
        for c in range(across):
            block = pieces[s, down_chunks + 8 * c:down_chunks + 8 * c + 8, :].astype(jnp.float32)
            up_panel[pl.ds(at, 8), c * LANES:(c + 1) * LANES] = block
            up_panel[pl.ds(R + at, 8), c * LANES:(c + 1) * LANES] = block
    panel = up_panel[...].astype(jnp.bfloat16)
    left = lax.broadcasted_iota(jnp.int32, (rows, LANES), 1) < R
    inner = total[:rows] + pltpu.roll(total[rows:], R, 1)
    inner = jnp.where(left, inner, 0.0).astype(jnp.bfloat16)
    g = g_ref[...]
    lifted_ref[...] = adapter_scale * dot(inner, panel)
    inner_grad = adapter_scale * dot_t(g, panel)
    diagonal = jnp.concatenate(
        [jnp.where(left, inner_grad, 0.0), jnp.where(left, 0.0, inner_grad)], axis=0
    ).astype(jnp.bfloat16)
    up_term = adapter_scale * t_dot(inner, g)
    up_panel[...] = up_term
    for s in range(count):
        owner = me ^ s
        outs[s, :down_chunks] = t_dot(xs_ref[owner], diagonal).astype(jnp.bfloat16)
        at = pl.multiple_of(owner * 8, 8)
        rows_here = up_panel[pl.ds(at, 8), :]
        up_part = jnp.concatenate(
            [rows_here[:, c * LANES:(c + 1) * LANES] for c in range(across)], axis=0
        )
        outs[s, down_chunks:] = up_part.astype(jnp.bfloat16)
        leaving[s].start()
    for copy in leaving:
        copy.wait()


def scatter_kernel(count, down_chunks, up_chunks, first_row, rows_here, rows_core, *rest):
    sources = rest[:count]
    down_out, up_out = rest[count + 2:count + 4]
    pieces, down_sum, up_sum, ordered, arrived, sem = rest[count + 4:]
    owned_rows = down_out.shape[0] * 8
    across = up_chunks // 8
    rows = [(rows_here if b < count // 2 else rows_core)[b % (count // 2)] - first_row[0] for b in range(count)]
    arriving = [pltpu.make_async_copy(sources[b], pieces.at[b], arrived.at[b]) for b in range(count)]
    for copy in arriving:
        copy.start()
    owned = [(row >= 0) & (row < owned_rows) for row in rows]
    slots, final = [], []
    for b in range(count):
        slot, last = jnp.int32(b), jnp.bool_(True)
        for e in range(b - 1, -1, -1):
            slot = jnp.where(rows[e] == rows[b], e, slot)
        for e in range(b + 1, count):
            last = last & (rows[e] != rows[b])
        slots.append(slot)
        final.append(last)

    def copies(b):
        return (
            pltpu.make_async_copy(down_sum.at[slots[b]], down_out.at[rows[b] // 8, :, rows[b] % 8], sem),
            pltpu.make_async_copy(up_sum.at[slots[b]], up_out.at[rows[b] // 8, :, rows[b] % 8], sem),
        )

    for b in range(count):
        arriving[b].wait()

        @pl.when(owned[b])
        def _():
            slot = slots[b]
            down = pieces[b, :down_chunks].astype(jnp.float32).reshape(down_chunks, 1, LANES)
            for c in range(across):
                ordered[pl.ds(c, 8, stride=across), :] = pieces[
                    b, down_chunks + 8 * c:down_chunks + 8 * c + 8
                ].astype(jnp.float32)
            up = ordered[...].reshape(up_chunks, 1, LANES)

            @pl.when(slot == b)
            def _():
                down_sum[b] = down
                up_sum[b] = up

            @pl.when(slot != b)
            def _():
                down_sum[slot] += down
                up_sum[slot] += up

            @pl.when(final[b])
            def _():
                for copy in copies(b):
                    copy.start()

    for b in range(count):
        @pl.when(owned[b] & final[b])
        def _():
            for copy in copies(b):
                copy.wait()


def base_kernel(*refs):
    x_refs, w_refs, own_ref, other_ref = refs[:4], refs[4:6], refs[-2], refs[-1]
    outer, _, depth = x_refs[0].shape
    rows, width = own_ref.shape[0], w_refs[0].shape[1]
    for h, w_ref in enumerate(w_refs):
        total = 0.0
        for k in range(outer):
            left = jnp.concatenate([ref[k] for ref in x_refs], axis=0)
            total += dot(left, w_ref[k * depth:(k + 1) * depth, :])
        own_ref[:, h * width:(h + 1) * width] = total[:rows]
        other_ref[:, h * width:(h + 1) * width] = total[rows:]


def fast_body(tokens, cotangent, frozen_value, down_store, up_store, block_adapter, adapter_slot):
    group, parts = lax.axis_size("tensor"), lax.axis_size("parts")
    outer = group // 2
    token_rows = tokens.shape[0]
    slice_width = D // group
    down_chunks = down_store.shape[1] // LANES
    up_chunks = up_store.shape[1] // LANES
    piece = jax.ShapeDtypeStruct((down_chunks + up_chunks, LANES), jnp.bfloat16)
    me, part, core = lax.axis_index("tensor"), lax.axis_index("parts"), lax.axis_index("dp")
    z, x = me // 2, me % 2
    here = jnp.stack([me, x, z, part])

    def exchange(value, s):
        return lax.ppermute(value, "tensor", [(t, t ^ s) for t in range(group)])

    def other_core(value):
        return lax.ppermute(value, "dp", [(0, 1), (1, 0)])

    def other_part(value):
        return lax.ppermute(value, "parts", [(a, parts - 1 - a) for a in range(parts)])

    row = jnp.broadcast_to(store_rows(block_adapter, adapter_slot), (LANES,))
    asked = [row] + [exchange(row, s) for s in range(1, group)]

    width = frozen_value.shape[1] // parts
    half = lax.dynamic_slice_in_dim(frozen_value, part * width, width, axis=1)
    lines = [list(range(0, group, 2)), list(range(1, group, 2))]
    half = lax.all_gather(half, "tensor", axis_index_groups=lines, axis=0, tiled=True)

    block = jax.ShapeDtypeStruct((outer, token_rows, slice_width), jnp.bfloat16)
    x_mine, x_theirs = pl.pallas_call(
        split_kernel, out_shape=(block, block), in_specs=[SMEM, VMEM], out_specs=(VMEM, VMEM),
        name="split_tokens",
    )(x[None], tokens)
    x_far = exchange(x_theirs, 1)
    y_mine = other_part(x_mine)

    xs = pl.pallas_call(
        interleave_kernel,
        out_shape=jax.ShapeDtypeStruct((group, 2 * token_rows, slice_width // 2), jnp.bfloat16),
        in_specs=[VMEM], out_specs=VMEM, name="pair_columns", compiler_params=LIMIT,
    )(tokens)

    def pick(first, count, after):
        return pl.pallas_call(
            functools.partial(gather_kernel, first, count, down_chunks, up_chunks),
            out_shape=[piece] * count + [jax.ShapeDtypeStruct((first + count,), jnp.int32)],
            in_specs=[ANY] * (first + count + 3),
            out_specs=[ANY] * count + [SMEM],
            scratch_shapes=[
                pltpu.VMEM((count, GROUP_ROWS, down_store.shape[1]), jnp.bfloat16),
                pltpu.VMEM((count, GROUP_ROWS, up_store.shape[1]), jnp.bfloat16),
                pltpu.VMEM((down_chunks * 8, LANES), jnp.float32),
                pltpu.VMEM((count, down_chunks + up_chunks, LANES), jnp.bfloat16),
                pltpu.SMEM((first + count, LANES), jnp.int32),
                pltpu.SemaphoreType.DMA((3 * count,)),
                pltpu.SemaphoreType.DMA(()),
            ],
            compiler_params=WIDE,
            name="pick_panels",
        )(*asked[:first + count], down_store, up_store, after)

    *sent, _ = pick(0, group // 2, row)
    *more, rows = pick(group // 2, group // 2, sent[0])
    sent += more
    panels = [sent[0]] + [exchange(sent[s], s) for s in range(1, group)]
    rows_core = other_core(rows)
    x_far, _ = lax.optimization_barrier((x_far, panels[2]))
    x_blocks = (x_mine, y_mine, x_far, other_part(x_far))

    owned_groups = ADAPTERS // lax.axis_size("dp") // 8
    down_shape = jax.ShapeDtypeStruct((owned_groups, down_chunks, 8, 1, LANES), jnp.float32)
    up_shape = jax.ShapeDtypeStruct((owned_groups, up_chunks, 8, 1, LANES), jnp.float32)
    down_zero, up_zero = pl.pallas_call(
        zero_kernel, out_shape=(down_shape, up_shape), in_specs=[ANY], out_specs=(ANY, ANY),
        scratch_shapes=[pltpu.VMEM((up_chunks, 8, 1, LANES), jnp.float32), pltpu.SemaphoreType.DMA((2,))],
        compiler_params=WIDE, name="clear_rows",
    )(sent[-1])

    results = pl.pallas_call(
        functools.partial(adapter_kernel, group, down_chunks),
        out_shape=[piece] * group + [jax.ShapeDtypeStruct((token_rows, VALUE_OUTPUTS), jnp.float32)],
        in_specs=[SMEM] + [VMEM] * 2 + [ANY] * (group + 1),
        out_specs=[ANY] * group + [VMEM],
        scratch_shapes=[
            pltpu.VMEM((2 * R, VALUE_OUTPUTS), jnp.float32),
            pltpu.VMEM((group,) + piece.shape, jnp.bfloat16),
            pltpu.VMEM((group,) + piece.shape, jnp.bfloat16),
            pltpu.SemaphoreType.DMA((2, group)),
        ],
        compiler_params=LIMIT,
        name="adapter",
    )(here, xs, cotangent, *panels, down_zero)
    terms, lifted = results[:group], results[group]
    back = [terms[0]] + [exchange(terms[s], s) for s in range(1, group)]
    back_core = [other_core(term) for term in back]

    grad_down, grad_up = pl.pallas_call(
        functools.partial(scatter_kernel, 2 * group, down_chunks, up_chunks),
        out_shape=(down_shape, up_shape),
        in_specs=[SMEM] * 3 + [ANY] * (2 * group + 2),
        out_specs=(ANY, ANY),
        input_output_aliases={3 + 2 * group: 0, 4 + 2 * group: 1},
        scratch_shapes=[
            pltpu.VMEM((2 * group,) + piece.shape, jnp.bfloat16),
            pltpu.VMEM((2 * group, down_chunks, 1, LANES), jnp.float32),
            pltpu.VMEM((2 * group, up_chunks, 1, LANES), jnp.float32),
            pltpu.VMEM((up_chunks, LANES), jnp.float32),
            pltpu.SemaphoreType.DMA((2 * group,)),
            pltpu.SemaphoreType.DMA(()),
        ],
        compiler_params=WIDE,
        name="place_rows",
    )((core * (ADAPTERS // lax.axis_size("dp")))[None], rows, rows_core, *back, *back_core,
      down_zero, up_zero)
    grad_down = grad_down.reshape(owned_groups, down_chunks, 8, LANES).transpose(0, 2, 1, 3)
    grad_up = grad_up.reshape(owned_groups, up_chunks, 8, LANES).transpose(0, 2, 1, 3)

    half, _ = lax.optimization_barrier((half, panels[-1]))
    both = (half, other_core(half))
    sums = jax.ShapeDtypeStruct((2 * token_rows, parts * width), jnp.float32)
    own, other = pl.pallas_call(
        base_kernel,
        out_shape=(sums, sums),
        in_specs=[VMEM] * 6 + [ANY],
        out_specs=(VMEM, VMEM),
        compiler_params=LIMIT,
        name="frozen_part",
    )(*x_blocks, *both, terms[0])
    columns = own + exchange(other, 1)
    kept, gone = columns[:token_rows], columns[token_rows:]
    got = other_part(gone)
    quarters = [[c[:, :width], c[:, width:]] for c in (kept, got)]

    def pick_quarter(c, a):
        first = quarters[a][0] if c == 0 else quarters[a][1]
        second = quarters[a][1] if c == 0 else quarters[a][0]
        return jnp.where(core == 0, first, second)

    def columns_of(c):
        low, high = pick_quarter(c, 0), pick_quarter(c, 1)
        return jnp.where(part == 0, low, high), jnp.where(part == 0, high, low)

    frozen_output = jnp.concatenate(columns_of(0) + columns_of(1), axis=1)
    mixed = (frozen_output + lifted).astype(jnp.bfloat16)
    return mixed, grad_down.reshape(owned_groups * 8, -1), grad_up.reshape(owned_groups * 8, -1)


def fits(mesh):
    group, cores, parts = mesh.shape["tensor"], mesh.shape["dp"], mesh.shape["parts"]
    return cores == 2 and parts == 2 and group <= 8 and group & (group - 1) == 0 and R == 8 * group


def body(mesh, tokens, *rest):
    block_adapter = rest[4]
    one_block = block_adapter.shape[0] == 1
    return (fast_body if fits(mesh) and one_block else plain_body)(tokens, *rest)


def solution(mesh):
    placed = (
        P(("parts", "dp", "tensor"), None),
        P(("parts", "dp", "tensor"), None),
        P("tensor", "dp"),
        P("parts", "tensor"),
        P("parts", "tensor"),
        P(("parts", "dp", "tensor")),
        P("parts"),
    )
    return jax.shard_map(
        functools.partial(body, mesh),
        mesh=mesh,
        in_specs=placed,
        out_specs=(
            P(("parts", "dp", "tensor"), None),
            P(("parts", "dp"), "tensor"),
            P(("parts", "dp"), "tensor"),
        ),
        check_vma=False,
    )
```

```python
import functools

import jax
import jax.numpy as jnp
from jax import lax
from jax.experimental import pallas as pl
from jax.experimental.pallas import tpu as pltpu
from jax.sharding import PartitionSpec as P

D = 5120
VALUE_OUTPUTS = 1024
R = 64
ADAPTERS = 256
LANES = 128
GROUP_ROWS = 16

adapter_scale = 2.0
VMEM = pl.BlockSpec(memory_space=pltpu.VMEM)
SMEM = pl.BlockSpec(memory_space=pltpu.SMEM)
ANY = pl.BlockSpec(memory_space=pl.ANY)
LIMIT = pltpu.CompilerParams(vmem_limit_bytes=16 * 1024 * 1024)
WIDE = pltpu.CompilerParams(vmem_limit_bytes=60 * 1024 * 1024)


def dot(a, b):
    return jnp.dot(a, b, preferred_element_type=jnp.float32)


def dot_t(a, b):
    return lax.dot_general(a, b, (((1,), (1,)), ((), ())), preferred_element_type=jnp.float32)


def t_dot(a, b):
    return lax.dot_general(a, b, (((0,), (0,)), ((), ())), preferred_element_type=jnp.float32)


def fold_rows(left, piece):
    return jnp.dot(left, piece, preferred_element_type=jnp.float32)


def store_rows(requests, adapter_slot):
    table = jnp.arange(adapter_slot.shape[0], dtype=jnp.int32)
    return jnp.sum(jnp.where(requests[:, None] == table[None, :], adapter_slot[None, :], 0), axis=1)


def plain_body(tokens, cotangent, frozen_value, down_store, up_store, block_adapter, adapter_slot):
    token_rows = tokens.shape[0]
    blocks_here = block_adapter.shape[0]
    block_rows = token_rows // blocks_here
    group = lax.axis_size("tensor")
    columns = lax.all_gather(frozen_value, "dp", axis=1, tiled=True)
    frozen_output = fold_rows(tokens, lax.all_gather(columns, "tensor", axis=0, tiled=True))
    requests = lax.all_gather(block_adapter, "tensor", axis=0, tiled=True)
    stored = store_rows(requests, adapter_slot)
    order = stored.reshape(group, blocks_here).T.reshape(-1)
    down_send = jnp.take(down_store, order, axis=0).reshape(blocks_here, group, -1)
    up_send = jnp.take(up_store, order, axis=0).reshape(blocks_here, group, -1)
    down_got = lax.all_to_all(down_send, "tensor", split_axis=1, concat_axis=1, tiled=True)
    up_got = lax.all_to_all(up_send, "tensor", split_axis=1, concat_axis=1, tiled=True)
    down_panel = down_got.reshape(blocks_here, D, R)
    up_panel = up_got.reshape(blocks_here, R, VALUE_OUTPUTS)
    token_blocks = tokens.reshape(blocks_here, block_rows, D)
    grad_blocks = cotangent.reshape(blocks_here, block_rows, VALUE_OUTPUTS)
    down_projected = jnp.einsum(
        "jtd,jdr->jtr", token_blocks, down_panel, preferred_element_type=jnp.float32
    ).astype(jnp.bfloat16)
    up_projected = jnp.einsum(
        "jtr,jrk->jtk", down_projected, up_panel, preferred_element_type=jnp.float32
    )
    mixed = (
        frozen_output + adapter_scale * up_projected.reshape(token_rows, VALUE_OUTPUTS)
    ).astype(jnp.bfloat16)
    down_projected_gradient = (
        adapter_scale
        * jnp.einsum("jtk,jrk->jtr", grad_blocks, up_panel, preferred_element_type=jnp.float32)
    ).astype(jnp.bfloat16)
    down_term = jnp.einsum(
        "jtd,jtr->jdr", token_blocks, down_projected_gradient, preferred_element_type=jnp.float32
    )
    up_weight_gradient = adapter_scale * jnp.einsum(
        "jtr,jtk->jrk", down_projected, grad_blocks, preferred_element_type=jnp.float32
    )
    down_back = lax.all_to_all(
        down_term.reshape(blocks_here, group, -1), "tensor", split_axis=1, concat_axis=1, tiled=True
    )
    up_back = lax.all_to_all(
        up_weight_gradient.reshape(blocks_here, group, -1), "tensor", split_axis=1, concat_axis=1, tiled=True
    )
    down_flat = down_back.reshape(blocks_here * group, -1)
    up_flat = up_back.reshape(blocks_here * group, -1)
    down_table = jax.ops.segment_sum(down_flat, order, num_segments=ADAPTERS)
    up_table = jax.ops.segment_sum(up_flat, order, num_segments=ADAPTERS)
    grad_down = lax.psum_scatter(down_table, "dp", scatter_dimension=0, tiled=True)
    grad_up = lax.psum_scatter(up_table, "dp", scatter_dimension=0, tiled=True)
    return mixed, grad_down, grad_up


def split_kernel(where, x_ref, mine_ref, theirs_ref):
    inner = where[0]
    outer, rows, width = mine_ref.shape
    for k in range(outer):
        own = pl.multiple_of((2 * k + inner) * width, LANES)
        other = pl.multiple_of((2 * k + 1 - inner) * width, LANES)
        mine_ref[k] = x_ref[:, pl.ds(own, width)]
        theirs_ref[k] = x_ref[:, pl.ds(other, width)]


def interleave_kernel(x_ref, xs_ref):
    group, rows2, half = xs_ref.shape
    rows, width = rows2 // 2, 2 * half
    source = lax.broadcasted_iota(jnp.int32, (width, half), 0)
    target = lax.broadcasted_iota(jnp.int32, (width, half), 1)
    even = (source == 2 * target).astype(jnp.bfloat16)
    odd = (source == 2 * target + 1).astype(jnp.bfloat16)
    for k in range(group):
        x = x_ref[:, k * width:(k + 1) * width]
        xs_ref[k, :rows] = dot(x, even).astype(jnp.bfloat16)
        xs_ref[k, rows:] = dot(x, odd).astype(jnp.bfloat16)


def gather_kernel(count, down_chunks, up_chunks, where, *refs):
    asked, (down_ref, up_ref, out_ref, rows_ref) = refs[:count], refs[count:count + 4]
    down_buf, up_buf, flat, built, rows, sems, row_sem = refs[count + 4:]
    me = where[0]
    for s in range(count):
        pltpu.make_async_copy(asked[s], rows.at[s], row_sem).start()
    for s in range(count):
        pltpu.make_async_copy(asked[s], rows.at[s], row_sem).wait()
    copies = []
    for s in range(count):
        start = pl.multiple_of((rows[s, 0] // GROUP_ROWS) * GROUP_ROWS, GROUP_ROWS)
        a = pltpu.make_async_copy(down_ref.at[pl.ds(start, GROUP_ROWS)], down_buf.at[s], sems.at[3 * s])
        b = pltpu.make_async_copy(up_ref.at[pl.ds(start, GROUP_ROWS)], up_buf.at[s], sems.at[3 * s + 1])
        a.start()
        b.start()
        copies.append((a, b, pltpu.make_async_copy(built.at[s], out_ref.at[me ^ s], sems.at[3 * s + 2])))
    for s in range(count):
        rows_ref[me ^ s] = rows[s, 0]
    step = 16
    for s in range(count):
        row = rows[s, 0] % GROUP_ROWS
        upper = row >= 8
        sub = row % 8

        def pick(buf, lane):
            tile = buf[s, :, pl.ds(pl.multiple_of(lane, LANES), LANES)].astype(jnp.float32)
            return jnp.where(upper, tile[8:], tile[:8])

        def some(i, carry):
            for u in range(step):
                j = i * step + u
                flat[pl.ds(pl.multiple_of(j * 8, 8), 8), :] = pick(down_buf, j * LANES)
            return carry

        copies[s][0].wait()
        lax.fori_loop(0, down_chunks // step, some, 0)
        built[s, :down_chunks] = flat[pl.ds(sub, down_chunks, stride=8), :].astype(jnp.bfloat16)
        across = up_chunks // 8
        copies[s][1].wait()
        for j in range(up_chunks):
            place = (j % across) * 8 + j // across
            flat[place * 8:place * 8 + 8, :] = pick(up_buf, j * LANES)
        built[s, down_chunks:] = flat[pl.ds(sub, up_chunks, stride=8), :].astype(jnp.bfloat16)
        copies[s][2].start()
    for s in range(count):
        copies[s][2].wait()


def zero_kernel(after_ref, down_ref, up_ref, done_ref, zeros, sems):
    del after_ref
    done_ref[0] = 0
    zeros[...] = jnp.zeros_like(zeros)
    part = zeros.shape[0]
    copies = []
    for ref, sem in ((down_ref, sems.at[0]), (up_ref, sems.at[1])):
        for g in range(ref.shape[0]):
            for c in range(ref.shape[1] // part):
                copies.append(pltpu.make_async_copy(zeros, ref.at[g, pl.ds(c * part, part)], sem))
    for c in copies:
        c.start()
    for c in copies:
        c.wait()


def adapter_kernel(count, down_chunks, xs_ref, g_ref, pieces, _, out_ref, lifted_ref, up_panel):
    rows = g_ref.shape[0]
    across = g_ref.shape[1] // LANES
    total = jnp.zeros((2 * rows, LANES), jnp.float32)
    for t in range(count):
        total += dot(xs_ref[t], pieces[t, :down_chunks])
        for c in range(across):
            block = pieces[t, down_chunks + 8 * c:down_chunks + 8 * c + 8, :].astype(jnp.float32)
            up_panel[8 * t:8 * t + 8, c * LANES:(c + 1) * LANES] = block
            up_panel[R + 8 * t:R + 8 * t + 8, c * LANES:(c + 1) * LANES] = block
    panel = up_panel[...].astype(jnp.bfloat16)
    left = lax.broadcasted_iota(jnp.int32, (rows, LANES), 1) < R
    inner = total[:rows] + pltpu.roll(total[rows:], R, 1)
    inner = jnp.where(left, inner, 0.0).astype(jnp.bfloat16)
    g = g_ref[...]
    lifted_ref[...] = adapter_scale * dot(inner, panel)
    inner_grad = adapter_scale * dot_t(g, panel)
    diagonal = jnp.concatenate(
        [jnp.where(left, inner_grad, 0.0), jnp.where(left, 0.0, inner_grad)], axis=0
    ).astype(jnp.bfloat16)
    up_term = adapter_scale * t_dot(inner, g)
    for t in range(count):
        out_ref[t, :down_chunks] = t_dot(xs_ref[t], diagonal).astype(jnp.bfloat16)
        up_part = jnp.concatenate(
            [up_term[8 * t:8 * t + 8, c * LANES:(c + 1) * LANES] for c in range(across)], axis=0
        )
        out_ref[t, down_chunks:] = up_part.astype(jnp.bfloat16)


def scatter_kernel(count, down_chunks, up_chunks, first_row, rows_here, rows_core, *rest):
    sources, (down_out, up_out) = rest[:2], rest[4:6]
    pieces, down_sum, up_sum, ordered, arrived, sem = rest[6:]
    half = count // 2
    owned_rows = down_out.shape[0] * 8
    across = up_chunks // 8
    rows = [(rows_here if b < half else rows_core)[b % half] - first_row[0] for b in range(count)]
    arriving = [pltpu.make_async_copy(sources[b // half].at[b % half], pieces.at[b], arrived.at[b]) for b in range(count)]
    for copy in arriving:
        copy.start()
    owned = [(row >= 0) & (row < owned_rows) for row in rows]
    slots, final = [], []
    for b in range(count):
        slot, last = jnp.int32(b), jnp.bool_(True)
        for e in range(b - 1, -1, -1):
            slot = jnp.where(rows[e] == rows[b], e, slot)
        for e in range(b + 1, count):
            last = last & (rows[e] != rows[b])
        slots.append(slot)
        final.append(last)

    def copies(b):
        return (
            pltpu.make_async_copy(down_sum.at[slots[b]], down_out.at[rows[b] // 8, :, rows[b] % 8], sem),
            pltpu.make_async_copy(up_sum.at[slots[b]], up_out.at[rows[b] // 8, :, rows[b] % 8], sem),
        )

    for b in range(count):
        arriving[b].wait()

        @pl.when(owned[b])
        def _():
            slot = slots[b]
            down = pieces[b, :down_chunks].astype(jnp.float32).reshape(down_chunks, 1, LANES)
            for c in range(across):
                ordered[pl.ds(c, 8, stride=across), :] = pieces[
                    b, down_chunks + 8 * c:down_chunks + 8 * c + 8
                ].astype(jnp.float32)
            up = ordered[...].reshape(up_chunks, 1, LANES)

            @pl.when(slot == b)
            def _():
                down_sum[b] = down
                up_sum[b] = up

            @pl.when(slot != b)
            def _():
                down_sum[slot] += down
                up_sum[slot] += up

            @pl.when(final[b])
            def _():
                for copy in copies(b):
                    copy.start()

    for b in range(count):
        @pl.when(owned[b] & final[b])
        def _():
            for copy in copies(b):
                copy.wait()


def base_kernel(*refs):
    x_refs, w_refs, own_ref, other_ref = refs[:4], refs[4:6], refs[-2], refs[-1]
    outer, _, depth = x_refs[0].shape
    rows, width = own_ref.shape[0], w_refs[0].shape[1]
    for h, w_ref in enumerate(w_refs):
        total = 0.0
        for k in range(outer):
            left = jnp.concatenate([ref[k] for ref in x_refs], axis=0)
            total += dot(left, w_ref[k * depth:(k + 1) * depth, :])
        own_ref[:, h * width:(h + 1) * width] = total[:rows]
        other_ref[:, h * width:(h + 1) * width] = total[rows:]


def fast_body(tokens, cotangent, frozen_value, down_store, up_store, block_adapter, adapter_slot):
    group, parts = lax.axis_size("tensor"), lax.axis_size("parts")
    outer = group // 2
    token_rows = tokens.shape[0]
    slice_width = D // group
    down_chunks = down_store.shape[1] // LANES
    up_chunks = up_store.shape[1] // LANES
    me, part, core = lax.axis_index("tensor"), lax.axis_index("parts"), lax.axis_index("dp")
    x = me % 2

    def exchange(value, s):
        return lax.ppermute(value, "tensor", [(t, t ^ s) for t in range(group)])

    def other_core(value):
        return lax.ppermute(value, "dp", [(0, 1), (1, 0)])

    def other_part(value):
        return lax.ppermute(value, "parts", [(a, parts - 1 - a) for a in range(parts)])

    row = jnp.broadcast_to(store_rows(block_adapter, adapter_slot), (LANES,))
    asked = [row] + [exchange(row, s) for s in range(1, group)]

    width = frozen_value.shape[1] // parts
    half = lax.dynamic_slice_in_dim(frozen_value, part * width, width, axis=1)
    lines = [list(range(0, group, 2)), list(range(1, group, 2))]
    half = lax.all_gather(half, "tensor", axis_index_groups=lines, axis=0, tiled=True)

    block = jax.ShapeDtypeStruct((outer, token_rows, slice_width), jnp.bfloat16)
    x_mine, x_theirs = pl.pallas_call(
        split_kernel, out_shape=(block, block), in_specs=[SMEM, VMEM], out_specs=(VMEM, VMEM),
        name="split_tokens",
    )(x[None], tokens)
    x_far = exchange(x_theirs, 1)
    y_mine = other_part(x_mine)

    xs = pl.pallas_call(
        interleave_kernel,
        out_shape=jax.ShapeDtypeStruct((group, 2 * token_rows, slice_width // 2), jnp.bfloat16),
        in_specs=[VMEM], out_specs=VMEM, name="pair_columns", compiler_params=LIMIT,
    )(tokens)

    pieces = jax.ShapeDtypeStruct((group, down_chunks + up_chunks, LANES), jnp.bfloat16)
    sent, rows = pl.pallas_call(
        functools.partial(gather_kernel, group, down_chunks, up_chunks),
        out_shape=(pieces, jax.ShapeDtypeStruct((group,), jnp.int32)),
        in_specs=[SMEM] + [ANY] * (group + 2),
        out_specs=(ANY, SMEM),
        scratch_shapes=[
            pltpu.VMEM((group, GROUP_ROWS, down_store.shape[1]), jnp.bfloat16),
            pltpu.VMEM((group, GROUP_ROWS, up_store.shape[1]), jnp.bfloat16),
            pltpu.VMEM((down_chunks * 8, LANES), jnp.float32),
            pltpu.VMEM(pieces.shape, jnp.bfloat16),
            pltpu.SMEM((group, LANES), jnp.int32),
            pltpu.SemaphoreType.DMA((3 * group,)),
            pltpu.SemaphoreType.DMA(()),
        ],
        compiler_params=WIDE,
        name="pick_panels",
    )(me[None], *asked, down_store, up_store)
    panels = lax.all_to_all(sent, "tensor", 0, 0)
    rows_core = other_core(rows)
    x_far, _ = lax.optimization_barrier((x_far, sent))
    x_blocks = (x_mine, y_mine, x_far, other_part(x_far))

    owned_groups = ADAPTERS // lax.axis_size("dp") // 8
    down_shape = jax.ShapeDtypeStruct((owned_groups, down_chunks, 8, 1, LANES), jnp.float32)
    up_shape = jax.ShapeDtypeStruct((owned_groups, up_chunks, 8, 1, LANES), jnp.float32)
    down_zero, up_zero, cleared = pl.pallas_call(
        zero_kernel, out_shape=(down_shape, up_shape, jax.ShapeDtypeStruct((1,), jnp.int32)),
        in_specs=[ANY], out_specs=(ANY, ANY, SMEM),
        scratch_shapes=[pltpu.VMEM((up_chunks, 8, 1, LANES), jnp.float32), pltpu.SemaphoreType.DMA((2,))],
        compiler_params=WIDE, name="clear_rows",
    )(sent)

    terms, lifted = pl.pallas_call(
        functools.partial(adapter_kernel, group, down_chunks),
        out_shape=(pieces, jax.ShapeDtypeStruct((token_rows, VALUE_OUTPUTS), jnp.float32)),
        in_specs=[VMEM] * 3 + [SMEM],
        out_specs=(VMEM, VMEM),
        scratch_shapes=[pltpu.VMEM((2 * R, VALUE_OUTPUTS), jnp.float32)],
        compiler_params=LIMIT,
        name="adapter",
    )(xs, cotangent, panels, cleared)
    half, _ = lax.optimization_barrier((half, panels))
    both = (half, other_core(half))
    sums = jax.ShapeDtypeStruct((2 * token_rows, parts * width), jnp.float32)
    own, other = pl.pallas_call(
        base_kernel,
        out_shape=(sums, sums),
        in_specs=[VMEM] * 6 + [ANY],
        out_specs=(VMEM, VMEM),
        compiler_params=LIMIT,
        name="frozen_part",
    )(*x_blocks, *both, terms)
    terms, other = lax.optimization_barrier((terms, other))
    far = exchange(other, 1)
    back = lax.all_to_all(terms, "tensor", 0, 0)
    back_core = other_core(back)

    grad_down, grad_up = pl.pallas_call(
        functools.partial(scatter_kernel, 2 * group, down_chunks, up_chunks),
        out_shape=(down_shape, up_shape),
        in_specs=[SMEM] * 3 + [ANY] * 4,
        out_specs=(ANY, ANY),
        input_output_aliases={5: 0, 6: 1},
        scratch_shapes=[
            pltpu.VMEM((2 * group,) + pieces.shape[1:], jnp.bfloat16),
            pltpu.VMEM((2 * group, down_chunks, 1, LANES), jnp.float32),
            pltpu.VMEM((2 * group, up_chunks, 1, LANES), jnp.float32),
            pltpu.VMEM((up_chunks, LANES), jnp.float32),
            pltpu.SemaphoreType.DMA((2 * group,)),
            pltpu.SemaphoreType.DMA(()),
        ],
        compiler_params=WIDE,
        name="place_rows",
    )((core * (ADAPTERS // lax.axis_size("dp")))[None], rows, rows_core, back, back_core,
      down_zero, up_zero)
    grad_down = grad_down.reshape(owned_groups, down_chunks, 8, LANES).transpose(0, 2, 1, 3)
    grad_up = grad_up.reshape(owned_groups, up_chunks, 8, LANES).transpose(0, 2, 1, 3)

    columns = own + far
    kept, gone = columns[:token_rows], columns[token_rows:]
    got = other_part(gone)
    quarters = [[c[:, :width], c[:, width:]] for c in (kept, got)]

    def pick_quarter(c, a):
        first = quarters[a][0] if c == 0 else quarters[a][1]
        second = quarters[a][1] if c == 0 else quarters[a][0]
        return jnp.where(core == 0, first, second)

    def columns_of(c):
        low, high = pick_quarter(c, 0), pick_quarter(c, 1)
        return jnp.where(part == 0, low, high), jnp.where(part == 0, high, low)

    frozen_output = jnp.concatenate(columns_of(0) + columns_of(1), axis=1)
    mixed = (frozen_output + lifted).astype(jnp.bfloat16)
    return mixed, grad_down.reshape(owned_groups * 8, -1), grad_up.reshape(owned_groups * 8, -1)


def fits(mesh):
    group, cores, parts = mesh.shape["tensor"], mesh.shape["dp"], mesh.shape["parts"]
    return cores == 2 and parts == 2 and group <= 8 and group & (group - 1) == 0 and R == 8 * group


def body(mesh, tokens, *rest):
    block_adapter = rest[4]
    one_block = block_adapter.shape[0] == 1
    return (fast_body if fits(mesh) and one_block else plain_body)(tokens, *rest)


def solution(mesh):
    placed = (
        P(("parts", "dp", "tensor"), None),
        P(("parts", "dp", "tensor"), None),
        P("tensor", "dp"),
        P("parts", "tensor"),
        P("parts", "tensor"),
        P(("parts", "dp", "tensor")),
        P("parts"),
    )
    return jax.shard_map(
        functools.partial(body, mesh),
        mesh=mesh,
        in_specs=placed,
        out_specs=(
            P(("parts", "dp", "tensor"), None),
            P(("parts", "dp"), "tensor"),
            P(("parts", "dp"), "tensor"),
        ),
        check_vma=False,
    )
```

```python
import functools

import jax
import jax.numpy as jnp
from jax import lax
from jax.experimental import pallas as pl
from jax.experimental.pallas import tpu as pltpu
from jax.sharding import PartitionSpec as P

D = 5120
VALUE_OUTPUTS = 1024
R = 64
ADAPTERS = 256
LANES = 128
GROUP_ROWS = 16

adapter_scale = 2.0
VMEM = pl.BlockSpec(memory_space=pltpu.VMEM)
SMEM = pl.BlockSpec(memory_space=pltpu.SMEM)
ANY = pl.BlockSpec(memory_space=pl.ANY)
LIMIT = pltpu.CompilerParams(vmem_limit_bytes=16 * 1024 * 1024)
WIDE = pltpu.CompilerParams(vmem_limit_bytes=60 * 1024 * 1024)


def dot(a, b):
    return jnp.dot(a, b, preferred_element_type=jnp.float32)


def dot_t(a, b):
    return lax.dot_general(a, b, (((1,), (1,)), ((), ())), preferred_element_type=jnp.float32)


def t_dot(a, b):
    return lax.dot_general(a, b, (((0,), (0,)), ((), ())), preferred_element_type=jnp.float32)


def fold_rows(left, piece):
    return jnp.dot(left, piece, preferred_element_type=jnp.float32)


def store_rows(requests, adapter_slot):
    table = jnp.arange(adapter_slot.shape[0], dtype=jnp.int32)
    return jnp.sum(jnp.where(requests[:, None] == table[None, :], adapter_slot[None, :], 0), axis=1)


def plain_body(tokens, cotangent, frozen_value, down_store, up_store, block_adapter, adapter_slot):
    token_rows = tokens.shape[0]
    blocks_here = block_adapter.shape[0]
    block_rows = token_rows // blocks_here
    group = lax.axis_size("tensor")
    columns = lax.all_gather(frozen_value, "dp", axis=1, tiled=True)
    frozen_output = fold_rows(tokens, lax.all_gather(columns, "tensor", axis=0, tiled=True))
    requests = lax.all_gather(block_adapter, "tensor", axis=0, tiled=True)
    stored = store_rows(requests, adapter_slot)
    order = stored.reshape(group, blocks_here).T.reshape(-1)
    down_send = jnp.take(down_store, order, axis=0).reshape(blocks_here, group, -1)
    up_send = jnp.take(up_store, order, axis=0).reshape(blocks_here, group, -1)
    down_got = lax.all_to_all(down_send, "tensor", split_axis=1, concat_axis=1, tiled=True)
    up_got = lax.all_to_all(up_send, "tensor", split_axis=1, concat_axis=1, tiled=True)
    down_panel = down_got.reshape(blocks_here, D, R)
    up_panel = up_got.reshape(blocks_here, R, VALUE_OUTPUTS)
    token_blocks = tokens.reshape(blocks_here, block_rows, D)
    grad_blocks = cotangent.reshape(blocks_here, block_rows, VALUE_OUTPUTS)
    down_projected = jnp.einsum(
        "jtd,jdr->jtr", token_blocks, down_panel, preferred_element_type=jnp.float32
    ).astype(jnp.bfloat16)
    up_projected = jnp.einsum(
        "jtr,jrk->jtk", down_projected, up_panel, preferred_element_type=jnp.float32
    )
    mixed = (
        frozen_output + adapter_scale * up_projected.reshape(token_rows, VALUE_OUTPUTS)
    ).astype(jnp.bfloat16)
    down_projected_gradient = (
        adapter_scale
        * jnp.einsum("jtk,jrk->jtr", grad_blocks, up_panel, preferred_element_type=jnp.float32)
    ).astype(jnp.bfloat16)
    down_term = jnp.einsum(
        "jtd,jtr->jdr", token_blocks, down_projected_gradient, preferred_element_type=jnp.float32
    )
    up_weight_gradient = adapter_scale * jnp.einsum(
        "jtr,jtk->jrk", down_projected, grad_blocks, preferred_element_type=jnp.float32
    )
    down_back = lax.all_to_all(
        down_term.reshape(blocks_here, group, -1), "tensor", split_axis=1, concat_axis=1, tiled=True
    )
    up_back = lax.all_to_all(
        up_weight_gradient.reshape(blocks_here, group, -1), "tensor", split_axis=1, concat_axis=1, tiled=True
    )
    down_flat = down_back.reshape(blocks_here * group, -1)
    up_flat = up_back.reshape(blocks_here * group, -1)
    down_table = jax.ops.segment_sum(down_flat, order, num_segments=ADAPTERS)
    up_table = jax.ops.segment_sum(up_flat, order, num_segments=ADAPTERS)
    grad_down = lax.psum_scatter(down_table, "dp", scatter_dimension=0, tiled=True)
    grad_up = lax.psum_scatter(up_table, "dp", scatter_dimension=0, tiled=True)
    return mixed, grad_down, grad_up


def split_kernel(where, x_ref, mine_ref, theirs_ref, done_ref):
    done_ref[0] = 0
    inner = where[0]
    outer, rows, width = mine_ref.shape
    for k in range(outer):
        own = pl.multiple_of((2 * k + inner) * width, LANES)
        other = pl.multiple_of((2 * k + 1 - inner) * width, LANES)
        mine_ref[k] = x_ref[:, pl.ds(own, width)]
        theirs_ref[k] = x_ref[:, pl.ds(other, width)]


def interleave_kernel(x_ref, xs_ref):
    group, rows2, half = xs_ref.shape
    rows, width = rows2 // 2, 2 * half
    source = lax.broadcasted_iota(jnp.int32, (width, half), 0)
    target = lax.broadcasted_iota(jnp.int32, (width, half), 1)
    even = (source == 2 * target).astype(jnp.bfloat16)
    odd = (source == 2 * target + 1).astype(jnp.bfloat16)
    for k in range(group):
        x = x_ref[:, k * width:(k + 1) * width]
        xs_ref[k, :rows] = dot(x, even).astype(jnp.bfloat16)
        xs_ref[k, rows:] = dot(x, odd).astype(jnp.bfloat16)


def gather_kernel(count, down_chunks, up_chunks, where, after, *refs):
    del after
    asked, (down_ref, up_ref, out_ref, rows_ref) = refs[:count], refs[count:count + 4]
    down_buf, up_buf, flat, built, rows, sems, row_sem = refs[count + 4:]
    me = where[0]
    across = up_chunks // 8
    for s in range(count):
        pltpu.make_async_copy(asked[s], rows.at[s], row_sem).start()
    for s in range(count):
        pltpu.make_async_copy(asked[s], rows.at[s], row_sem).wait()

    def copies(s):
        start = pl.multiple_of((rows[s, 0] // GROUP_ROWS) * GROUP_ROWS, GROUP_ROWS)
        return (
            pltpu.make_async_copy(down_ref.at[pl.ds(start, GROUP_ROWS)], down_buf.at[s], sems.at[0, s]),
            pltpu.make_async_copy(up_ref.at[pl.ds(start, GROUP_ROWS)], up_buf.at[s], sems.at[1, s]),
            pltpu.make_async_copy(built.at[s], out_ref.at[me ^ s], sems.at[2, s]),
        )

    for s in range(count):
        down, up, _ = copies(s)
        down.start()
        up.start()
        rows_ref[me ^ s] = rows[s, 0]

    def one(s, carry):
        row = rows[s, 0] % GROUP_ROWS
        upper = row >= 8
        sub = row % 8

        def pick(buf, lane):
            tile = buf[s, :, lane:lane + LANES].astype(jnp.float32)
            return jnp.where(upper, tile[8:], tile[:8])

        down, up, leave = copies(s)
        up.wait()
        for j in range(up_chunks):
            place = down_chunks + (j % across) * 8 + j // across
            flat[place * 8:place * 8 + 8, :] = pick(up_buf, j * LANES)
        down.wait()
        for j in range(down_chunks):
            flat[j * 8:j * 8 + 8, :] = pick(down_buf, j * LANES)
        built[s] = flat[pl.ds(sub, down_chunks + up_chunks, stride=8), :].astype(jnp.bfloat16)
        leave.start()
        return carry

    lax.fori_loop(0, count, one, 0)
    for s in range(count):
        copies(s)[2].wait()


def zero_kernel(after_ref, down_ref, up_ref, done_ref, zeros, sems):
    del after_ref
    done_ref[0] = 0
    zeros[...] = jnp.zeros_like(zeros)
    part = zeros.shape[0]
    copies = []
    for ref, sem in ((down_ref, sems.at[0]), (up_ref, sems.at[1])):
        for g in range(ref.shape[0]):
            for c in range(ref.shape[1] // part):
                copies.append(pltpu.make_async_copy(zeros, ref.at[g, pl.ds(c * part, part)], sem))
    for c in copies:
        c.start()
    for c in copies:
        c.wait()


def adapter_kernel(count, down_chunks, xs_ref, g_ref, pieces, _, out_ref, lifted_ref, up_panel):
    rows = g_ref.shape[0]
    across = g_ref.shape[1] // LANES
    total = jnp.zeros((2 * rows, LANES), jnp.float32)
    for t in range(count):
        total += dot(xs_ref[t], pieces[t, :down_chunks])
        for c in range(across):
            block = pieces[t, down_chunks + 8 * c:down_chunks + 8 * c + 8, :].astype(jnp.float32)
            up_panel[8 * t:8 * t + 8, c * LANES:(c + 1) * LANES] = block
            up_panel[R + 8 * t:R + 8 * t + 8, c * LANES:(c + 1) * LANES] = block
    panel = up_panel[...].astype(jnp.bfloat16)
    left = lax.broadcasted_iota(jnp.int32, (rows, LANES), 1) < R
    inner = total[:rows] + pltpu.roll(total[rows:], R, 1)
    inner = jnp.where(left, inner, 0.0).astype(jnp.bfloat16)
    g = g_ref[...]
    lifted_ref[...] = adapter_scale * dot(inner, panel)
    inner_grad = adapter_scale * dot_t(g, panel)
    diagonal = jnp.concatenate(
        [jnp.where(left, inner_grad, 0.0), jnp.where(left, 0.0, inner_grad)], axis=0
    ).astype(jnp.bfloat16)
    up_term = adapter_scale * t_dot(inner, g)
    for t in range(count):
        out_ref[t, :down_chunks] = t_dot(xs_ref[t], diagonal).astype(jnp.bfloat16)
        up_part = jnp.concatenate(
            [up_term[8 * t:8 * t + 8, c * LANES:(c + 1) * LANES] for c in range(across)], axis=0
        )
        out_ref[t, down_chunks:] = up_part.astype(jnp.bfloat16)


def scatter_kernel(count, down_chunks, up_chunks, first_row, rows_here, rows_core, *rest):
    sources, (down_out, up_out) = rest[:2], rest[4:6]
    pieces, down_sum, up_sum, ordered, arrived, sem = rest[6:]
    half = count // 2
    owned_rows = down_out.shape[0] * 8
    across = up_chunks // 8
    rows = [(rows_here if b < half else rows_core)[b % half] - first_row[0] for b in range(count)]
    arriving = [pltpu.make_async_copy(sources[b // half].at[b % half], pieces.at[b], arrived.at[b]) for b in range(count)]
    for copy in arriving:
        copy.start()
    owned = [(row >= 0) & (row < owned_rows) for row in rows]
    slots, final = [], []
    for b in range(count):
        slot, last = jnp.int32(b), jnp.bool_(True)
        for e in range(b - 1, -1, -1):
            slot = jnp.where(rows[e] == rows[b], e, slot)
        for e in range(b + 1, count):
            last = last & (rows[e] != rows[b])
        slots.append(slot)
        final.append(last)

    def copies(b):
        return (
            pltpu.make_async_copy(down_sum.at[slots[b]], down_out.at[rows[b] // 8, :, rows[b] % 8], sem),
            pltpu.make_async_copy(up_sum.at[slots[b]], up_out.at[rows[b] // 8, :, rows[b] % 8], sem),
        )

    for b in range(count):
        arriving[b].wait()

        @pl.when(owned[b])
        def _():
            slot = slots[b]
            down = pieces[b, :down_chunks].astype(jnp.float32).reshape(down_chunks, 1, LANES)
            for c in range(across):
                ordered[pl.ds(c, 8, stride=across), :] = pieces[
                    b, down_chunks + 8 * c:down_chunks + 8 * c + 8
                ].astype(jnp.float32)
            up = ordered[...].reshape(up_chunks, 1, LANES)

            @pl.when(slot == b)
            def _():
                down_sum[b] = down
                up_sum[b] = up

            @pl.when(slot != b)
            def _():
                down_sum[slot] += down
                up_sum[slot] += up

            @pl.when(final[b])
            def _():
                for copy in copies(b):
                    copy.start()

    for b in range(count):
        @pl.when(owned[b] & final[b])
        def _():
            for copy in copies(b):
                copy.wait()


def base_kernel(*refs):
    x_refs, w_refs, out_refs = refs[:4], refs[4:6], refs[-4:]
    outer, rows, depth = x_refs[0].shape
    width = w_refs[0].shape[1]
    for h, w_ref in enumerate(w_refs):
        total = 0.0
        for k in range(outer):
            left = jnp.concatenate([ref[k] for ref in x_refs], axis=0)
            total += dot(left, w_ref[k * depth:(k + 1) * depth, :])
        for b, ref in enumerate(out_refs):
            ref[:, h * width:(h + 1) * width] = total[b * rows:(b + 1) * rows]


def fast_body(tokens, cotangent, frozen_value, down_store, up_store, block_adapter, adapter_slot):
    group, parts = lax.axis_size("tensor"), lax.axis_size("parts")
    outer = group // 2
    token_rows = tokens.shape[0]
    slice_width = D // group
    down_chunks = down_store.shape[1] // LANES
    up_chunks = up_store.shape[1] // LANES
    me, part, core = lax.axis_index("tensor"), lax.axis_index("parts"), lax.axis_index("dp")
    x = me % 2

    def exchange(value, s):
        return lax.ppermute(value, "tensor", [(t, t ^ s) for t in range(group)])

    def other_core(value):
        return lax.ppermute(value, "dp", [(0, 1), (1, 0)])

    def other_part(value):
        return lax.ppermute(value, "parts", [(a, parts - 1 - a) for a in range(parts)])

    row = jnp.broadcast_to(store_rows(block_adapter, adapter_slot), (LANES,))
    asked = [row] + [exchange(row, s) for s in range(1, group)]

    width = frozen_value.shape[1] // parts
    half = lax.dynamic_slice_in_dim(frozen_value, part * width, width, axis=1)
    lines = [list(range(0, group, 2)), list(range(1, group, 2))]
    half = lax.all_gather(half, "tensor", axis_index_groups=lines, axis=0, tiled=True)

    block = jax.ShapeDtypeStruct((outer, token_rows, slice_width), jnp.bfloat16)
    token = jax.ShapeDtypeStruct((1,), jnp.int32)
    x_mine, x_theirs, split = pl.pallas_call(
        split_kernel, out_shape=(block, block, token), in_specs=[SMEM, VMEM], out_specs=(VMEM, VMEM, SMEM),
        name="split_tokens", compiler_params=LIMIT,
    )(x[None], tokens)
    x_far = exchange(x_theirs, 1)
    y_mine = other_part(x_mine)

    xs = pl.pallas_call(
        interleave_kernel,
        out_shape=jax.ShapeDtypeStruct((group, 2 * token_rows, slice_width // 2), jnp.bfloat16),
        in_specs=[VMEM], out_specs=VMEM, name="pair_columns", compiler_params=LIMIT,
    )(tokens)

    pieces = jax.ShapeDtypeStruct((group, down_chunks + up_chunks, LANES), jnp.bfloat16)
    sent, rows = pl.pallas_call(
        functools.partial(gather_kernel, group, down_chunks, up_chunks),
        out_shape=(pieces, jax.ShapeDtypeStruct((group,), jnp.int32)),
        in_specs=[SMEM, SMEM] + [ANY] * (group + 2),
        out_specs=(ANY, SMEM),
        scratch_shapes=[
            pltpu.VMEM((group, GROUP_ROWS, down_store.shape[1]), jnp.bfloat16),
            pltpu.VMEM((group, GROUP_ROWS, up_store.shape[1]), jnp.bfloat16),
            pltpu.VMEM(((down_chunks + up_chunks) * 8, LANES), jnp.float32),
            pltpu.VMEM(pieces.shape, jnp.bfloat16),
            pltpu.SMEM((group, LANES), jnp.int32),
            pltpu.SemaphoreType.DMA((3, group)),
            pltpu.SemaphoreType.DMA(()),
        ],
        compiler_params=WIDE,
        name="pick_panels",
    )(me[None], split, *asked, down_store, up_store)
    panels = lax.all_to_all(sent, "tensor", 0, 0)
    rows_core = other_core(rows)
    x_far, _ = lax.optimization_barrier((x_far, sent))
    x_blocks = (x_mine, y_mine, x_far, other_part(x_far))

    owned_groups = ADAPTERS // lax.axis_size("dp") // 8
    down_shape = jax.ShapeDtypeStruct((owned_groups, down_chunks, 8, 1, LANES), jnp.float32)
    up_shape = jax.ShapeDtypeStruct((owned_groups, up_chunks, 8, 1, LANES), jnp.float32)
    down_zero, up_zero, cleared = pl.pallas_call(
        zero_kernel, out_shape=(down_shape, up_shape, token),
        in_specs=[ANY], out_specs=(ANY, ANY, SMEM),
        scratch_shapes=[pltpu.VMEM((up_chunks, 8, 1, LANES), jnp.float32), pltpu.SemaphoreType.DMA((2,))],
        compiler_params=WIDE, name="clear_rows",
    )(sent)

    terms, lifted = pl.pallas_call(
        functools.partial(adapter_kernel, group, down_chunks),
        out_shape=(pieces, jax.ShapeDtypeStruct((token_rows, VALUE_OUTPUTS), jnp.float32)),
        in_specs=[VMEM] * 3 + [SMEM],
        out_specs=(VMEM, VMEM),
        scratch_shapes=[pltpu.VMEM((2 * R, VALUE_OUTPUTS), jnp.float32)],
        compiler_params=LIMIT,
        name="adapter",
    )(xs, cotangent, panels, cleared)
    half, _ = lax.optimization_barrier((half, cleared))
    both = (half, other_core(half))
    sums = jax.ShapeDtypeStruct((token_rows, parts * width), jnp.float32)
    own, to_part, to_inner, to_both = pl.pallas_call(
        base_kernel,
        out_shape=[sums] * 4,
        in_specs=[VMEM] * 6 + [ANY],
        out_specs=[VMEM] * 4,
        compiler_params=LIMIT,
        name="frozen_part",
    )(*x_blocks, *both, terms)
    opposite = [(a * group + t, (parts - 1 - a) * group + (t ^ 1)) for a in range(parts) for t in range(group)]
    kept = own + exchange(to_inner, 1)
    got = other_part(to_part) + lax.ppermute(to_both, ("parts", "tensor"), opposite)
    back = lax.all_to_all(terms, "tensor", 0, 0)
    back_core = other_core(back)

    grad_down, grad_up = pl.pallas_call(
        functools.partial(scatter_kernel, 2 * group, down_chunks, up_chunks),
        out_shape=(down_shape, up_shape),
        in_specs=[SMEM] * 3 + [ANY] * 4,
        out_specs=(ANY, ANY),
        input_output_aliases={5: 0, 6: 1},
        scratch_shapes=[
            pltpu.VMEM((2 * group,) + pieces.shape[1:], jnp.bfloat16),
            pltpu.VMEM((2 * group, down_chunks, 1, LANES), jnp.float32),
            pltpu.VMEM((2 * group, up_chunks, 1, LANES), jnp.float32),
            pltpu.VMEM((up_chunks, LANES), jnp.float32),
            pltpu.SemaphoreType.DMA((2 * group,)),
            pltpu.SemaphoreType.DMA(()),
        ],
        compiler_params=LIMIT,
        name="place_rows",
    )((core * (ADAPTERS // lax.axis_size("dp")))[None], rows, rows_core, back, back_core,
      down_zero, up_zero)
    grad_down = grad_down.reshape(owned_groups, down_chunks, 8, LANES).transpose(0, 2, 1, 3)
    grad_up = grad_up.reshape(owned_groups, up_chunks, 8, LANES).transpose(0, 2, 1, 3)

    quarters = [[c[:, :width], c[:, width:]] for c in (kept, got)]

    def pick_quarter(c, a):
        first = quarters[a][0] if c == 0 else quarters[a][1]
        second = quarters[a][1] if c == 0 else quarters[a][0]
        return jnp.where(core == 0, first, second)

    def columns_of(c):
        low, high = pick_quarter(c, 0), pick_quarter(c, 1)
        return jnp.where(part == 0, low, high), jnp.where(part == 0, high, low)

    frozen_output = jnp.concatenate(columns_of(0) + columns_of(1), axis=1)
    mixed = (frozen_output + lifted).astype(jnp.bfloat16)
    return mixed, grad_down.reshape(owned_groups * 8, -1), grad_up.reshape(owned_groups * 8, -1)


def fits(mesh):
    group, cores, parts = mesh.shape["tensor"], mesh.shape["dp"], mesh.shape["parts"]
    return cores == 2 and parts == 2 and group <= 8 and group & (group - 1) == 0 and R == 8 * group


def body(mesh, tokens, *rest):
    block_adapter = rest[4]
    one_block = block_adapter.shape[0] == 1
    return (fast_body if fits(mesh) and one_block else plain_body)(tokens, *rest)


def solution(mesh):
    placed = (
        P(("parts", "dp", "tensor"), None),
        P(("parts", "dp", "tensor"), None),
        P("tensor", "dp"),
        P("parts", "tensor"),
        P("parts", "tensor"),
        P(("parts", "dp", "tensor")),
        P("parts"),
    )
    return jax.shard_map(
        functools.partial(body, mesh),
        mesh=mesh,
        in_specs=placed,
        out_specs=(
            P(("parts", "dp", "tensor"), None),
            P(("parts", "dp"), "tensor"),
            P(("parts", "dp"), "tensor"),
        ),
        check_vma=False,
    )
```

```python
import functools

import jax
import jax.numpy as jnp
from jax import lax
from jax.experimental import pallas as pl
from jax.experimental.pallas import tpu as pltpu
from jax.sharding import PartitionSpec as P

D = 5120
VALUE_OUTPUTS = 1024
R = 64
ADAPTERS = 256
LANES = 128
GROUP_ROWS = 16

adapter_scale = 2.0
VMEM = pl.BlockSpec(memory_space=pltpu.VMEM)
SMEM = pl.BlockSpec(memory_space=pltpu.SMEM)
ANY = pl.BlockSpec(memory_space=pl.ANY)
LIMIT = pltpu.CompilerParams(vmem_limit_bytes=16 * 1024 * 1024)
WIDE = pltpu.CompilerParams(vmem_limit_bytes=60 * 1024 * 1024)


def dot(a, b):
    return jnp.dot(a, b, preferred_element_type=jnp.float32)


def dot_t(a, b):
    return lax.dot_general(a, b, (((1,), (1,)), ((), ())), preferred_element_type=jnp.float32)


def t_dot(a, b):
    return lax.dot_general(a, b, (((0,), (0,)), ((), ())), preferred_element_type=jnp.float32)


def fold_rows(left, piece):
    return jnp.dot(left, piece, preferred_element_type=jnp.float32)


def store_rows(requests, adapter_slot):
    table = jnp.arange(adapter_slot.shape[0], dtype=jnp.int32)
    return jnp.sum(jnp.where(requests[:, None] == table[None, :], adapter_slot[None, :], 0), axis=1)


def plain_body(tokens, cotangent, frozen_value, down_store, up_store, block_adapter, adapter_slot):
    token_rows = tokens.shape[0]
    blocks_here = block_adapter.shape[0]
    block_rows = token_rows // blocks_here
    group = lax.axis_size("tensor")
    columns = lax.all_gather(frozen_value, "dp", axis=1, tiled=True)
    frozen_output = fold_rows(tokens, lax.all_gather(columns, "tensor", axis=0, tiled=True))
    requests = lax.all_gather(block_adapter, "tensor", axis=0, tiled=True)
    stored = store_rows(requests, adapter_slot)
    order = stored.reshape(group, blocks_here).T.reshape(-1)
    down_send = jnp.take(down_store, order, axis=0).reshape(blocks_here, group, -1)
    up_send = jnp.take(up_store, order, axis=0).reshape(blocks_here, group, -1)
    down_got = lax.all_to_all(down_send, "tensor", split_axis=1, concat_axis=1, tiled=True)
    up_got = lax.all_to_all(up_send, "tensor", split_axis=1, concat_axis=1, tiled=True)
    down_panel = down_got.reshape(blocks_here, D, R)
    up_panel = up_got.reshape(blocks_here, R, VALUE_OUTPUTS)
    token_blocks = tokens.reshape(blocks_here, block_rows, D)
    grad_blocks = cotangent.reshape(blocks_here, block_rows, VALUE_OUTPUTS)
    down_projected = jnp.einsum(
        "jtd,jdr->jtr", token_blocks, down_panel, preferred_element_type=jnp.float32
    ).astype(jnp.bfloat16)
    up_projected = jnp.einsum(
        "jtr,jrk->jtk", down_projected, up_panel, preferred_element_type=jnp.float32
    )
    mixed = (
        frozen_output + adapter_scale * up_projected.reshape(token_rows, VALUE_OUTPUTS)
    ).astype(jnp.bfloat16)
    down_projected_gradient = (
        adapter_scale
        * jnp.einsum("jtk,jrk->jtr", grad_blocks, up_panel, preferred_element_type=jnp.float32)
    ).astype(jnp.bfloat16)
    down_term = jnp.einsum(
        "jtd,jtr->jdr", token_blocks, down_projected_gradient, preferred_element_type=jnp.float32
    )
    up_weight_gradient = adapter_scale * jnp.einsum(
        "jtr,jtk->jrk", down_projected, grad_blocks, preferred_element_type=jnp.float32
    )
    down_back = lax.all_to_all(
        down_term.reshape(blocks_here, group, -1), "tensor", split_axis=1, concat_axis=1, tiled=True
    )
    up_back = lax.all_to_all(
        up_weight_gradient.reshape(blocks_here, group, -1), "tensor", split_axis=1, concat_axis=1, tiled=True
    )
    down_flat = down_back.reshape(blocks_here * group, -1)
    up_flat = up_back.reshape(blocks_here * group, -1)
    down_table = jax.ops.segment_sum(down_flat, order, num_segments=ADAPTERS)
    up_table = jax.ops.segment_sum(up_flat, order, num_segments=ADAPTERS)
    grad_down = lax.psum_scatter(down_table, "dp", scatter_dimension=0, tiled=True)
    grad_up = lax.psum_scatter(up_table, "dp", scatter_dimension=0, tiled=True)
    return mixed, grad_down, grad_up


def split_kernel(where, x_ref, mine_ref, theirs_ref, done_ref):
    done_ref[0] = 0
    inner = where[0]
    outer, rows, width = mine_ref.shape
    for k in range(outer):
        own = pl.multiple_of((2 * k + inner) * width, LANES)
        other = pl.multiple_of((2 * k + 1 - inner) * width, LANES)
        mine_ref[k] = x_ref[:, pl.ds(own, width)]
        theirs_ref[k] = x_ref[:, pl.ds(other, width)]


def interleave_kernel(x_ref, xs_ref):
    group, rows2, half = xs_ref.shape
    rows, width = rows2 // 2, 2 * half
    source = lax.broadcasted_iota(jnp.int32, (width, half), 0)
    target = lax.broadcasted_iota(jnp.int32, (width, half), 1)
    even = (source == 2 * target).astype(jnp.bfloat16)
    odd = (source == 2 * target + 1).astype(jnp.bfloat16)
    for k in range(group):
        x = x_ref[:, k * width:(k + 1) * width]
        xs_ref[k, :rows] = dot(x, even).astype(jnp.bfloat16)
        xs_ref[k, rows:] = dot(x, odd).astype(jnp.bfloat16)


def gather_kernel(count, down_chunks, up_chunks, where, after, *refs):
    del after
    asked, (down_ref, up_ref, out_ref, rows_ref) = refs[:count], refs[count:count + 4]
    down_buf, up_buf, flat, built, rows, sems, row_sem = refs[count + 4:]
    me = where[0]
    across = up_chunks // 8
    for s in range(count):
        pltpu.make_async_copy(asked[s], rows.at[s], row_sem).start()
    for s in range(count):
        pltpu.make_async_copy(asked[s], rows.at[s], row_sem).wait()

    def copies(s):
        start = pl.multiple_of((rows[s, 0] // GROUP_ROWS) * GROUP_ROWS, GROUP_ROWS)
        return (
            pltpu.make_async_copy(down_ref.at[pl.ds(start, GROUP_ROWS)], down_buf.at[s], sems.at[0, s]),
            pltpu.make_async_copy(up_ref.at[pl.ds(start, GROUP_ROWS)], up_buf.at[s], sems.at[1, s]),
            pltpu.make_async_copy(built.at[s], out_ref.at[me ^ s], sems.at[2, s]),
        )

    for s in range(count):
        down, up, _ = copies(s)
        down.start()
        up.start()
        rows_ref[me ^ s] = rows[s, 0]

    def one(s, carry):
        row = rows[s, 0] % GROUP_ROWS
        upper = row >= 8
        sub = row % 8

        def pick(buf, lane):
            tile = buf[s, :, lane:lane + LANES].astype(jnp.float32)
            return jnp.where(upper, tile[8:], tile[:8])

        down, up, leave = copies(s)
        up.wait()
        for j in range(up_chunks):
            place = down_chunks + (j % across) * 8 + j // across
            flat[place * 8:place * 8 + 8, :] = pick(up_buf, j * LANES)
        down.wait()
        for j in range(down_chunks):
            flat[j * 8:j * 8 + 8, :] = pick(down_buf, j * LANES)
        built[s] = flat[pl.ds(sub, down_chunks + up_chunks, stride=8), :].astype(jnp.bfloat16)
        leave.start()
        return carry

    lax.fori_loop(0, count, one, 0)
    for s in range(count):
        copies(s)[2].wait()


def zero_kernel(after_ref, down_ref, up_ref, done_ref, zeros, sems):
    del after_ref
    done_ref[0] = 0
    zeros[...] = jnp.zeros_like(zeros)
    part = zeros.shape[0]
    copies = []
    for ref, sem in ((down_ref, sems.at[0]), (up_ref, sems.at[1])):
        for g in range(ref.shape[0]):
            for c in range(ref.shape[1] // part):
                copies.append(pltpu.make_async_copy(zeros, ref.at[g, pl.ds(c * part, part)], sem))
    for c in copies:
        c.start()
    for c in copies:
        c.wait()


def adapter_kernel(count, down_chunks, xs_ref, g_ref, pieces, _, out_ref, lifted_ref, up_panel):
    rows = g_ref.shape[0]
    across = g_ref.shape[1] // LANES
    total = jnp.zeros((2 * rows, LANES), jnp.float32)
    for t in range(count):
        total += dot(xs_ref[t], pieces[t, :down_chunks])
        for c in range(across):
            block = pieces[t, down_chunks + 8 * c:down_chunks + 8 * c + 8, :].astype(jnp.float32)
            up_panel[8 * t:8 * t + 8, c * LANES:(c + 1) * LANES] = block
            up_panel[R + 8 * t:R + 8 * t + 8, c * LANES:(c + 1) * LANES] = block
    panel = up_panel[...].astype(jnp.bfloat16)
    left = lax.broadcasted_iota(jnp.int32, (rows, LANES), 1) < R
    inner = total[:rows] + pltpu.roll(total[rows:], R, 1)
    inner = jnp.where(left, inner, 0.0).astype(jnp.bfloat16)
    g = g_ref[...]
    lifted_ref[...] = adapter_scale * dot(inner, panel)
    inner_grad = adapter_scale * dot_t(g, panel)
    diagonal = jnp.concatenate(
        [jnp.where(left, inner_grad, 0.0), jnp.where(left, 0.0, inner_grad)], axis=0
    ).astype(jnp.bfloat16)
    up_term = adapter_scale * t_dot(inner, g)
    for t in range(count):
        out_ref[t, :down_chunks] = t_dot(xs_ref[t], diagonal).astype(jnp.bfloat16)
        up_part = jnp.concatenate(
            [up_term[8 * t:8 * t + 8, c * LANES:(c + 1) * LANES] for c in range(across)], axis=0
        )
        out_ref[t, down_chunks:] = up_part.astype(jnp.bfloat16)


def scatter_kernel(count, down_chunks, up_chunks, first_row, rows_here, rows_core, *rest):
    sources, (down_out, up_out) = rest[:2], rest[4:6]
    pieces, down_sum, up_sum, ordered, arrived, sem = rest[6:]
    half = count // 2
    owned_rows = down_out.shape[0] * 8
    across = up_chunks // 8
    rows = [(rows_here if b < half else rows_core)[b % half] - first_row[0] for b in range(count)]
    arriving = [pltpu.make_async_copy(sources[b // half].at[b % half], pieces.at[b], arrived.at[b]) for b in range(count)]
    for copy in arriving:
        copy.start()
    owned = [(row >= 0) & (row < owned_rows) for row in rows]
    slots, final = [], []
    for b in range(count):
        slot, last = jnp.int32(b), jnp.bool_(True)
        for e in range(b - 1, -1, -1):
            slot = jnp.where(rows[e] == rows[b], e, slot)
        for e in range(b + 1, count):
            last = last & (rows[e] != rows[b])
        slots.append(slot)
        final.append(last)

    def copies(b):
        return (
            pltpu.make_async_copy(down_sum.at[slots[b]], down_out.at[rows[b] // 8, :, rows[b] % 8], sem),
            pltpu.make_async_copy(up_sum.at[slots[b]], up_out.at[rows[b] // 8, :, rows[b] % 8], sem),
        )

    for b in range(count):
        arriving[b].wait()

        @pl.when(owned[b])
        def _():
            slot = slots[b]
            down = pieces[b, :down_chunks].astype(jnp.float32).reshape(down_chunks, 1, LANES)
            for c in range(across):
                ordered[pl.ds(c, 8, stride=across), :] = pieces[
                    b, down_chunks + 8 * c:down_chunks + 8 * c + 8
                ].astype(jnp.float32)
            up = ordered[...].reshape(up_chunks, 1, LANES)

            @pl.when(slot == b)
            def _():
                down_sum[b] = down
                up_sum[b] = up

            @pl.when(slot != b)
            def _():
                down_sum[slot] += down
                up_sum[slot] += up

            @pl.when(final[b])
            def _():
                for copy in copies(b):
                    copy.start()

    for b in range(count):
        @pl.when(owned[b] & final[b])
        def _():
            for copy in copies(b):
                copy.wait()


def base_kernel(*refs):
    x_refs, w_refs, out_refs = refs[:4], refs[4:6], refs[-4:]
    outer, rows, depth = x_refs[0].shape
    width = w_refs[0].shape[1]
    for h, w_ref in enumerate(w_refs):
        total = 0.0
        for k in range(outer):
            left = jnp.concatenate([ref[k] for ref in x_refs], axis=0)
            total += dot(left, w_ref[k * depth:(k + 1) * depth, :])
        for b, ref in enumerate(out_refs):
            ref[:, h * width:(h + 1) * width] = total[b * rows:(b + 1) * rows]


def fast_body(tokens, cotangent, frozen_value, down_store, up_store, block_adapter, adapter_slot):
    group, parts = lax.axis_size("tensor"), lax.axis_size("parts")
    outer = group // 2
    token_rows = tokens.shape[0]
    slice_width = D // group
    down_chunks = down_store.shape[1] // LANES
    up_chunks = up_store.shape[1] // LANES
    me, part, core = lax.axis_index("tensor"), lax.axis_index("parts"), lax.axis_index("dp")
    x = me % 2

    def exchange(value, s):
        return lax.ppermute(value, "tensor", [(t, t ^ s) for t in range(group)])

    def other_core(value):
        return lax.ppermute(value, "dp", [(0, 1), (1, 0)])

    def other_part(value):
        return lax.ppermute(value, "parts", [(a, parts - 1 - a) for a in range(parts)])

    row = jnp.broadcast_to(store_rows(block_adapter, adapter_slot), (LANES,))
    asked = [row] + [exchange(row, s) for s in range(1, group)]

    width = frozen_value.shape[1] // parts
    half = lax.dynamic_slice_in_dim(frozen_value, part * width, width, axis=1)
    lines = [list(range(0, group, 2)), list(range(1, group, 2))]
    half = lax.all_gather(half, "tensor", axis_index_groups=lines, axis=0, tiled=True)

    block = jax.ShapeDtypeStruct((outer, token_rows, slice_width), jnp.bfloat16)
    token = jax.ShapeDtypeStruct((1,), jnp.int32)
    x_mine, x_theirs, split = pl.pallas_call(
        split_kernel, out_shape=(block, block, token), in_specs=[SMEM, VMEM], out_specs=(VMEM, VMEM, SMEM),
        name="split_tokens", compiler_params=LIMIT,
    )(x[None], tokens)
    x_far = exchange(x_theirs, 1)
    y_mine = other_part(x_mine)
    split, x_far, y_mine = lax.optimization_barrier((split, x_far, y_mine))

    xs = pl.pallas_call(
        interleave_kernel,
        out_shape=jax.ShapeDtypeStruct((group, 2 * token_rows, slice_width // 2), jnp.bfloat16),
        in_specs=[VMEM], out_specs=VMEM, name="pair_columns", compiler_params=LIMIT,
    )(tokens)

    pieces = jax.ShapeDtypeStruct((group, down_chunks + up_chunks, LANES), jnp.bfloat16)
    sent, rows = pl.pallas_call(
        functools.partial(gather_kernel, group, down_chunks, up_chunks),
        out_shape=(pieces, jax.ShapeDtypeStruct((group,), jnp.int32)),
        in_specs=[SMEM, SMEM] + [ANY] * (group + 2),
        out_specs=(ANY, SMEM),
        scratch_shapes=[
            pltpu.VMEM((group, GROUP_ROWS, down_store.shape[1]), jnp.bfloat16),
            pltpu.VMEM((group, GROUP_ROWS, up_store.shape[1]), jnp.bfloat16),
            pltpu.VMEM(((down_chunks + up_chunks) * 8, LANES), jnp.float32),
            pltpu.VMEM(pieces.shape, jnp.bfloat16),
            pltpu.SMEM((group, LANES), jnp.int32),
            pltpu.SemaphoreType.DMA((3, group)),
            pltpu.SemaphoreType.DMA(()),
        ],
        compiler_params=WIDE,
        name="pick_panels",
    )(me[None], split, *asked, down_store, up_store)
    panels = lax.all_to_all(sent, "tensor", 0, 0)
    rows_core = other_core(rows)
    x_far, _ = lax.optimization_barrier((x_far, rows))
    y_far = other_part(x_far)

    owned_groups = ADAPTERS // lax.axis_size("dp") // 8
    down_shape = jax.ShapeDtypeStruct((owned_groups, down_chunks, 8, 1, LANES), jnp.float32)
    up_shape = jax.ShapeDtypeStruct((owned_groups, up_chunks, 8, 1, LANES), jnp.float32)
    down_zero, up_zero, cleared = pl.pallas_call(
        zero_kernel, out_shape=(down_shape, up_shape, token),
        in_specs=[SMEM], out_specs=(ANY, ANY, SMEM),
        scratch_shapes=[pltpu.VMEM((up_chunks, 8, 1, LANES), jnp.float32), pltpu.SemaphoreType.DMA((2,))],
        compiler_params=LIMIT, name="clear_rows",
    )(rows)
    half, _ = lax.optimization_barrier((half, cleared))
    half_core = other_core(half)
    panels, y_far, half_core = lax.optimization_barrier((panels, y_far, half_core))

    terms, lifted = pl.pallas_call(
        functools.partial(adapter_kernel, group, down_chunks),
        out_shape=(pieces, jax.ShapeDtypeStruct((token_rows, VALUE_OUTPUTS), jnp.float32)),
        in_specs=[VMEM] * 3 + [SMEM],
        out_specs=(VMEM, VMEM),
        scratch_shapes=[pltpu.VMEM((2 * R, VALUE_OUTPUTS), jnp.float32)],
        compiler_params=LIMIT,
        name="adapter",
    )(xs, cotangent, panels, cleared)
    sums = jax.ShapeDtypeStruct((token_rows, parts * width), jnp.float32)
    own, to_part, to_inner, to_both = pl.pallas_call(
        base_kernel,
        out_shape=[sums] * 4,
        in_specs=[VMEM] * 6 + [ANY],
        out_specs=[VMEM] * 4,
        compiler_params=LIMIT,
        name="frozen_part",
    )(x_mine, y_mine, x_far, y_far, half, half_core, terms)
    opposite = [(a * group + t, (parts - 1 - a) * group + (t ^ 1)) for a in range(parts) for t in range(group)]
    kept = own + exchange(to_inner, 1)
    got = other_part(to_part) + lax.ppermute(to_both, ("parts", "tensor"), opposite)
    back = lax.all_to_all(terms, "tensor", 0, 0)
    back_core = other_core(back)

    grad_down, grad_up = pl.pallas_call(
        functools.partial(scatter_kernel, 2 * group, down_chunks, up_chunks),
        out_shape=(down_shape, up_shape),
        in_specs=[SMEM] * 3 + [ANY] * 4,
        out_specs=(ANY, ANY),
        input_output_aliases={5: 0, 6: 1},
        scratch_shapes=[
            pltpu.VMEM((2 * group,) + pieces.shape[1:], jnp.bfloat16),
            pltpu.VMEM((2 * group, down_chunks, 1, LANES), jnp.float32),
            pltpu.VMEM((2 * group, up_chunks, 1, LANES), jnp.float32),
            pltpu.VMEM((up_chunks, LANES), jnp.float32),
            pltpu.SemaphoreType.DMA((2 * group,)),
            pltpu.SemaphoreType.DMA(()),
        ],
        compiler_params=LIMIT,
        name="place_rows",
    )((core * (ADAPTERS // lax.axis_size("dp")))[None], rows, rows_core, back, back_core,
      down_zero, up_zero)
    grad_down = grad_down.reshape(owned_groups, down_chunks, 8, LANES).transpose(0, 2, 1, 3)
    grad_up = grad_up.reshape(owned_groups, up_chunks, 8, LANES).transpose(0, 2, 1, 3)

    quarters = [[c[:, :width], c[:, width:]] for c in (kept, got)]

    def pick_quarter(c, a):
        first = quarters[a][0] if c == 0 else quarters[a][1]
        second = quarters[a][1] if c == 0 else quarters[a][0]
        return jnp.where(core == 0, first, second)

    def columns_of(c):
        low, high = pick_quarter(c, 0), pick_quarter(c, 1)
        return jnp.where(part == 0, low, high), jnp.where(part == 0, high, low)

    frozen_output = jnp.concatenate(columns_of(0) + columns_of(1), axis=1)
    mixed = (frozen_output + lifted).astype(jnp.bfloat16)
    return mixed, grad_down.reshape(owned_groups * 8, -1), grad_up.reshape(owned_groups * 8, -1)


def fits(mesh):
    group, cores, parts = mesh.shape["tensor"], mesh.shape["dp"], mesh.shape["parts"]
    return cores == 2 and parts == 2 and group <= 8 and group & (group - 1) == 0 and R == 8 * group


def body(mesh, tokens, *rest):
    block_adapter = rest[4]
    one_block = block_adapter.shape[0] == 1
    return (fast_body if fits(mesh) and one_block else plain_body)(tokens, *rest)


def solution(mesh):
    placed = (
        P(("parts", "dp", "tensor"), None),
        P(("parts", "dp", "tensor"), None),
        P("tensor", "dp"),
        P("parts", "tensor"),
        P("parts", "tensor"),
        P(("parts", "dp", "tensor")),
        P("parts"),
    )
    return jax.shard_map(
        functools.partial(body, mesh),
        mesh=mesh,
        in_specs=placed,
        out_specs=(
            P(("parts", "dp", "tensor"), None),
            P(("parts", "dp"), "tensor"),
            P(("parts", "dp"), "tensor"),
        ),
        check_vma=False,
    )
```

```python
import functools

import jax
import jax.numpy as jnp
from jax import lax
from jax.experimental import pallas as pl
from jax.experimental.pallas import tpu as pltpu
from jax.sharding import PartitionSpec as P

D = 5120
VALUE_OUTPUTS = 1024
R = 64
ADAPTERS = 256
LANES = 128
TILE_ROWS = 8

adapter_scale = 2.0
VMEM = pl.BlockSpec(memory_space=pltpu.VMEM)
SMEM = pl.BlockSpec(memory_space=pltpu.SMEM)
ANY = pl.BlockSpec(memory_space=pl.ANY)
LIMIT = pltpu.CompilerParams(vmem_limit_bytes=16 * 1024 * 1024)
WIDE = pltpu.CompilerParams(vmem_limit_bytes=60 * 1024 * 1024)


def cost(flops=0, read=0):
    return pl.CostEstimate(flops=flops, bytes_accessed=read, transcendentals=0)


def dot(a, b):
    return jnp.dot(a, b, preferred_element_type=jnp.float32)


def dot_t(a, b):
    return lax.dot_general(a, b, (((1,), (1,)), ((), ())), preferred_element_type=jnp.float32)


def t_dot(a, b):
    return lax.dot_general(a, b, (((0,), (0,)), ((), ())), preferred_element_type=jnp.float32)


def fold_rows(left, piece):
    return jnp.dot(left, piece, preferred_element_type=jnp.float32)


def store_rows(requests, adapter_slot):
    table = jnp.arange(adapter_slot.shape[0], dtype=jnp.int32)
    return jnp.sum(jnp.where(requests[:, None] == table[None, :], adapter_slot[None, :], 0), axis=1)


def plain_body(tokens, cotangent, frozen_value, down_store, up_store, block_adapter, adapter_slot):
    token_rows = tokens.shape[0]
    blocks_here = block_adapter.shape[0]
    block_rows = token_rows // blocks_here
    group = lax.axis_size("tensor")
    columns = lax.all_gather(frozen_value, "dp", axis=1, tiled=True)
    frozen_output = fold_rows(tokens, lax.all_gather(columns, "tensor", axis=0, tiled=True))
    requests = lax.all_gather(block_adapter, "tensor", axis=0, tiled=True)
    stored = store_rows(requests, adapter_slot)
    order = stored.reshape(group, blocks_here).T.reshape(-1)
    down_send = jnp.take(down_store, order, axis=0).reshape(blocks_here, group, -1)
    up_send = jnp.take(up_store, order, axis=0).reshape(blocks_here, group, -1)
    down_got = lax.all_to_all(down_send, "tensor", split_axis=1, concat_axis=1, tiled=True)
    up_got = lax.all_to_all(up_send, "tensor", split_axis=1, concat_axis=1, tiled=True)
    down_panel = down_got.reshape(blocks_here, D, R)
    up_panel = up_got.reshape(blocks_here, R, VALUE_OUTPUTS)
    token_blocks = tokens.reshape(blocks_here, block_rows, D)
    grad_blocks = cotangent.reshape(blocks_here, block_rows, VALUE_OUTPUTS)
    down_projected = jnp.einsum(
        "jtd,jdr->jtr", token_blocks, down_panel, preferred_element_type=jnp.float32
    ).astype(jnp.bfloat16)
    up_projected = jnp.einsum(
        "jtr,jrk->jtk", down_projected, up_panel, preferred_element_type=jnp.float32
    )
    mixed = (
        frozen_output + adapter_scale * up_projected.reshape(token_rows, VALUE_OUTPUTS)
    ).astype(jnp.bfloat16)
    down_projected_gradient = (
        adapter_scale
        * jnp.einsum("jtk,jrk->jtr", grad_blocks, up_panel, preferred_element_type=jnp.float32)
    ).astype(jnp.bfloat16)
    down_term = jnp.einsum(
        "jtd,jtr->jdr", token_blocks, down_projected_gradient, preferred_element_type=jnp.float32
    )
    up_weight_gradient = adapter_scale * jnp.einsum(
        "jtr,jtk->jrk", down_projected, grad_blocks, preferred_element_type=jnp.float32
    )
    down_back = lax.all_to_all(
        down_term.reshape(blocks_here, group, -1), "tensor", split_axis=1, concat_axis=1, tiled=True
    )
    up_back = lax.all_to_all(
        up_weight_gradient.reshape(blocks_here, group, -1), "tensor", split_axis=1, concat_axis=1, tiled=True
    )
    down_flat = down_back.reshape(blocks_here * group, -1)
    up_flat = up_back.reshape(blocks_here * group, -1)
    down_table = jax.ops.segment_sum(down_flat, order, num_segments=ADAPTERS)
    up_table = jax.ops.segment_sum(up_flat, order, num_segments=ADAPTERS)
    grad_down = lax.psum_scatter(down_table, "dp", scatter_dimension=0, tiled=True)
    grad_up = lax.psum_scatter(up_table, "dp", scatter_dimension=0, tiled=True)
    return mixed, grad_down, grad_up


def split_kernel(where, x_ref, mine_ref, theirs_ref, done_ref):
    done_ref[0] = 0
    inner = where[0]
    outer, rows, width = mine_ref.shape
    for k in range(outer):
        own = pl.multiple_of((2 * k + inner) * width, LANES)
        other = pl.multiple_of((2 * k + 1 - inner) * width, LANES)
        mine_ref[k] = x_ref[:, pl.ds(own, width)]
        theirs_ref[k] = x_ref[:, pl.ds(other, width)]


def interleave_kernel(x_ref, xs_ref):
    group, rows2, half = xs_ref.shape
    rows, width = rows2 // 2, 2 * half
    source = lax.broadcasted_iota(jnp.int32, (width, half), 0)
    target = lax.broadcasted_iota(jnp.int32, (width, half), 1)
    even = (source == 2 * target).astype(jnp.bfloat16)
    odd = (source == 2 * target + 1).astype(jnp.bfloat16)
    for k in range(group):
        x = x_ref[:, k * width:(k + 1) * width]
        xs_ref[k, :rows] = dot(x, even).astype(jnp.bfloat16)
        xs_ref[k, rows:] = dot(x, odd).astype(jnp.bfloat16)


def gather_kernel(after, asked, down_ref, up_ref, out_ref, rows_ref, down_buf, up_buf, flat, built, sems):
    del after
    count, down_chunks, up_chunks = down_buf.shape[0], down_buf.shape[1], up_buf.shape[1]
    across = up_chunks // 8

    def copies(t):
        tile = asked[t, 0] // TILE_ROWS
        return (
            pltpu.make_async_copy(down_ref.at[tile], down_buf.at[t], sems.at[0, t]),
            pltpu.make_async_copy(up_ref.at[tile], up_buf.at[t], sems.at[1, t]),
            pltpu.make_async_copy(built.at[t], out_ref.at[t], sems.at[2, t]),
        )

    for t in range(count):
        down, up, _ = copies(t)
        down.start()
        up.start()
        rows_ref[t] = asked[t, 0]

    def one(t, carry):
        down, up, leave = copies(t)
        up.wait()
        for j in range(up_chunks):
            place = down_chunks + (j % across) * 8 + j // across
            flat[place * 8:place * 8 + 8, :] = up_buf[t, j].astype(jnp.float32)
        down.wait()
        for j in range(down_chunks):
            flat[j * 8:j * 8 + 8, :] = down_buf[t, j].astype(jnp.float32)
        sub = asked[t, 0] % TILE_ROWS
        built[t] = flat[pl.ds(sub, down_chunks + up_chunks, stride=8), :].astype(jnp.bfloat16)
        leave.start()
        return carry

    lax.fori_loop(0, count, one, 0)
    for t in range(count):
        copies(t)[2].wait()


def zero_kernel(after_ref, down_ref, up_ref, done_ref, zeros, sems):
    del after_ref
    done_ref[0] = 0
    zeros[...] = jnp.zeros_like(zeros)
    part = zeros.shape[0]
    copies = []
    for ref, sem in ((down_ref, sems.at[0]), (up_ref, sems.at[1])):
        for g in range(ref.shape[0]):
            for c in range(ref.shape[1] // part):
                copies.append(pltpu.make_async_copy(zeros, ref.at[g, pl.ds(c * part, part)], sem))
    for c in copies:
        c.start()
    for c in copies:
        c.wait()


def adapter_kernel(count, down_chunks, xs_ref, g_ref, pieces, _, out_ref, lifted_ref, up_panel):
    rows = g_ref.shape[0]
    across = g_ref.shape[1] // LANES
    total = jnp.zeros((2 * rows, LANES), jnp.float32)
    for t in range(count):
        total += dot(xs_ref[t], pieces[t, :down_chunks])
        for c in range(across):
            block = pieces[t, down_chunks + 8 * c:down_chunks + 8 * c + 8, :].astype(jnp.float32)
            up_panel[8 * t:8 * t + 8, c * LANES:(c + 1) * LANES] = block
            up_panel[R + 8 * t:R + 8 * t + 8, c * LANES:(c + 1) * LANES] = block
    panel = up_panel[...].astype(jnp.bfloat16)
    left = lax.broadcasted_iota(jnp.int32, (rows, LANES), 1) < R
    inner = total[:rows] + pltpu.roll(total[rows:], R, 1)
    inner = jnp.where(left, inner, 0.0).astype(jnp.bfloat16)
    g = g_ref[...]
    lifted_ref[...] = adapter_scale * dot(inner, panel)
    inner_grad = adapter_scale * dot_t(g, panel)
    diagonal = jnp.concatenate(
        [jnp.where(left, inner_grad, 0.0), jnp.where(left, 0.0, inner_grad)], axis=0
    ).astype(jnp.bfloat16)
    up_term = adapter_scale * t_dot(inner, g)
    for t in range(count):
        out_ref[t, :down_chunks] = t_dot(xs_ref[t], diagonal).astype(jnp.bfloat16)
        up_part = jnp.concatenate(
            [up_term[8 * t:8 * t + 8, c * LANES:(c + 1) * LANES] for c in range(across)], axis=0
        )
        out_ref[t, down_chunks:] = up_part.astype(jnp.bfloat16)


def scatter_kernel(count, down_chunks, up_chunks, first_row, rows_here, rows_core, *rest):
    sources, (down_out, up_out) = rest[:2], rest[4:6]
    pieces, down_sum, up_sum, ordered, arrived, sem = rest[6:]
    half = count // 2
    owned_rows = down_out.shape[0] * 8
    across = up_chunks // 8
    rows = [(rows_here if b < half else rows_core)[b % half] - first_row[0] for b in range(count)]
    arriving = [pltpu.make_async_copy(sources[b // half].at[b % half], pieces.at[b], arrived.at[b]) for b in range(count)]
    for copy in arriving:
        copy.start()
    owned = [(row >= 0) & (row < owned_rows) for row in rows]
    slots, final = [], []
    for b in range(count):
        slot, last = jnp.int32(b), jnp.bool_(True)
        for e in range(b - 1, -1, -1):
            slot = jnp.where(rows[e] == rows[b], e, slot)
        for e in range(b + 1, count):
            last = last & (rows[e] != rows[b])
        slots.append(slot)
        final.append(last)

    def copies(b):
        return (
            pltpu.make_async_copy(down_sum.at[slots[b]], down_out.at[rows[b] // 8, :, rows[b] % 8], sem),
            pltpu.make_async_copy(up_sum.at[slots[b]], up_out.at[rows[b] // 8, :, rows[b] % 8], sem),
        )

    for b in range(count):
        arriving[b].wait()

        @pl.when(owned[b])
        def _():
            slot = slots[b]
            down = pieces[b, :down_chunks].astype(jnp.float32).reshape(down_chunks, 1, LANES)
            for c in range(across):
                ordered[pl.ds(c, 8, stride=across), :] = pieces[
                    b, down_chunks + 8 * c:down_chunks + 8 * c + 8
                ].astype(jnp.float32)
            up = ordered[...].reshape(up_chunks, 1, LANES)

            @pl.when(slot == b)
            def _():
                down_sum[b] = down
                up_sum[b] = up

            @pl.when(slot != b)
            def _():
                down_sum[slot] += down
                up_sum[slot] += up

            @pl.when(final[b])
            def _():
                for copy in copies(b):
                    copy.start()

    for b in range(count):
        @pl.when(owned[b] & final[b])
        def _():
            for copy in copies(b):
                copy.wait()


def base_kernel(where, *refs):
    x_refs, out_refs = refs[:4], refs[-4:]
    outer, rows, _ = x_refs[0].shape
    width = refs[4].shape[1]
    for h in range(2):
        total = 0.0
        for k in range(outer):
            left = jnp.concatenate([ref[where[0] ^ k] for ref in x_refs], axis=0)
            total += dot(left, refs[4 + h * outer + k][...])
        for b, ref in enumerate(out_refs):
            ref[:, h * width:(h + 1) * width] = total[b * rows:(b + 1) * rows]


def fast_body(tokens, cotangent, frozen_value, down_store, up_store, block_adapter, adapter_slot):
    group, parts = lax.axis_size("tensor"), lax.axis_size("parts")
    outer = group // 2
    token_rows = tokens.shape[0]
    slice_width = D // group
    down_chunks = down_store.shape[1] // LANES
    up_chunks = up_store.shape[1] // LANES
    me, part, core = lax.axis_index("tensor"), lax.axis_index("parts"), lax.axis_index("dp")
    z, x = me // 2, me % 2

    def exchange(value, s):
        return lax.ppermute(value, "tensor", [(t, t ^ s) for t in range(group)])

    def other_core(value):
        return lax.ppermute(value, "dp", [(0, 1), (1, 0)])

    def other_part(value):
        return lax.ppermute(value, "parts", [(a, parts - 1 - a) for a in range(parts)])

    row = store_rows(block_adapter, adapter_slot)
    asked = lax.all_to_all(jnp.broadcast_to(row, (group, LANES)), "tensor", 0, 0)

    width = frozen_value.shape[1] // parts
    half = lax.dynamic_slice_in_dim(frozen_value, part * width, width, axis=1)
    quarter = [half] + [exchange(half, 2 * k) for k in range(1, outer)]

    block = jax.ShapeDtypeStruct((outer, token_rows, slice_width), jnp.bfloat16)
    token = jax.ShapeDtypeStruct((1,), jnp.int32)
    x_mine, x_theirs, split = pl.pallas_call(
        split_kernel, out_shape=(block, block, token), in_specs=[SMEM, VMEM], out_specs=(VMEM, VMEM, SMEM),
        name="split_tokens", compiler_params=LIMIT,
    )(x[None], tokens)
    x_far = exchange(x_theirs, 1)
    y_mine = other_part(x_mine)
    xs = pl.pallas_call(
        interleave_kernel,
        out_shape=jax.ShapeDtypeStruct((group, 2 * token_rows, slice_width // 2), jnp.bfloat16),
        in_specs=[VMEM], out_specs=VMEM, name="pair_columns", compiler_params=LIMIT,
        cost_estimate=cost(flops=2 << 30, read=4 << 20),
    )(tokens)

    split, x_far, y_mine, xs = lax.optimization_barrier((split, x_far, y_mine, xs))
    pieces = jax.ShapeDtypeStruct((group, down_chunks + up_chunks, LANES), jnp.bfloat16)
    def tiles(store):
        view = store.reshape(store.shape[0] // TILE_ROWS, TILE_ROWS, store.shape[1] // LANES, LANES)
        return view.transpose(0, 2, 1, 3)

    sent, rows = pl.pallas_call(
        gather_kernel,
        out_shape=(pieces, jax.ShapeDtypeStruct((group,), jnp.int32)),
        in_specs=[SMEM, SMEM, ANY, ANY],
        out_specs=(ANY, SMEM),
        scratch_shapes=[
            pltpu.VMEM((group, down_chunks, TILE_ROWS, LANES), jnp.bfloat16),
            pltpu.VMEM((group, up_chunks, TILE_ROWS, LANES), jnp.bfloat16),
            pltpu.VMEM(((down_chunks + up_chunks) * 8, LANES), jnp.float32),
            pltpu.VMEM(pieces.shape, jnp.bfloat16),
            pltpu.SemaphoreType.DMA((3, group)),
        ],
        compiler_params=WIDE,
        cost_estimate=cost(read=40 << 20),
        name="pick_panels",
    )(split, asked, tiles(down_store), tiles(up_store))
    panels = lax.all_to_all(sent, "tensor", 0, 0)
    rows_core = other_core(rows)
    x_far, quarter, _ = lax.optimization_barrier((x_far, quarter, rows))
    y_far = other_part(x_far)

    owned_groups = ADAPTERS // lax.axis_size("dp") // 8
    down_shape = jax.ShapeDtypeStruct((owned_groups, down_chunks, 8, 1, LANES), jnp.float32)
    up_shape = jax.ShapeDtypeStruct((owned_groups, up_chunks, 8, 1, LANES), jnp.float32)
    down_zero, up_zero, cleared = pl.pallas_call(
        zero_kernel, out_shape=(down_shape, up_shape, token),
        in_specs=[SMEM], out_specs=(ANY, ANY, SMEM),
        scratch_shapes=[pltpu.VMEM((up_chunks, 8, 1, LANES), jnp.float32), pltpu.SemaphoreType.DMA((2,))],
        compiler_params=LIMIT, cost_estimate=cost(read=28 << 20), name="clear_rows",
    )(rows)
    quarter_core = [other_core(w) for w in quarter]
    panels, y_far, quarter_core = lax.optimization_barrier((panels, y_far, quarter_core))

    terms, lifted = pl.pallas_call(
        functools.partial(adapter_kernel, group, down_chunks),
        out_shape=(pieces, jax.ShapeDtypeStruct((token_rows, VALUE_OUTPUTS), jnp.float32)),
        in_specs=[VMEM] * 3 + [SMEM],
        out_specs=(VMEM, VMEM),
        scratch_shapes=[pltpu.VMEM((2 * R, VALUE_OUTPUTS), jnp.float32)],
        compiler_params=LIMIT,
        cost_estimate=cost(flops=3 << 30, read=8 << 20),
        name="adapter",
    )(xs, cotangent, panels, cleared)
    sums = jax.ShapeDtypeStruct((token_rows, parts * width), jnp.float32)
    own, to_part, to_inner, to_both = pl.pallas_call(
        base_kernel,
        out_shape=[sums] * 4,
        in_specs=[SMEM] + [VMEM] * (4 + 2 * outer) + [ANY],
        out_specs=[VMEM] * 4,
        compiler_params=LIMIT,
        cost_estimate=cost(flops=4 << 30, read=8 << 20),
        name="frozen_part",
    )(z[None], x_mine, y_mine, x_far, y_far, *quarter, *quarter_core, terms)
    opposite = [(a * group + t, (parts - 1 - a) * group + (t ^ 1)) for a in range(parts) for t in range(group)]
    back = lax.all_to_all(terms, "tensor", 0, 0)
    back, own = lax.optimization_barrier((back, own))
    back_core = other_core(back)

    grad_down, grad_up = pl.pallas_call(
        functools.partial(scatter_kernel, 2 * group, down_chunks, up_chunks),
        out_shape=(down_shape, up_shape),
        in_specs=[SMEM] * 3 + [ANY] * 4,
        out_specs=(ANY, ANY),
        input_output_aliases={5: 0, 6: 1},
        scratch_shapes=[
            pltpu.VMEM((2 * group,) + pieces.shape[1:], jnp.bfloat16),
            pltpu.VMEM((2 * group, down_chunks, 1, LANES), jnp.float32),
            pltpu.VMEM((2 * group, up_chunks, 1, LANES), jnp.float32),
            pltpu.VMEM((up_chunks, LANES), jnp.float32),
            pltpu.SemaphoreType.DMA((2 * group,)),
            pltpu.SemaphoreType.DMA(()),
        ],
        compiler_params=LIMIT,
        cost_estimate=cost(read=16 << 20),
        name="place_rows",
    )((core * (ADAPTERS // lax.axis_size("dp")))[None], rows, rows_core, back, back_core,
      down_zero, up_zero)
    grad_down = grad_down.reshape(owned_groups, down_chunks, 8, LANES).transpose(0, 2, 1, 3)
    grad_up = grad_up.reshape(owned_groups, up_chunks, 8, LANES).transpose(0, 2, 1, 3)

    kept = own + exchange(to_inner, 1)
    got = other_part(to_part) + lax.ppermute(to_both, ("parts", "tensor"), opposite)
    quarters = [[c[:, :width], c[:, width:]] for c in (kept, got)]

    def pick_quarter(c, a):
        first = quarters[a][0] if c == 0 else quarters[a][1]
        second = quarters[a][1] if c == 0 else quarters[a][0]
        return jnp.where(core == 0, first, second)

    def columns_of(c):
        low, high = pick_quarter(c, 0), pick_quarter(c, 1)
        return jnp.where(part == 0, low, high), jnp.where(part == 0, high, low)

    frozen_output = jnp.concatenate(columns_of(0) + columns_of(1), axis=1)
    mixed = (frozen_output + lifted).astype(jnp.bfloat16)
    return mixed, grad_down.reshape(owned_groups * 8, -1), grad_up.reshape(owned_groups * 8, -1)


def fits(mesh):
    group, cores, parts = mesh.shape["tensor"], mesh.shape["dp"], mesh.shape["parts"]
    return cores == 2 and parts == 2 and group <= 8 and group & (group - 1) == 0 and R == 8 * group


def body(mesh, tokens, *rest):
    block_adapter = rest[4]
    one_block = block_adapter.shape[0] == 1
    return (fast_body if fits(mesh) and one_block else plain_body)(tokens, *rest)


def solution(mesh):
    placed = (
        P(("parts", "dp", "tensor"), None),
        P(("parts", "dp", "tensor"), None),
        P("tensor", "dp"),
        P("parts", "tensor"),
        P("parts", "tensor"),
        P(("parts", "dp", "tensor")),
        P("parts"),
    )
    return jax.shard_map(
        functools.partial(body, mesh),
        mesh=mesh,
        in_specs=placed,
        out_specs=(
            P(("parts", "dp", "tensor"), None),
            P(("parts", "dp"), "tensor"),
            P(("parts", "dp"), "tensor"),
        ),
        check_vma=False,
    )
```

```python
import functools

import jax
import jax.numpy as jnp
from jax import lax
from jax.experimental import pallas as pl
from jax.experimental.pallas import tpu as pltpu
from jax.sharding import PartitionSpec as P

D = 5120
VALUE_OUTPUTS = 1024
R = 64
ADAPTERS = 256
LANES = 128
TILE_ROWS = 8

adapter_scale = 2.0
VMEM = pl.BlockSpec(memory_space=pltpu.VMEM)
SMEM = pl.BlockSpec(memory_space=pltpu.SMEM)
ANY = pl.BlockSpec(memory_space=pl.ANY)
LIMIT = pltpu.CompilerParams(vmem_limit_bytes=16 * 1024 * 1024)
WIDE = pltpu.CompilerParams(vmem_limit_bytes=60 * 1024 * 1024)


def cost(flops=0, read=0):
    return pl.CostEstimate(flops=flops, bytes_accessed=read, transcendentals=0)


def dot(a, b):
    return jnp.dot(a, b, preferred_element_type=jnp.float32)


def dot_t(a, b):
    return lax.dot_general(a, b, (((1,), (1,)), ((), ())), preferred_element_type=jnp.float32)


def t_dot(a, b):
    return lax.dot_general(a, b, (((0,), (0,)), ((), ())), preferred_element_type=jnp.float32)


def fold_rows(left, piece):
    return jnp.dot(left, piece, preferred_element_type=jnp.float32)


def store_rows(requests, adapter_slot):
    table = jnp.arange(adapter_slot.shape[0], dtype=jnp.int32)
    return jnp.sum(jnp.where(requests[:, None] == table[None, :], adapter_slot[None, :], 0), axis=1)


def plain_body(tokens, cotangent, frozen_value, down_store, up_store, block_adapter, adapter_slot):
    token_rows = tokens.shape[0]
    blocks_here = block_adapter.shape[0]
    block_rows = token_rows // blocks_here
    group = lax.axis_size("tensor")
    columns = lax.all_gather(frozen_value, "dp", axis=1, tiled=True)
    frozen_output = fold_rows(tokens, lax.all_gather(columns, "tensor", axis=0, tiled=True))
    requests = lax.all_gather(block_adapter, "tensor", axis=0, tiled=True)
    stored = store_rows(requests, adapter_slot)
    order = stored.reshape(group, blocks_here).T.reshape(-1)
    down_send = jnp.take(down_store, order, axis=0).reshape(blocks_here, group, -1)
    up_send = jnp.take(up_store, order, axis=0).reshape(blocks_here, group, -1)
    down_got = lax.all_to_all(down_send, "tensor", split_axis=1, concat_axis=1, tiled=True)
    up_got = lax.all_to_all(up_send, "tensor", split_axis=1, concat_axis=1, tiled=True)
    down_panel = down_got.reshape(blocks_here, D, R)
    up_panel = up_got.reshape(blocks_here, R, VALUE_OUTPUTS)
    token_blocks = tokens.reshape(blocks_here, block_rows, D)
    grad_blocks = cotangent.reshape(blocks_here, block_rows, VALUE_OUTPUTS)
    down_projected = jnp.einsum(
        "jtd,jdr->jtr", token_blocks, down_panel, preferred_element_type=jnp.float32
    ).astype(jnp.bfloat16)
    up_projected = jnp.einsum(
        "jtr,jrk->jtk", down_projected, up_panel, preferred_element_type=jnp.float32
    )
    mixed = (
        frozen_output + adapter_scale * up_projected.reshape(token_rows, VALUE_OUTPUTS)
    ).astype(jnp.bfloat16)
    down_projected_gradient = (
        adapter_scale
        * jnp.einsum("jtk,jrk->jtr", grad_blocks, up_panel, preferred_element_type=jnp.float32)
    ).astype(jnp.bfloat16)
    down_term = jnp.einsum(
        "jtd,jtr->jdr", token_blocks, down_projected_gradient, preferred_element_type=jnp.float32
    )
    up_weight_gradient = adapter_scale * jnp.einsum(
        "jtr,jtk->jrk", down_projected, grad_blocks, preferred_element_type=jnp.float32
    )
    down_back = lax.all_to_all(
        down_term.reshape(blocks_here, group, -1), "tensor", split_axis=1, concat_axis=1, tiled=True
    )
    up_back = lax.all_to_all(
        up_weight_gradient.reshape(blocks_here, group, -1), "tensor", split_axis=1, concat_axis=1, tiled=True
    )
    down_flat = down_back.reshape(blocks_here * group, -1)
    up_flat = up_back.reshape(blocks_here * group, -1)
    down_table = jax.ops.segment_sum(down_flat, order, num_segments=ADAPTERS)
    up_table = jax.ops.segment_sum(up_flat, order, num_segments=ADAPTERS)
    grad_down = lax.psum_scatter(down_table, "dp", scatter_dimension=0, tiled=True)
    grad_up = lax.psum_scatter(up_table, "dp", scatter_dimension=0, tiled=True)
    return mixed, grad_down, grad_up


def row_kernel(block_ref, slot_ref, out_ref):
    out_ref[...] = jnp.full(out_ref.shape, slot_ref[block_ref[0]], jnp.int32)


def split_kernel(where, x_ref, mine_ref, theirs_ref):
    inner = where[0]
    outer, rows, width = mine_ref.shape
    for k in range(outer):
        own = pl.multiple_of((2 * k + inner) * width, LANES)
        other = pl.multiple_of((2 * k + 1 - inner) * width, LANES)
        mine_ref[k] = x_ref[:, pl.ds(own, width)]
        theirs_ref[k] = x_ref[:, pl.ds(other, width)]


def interleave_kernel(x_ref, xs_ref):
    group, rows2, half = xs_ref.shape
    rows, width = rows2 // 2, 2 * half
    source = lax.broadcasted_iota(jnp.int32, (width, half), 0)
    target = lax.broadcasted_iota(jnp.int32, (width, half), 1)
    even = (source == 2 * target).astype(jnp.bfloat16)
    odd = (source == 2 * target + 1).astype(jnp.bfloat16)
    for k in range(group):
        x = x_ref[:, k * width:(k + 1) * width]
        xs_ref[k, :rows] = dot(x, even).astype(jnp.bfloat16)
        xs_ref[k, rows:] = dot(x, odd).astype(jnp.bfloat16)


def gather_kernel(asked, down_ref, up_ref, out_ref, rows_ref, down_buf, up_buf, flat, built, sems):
    count, down_chunks, up_chunks = down_buf.shape[0], down_buf.shape[1], up_buf.shape[1]
    across = up_chunks // 8

    def copies(t):
        tile = asked[t, 0, 0] // TILE_ROWS
        return (
            pltpu.make_async_copy(down_ref.at[tile], down_buf.at[t], sems.at[0, t]),
            pltpu.make_async_copy(up_ref.at[tile], up_buf.at[t], sems.at[1, t]),
            pltpu.make_async_copy(built.at[t], out_ref.at[t], sems.at[2, t]),
        )

    for t in range(count):
        down, up, _ = copies(t)
        down.start()
        up.start()
        rows_ref[t] = asked[t, 0, 0]

    def one(t, carry):
        down, up, leave = copies(t)
        up.wait()
        for j in range(up_chunks):
            place = down_chunks + (j % across) * 8 + j // across
            flat[place * 8:place * 8 + 8, :] = up_buf[t, j].astype(jnp.float32)
        down.wait()
        for j in range(down_chunks):
            flat[j * 8:j * 8 + 8, :] = down_buf[t, j].astype(jnp.float32)
        sub = asked[t, 0, 0] % TILE_ROWS
        built[t] = flat[pl.ds(sub, down_chunks + up_chunks, stride=8), :].astype(jnp.bfloat16)
        leave.start()
        return carry

    lax.fori_loop(0, count, one, 0)
    for t in range(count):
        copies(t)[2].wait()


def zero_kernel(after_ref, down_ref, up_ref, done_ref, zeros, sems):
    del after_ref
    done_ref[0] = 0
    zeros[...] = jnp.zeros_like(zeros)
    part = zeros.shape[0]
    copies = []
    for ref, sem in ((down_ref, sems.at[0]), (up_ref, sems.at[1])):
        for g in range(ref.shape[0]):
            for c in range(ref.shape[1] // part):
                copies.append(pltpu.make_async_copy(zeros, ref.at[g, pl.ds(c * part, part)], sem))
    for c in copies:
        c.start()
    for c in copies:
        c.wait()


def adapter_kernel(count, down_chunks, xs_ref, g_ref, pieces, _, out_ref, lifted_ref, up_panel):
    rows = g_ref.shape[0]
    across = g_ref.shape[1] // LANES
    total = jnp.zeros((2 * rows, LANES), jnp.float32)
    for t in range(count):
        total += dot(xs_ref[t], pieces[t, :down_chunks])
        for c in range(across):
            block = pieces[t, down_chunks + 8 * c:down_chunks + 8 * c + 8, :].astype(jnp.float32)
            up_panel[8 * t:8 * t + 8, c * LANES:(c + 1) * LANES] = block
            up_panel[R + 8 * t:R + 8 * t + 8, c * LANES:(c + 1) * LANES] = block
    panel = up_panel[...].astype(jnp.bfloat16)
    left = lax.broadcasted_iota(jnp.int32, (rows, LANES), 1) < R
    inner = total[:rows] + pltpu.roll(total[rows:], R, 1)
    inner = jnp.where(left, inner, 0.0).astype(jnp.bfloat16)
    g = g_ref[...]
    lifted_ref[...] = adapter_scale * dot(inner, panel)
    inner_grad = adapter_scale * dot_t(g, panel)
    diagonal = jnp.concatenate(
        [jnp.where(left, inner_grad, 0.0), jnp.where(left, 0.0, inner_grad)], axis=0
    ).astype(jnp.bfloat16)
    up_term = adapter_scale * t_dot(inner, g)
    for t in range(count):
        out_ref[t, :down_chunks] = t_dot(xs_ref[t], diagonal).astype(jnp.bfloat16)
        up_part = jnp.concatenate(
            [up_term[8 * t:8 * t + 8, c * LANES:(c + 1) * LANES] for c in range(across)], axis=0
        )
        out_ref[t, down_chunks:] = up_part.astype(jnp.bfloat16)


def scatter_kernel(count, down_chunks, up_chunks, first_row, rows_here, rows_core, *rest):
    sources, (down_out, up_out) = rest[:2], rest[4:6]
    pieces, down_sum, up_sum, ordered, arrived, sem = rest[6:]
    half = count // 2
    owned_rows = down_out.shape[0] * 8
    across = up_chunks // 8
    rows = [(rows_here if b < half else rows_core)[b % half] - first_row[0] for b in range(count)]
    arriving = [pltpu.make_async_copy(sources[b // half].at[b % half], pieces.at[b], arrived.at[b]) for b in range(count)]
    for copy in arriving:
        copy.start()
    owned = [(row >= 0) & (row < owned_rows) for row in rows]
    slots, final = [], []
    for b in range(count):
        slot, last = jnp.int32(b), jnp.bool_(True)
        for e in range(b - 1, -1, -1):
            slot = jnp.where(rows[e] == rows[b], e, slot)
        for e in range(b + 1, count):
            last = last & (rows[e] != rows[b])
        slots.append(slot)
        final.append(last)

    def copies(b):
        return (
            pltpu.make_async_copy(down_sum.at[slots[b]], down_out.at[rows[b] // 8, :, rows[b] % 8], sem),
            pltpu.make_async_copy(up_sum.at[slots[b]], up_out.at[rows[b] // 8, :, rows[b] % 8], sem),
        )

    for b in range(count):
        arriving[b].wait()

        @pl.when(owned[b])
        def _():
            slot = slots[b]
            down = pieces[b, :down_chunks].astype(jnp.float32).reshape(down_chunks, 1, LANES)
            for c in range(across):
                ordered[pl.ds(c, 8, stride=across), :] = pieces[
                    b, down_chunks + 8 * c:down_chunks + 8 * c + 8
                ].astype(jnp.float32)
            up = ordered[...].reshape(up_chunks, 1, LANES)

            @pl.when(slot == b)
            def _():
                down_sum[b] = down
                up_sum[b] = up

            @pl.when(slot != b)
            def _():
                down_sum[slot] += down
                up_sum[slot] += up

            @pl.when(final[b])
            def _():
                for copy in copies(b):
                    copy.start()

    for b in range(count):
        @pl.when(owned[b] & final[b])
        def _():
            for copy in copies(b):
                copy.wait()


def base_kernel(where, *refs):
    x_refs, out_refs = refs[:4], refs[-4:]
    outer, rows, _ = x_refs[0].shape
    width = refs[4].shape[1]
    for h in range(2):
        total = 0.0
        for k in range(outer):
            left = jnp.concatenate([ref[where[0] ^ k] for ref in x_refs], axis=0)
            total += dot(left, refs[4 + h * outer + k][...])
        for b, ref in enumerate(out_refs):
            ref[:, h * width:(h + 1) * width] = total[b * rows:(b + 1) * rows]


def fast_body(tokens, cotangent, frozen_value, down_store, up_store, block_adapter, adapter_slot):
    group, parts = lax.axis_size("tensor"), lax.axis_size("parts")
    outer = group // 2
    token_rows = tokens.shape[0]
    slice_width = D // group
    down_chunks = down_store.shape[1] // LANES
    up_chunks = up_store.shape[1] // LANES
    me, part, core = lax.axis_index("tensor"), lax.axis_index("parts"), lax.axis_index("dp")
    z, x = me // 2, me % 2

    def exchange(value, s):
        return lax.ppermute(value, "tensor", [(t, t ^ s) for t in range(group)])

    def other_core(value):
        return lax.ppermute(value, "dp", [(0, 1), (1, 0)])

    def other_part(value):
        return lax.ppermute(value, "parts", [(a, parts - 1 - a) for a in range(parts)])

    row = pl.pallas_call(
        row_kernel, out_shape=jax.ShapeDtypeStruct((group, 1, LANES), jnp.int32),
        in_specs=[SMEM, SMEM], out_specs=VMEM, name="own_row",
    )(block_adapter, adapter_slot)
    asked = lax.all_to_all(row, "tensor", 0, 0)
    split_from, row = lax.optimization_barrier((tokens, row))

    width = frozen_value.shape[1] // parts
    half = lax.dynamic_slice_in_dim(frozen_value, part * width, width, axis=1)
    quarter = [half] + [exchange(half, 2 * k) for k in range(1, outer)]

    block = jax.ShapeDtypeStruct((outer, token_rows, slice_width), jnp.bfloat16)
    token = jax.ShapeDtypeStruct((1,), jnp.int32)
    x_mine, x_theirs = pl.pallas_call(
        split_kernel, out_shape=(block, block), in_specs=[SMEM, VMEM], out_specs=(VMEM, VMEM),
        name="split_tokens", compiler_params=LIMIT,
    )(x[None], split_from)
    x_far = exchange(x_theirs, 1)
    y_mine = other_part(x_mine)
    pieces = jax.ShapeDtypeStruct((group, down_chunks + up_chunks, LANES), jnp.bfloat16)
    def tiles(store):
        view = store.reshape(store.shape[0] // TILE_ROWS, TILE_ROWS, store.shape[1] // LANES, LANES)
        return view.transpose(0, 2, 1, 3)

    sent, rows = pl.pallas_call(
        gather_kernel,
        out_shape=(pieces, jax.ShapeDtypeStruct((group,), jnp.int32)),
        in_specs=[SMEM, ANY, ANY],
        out_specs=(ANY, SMEM),
        scratch_shapes=[
            pltpu.VMEM((group, down_chunks, TILE_ROWS, LANES), jnp.bfloat16),
            pltpu.VMEM((group, up_chunks, TILE_ROWS, LANES), jnp.bfloat16),
            pltpu.VMEM(((down_chunks + up_chunks) * 8, LANES), jnp.float32),
            pltpu.VMEM(pieces.shape, jnp.bfloat16),
            pltpu.SemaphoreType.DMA((3, group)),
        ],
        compiler_params=WIDE,
        cost_estimate=cost(read=40 << 20),
        name="pick_panels",
    )(asked, tiles(down_store), tiles(up_store))
    sent, quarter = lax.optimization_barrier((sent, quarter))
    panels = lax.all_to_all(sent, "tensor", 0, 0)
    rows_core = other_core(rows)
    x_far, y_mine, picked = lax.optimization_barrier((x_far, y_mine, rows))
    y_far = other_part(x_far)
    pair_from, _ = lax.optimization_barrier((tokens, rows))
    xs = pl.pallas_call(
        interleave_kernel,
        out_shape=jax.ShapeDtypeStruct((group, 2 * token_rows, slice_width // 2), jnp.bfloat16),
        in_specs=[VMEM], out_specs=VMEM, name="pair_columns", compiler_params=LIMIT,
        cost_estimate=cost(flops=2 << 30, read=4 << 20),
    )(pair_from)

    owned_groups = ADAPTERS // lax.axis_size("dp") // 8
    down_shape = jax.ShapeDtypeStruct((owned_groups, down_chunks, 8, 1, LANES), jnp.float32)
    up_shape = jax.ShapeDtypeStruct((owned_groups, up_chunks, 8, 1, LANES), jnp.float32)
    down_zero, up_zero, cleared = pl.pallas_call(
        zero_kernel, out_shape=(down_shape, up_shape, token),
        in_specs=[SMEM], out_specs=(ANY, ANY, SMEM),
        scratch_shapes=[pltpu.VMEM((up_chunks, 8, 1, LANES), jnp.float32), pltpu.SemaphoreType.DMA((2,))],
        compiler_params=LIMIT, cost_estimate=cost(read=28 << 20), name="clear_rows",
    )(picked)
    quarter_core = [other_core(w) for w in quarter]
    panels, y_far, quarter_core = lax.optimization_barrier((panels, y_far, quarter_core))

    terms, lifted = pl.pallas_call(
        functools.partial(adapter_kernel, group, down_chunks),
        out_shape=(pieces, jax.ShapeDtypeStruct((token_rows, VALUE_OUTPUTS), jnp.float32)),
        in_specs=[VMEM] * 3 + [SMEM],
        out_specs=(VMEM, VMEM),
        scratch_shapes=[pltpu.VMEM((2 * R, VALUE_OUTPUTS), jnp.float32)],
        compiler_params=LIMIT,
        cost_estimate=cost(flops=3 << 30, read=8 << 20),
        name="adapter",
    )(xs, cotangent, panels, cleared)
    sums = jax.ShapeDtypeStruct((token_rows, parts * width), jnp.float32)
    own, to_part, to_inner, to_both = pl.pallas_call(
        base_kernel,
        out_shape=[sums] * 4,
        in_specs=[SMEM] + [VMEM] * (4 + 2 * outer) + [ANY],
        out_specs=[VMEM] * 4,
        compiler_params=LIMIT,
        cost_estimate=cost(flops=4 << 30, read=8 << 20),
        name="frozen_part",
    )(z[None], x_mine, y_mine, x_far, y_far, *quarter, *quarter_core, terms)
    opposite = [(a * group + t, (parts - 1 - a) * group + (t ^ 1)) for a in range(parts) for t in range(group)]
    back = lax.all_to_all(terms, "tensor", 0, 0)
    arrived = (exchange(to_inner, 1), other_part(to_part), lax.ppermute(to_both, ("parts", "tensor"), opposite))
    back, arrived = lax.optimization_barrier((back, arrived))
    back_core = other_core(back)

    grad_down, grad_up = pl.pallas_call(
        functools.partial(scatter_kernel, 2 * group, down_chunks, up_chunks),
        out_shape=(down_shape, up_shape),
        in_specs=[SMEM] * 3 + [ANY] * 4,
        out_specs=(ANY, ANY),
        input_output_aliases={5: 0, 6: 1},
        scratch_shapes=[
            pltpu.VMEM((2 * group,) + pieces.shape[1:], jnp.bfloat16),
            pltpu.VMEM((2 * group, down_chunks, 1, LANES), jnp.float32),
            pltpu.VMEM((2 * group, up_chunks, 1, LANES), jnp.float32),
            pltpu.VMEM((up_chunks, LANES), jnp.float32),
            pltpu.SemaphoreType.DMA((2 * group,)),
            pltpu.SemaphoreType.DMA(()),
        ],
        compiler_params=LIMIT,
        cost_estimate=cost(read=16 << 20),
        name="place_rows",
    )((core * (ADAPTERS // lax.axis_size("dp")))[None], rows, rows_core, back, back_core,
      down_zero, up_zero)
    grad_down = grad_down.reshape(owned_groups, down_chunks, 8, LANES).transpose(0, 2, 1, 3)
    grad_up = grad_up.reshape(owned_groups, up_chunks, 8, LANES).transpose(0, 2, 1, 3)

    kept, got = own + arrived[0], arrived[1] + arrived[2]
    quarters = [[c[:, :width], c[:, width:]] for c in (kept, got)]

    def pick_quarter(c, a):
        first = quarters[a][0] if c == 0 else quarters[a][1]
        second = quarters[a][1] if c == 0 else quarters[a][0]
        return jnp.where(core == 0, first, second)

    def columns_of(c):
        low, high = pick_quarter(c, 0), pick_quarter(c, 1)
        return jnp.where(part == 0, low, high), jnp.where(part == 0, high, low)

    frozen_output = jnp.concatenate(columns_of(0) + columns_of(1), axis=1)
    mixed = (frozen_output + lifted).astype(jnp.bfloat16)
    return mixed, grad_down.reshape(owned_groups * 8, -1), grad_up.reshape(owned_groups * 8, -1)


def fits(mesh):
    group, cores, parts = mesh.shape["tensor"], mesh.shape["dp"], mesh.shape["parts"]
    return cores == 2 and parts == 2 and group <= 8 and group & (group - 1) == 0 and R == 8 * group


def body(mesh, tokens, *rest):
    block_adapter = rest[4]
    one_block = block_adapter.shape[0] == 1
    return (fast_body if fits(mesh) and one_block else plain_body)(tokens, *rest)


def solution(mesh):
    placed = (
        P(("parts", "dp", "tensor"), None),
        P(("parts", "dp", "tensor"), None),
        P("tensor", "dp"),
        P("parts", "tensor"),
        P("parts", "tensor"),
        P(("parts", "dp", "tensor")),
        P("parts"),
    )
    return jax.shard_map(
        functools.partial(body, mesh),
        mesh=mesh,
        in_specs=placed,
        out_specs=(
            P(("parts", "dp", "tensor"), None),
            P(("parts", "dp"), "tensor"),
            P(("parts", "dp"), "tensor"),
        ),
        check_vma=False,
    )
```

```python
import functools

import jax
import jax.numpy as jnp
from jax import lax
from jax.experimental import pallas as pl
from jax.experimental.pallas import tpu as pltpu
from jax.sharding import PartitionSpec as P

D = 5120
VALUE_OUTPUTS = 1024
R = 64
ADAPTERS = 256
LANES = 128
TILE_ROWS = 8

adapter_scale = 2.0
VMEM = pl.BlockSpec(memory_space=pltpu.VMEM)
SMEM = pl.BlockSpec(memory_space=pltpu.SMEM)
ANY = pl.BlockSpec(memory_space=pl.ANY)
LIMIT = pltpu.CompilerParams(vmem_limit_bytes=16 * 1024 * 1024)
WIDE = pltpu.CompilerParams(vmem_limit_bytes=60 * 1024 * 1024)


def cost(flops=0, read=0):
    return pl.CostEstimate(flops=flops, bytes_accessed=read, transcendentals=0)


def dot(a, b):
    return jnp.dot(a, b, preferred_element_type=jnp.float32)


def dot_t(a, b):
    return lax.dot_general(a, b, (((1,), (1,)), ((), ())), preferred_element_type=jnp.float32)


def t_dot(a, b):
    return lax.dot_general(a, b, (((0,), (0,)), ((), ())), preferred_element_type=jnp.float32)


def fold_rows(left, piece):
    return jnp.dot(left, piece, preferred_element_type=jnp.float32)


def store_rows(requests, adapter_slot):
    table = jnp.arange(adapter_slot.shape[0], dtype=jnp.int32)
    return jnp.sum(jnp.where(requests[:, None] == table[None, :], adapter_slot[None, :], 0), axis=1)


def plain_body(tokens, cotangent, frozen_value, down_store, up_store, block_adapter, adapter_slot):
    token_rows = tokens.shape[0]
    blocks_here = block_adapter.shape[0]
    block_rows = token_rows // blocks_here
    group = lax.axis_size("tensor")
    columns = lax.all_gather(frozen_value, "dp", axis=1, tiled=True)
    frozen_output = fold_rows(tokens, lax.all_gather(columns, "tensor", axis=0, tiled=True))
    requests = lax.all_gather(block_adapter, "tensor", axis=0, tiled=True)
    stored = store_rows(requests, adapter_slot)
    order = stored.reshape(group, blocks_here).T.reshape(-1)
    down_send = jnp.take(down_store, order, axis=0).reshape(blocks_here, group, -1)
    up_send = jnp.take(up_store, order, axis=0).reshape(blocks_here, group, -1)
    down_got = lax.all_to_all(down_send, "tensor", split_axis=1, concat_axis=1, tiled=True)
    up_got = lax.all_to_all(up_send, "tensor", split_axis=1, concat_axis=1, tiled=True)
    down_panel = down_got.reshape(blocks_here, D, R)
    up_panel = up_got.reshape(blocks_here, R, VALUE_OUTPUTS)
    token_blocks = tokens.reshape(blocks_here, block_rows, D)
    grad_blocks = cotangent.reshape(blocks_here, block_rows, VALUE_OUTPUTS)
    down_projected = jnp.einsum(
        "jtd,jdr->jtr", token_blocks, down_panel, preferred_element_type=jnp.float32
    ).astype(jnp.bfloat16)
    up_projected = jnp.einsum(
        "jtr,jrk->jtk", down_projected, up_panel, preferred_element_type=jnp.float32
    )
    mixed = (
        frozen_output + adapter_scale * up_projected.reshape(token_rows, VALUE_OUTPUTS)
    ).astype(jnp.bfloat16)
    down_projected_gradient = (
        adapter_scale
        * jnp.einsum("jtk,jrk->jtr", grad_blocks, up_panel, preferred_element_type=jnp.float32)
    ).astype(jnp.bfloat16)
    down_term = jnp.einsum(
        "jtd,jtr->jdr", token_blocks, down_projected_gradient, preferred_element_type=jnp.float32
    )
    up_weight_gradient = adapter_scale * jnp.einsum(
        "jtr,jtk->jrk", down_projected, grad_blocks, preferred_element_type=jnp.float32
    )
    down_back = lax.all_to_all(
        down_term.reshape(blocks_here, group, -1), "tensor", split_axis=1, concat_axis=1, tiled=True
    )
    up_back = lax.all_to_all(
        up_weight_gradient.reshape(blocks_here, group, -1), "tensor", split_axis=1, concat_axis=1, tiled=True
    )
    down_flat = down_back.reshape(blocks_here * group, -1)
    up_flat = up_back.reshape(blocks_here * group, -1)
    down_table = jax.ops.segment_sum(down_flat, order, num_segments=ADAPTERS)
    up_table = jax.ops.segment_sum(up_flat, order, num_segments=ADAPTERS)
    grad_down = lax.psum_scatter(down_table, "dp", scatter_dimension=0, tiled=True)
    grad_up = lax.psum_scatter(up_table, "dp", scatter_dimension=0, tiled=True)
    return mixed, grad_down, grad_up


def row_kernel(block_ref, slot_ref, out_ref):
    out_ref[...] = jnp.full(out_ref.shape, slot_ref[block_ref[0]], jnp.int32)


def split_kernel(where, x_ref, mine_ref, theirs_ref):
    inner = where[0]
    outer, rows, width = mine_ref.shape
    for k in range(outer):
        own = pl.multiple_of((2 * k + inner) * width, LANES)
        other = pl.multiple_of((2 * k + 1 - inner) * width, LANES)
        mine_ref[k] = x_ref[:, pl.ds(own, width)]
        theirs_ref[k] = x_ref[:, pl.ds(other, width)]


def interleave_kernel(x_ref, xs_ref):
    group, rows2, half = xs_ref.shape
    rows, width = rows2 // 2, 2 * half
    source = lax.broadcasted_iota(jnp.int32, (width, half), 0)
    target = lax.broadcasted_iota(jnp.int32, (width, half), 1)
    even = (source == 2 * target).astype(jnp.bfloat16)
    odd = (source == 2 * target + 1).astype(jnp.bfloat16)
    for k in range(group):
        x = x_ref[:, k * width:(k + 1) * width]
        xs_ref[k, :rows] = dot(x, even).astype(jnp.bfloat16)
        xs_ref[k, rows:] = dot(x, odd).astype(jnp.bfloat16)


def gather_kernel(asked, down_ref, up_ref, out_ref, rows_ref, down_buf, up_buf, flat, built, sems):
    count, down_chunks, up_chunks = down_buf.shape[0], down_buf.shape[1], up_buf.shape[1]
    across = up_chunks // 8

    def copies(t):
        tile = asked[t, 0, 0] // TILE_ROWS
        return (
            pltpu.make_async_copy(down_ref.at[tile], down_buf.at[t], sems.at[0, t]),
            pltpu.make_async_copy(up_ref.at[tile], up_buf.at[t], sems.at[1, t]),
            pltpu.make_async_copy(built.at[t], out_ref.at[t], sems.at[2, t]),
        )

    for t in range(count):
        down, up, _ = copies(t)
        down.start()
        up.start()
        rows_ref[t] = asked[t, 0, 0]

    def one(t, carry):
        down, up, leave = copies(t)
        up.wait()
        for j in range(up_chunks):
            place = down_chunks + (j % across) * 8 + j // across
            flat[place * 8:place * 8 + 8, :] = up_buf[t, j].astype(jnp.float32)
        down.wait()
        for j in range(down_chunks):
            flat[j * 8:j * 8 + 8, :] = down_buf[t, j].astype(jnp.float32)
        sub = asked[t, 0, 0] % TILE_ROWS
        built[t] = flat[pl.ds(sub, down_chunks + up_chunks, stride=8), :].astype(jnp.bfloat16)
        leave.start()
        return carry

    lax.fori_loop(0, count, one, 0)
    for t in range(count):
        copies(t)[2].wait()


def zero_kernel(after_ref, down_ref, up_ref, done_ref, zeros, sems):
    del after_ref
    done_ref[0] = 0
    zeros[...] = jnp.zeros_like(zeros)
    part = zeros.shape[0]
    copies = []
    for ref, sem in ((down_ref, sems.at[0]), (up_ref, sems.at[1])):
        for g in range(ref.shape[0]):
            for c in range(ref.shape[1] // part):
                copies.append(pltpu.make_async_copy(zeros, ref.at[g, pl.ds(c * part, part)], sem))
    for c in copies:
        c.start()
    for c in copies:
        c.wait()


def adapter_kernel(
    count, down_chunks, xs_from, g_from, pieces_from, after, out_to, lifted_ref,
    up_panel, xs_ref, g_ref, pieces, out_ref, sems,
):
    del after
    rows = g_ref.shape[0]
    across = g_ref.shape[1] // LANES
    fetch_g = pltpu.make_async_copy(g_from, g_ref, sems.at[3, 0])
    fetch = [
        (
            pltpu.make_async_copy(pieces_from.at[t], pieces.at[t], sems.at[0, t]),
            pltpu.make_async_copy(xs_from.at[t], xs_ref.at[t], sems.at[1, t]),
        )
        for t in range(count)
    ]
    leave = [pltpu.make_async_copy(out_ref.at[t], out_to.at[t], sems.at[2, t]) for t in range(count)]
    for panel_copy, x_copy in fetch:
        panel_copy.start()
        x_copy.start()
    fetch_g.start()
    total = jnp.zeros((2 * rows, LANES), jnp.float32)
    for t in range(count):
        for copy in fetch[t]:
            copy.wait()
        total += dot(xs_ref[t], pieces[t, :down_chunks])
        for c in range(across):
            block = pieces[t, down_chunks + 8 * c:down_chunks + 8 * c + 8, :].astype(jnp.float32)
            up_panel[8 * t:8 * t + 8, c * LANES:(c + 1) * LANES] = block
            up_panel[R + 8 * t:R + 8 * t + 8, c * LANES:(c + 1) * LANES] = block
    fetch_g.wait()
    panel = up_panel[...].astype(jnp.bfloat16)
    left = lax.broadcasted_iota(jnp.int32, (rows, LANES), 1) < R
    inner = total[:rows] + pltpu.roll(total[rows:], R, 1)
    inner = jnp.where(left, inner, 0.0).astype(jnp.bfloat16)
    g = g_ref[...]
    lifted_ref[...] = adapter_scale * dot(inner, panel)
    inner_grad = adapter_scale * dot_t(g, panel)
    diagonal = jnp.concatenate(
        [jnp.where(left, inner_grad, 0.0), jnp.where(left, 0.0, inner_grad)], axis=0
    ).astype(jnp.bfloat16)
    up_term = adapter_scale * t_dot(inner, g)
    for t in range(count):
        out_ref[t, :down_chunks] = t_dot(xs_ref[t], diagonal).astype(jnp.bfloat16)
        up_part = jnp.concatenate(
            [up_term[8 * t:8 * t + 8, c * LANES:(c + 1) * LANES] for c in range(across)], axis=0
        )
        out_ref[t, down_chunks:] = up_part.astype(jnp.bfloat16)
        leave[t].start()
    for copy in leave:
        copy.wait()


def scatter_kernel(count, down_chunks, up_chunks, first_row, rows_here, rows_core, *rest):
    sources, (down_out, up_out) = rest[:2], rest[4:6]
    pieces, down_sum, up_sum, ordered, arrived, sem = rest[6:]
    half = count // 2
    owned_rows = down_out.shape[0] * 8
    across = up_chunks // 8
    rows = [(rows_here if b < half else rows_core)[b % half] - first_row[0] for b in range(count)]
    arriving = [pltpu.make_async_copy(sources[b // half].at[b % half], pieces.at[b], arrived.at[b]) for b in range(count)]
    for copy in arriving:
        copy.start()
    owned = [(row >= 0) & (row < owned_rows) for row in rows]
    slots, final = [], []
    for b in range(count):
        slot, last = jnp.int32(b), jnp.bool_(True)
        for e in range(b - 1, -1, -1):
            slot = jnp.where(rows[e] == rows[b], e, slot)
        for e in range(b + 1, count):
            last = last & (rows[e] != rows[b])
        slots.append(slot)
        final.append(last)

    def copies(b):
        return (
            pltpu.make_async_copy(down_sum.at[slots[b]], down_out.at[rows[b] // 8, :, rows[b] % 8], sem),
            pltpu.make_async_copy(up_sum.at[slots[b]], up_out.at[rows[b] // 8, :, rows[b] % 8], sem),
        )

    for b in range(count):
        arriving[b].wait()

        @pl.when(owned[b])
        def _():
            slot = slots[b]
            down = pieces[b, :down_chunks].astype(jnp.float32).reshape(down_chunks, 1, LANES)
            for c in range(across):
                ordered[pl.ds(c, 8, stride=across), :] = pieces[
                    b, down_chunks + 8 * c:down_chunks + 8 * c + 8
                ].astype(jnp.float32)
            up = ordered[...].reshape(up_chunks, 1, LANES)

            @pl.when(slot == b)
            def _():
                down_sum[b] = down
                up_sum[b] = up

            @pl.when(slot != b)
            def _():
                down_sum[slot] += down
                up_sum[slot] += up

            @pl.when(final[b])
            def _():
                for copy in copies(b):
                    copy.start()

    for b in range(count):
        @pl.when(owned[b] & final[b])
        def _():
            for copy in copies(b):
                copy.wait()


def base_kernel(where, *refs):
    x_from, w_from, out_refs = refs[:4], refs[4:-8], refs[-7:-3]
    x_buf, w_buf, sems = refs[-3:]
    outer, rows, _ = x_from[0].shape
    width = w_buf.shape[2]
    fetch_x = [pltpu.make_async_copy(ref, x_buf.at[b], sems.at[0, b]) for b, ref in enumerate(x_from)]
    fetch_w = [pltpu.make_async_copy(ref, w_buf.at[b], sems.at[1, b]) for b, ref in enumerate(w_from)]
    for copy in fetch_x + fetch_w:
        copy.start()
    for copy in fetch_x:
        copy.wait()
    for h in range(2):
        total = 0.0
        for k in range(outer):
            fetch_w[h * outer + k].wait()
            left = jnp.concatenate([x_buf[b, where[k]] for b in range(4)], axis=0)
            total += dot(left, w_buf[h * outer + k])
        for b, ref in enumerate(out_refs):
            ref[:, h * width:(h + 1) * width] = total[b * rows:(b + 1) * rows]


def fast_body(tokens, cotangent, frozen_value, down_store, up_store, block_adapter, adapter_slot):
    group, parts = lax.axis_size("tensor"), lax.axis_size("parts")
    outer = group // 2
    token_rows = tokens.shape[0]
    slice_width = D // group
    down_chunks = down_store.shape[1] // LANES
    up_chunks = up_store.shape[1] // LANES
    me, part, core = lax.axis_index("tensor"), lax.axis_index("parts"), lax.axis_index("dp")
    z, x = me // 2, me % 2

    def exchange(value, s):
        return lax.ppermute(value, "tensor", [(t, t ^ s) for t in range(group)])

    def other_core(value):
        return lax.ppermute(value, "dp", [(0, 1), (1, 0)])

    def other_part(value):
        return lax.ppermute(value, "parts", [(a, parts - 1 - a) for a in range(parts)])

    row = pl.pallas_call(
        row_kernel, out_shape=jax.ShapeDtypeStruct((group, 1, LANES), jnp.int32),
        in_specs=[SMEM, SMEM], out_specs=VMEM, name="own_row",
    )(block_adapter, adapter_slot)
    asked = lax.all_to_all(row, "tensor", 0, 0)

    width = frozen_value.shape[1] // parts
    half = lax.dynamic_slice_in_dim(frozen_value, part * width, width, axis=1)
    split_from, half, asked = lax.optimization_barrier((tokens, half, asked))
    near = exchange(half, 2)

    block = jax.ShapeDtypeStruct((outer, token_rows, slice_width), jnp.bfloat16)
    token = jax.ShapeDtypeStruct((1,), jnp.int32)
    x_mine, x_theirs = pl.pallas_call(
        split_kernel, out_shape=(block, block), in_specs=[SMEM, VMEM], out_specs=(VMEM, VMEM),
        name="split_tokens", compiler_params=LIMIT,
    )(x[None], split_from)
    x_far = exchange(x_theirs, 1)
    y_mine = other_part(x_mine)
    pieces = jax.ShapeDtypeStruct((group, down_chunks + up_chunks, LANES), jnp.bfloat16)
    def tiles(store):
        view = store.reshape(store.shape[0] // TILE_ROWS, TILE_ROWS, store.shape[1] // LANES, LANES)
        return view.transpose(0, 2, 1, 3)

    sent, rows = pl.pallas_call(
        gather_kernel,
        out_shape=(pieces, jax.ShapeDtypeStruct((group,), jnp.int32)),
        in_specs=[SMEM, ANY, ANY],
        out_specs=(ANY, SMEM),
        scratch_shapes=[
            pltpu.VMEM((group, down_chunks, TILE_ROWS, LANES), jnp.bfloat16),
            pltpu.VMEM((group, up_chunks, TILE_ROWS, LANES), jnp.bfloat16),
            pltpu.VMEM(((down_chunks + up_chunks) * 8, LANES), jnp.float32),
            pltpu.VMEM(pieces.shape, jnp.bfloat16),
            pltpu.SemaphoreType.DMA((3, group)),
        ],
        compiler_params=WIDE,
        cost_estimate=cost(read=40 << 20),
        name="pick_panels",
    )(asked, tiles(down_store), tiles(up_store))
    sent, near, half, x_far, y_mine = lax.optimization_barrier((sent, near, half, x_far, y_mine))
    panels = lax.all_to_all(sent, "tensor", 0, 0)
    rows_core = other_core(rows)
    y_far = other_part(x_far)
    middle = [(t, t ^ 6) for t in range(group) if t // 2 in (1, 2)]
    ends = [(t, t ^ 2) for t in range(group) if t // 2 in (1, 2)]
    passed = [lax.ppermute(w, "tensor", middle) for w in (half, near)]
    early_core = [other_core(w) for w in (half, near)]
    pair_from, _ = lax.optimization_barrier((tokens, rows))
    xs = pl.pallas_call(
        interleave_kernel,
        out_shape=jax.ShapeDtypeStruct((group, 2 * token_rows, slice_width // 2), jnp.bfloat16),
        in_specs=[VMEM], out_specs=VMEM, name="pair_columns", compiler_params=LIMIT,
        cost_estimate=cost(flops=2 << 30, read=4 << 20),
    )(pair_from)

    owned_groups = ADAPTERS // lax.axis_size("dp") // 8
    down_shape = jax.ShapeDtypeStruct((owned_groups, down_chunks, 8, 1, LANES), jnp.float32)
    up_shape = jax.ShapeDtypeStruct((owned_groups, up_chunks, 8, 1, LANES), jnp.float32)
    down_zero, up_zero, cleared = pl.pallas_call(
        zero_kernel, out_shape=(down_shape, up_shape, token),
        in_specs=[SMEM], out_specs=(ANY, ANY, SMEM),
        scratch_shapes=[pltpu.VMEM((up_chunks, 8, 1, LANES), jnp.float32), pltpu.SemaphoreType.DMA((2,))],
        compiler_params=LIMIT, cost_estimate=cost(read=28 << 20), name="clear_rows",
    )(rows)
    panels, passed, y_far, early_core = lax.optimization_barrier((panels, passed, y_far, early_core))

    terms, lifted = pl.pallas_call(
        functools.partial(adapter_kernel, group, down_chunks),
        out_shape=(pieces, jax.ShapeDtypeStruct((token_rows, VALUE_OUTPUTS), jnp.float32)),
        in_specs=[ANY] * 3 + [SMEM],
        out_specs=(ANY, VMEM),
        scratch_shapes=[
            pltpu.VMEM((2 * R, VALUE_OUTPUTS), jnp.float32),
            pltpu.VMEM(xs.shape, jnp.bfloat16),
            pltpu.VMEM(cotangent.shape, jnp.bfloat16),
            pltpu.VMEM(pieces.shape, jnp.bfloat16),
            pltpu.VMEM(pieces.shape, jnp.bfloat16),
            pltpu.SemaphoreType.DMA((4, group)),
        ],
        compiler_params=WIDE,
        cost_estimate=cost(flops=3 << 30, read=8 << 20),
        name="adapter",
    )(xs, cotangent, panels, cleared)
    _, passed = lax.optimization_barrier((terms, passed))
    inside = (z == 1) | (z == 2)
    far = [jnp.where(inside, w, lax.ppermute(w, "tensor", ends)) for w in passed]
    quarters = [half, near] + far + early_core + [other_core(w) for w in far]
    source = jnp.stack([z, z ^ 1, jnp.where(z < 2, 2, 1), jnp.where(z < 2, 3, 0)])
    sums = jax.ShapeDtypeStruct((token_rows, parts * width), jnp.float32)
    own, to_part, to_inner, to_both = pl.pallas_call(
        base_kernel,
        out_shape=[sums] * 4,
        in_specs=[SMEM] + [ANY] * (5 + 2 * outer),
        out_specs=[VMEM] * 4,
        scratch_shapes=[
            pltpu.VMEM((4,) + block.shape, jnp.bfloat16),
            pltpu.VMEM((2 * outer, slice_width, width), jnp.bfloat16),
            pltpu.SemaphoreType.DMA((2, 2 * outer)),
        ],
        compiler_params=WIDE,
        cost_estimate=cost(flops=4 << 30, read=8 << 20),
        name="frozen_part",
    )(source, x_mine, y_mine, x_far, y_far, *quarters, terms)
    opposite = [(a * group + t, (parts - 1 - a) * group + (t ^ 1)) for a in range(parts) for t in range(group)]
    back = lax.all_to_all(terms, "tensor", 0, 0)
    arrived = (exchange(to_inner, 1), other_part(to_part), lax.ppermute(to_both, ("parts", "tensor"), opposite))
    back, arrived = lax.optimization_barrier((back, arrived))
    back_core = other_core(back)

    grad_down, grad_up = pl.pallas_call(
        functools.partial(scatter_kernel, 2 * group, down_chunks, up_chunks),
        out_shape=(down_shape, up_shape),
        in_specs=[SMEM] * 3 + [ANY] * 4,
        out_specs=(ANY, ANY),
        input_output_aliases={5: 0, 6: 1},
        scratch_shapes=[
            pltpu.VMEM((2 * group,) + pieces.shape[1:], jnp.bfloat16),
            pltpu.VMEM((2 * group, down_chunks, 1, LANES), jnp.float32),
            pltpu.VMEM((2 * group, up_chunks, 1, LANES), jnp.float32),
            pltpu.VMEM((up_chunks, LANES), jnp.float32),
            pltpu.SemaphoreType.DMA((2 * group,)),
            pltpu.SemaphoreType.DMA(()),
        ],
        compiler_params=LIMIT,
        cost_estimate=cost(read=16 << 20),
        name="place_rows",
    )((core * (ADAPTERS // lax.axis_size("dp")))[None], rows, rows_core, back, back_core,
      down_zero, up_zero)
    grad_down = grad_down.reshape(owned_groups, down_chunks, 8, LANES).transpose(0, 2, 1, 3)
    grad_up = grad_up.reshape(owned_groups, up_chunks, 8, LANES).transpose(0, 2, 1, 3)

    kept, got = own + arrived[0], arrived[1] + arrived[2]
    quarters = [[c[:, :width], c[:, width:]] for c in (kept, got)]

    def pick_quarter(c, a):
        first = quarters[a][0] if c == 0 else quarters[a][1]
        second = quarters[a][1] if c == 0 else quarters[a][0]
        return jnp.where(core == 0, first, second)

    def columns_of(c):
        low, high = pick_quarter(c, 0), pick_quarter(c, 1)
        return jnp.where(part == 0, low, high), jnp.where(part == 0, high, low)

    frozen_output = jnp.concatenate(columns_of(0) + columns_of(1), axis=1)
    mixed = (frozen_output + lifted).astype(jnp.bfloat16)
    return mixed, grad_down.reshape(owned_groups * 8, -1), grad_up.reshape(owned_groups * 8, -1)


def fits(mesh):
    group, cores, parts = mesh.shape["tensor"], mesh.shape["dp"], mesh.shape["parts"]
    return cores == 2 and parts == 2 and group <= 8 and group & (group - 1) == 0 and R == 8 * group


def body(mesh, tokens, *rest):
    block_adapter = rest[4]
    one_block = block_adapter.shape[0] == 1
    return (fast_body if fits(mesh) and one_block else plain_body)(tokens, *rest)


def solution(mesh):
    placed = (
        P(("parts", "dp", "tensor"), None),
        P(("parts", "dp", "tensor"), None),
        P("tensor", "dp"),
        P("parts", "tensor"),
        P("parts", "tensor"),
        P(("parts", "dp", "tensor")),
        P("parts"),
    )
    return jax.shard_map(
        functools.partial(body, mesh),
        mesh=mesh,
        in_specs=placed,
        out_specs=(
            P(("parts", "dp", "tensor"), None),
            P(("parts", "dp"), "tensor"),
            P(("parts", "dp"), "tensor"),
        ),
        check_vma=False,
    )
```

```python
import functools

import jax
import jax.numpy as jnp
from jax import lax
from jax.experimental import pallas as pl
from jax.experimental.pallas import tpu as pltpu
from jax.sharding import PartitionSpec as P

D = 5120
VALUE_OUTPUTS = 1024
R = 64
ADAPTERS = 256
LANES = 128
TILE_ROWS = 8

adapter_scale = 2.0
VMEM = pl.BlockSpec(memory_space=pltpu.VMEM)
SMEM = pl.BlockSpec(memory_space=pltpu.SMEM)
ANY = pl.BlockSpec(memory_space=pl.ANY)
LIMIT = pltpu.CompilerParams(vmem_limit_bytes=16 * 1024 * 1024)
WIDE = pltpu.CompilerParams(vmem_limit_bytes=60 * 1024 * 1024)


def cost(flops=0, read=0):
    return pl.CostEstimate(flops=flops, bytes_accessed=read, transcendentals=0)


def dot(a, b):
    return jnp.dot(a, b, preferred_element_type=jnp.float32)


def dot_t(a, b):
    return lax.dot_general(a, b, (((1,), (1,)), ((), ())), preferred_element_type=jnp.float32)


def t_dot(a, b):
    return lax.dot_general(a, b, (((0,), (0,)), ((), ())), preferred_element_type=jnp.float32)


def fold_rows(left, piece):
    return jnp.dot(left, piece, preferred_element_type=jnp.float32)


def store_rows(requests, adapter_slot):
    table = jnp.arange(adapter_slot.shape[0], dtype=jnp.int32)
    return jnp.sum(jnp.where(requests[:, None] == table[None, :], adapter_slot[None, :], 0), axis=1)


def plain_body(tokens, cotangent, frozen_value, down_store, up_store, block_adapter, adapter_slot):
    token_rows = tokens.shape[0]
    blocks_here = block_adapter.shape[0]
    block_rows = token_rows // blocks_here
    group = lax.axis_size("tensor")
    columns = lax.all_gather(frozen_value, "dp", axis=1, tiled=True)
    frozen_output = fold_rows(tokens, lax.all_gather(columns, "tensor", axis=0, tiled=True))
    requests = lax.all_gather(block_adapter, "tensor", axis=0, tiled=True)
    stored = store_rows(requests, adapter_slot)
    order = stored.reshape(group, blocks_here).T.reshape(-1)
    down_send = jnp.take(down_store, order, axis=0).reshape(blocks_here, group, -1)
    up_send = jnp.take(up_store, order, axis=0).reshape(blocks_here, group, -1)
    down_got = lax.all_to_all(down_send, "tensor", split_axis=1, concat_axis=1, tiled=True)
    up_got = lax.all_to_all(up_send, "tensor", split_axis=1, concat_axis=1, tiled=True)
    down_panel = down_got.reshape(blocks_here, D, R)
    up_panel = up_got.reshape(blocks_here, R, VALUE_OUTPUTS)
    token_blocks = tokens.reshape(blocks_here, block_rows, D)
    grad_blocks = cotangent.reshape(blocks_here, block_rows, VALUE_OUTPUTS)
    down_projected = jnp.einsum(
        "jtd,jdr->jtr", token_blocks, down_panel, preferred_element_type=jnp.float32
    ).astype(jnp.bfloat16)
    up_projected = jnp.einsum(
        "jtr,jrk->jtk", down_projected, up_panel, preferred_element_type=jnp.float32
    )
    mixed = (
        frozen_output + adapter_scale * up_projected.reshape(token_rows, VALUE_OUTPUTS)
    ).astype(jnp.bfloat16)
    down_projected_gradient = (
        adapter_scale
        * jnp.einsum("jtk,jrk->jtr", grad_blocks, up_panel, preferred_element_type=jnp.float32)
    ).astype(jnp.bfloat16)
    down_term = jnp.einsum(
        "jtd,jtr->jdr", token_blocks, down_projected_gradient, preferred_element_type=jnp.float32
    )
    up_weight_gradient = adapter_scale * jnp.einsum(
        "jtr,jtk->jrk", down_projected, grad_blocks, preferred_element_type=jnp.float32
    )
    down_back = lax.all_to_all(
        down_term.reshape(blocks_here, group, -1), "tensor", split_axis=1, concat_axis=1, tiled=True
    )
    up_back = lax.all_to_all(
        up_weight_gradient.reshape(blocks_here, group, -1), "tensor", split_axis=1, concat_axis=1, tiled=True
    )
    down_flat = down_back.reshape(blocks_here * group, -1)
    up_flat = up_back.reshape(blocks_here * group, -1)
    down_table = jax.ops.segment_sum(down_flat, order, num_segments=ADAPTERS)
    up_table = jax.ops.segment_sum(up_flat, order, num_segments=ADAPTERS)
    grad_down = lax.psum_scatter(down_table, "dp", scatter_dimension=0, tiled=True)
    grad_up = lax.psum_scatter(up_table, "dp", scatter_dimension=0, tiled=True)
    return mixed, grad_down, grad_up


def row_kernel(block_ref, slot_ref, out_ref):
    out_ref[...] = jnp.full(out_ref.shape, slot_ref[block_ref[0]], jnp.int32)


def split_kernel(where, x_ref, mine_ref, theirs_ref):
    inner = where[0]
    outer, rows, width = mine_ref.shape
    for k in range(outer):
        own = pl.multiple_of((2 * k + inner) * width, LANES)
        other = pl.multiple_of((2 * k + 1 - inner) * width, LANES)
        mine_ref[k] = x_ref[:, pl.ds(own, width)]
        theirs_ref[k] = x_ref[:, pl.ds(other, width)]


def interleave_kernel(x_ref, xs_ref):
    group, rows2, half = xs_ref.shape
    rows, width = rows2 // 2, 2 * half
    source = lax.broadcasted_iota(jnp.int32, (width, half), 0)
    target = lax.broadcasted_iota(jnp.int32, (width, half), 1)
    even = (source == 2 * target).astype(jnp.bfloat16)
    odd = (source == 2 * target + 1).astype(jnp.bfloat16)
    for k in range(group):
        x = x_ref[:, k * width:(k + 1) * width]
        xs_ref[k, :rows] = dot(x, even).astype(jnp.bfloat16)
        xs_ref[k, rows:] = dot(x, odd).astype(jnp.bfloat16)


def gather_kernel(asked, down_ref, up_ref, out_ref, rows_ref, down_buf, up_buf, flat, built, sems):
    count, down_chunks, up_chunks = down_buf.shape[0], down_buf.shape[1], up_buf.shape[1]
    across = up_chunks // 8

    def copies(t):
        tile = asked[t, 0, 0] // TILE_ROWS
        return (
            pltpu.make_async_copy(down_ref.at[tile], down_buf.at[t], sems.at[0, t]),
            pltpu.make_async_copy(up_ref.at[tile], up_buf.at[t], sems.at[1, t]),
            pltpu.make_async_copy(built.at[t], out_ref.at[t], sems.at[2, t]),
        )

    for t in range(count):
        down, up, _ = copies(t)
        down.start()
        up.start()
        rows_ref[t] = asked[t, 0, 0]

    def one(t, carry):
        down, up, leave = copies(t)
        up.wait()
        for j in range(up_chunks):
            place = down_chunks + (j % across) * 8 + j // across
            flat[place * 8:place * 8 + 8, :] = up_buf[t, j].astype(jnp.float32)
        down.wait()
        for j in range(down_chunks):
            flat[j * 8:j * 8 + 8, :] = down_buf[t, j].astype(jnp.float32)
        sub = asked[t, 0, 0] % TILE_ROWS
        built[t] = flat[pl.ds(sub, down_chunks + up_chunks, stride=8), :].astype(jnp.bfloat16)
        leave.start()
        return carry

    lax.fori_loop(0, count, one, 0)
    for t in range(count):
        copies(t)[2].wait()


def zero_kernel(after_ref, down_ref, up_ref, done_ref, zeros, sems):
    del after_ref
    done_ref[0] = 0
    zeros[...] = jnp.zeros_like(zeros)
    part = zeros.shape[0]
    copies = []
    for ref, sem in ((down_ref, sems.at[0]), (up_ref, sems.at[1])):
        for g in range(ref.shape[0]):
            for c in range(ref.shape[1] // part):
                copies.append(pltpu.make_async_copy(zeros, ref.at[g, pl.ds(c * part, part)], sem))
    for c in copies:
        c.start()
    for c in copies:
        c.wait()


def adapter_kernel(count, down_chunks, xs_ref, g_ref, pieces, _, out_ref, lifted_ref, up_panel):
    rows = g_ref.shape[0]
    across = g_ref.shape[1] // LANES
    total = jnp.zeros((2 * rows, LANES), jnp.float32)
    for t in range(count):
        total += dot(xs_ref[t], pieces[t, :down_chunks])
        for c in range(across):
            block = pieces[t, down_chunks + 8 * c:down_chunks + 8 * c + 8, :].astype(jnp.float32)
            up_panel[8 * t:8 * t + 8, c * LANES:(c + 1) * LANES] = block
            up_panel[R + 8 * t:R + 8 * t + 8, c * LANES:(c + 1) * LANES] = block
    panel = up_panel[...].astype(jnp.bfloat16)
    left = lax.broadcasted_iota(jnp.int32, (rows, LANES), 1) < R
    inner = total[:rows] + pltpu.roll(total[rows:], R, 1)
    inner = jnp.where(left, inner, 0.0).astype(jnp.bfloat16)
    g = g_ref[...]
    lifted_ref[...] = adapter_scale * dot(inner, panel)
    inner_grad = adapter_scale * dot_t(g, panel)
    diagonal = jnp.concatenate(
        [jnp.where(left, inner_grad, 0.0), jnp.where(left, 0.0, inner_grad)], axis=0
    ).astype(jnp.bfloat16)
    up_term = adapter_scale * t_dot(inner, g)
    for t in range(count):
        out_ref[t, :down_chunks] = t_dot(xs_ref[t], diagonal).astype(jnp.bfloat16)
        up_part = jnp.concatenate(
            [up_term[8 * t:8 * t + 8, c * LANES:(c + 1) * LANES] for c in range(across)], axis=0
        )
        out_ref[t, down_chunks:] = up_part.astype(jnp.bfloat16)


def scatter_kernel(count, down_chunks, up_chunks, first_row, rows_here, rows_core, *rest):
    sources, (down_out, up_out) = rest[:2], rest[4:6]
    pieces, down_sum, up_sum, ordered, arrived, sem = rest[6:]
    half = count // 2
    owned_rows = down_out.shape[0] * 8
    across = up_chunks // 8
    rows = [(rows_here if b < half else rows_core)[b % half] - first_row[0] for b in range(count)]
    arriving = [pltpu.make_async_copy(sources[b // half].at[b % half], pieces.at[b], arrived.at[b]) for b in range(count)]
    for copy in arriving:
        copy.start()
    owned = [(row >= 0) & (row < owned_rows) for row in rows]
    slots, final = [], []
    for b in range(count):
        slot, last = jnp.int32(b), jnp.bool_(True)
        for e in range(b - 1, -1, -1):
            slot = jnp.where(rows[e] == rows[b], e, slot)
        for e in range(b + 1, count):
            last = last & (rows[e] != rows[b])
        slots.append(slot)
        final.append(last)

    def copies(b):
        return (
            pltpu.make_async_copy(down_sum.at[slots[b]], down_out.at[rows[b] // 8, :, rows[b] % 8], sem),
            pltpu.make_async_copy(up_sum.at[slots[b]], up_out.at[rows[b] // 8, :, rows[b] % 8], sem),
        )

    for b in range(count):
        arriving[b].wait()

        @pl.when(owned[b])
        def _():
            slot = slots[b]
            down = pieces[b, :down_chunks].astype(jnp.float32).reshape(down_chunks, 1, LANES)
            for c in range(across):
                ordered[pl.ds(c, 8, stride=across), :] = pieces[
                    b, down_chunks + 8 * c:down_chunks + 8 * c + 8
                ].astype(jnp.float32)
            up = ordered[...].reshape(up_chunks, 1, LANES)

            @pl.when(slot == b)
            def _():
                down_sum[b] = down
                up_sum[b] = up

            @pl.when(slot != b)
            def _():
                down_sum[slot] += down
                up_sum[slot] += up

            @pl.when(final[b])
            def _():
                for copy in copies(b):
                    copy.start()

    for b in range(count):
        @pl.when(owned[b] & final[b])
        def _():
            for copy in copies(b):
                copy.wait()


def base_kernel(where, *refs):
    x_from, w_from, out_refs = refs[:4], refs[4:-8], refs[-7:-3]
    x_buf, w_buf, sems = refs[-3:]
    outer, _, rows, depth = x_buf.shape
    width = w_buf.shape[2]
    fetch_x = [
        [pltpu.make_async_copy(ref.at[where[k]], x_buf.at[k, b], sems.at[k, b]) for b, ref in enumerate(x_from)]
        for k in range(outer)
    ]
    fetch_w = [
        [pltpu.make_async_copy(w_from[h * outer + k], w_buf.at[h * outer + k], sems.at[k, 4 + h]) for h in range(2)]
        for k in range(outer)
    ]
    for k in range(outer):
        for copy in fetch_x[k] + fetch_w[k]:
            copy.start()
    total = [0.0, 0.0]
    for k in range(outer):
        for copy in fetch_x[k] + fetch_w[k]:
            copy.wait()
        left = x_buf[k].reshape(4 * rows, depth)
        for h in range(2):
            total[h] += dot(left, w_buf[h * outer + k])
    for h in range(2):
        for b, ref in enumerate(out_refs):
            ref[:, h * width:(h + 1) * width] = total[h][b * rows:(b + 1) * rows]


def fast_body(tokens, cotangent, frozen_value, down_store, up_store, block_adapter, adapter_slot):
    group, parts = lax.axis_size("tensor"), lax.axis_size("parts")
    outer = group // 2
    token_rows = tokens.shape[0]
    slice_width = D // group
    down_chunks = down_store.shape[1] // LANES
    up_chunks = up_store.shape[1] // LANES
    me, part, core = lax.axis_index("tensor"), lax.axis_index("parts"), lax.axis_index("dp")
    z, x = me // 2, me % 2

    def exchange(value, s):
        return lax.ppermute(value, "tensor", [(t, t ^ s) for t in range(group)])

    def other_core(value):
        return lax.ppermute(value, "dp", [(0, 1), (1, 0)])

    def other_part(value):
        return lax.ppermute(value, "parts", [(a, parts - 1 - a) for a in range(parts)])

    row = pl.pallas_call(
        row_kernel, out_shape=jax.ShapeDtypeStruct((group, 1, LANES), jnp.int32),
        in_specs=[SMEM, SMEM], out_specs=VMEM, name="own_row",
    )(block_adapter, adapter_slot)
    asked = lax.all_to_all(row, "tensor", 0, 0)

    width = frozen_value.shape[1] // parts
    half = lax.dynamic_slice_in_dim(frozen_value, part * width, width, axis=1)
    block = jax.ShapeDtypeStruct((outer, token_rows, slice_width), jnp.bfloat16)
    token = jax.ShapeDtypeStruct((1,), jnp.int32)
    x_mine, x_theirs = pl.pallas_call(
        split_kernel, out_shape=(block, block), in_specs=[SMEM, VMEM], out_specs=(VMEM, VMEM),
        name="split_tokens", compiler_params=LIMIT,
    )(x[None], tokens)
    x_mine, x_theirs, half, asked = lax.optimization_barrier((x_mine, x_theirs, half, asked))
    x_far = exchange(x_theirs, 1)
    y_mine = other_part(x_mine)
    quarter = [half] + [exchange(half, 2 * k) for k in range(1, outer - 1)]
    pieces = jax.ShapeDtypeStruct((group, down_chunks + up_chunks, LANES), jnp.bfloat16)
    def tiles(store):
        view = store.reshape(store.shape[0] // TILE_ROWS, TILE_ROWS, store.shape[1] // LANES, LANES)
        return view.transpose(0, 2, 1, 3)

    sent, rows = pl.pallas_call(
        gather_kernel,
        out_shape=(pieces, jax.ShapeDtypeStruct((group,), jnp.int32)),
        in_specs=[SMEM, ANY, ANY],
        out_specs=(ANY, SMEM),
        scratch_shapes=[
            pltpu.VMEM((group, down_chunks, TILE_ROWS, LANES), jnp.bfloat16),
            pltpu.VMEM((group, up_chunks, TILE_ROWS, LANES), jnp.bfloat16),
            pltpu.VMEM(((down_chunks + up_chunks) * 8, LANES), jnp.float32),
            pltpu.VMEM(pieces.shape, jnp.bfloat16),
            pltpu.SemaphoreType.DMA((3, group)),
        ],
        compiler_params=WIDE,
        cost_estimate=cost(read=40 << 20),
        name="pick_panels",
    )(asked, tiles(down_store), tiles(up_store))
    sent, rows, quarter, x_far, y_mine = lax.optimization_barrier((sent, rows, quarter, x_far, y_mine))
    panels = lax.all_to_all(sent, "tensor", 0, 0)
    rows_core = other_core(rows)
    y_far = other_part(x_far)
    last = exchange(quarter[0], 2 * (outer - 1))
    quarter_core = [other_core(w) for w in quarter]
    owned_groups = ADAPTERS // lax.axis_size("dp") // 8
    down_shape = jax.ShapeDtypeStruct((owned_groups, down_chunks, 8, 1, LANES), jnp.float32)
    up_shape = jax.ShapeDtypeStruct((owned_groups, up_chunks, 8, 1, LANES), jnp.float32)
    down_zero, up_zero, cleared = pl.pallas_call(
        zero_kernel, out_shape=(down_shape, up_shape, token),
        in_specs=[SMEM], out_specs=(ANY, ANY, SMEM),
        scratch_shapes=[pltpu.VMEM((up_chunks, 8, 1, LANES), jnp.float32), pltpu.SemaphoreType.DMA((2,))],
        compiler_params=LIMIT, cost_estimate=cost(read=28 << 20), name="clear_rows",
    )(rows)
    pair_from, _ = lax.optimization_barrier((tokens, cleared))
    xs = pl.pallas_call(
        interleave_kernel,
        out_shape=jax.ShapeDtypeStruct((group, 2 * token_rows, slice_width // 2), jnp.bfloat16),
        in_specs=[VMEM], out_specs=VMEM, name="pair_columns", compiler_params=LIMIT,
        cost_estimate=cost(flops=2 << 30, read=4 << 20),
    )(pair_from)
    panels, last, y_far, quarter_core = lax.optimization_barrier((panels, last, y_far, quarter_core))

    terms, lifted = pl.pallas_call(
        functools.partial(adapter_kernel, group, down_chunks),
        out_shape=(pieces, jax.ShapeDtypeStruct((token_rows, VALUE_OUTPUTS), jnp.float32)),
        in_specs=[VMEM] * 3 + [SMEM],
        out_specs=(VMEM, VMEM),
        scratch_shapes=[pltpu.VMEM((2 * R, VALUE_OUTPUTS), jnp.float32)],
        compiler_params=LIMIT,
        cost_estimate=cost(flops=3 << 30, read=8 << 20),
        name="adapter",
    )(xs, cotangent, panels, cleared)
    _, last = lax.optimization_barrier((terms, last))
    quarters = quarter + [last] + quarter_core + [other_core(last)]
    source = jnp.stack([z ^ k for k in range(outer)])
    sums = jax.ShapeDtypeStruct((token_rows, parts * width), jnp.float32)
    own, to_part, to_inner, to_both = pl.pallas_call(
        base_kernel,
        out_shape=[sums] * 4,
        in_specs=[SMEM] + [ANY] * (5 + 2 * outer),
        out_specs=[VMEM] * 4,
        scratch_shapes=[
            pltpu.VMEM((outer, 4, token_rows, slice_width), jnp.bfloat16),
            pltpu.VMEM((2 * outer, slice_width, width), jnp.bfloat16),
            pltpu.SemaphoreType.DMA((outer, 6)),
        ],
        compiler_params=WIDE,
        cost_estimate=cost(flops=4 << 30, read=8 << 20),
        name="frozen_part",
    )(source, x_mine, y_mine, x_far, y_far, *quarters, terms)
    opposite = [(a * group + t, (parts - 1 - a) * group + (t ^ 1)) for a in range(parts) for t in range(group)]
    back = lax.all_to_all(terms, "tensor", 0, 0)
    arrived = (exchange(to_inner, 1), other_part(to_part), lax.ppermute(to_both, ("parts", "tensor"), opposite))
    back, arrived = lax.optimization_barrier((back, arrived))
    back_core = other_core(back)

    grad_down, grad_up = pl.pallas_call(
        functools.partial(scatter_kernel, 2 * group, down_chunks, up_chunks),
        out_shape=(down_shape, up_shape),
        in_specs=[SMEM] * 3 + [ANY] * 4,
        out_specs=(ANY, ANY),
        input_output_aliases={5: 0, 6: 1},
        scratch_shapes=[
            pltpu.VMEM((2 * group,) + pieces.shape[1:], jnp.bfloat16),
            pltpu.VMEM((2 * group, down_chunks, 1, LANES), jnp.float32),
            pltpu.VMEM((2 * group, up_chunks, 1, LANES), jnp.float32),
            pltpu.VMEM((up_chunks, LANES), jnp.float32),
            pltpu.SemaphoreType.DMA((2 * group,)),
            pltpu.SemaphoreType.DMA(()),
        ],
        compiler_params=LIMIT,
        cost_estimate=cost(read=16 << 20),
        name="place_rows",
    )((core * (ADAPTERS // lax.axis_size("dp")))[None], rows, rows_core, back, back_core,
      down_zero, up_zero)
    grad_down = grad_down.reshape(owned_groups, down_chunks, 8, LANES).transpose(0, 2, 1, 3)
    grad_up = grad_up.reshape(owned_groups, up_chunks, 8, LANES).transpose(0, 2, 1, 3)

    kept, got = own + arrived[0], arrived[1] + arrived[2]
    quarters = [[c[:, :width], c[:, width:]] for c in (kept, got)]

    def pick_quarter(c, a):
        first = quarters[a][0] if c == 0 else quarters[a][1]
        second = quarters[a][1] if c == 0 else quarters[a][0]
        return jnp.where(core == 0, first, second)

    def columns_of(c):
        low, high = pick_quarter(c, 0), pick_quarter(c, 1)
        return jnp.where(part == 0, low, high), jnp.where(part == 0, high, low)

    frozen_output = jnp.concatenate(columns_of(0) + columns_of(1), axis=1)
    mixed = (frozen_output + lifted).astype(jnp.bfloat16)
    return mixed, grad_down.reshape(owned_groups * 8, -1), grad_up.reshape(owned_groups * 8, -1)


def fits(mesh):
    group, cores, parts = mesh.shape["tensor"], mesh.shape["dp"], mesh.shape["parts"]
    return cores == 2 and parts == 2 and group <= 8 and group & (group - 1) == 0 and R == 8 * group


def body(mesh, tokens, *rest):
    block_adapter = rest[4]
    one_block = block_adapter.shape[0] == 1
    return (fast_body if fits(mesh) and one_block else plain_body)(tokens, *rest)


def solution(mesh):
    placed = (
        P(("parts", "dp", "tensor"), None),
        P(("parts", "dp", "tensor"), None),
        P("tensor", "dp"),
        P("parts", "tensor"),
        P("parts", "tensor"),
        P(("parts", "dp", "tensor")),
        P("parts"),
    )
    return jax.shard_map(
        functools.partial(body, mesh),
        mesh=mesh,
        in_specs=placed,
        out_specs=(
            P(("parts", "dp", "tensor"), None),
            P(("parts", "dp"), "tensor"),
            P(("parts", "dp"), "tensor"),
        ),
        check_vma=False,
    )
```

```python
import functools

import jax
import jax.numpy as jnp
from jax import lax
from jax.experimental import pallas as pl
from jax.experimental.pallas import tpu as pltpu
from jax.sharding import PartitionSpec as P

D = 5120
VALUE_OUTPUTS = 1024
R = 64
ADAPTERS = 256
LANES = 128
TILE_ROWS = 8

adapter_scale = 2.0
VMEM = pl.BlockSpec(memory_space=pltpu.VMEM)
SMEM = pl.BlockSpec(memory_space=pltpu.SMEM)
ANY = pl.BlockSpec(memory_space=pl.ANY)
LIMIT = pltpu.CompilerParams(vmem_limit_bytes=16 * 1024 * 1024)
WIDE = pltpu.CompilerParams(vmem_limit_bytes=60 * 1024 * 1024)


def cost(flops=0, read=0):
    return pl.CostEstimate(flops=flops, bytes_accessed=read, transcendentals=0)


def dot(a, b):
    return jnp.dot(a, b, preferred_element_type=jnp.float32)


def dot_t(a, b):
    return lax.dot_general(a, b, (((1,), (1,)), ((), ())), preferred_element_type=jnp.float32)


def t_dot(a, b):
    return lax.dot_general(a, b, (((0,), (0,)), ((), ())), preferred_element_type=jnp.float32)


def fold_rows(left, piece):
    return jnp.dot(left, piece, preferred_element_type=jnp.float32)


def store_rows(requests, adapter_slot):
    table = jnp.arange(adapter_slot.shape[0], dtype=jnp.int32)
    return jnp.sum(jnp.where(requests[:, None] == table[None, :], adapter_slot[None, :], 0), axis=1)


def plain_body(tokens, cotangent, frozen_value, down_store, up_store, block_adapter, adapter_slot):
    token_rows = tokens.shape[0]
    blocks_here = block_adapter.shape[0]
    block_rows = token_rows // blocks_here
    group = lax.axis_size("tensor")
    columns = lax.all_gather(frozen_value, "dp", axis=1, tiled=True)
    frozen_output = fold_rows(tokens, lax.all_gather(columns, "tensor", axis=0, tiled=True))
    requests = lax.all_gather(block_adapter, "tensor", axis=0, tiled=True)
    stored = store_rows(requests, adapter_slot)
    order = stored.reshape(group, blocks_here).T.reshape(-1)
    down_send = jnp.take(down_store, order, axis=0).reshape(blocks_here, group, -1)
    up_send = jnp.take(up_store, order, axis=0).reshape(blocks_here, group, -1)
    down_got = lax.all_to_all(down_send, "tensor", split_axis=1, concat_axis=1, tiled=True)
    up_got = lax.all_to_all(up_send, "tensor", split_axis=1, concat_axis=1, tiled=True)
    down_panel = down_got.reshape(blocks_here, D, R)
    up_panel = up_got.reshape(blocks_here, R, VALUE_OUTPUTS)
    token_blocks = tokens.reshape(blocks_here, block_rows, D)
    grad_blocks = cotangent.reshape(blocks_here, block_rows, VALUE_OUTPUTS)
    down_projected = jnp.einsum(
        "jtd,jdr->jtr", token_blocks, down_panel, preferred_element_type=jnp.float32
    ).astype(jnp.bfloat16)
    up_projected = jnp.einsum(
        "jtr,jrk->jtk", down_projected, up_panel, preferred_element_type=jnp.float32
    )
    mixed = (
        frozen_output + adapter_scale * up_projected.reshape(token_rows, VALUE_OUTPUTS)
    ).astype(jnp.bfloat16)
    down_projected_gradient = (
        adapter_scale
        * jnp.einsum("jtk,jrk->jtr", grad_blocks, up_panel, preferred_element_type=jnp.float32)
    ).astype(jnp.bfloat16)
    down_term = jnp.einsum(
        "jtd,jtr->jdr", token_blocks, down_projected_gradient, preferred_element_type=jnp.float32
    )
    up_weight_gradient = adapter_scale * jnp.einsum(
        "jtr,jtk->jrk", down_projected, grad_blocks, preferred_element_type=jnp.float32
    )
    down_back = lax.all_to_all(
        down_term.reshape(blocks_here, group, -1), "tensor", split_axis=1, concat_axis=1, tiled=True
    )
    up_back = lax.all_to_all(
        up_weight_gradient.reshape(blocks_here, group, -1), "tensor", split_axis=1, concat_axis=1, tiled=True
    )
    down_flat = down_back.reshape(blocks_here * group, -1)
    up_flat = up_back.reshape(blocks_here * group, -1)
    down_table = jax.ops.segment_sum(down_flat, order, num_segments=ADAPTERS)
    up_table = jax.ops.segment_sum(up_flat, order, num_segments=ADAPTERS)
    grad_down = lax.psum_scatter(down_table, "dp", scatter_dimension=0, tiled=True)
    grad_up = lax.psum_scatter(up_table, "dp", scatter_dimension=0, tiled=True)
    return mixed, grad_down, grad_up


def row_kernel(block_ref, slot_ref, out_ref):
    out_ref[...] = jnp.full(out_ref.shape, slot_ref[block_ref[0]], jnp.int32)


def split_kernel(where, x_ref, mine_ref, theirs_ref):
    inner = where[0]
    outer, rows, width = mine_ref.shape
    for k in range(outer):
        own = pl.multiple_of((2 * k + inner) * width, LANES)
        other = pl.multiple_of((2 * k + 1 - inner) * width, LANES)
        mine_ref[k] = x_ref[:, pl.ds(own, width)]
        theirs_ref[k] = x_ref[:, pl.ds(other, width)]


def interleave_kernel(x_ref, out_ref, xs_ref, sems):
    group, rows2, half = xs_ref.shape
    leave = [pltpu.make_async_copy(xs_ref.at[k], out_ref.at[k], sems.at[k]) for k in range(group)]
    rows, width = rows2 // 2, 2 * half
    source = lax.broadcasted_iota(jnp.int32, (width, half), 0)
    target = lax.broadcasted_iota(jnp.int32, (width, half), 1)
    even = (source == 2 * target).astype(jnp.bfloat16)
    odd = (source == 2 * target + 1).astype(jnp.bfloat16)
    for k in range(group):
        x = x_ref[:, k * width:(k + 1) * width]
        xs_ref[k, :rows] = dot(x, even).astype(jnp.bfloat16)
        xs_ref[k, rows:] = dot(x, odd).astype(jnp.bfloat16)
        leave[k].start()
    for copy in leave:
        copy.wait()


def gather_kernel(asked, down_ref, up_ref, out_ref, rows_ref, down_buf, up_buf, flat, built, sems):
    count, down_chunks, up_chunks = down_buf.shape[0], down_buf.shape[1], up_buf.shape[1]
    across = up_chunks // 8

    def copies(t):
        tile = asked[t, 0, 0] // TILE_ROWS
        return (
            pltpu.make_async_copy(down_ref.at[tile], down_buf.at[t], sems.at[0, t]),
            pltpu.make_async_copy(up_ref.at[tile], up_buf.at[t], sems.at[1, t]),
            pltpu.make_async_copy(built.at[t], out_ref.at[t], sems.at[2, t]),
        )

    for t in range(count):
        down, up, _ = copies(t)
        down.start()
        up.start()
        rows_ref[t] = asked[t, 0, 0]

    def one(t, carry):
        down, up, leave = copies(t)
        up.wait()
        for j in range(up_chunks):
            place = down_chunks + (j % across) * 8 + j // across
            flat[place * 8:place * 8 + 8, :] = up_buf[t, j].astype(jnp.float32)
        down.wait()
        for j in range(down_chunks):
            flat[j * 8:j * 8 + 8, :] = down_buf[t, j].astype(jnp.float32)
        sub = asked[t, 0, 0] % TILE_ROWS
        built[t] = flat[pl.ds(sub, down_chunks + up_chunks, stride=8), :].astype(jnp.bfloat16)
        leave.start()
        return carry

    lax.fori_loop(0, count, one, 0)
    for t in range(count):
        copies(t)[2].wait()


def zero_kernel(after_ref, down_ref, up_ref, done_ref, zeros, sems):
    del after_ref
    done_ref[0] = 0
    zeros[...] = jnp.zeros_like(zeros)
    part = zeros.shape[0]
    copies = []
    for ref, sem in ((down_ref, sems.at[0]), (up_ref, sems.at[1])):
        for g in range(ref.shape[0]):
            for c in range(ref.shape[1] // part):
                copies.append(pltpu.make_async_copy(zeros, ref.at[g, pl.ds(c * part, part)], sem))
    for c in copies:
        c.start()
    for c in copies:
        c.wait()


def adapter_kernel(count, down_chunks, xs_ref, g_ref, pieces, _, out_ref, lifted_ref, up_panel):
    rows = g_ref.shape[0]
    across = g_ref.shape[1] // LANES
    total = jnp.zeros((2 * rows, LANES), jnp.float32)
    for t in range(count):
        total += dot(xs_ref[t], pieces[t, :down_chunks])
        for c in range(across):
            block = pieces[t, down_chunks + 8 * c:down_chunks + 8 * c + 8, :].astype(jnp.float32)
            up_panel[8 * t:8 * t + 8, c * LANES:(c + 1) * LANES] = block
            up_panel[R + 8 * t:R + 8 * t + 8, c * LANES:(c + 1) * LANES] = block
    panel = up_panel[...].astype(jnp.bfloat16)
    left = lax.broadcasted_iota(jnp.int32, (rows, LANES), 1) < R
    inner = total[:rows] + pltpu.roll(total[rows:], R, 1)
    inner = jnp.where(left, inner, 0.0).astype(jnp.bfloat16)
    g = g_ref[...]
    lifted_ref[...] = adapter_scale * dot(inner, panel)
    inner_grad = adapter_scale * dot_t(g, panel)
    diagonal = jnp.concatenate(
        [jnp.where(left, inner_grad, 0.0), jnp.where(left, 0.0, inner_grad)], axis=0
    ).astype(jnp.bfloat16)
    up_term = adapter_scale * t_dot(inner, g)
    for t in range(count):
        out_ref[t, :down_chunks] = t_dot(xs_ref[t], diagonal).astype(jnp.bfloat16)
        up_part = jnp.concatenate(
            [up_term[8 * t:8 * t + 8, c * LANES:(c + 1) * LANES] for c in range(across)], axis=0
        )
        out_ref[t, down_chunks:] = up_part.astype(jnp.bfloat16)


def scatter_kernel(count, down_chunks, up_chunks, first_row, rows_here, rows_core, *rest):
    sources, (down_out, up_out) = rest[:2], rest[4:6]
    pieces, down_sum, up_sum, ordered, arrived, sem = rest[6:]
    half = count // 2
    owned_rows = down_out.shape[0] * 8
    across = up_chunks // 8
    rows = [(rows_here if b < half else rows_core)[b % half] - first_row[0] for b in range(count)]
    arriving = [pltpu.make_async_copy(sources[b // half].at[b % half], pieces.at[b], arrived.at[b]) for b in range(count)]
    owned = [(row >= 0) & (row < owned_rows) for row in rows]
    for b in range(count):
        @pl.when(owned[b])
        def _():
            arriving[b].start()

    slots, final = [], []
    for b in range(count):
        slot, last = jnp.int32(b), jnp.bool_(True)
        for e in range(b - 1, -1, -1):
            slot = jnp.where(rows[e] == rows[b], e, slot)
        for e in range(b + 1, count):
            last = last & (rows[e] != rows[b])
        slots.append(slot)
        final.append(last)

    def copies(b):
        return (
            pltpu.make_async_copy(down_sum.at[slots[b]], down_out.at[rows[b] // 8, :, rows[b] % 8, 0], sem),
            pltpu.make_async_copy(up_sum.at[slots[b]], up_out.at[rows[b] // 8, :, rows[b] % 8, 0], sem),
        )

    for b in range(count):
        @pl.when(owned[b])
        def _():
            arriving[b].wait()
            slot = slots[b]
            down = pieces[b, :down_chunks].astype(jnp.float32)
            for c in range(across):
                ordered[pl.ds(c, 8, stride=across), :] = pieces[
                    b, down_chunks + 8 * c:down_chunks + 8 * c + 8
                ].astype(jnp.float32)
            up = ordered[...]

            @pl.when(slot == b)
            def _():
                down_sum[b] = down
                up_sum[b] = up

            @pl.when(slot != b)
            def _():
                down_sum[slot] += down
                up_sum[slot] += up

            @pl.when(final[b])
            def _():
                for copy in copies(b):
                    copy.start()

    for b in range(count):
        @pl.when(owned[b] & final[b])
        def _():
            for copy in copies(b):
                copy.wait()


def base_kernel(where, *refs):
    x_from, w_from, out_refs = refs[:4], refs[4:-8], refs[-7:-3]
    x_buf, w_buf, sems = refs[-3:]
    outer, _, rows, depth = x_buf.shape
    width = w_buf.shape[2]
    fetch_x = [
        [pltpu.make_async_copy(ref.at[where[k]], x_buf.at[k, b], sems.at[k, b]) for b, ref in enumerate(x_from)]
        for k in range(outer)
    ]
    fetch_w = [
        [pltpu.make_async_copy(w_from[h * outer + k], w_buf.at[h * outer + k], sems.at[k, 4 + h]) for h in range(2)]
        for k in range(outer)
    ]
    for k in range(outer):
        for copy in fetch_x[k] + fetch_w[k]:
            copy.start()
    total = [0.0, 0.0]
    for k in range(outer):
        for copy in fetch_x[k] + fetch_w[k]:
            copy.wait()
        left = x_buf[k].reshape(4 * rows, depth)
        for h in range(2):
            total[h] += dot(left, w_buf[h * outer + k])
    for h in range(2):
        for b, ref in enumerate(out_refs):
            ref[:, h * width:(h + 1) * width] = total[h][b * rows:(b + 1) * rows].astype(ref.dtype)


def fast_body(tokens, cotangent, frozen_value, down_store, up_store, block_adapter, adapter_slot):
    group, parts = lax.axis_size("tensor"), lax.axis_size("parts")
    outer = group // 2
    token_rows = tokens.shape[0]
    slice_width = D // group
    down_chunks = down_store.shape[1] // LANES
    up_chunks = up_store.shape[1] // LANES
    me, part, core = lax.axis_index("tensor"), lax.axis_index("parts"), lax.axis_index("dp")
    z, x = me // 2, me % 2

    def exchange(value, s):
        return lax.ppermute(value, "tensor", [(t, t ^ s) for t in range(group)])

    def other_core(value):
        return lax.ppermute(value, "dp", [(0, 1), (1, 0)])

    def other_part(value):
        return lax.ppermute(value, "parts", [(a, parts - 1 - a) for a in range(parts)])

    row = pl.pallas_call(
        row_kernel, out_shape=jax.ShapeDtypeStruct((group, 1, LANES), jnp.int32),
        in_specs=[SMEM, SMEM], out_specs=VMEM, name="own_row",
    )(block_adapter, adapter_slot)
    asked = lax.all_to_all(row, "tensor", 0, 0)
    split_from, half_from, row = lax.optimization_barrier((tokens, frozen_value, row))

    width = frozen_value.shape[1] // parts
    half = lax.dynamic_slice_in_dim(half_from, part * width, width, axis=1)
    block = jax.ShapeDtypeStruct((outer, token_rows, slice_width), jnp.bfloat16)
    token = jax.ShapeDtypeStruct((1,), jnp.int32)
    x_mine, x_theirs = pl.pallas_call(
        split_kernel, out_shape=(block, block), in_specs=[SMEM, VMEM], out_specs=(VMEM, VMEM),
        name="split_tokens", compiler_params=LIMIT,
    )(x[None], split_from)
    x_far = exchange(x_theirs, 1)
    y_mine = other_part(x_mine)
    middle = [(t, t ^ 6) for t in range(group) if t // 2 in (1, 2)]
    ends = [(t, t ^ 2) for t in range(group) if t // 2 in (1, 2)]
    near = exchange(half, 2)
    over = lax.ppermute(half, "tensor", middle)
    near, over, asked = lax.optimization_barrier((near, over, asked))
    over_near = lax.ppermute(near, "tensor", middle)
    passed = lax.ppermute(over, "tensor", ends)
    pieces = jax.ShapeDtypeStruct((group, down_chunks + up_chunks, LANES), jnp.bfloat16)
    def tiles(store):
        view = store.reshape(store.shape[0] // TILE_ROWS, TILE_ROWS, store.shape[1] // LANES, LANES)
        return view.transpose(0, 2, 1, 3)

    sent, rows = pl.pallas_call(
        gather_kernel,
        out_shape=(pieces, jax.ShapeDtypeStruct((group,), jnp.int32)),
        in_specs=[SMEM, ANY, ANY],
        out_specs=(ANY, SMEM),
        scratch_shapes=[
            pltpu.VMEM((group, down_chunks, TILE_ROWS, LANES), jnp.bfloat16),
            pltpu.VMEM((group, up_chunks, TILE_ROWS, LANES), jnp.bfloat16),
            pltpu.VMEM(((down_chunks + up_chunks) * 8, LANES), jnp.float32),
            pltpu.VMEM(pieces.shape, jnp.bfloat16),
            pltpu.SemaphoreType.DMA((3, group)),
        ],
        compiler_params=WIDE,
        cost_estimate=cost(read=40 << 20),
        name="pick_panels",
    )(asked, tiles(down_store), tiles(up_store))
    sent, rows, x_far, y_mine, half, near, over, over_near, passed = lax.optimization_barrier(
        (sent, rows, x_far, y_mine, half, near, over, over_near, passed)
    )
    panels = lax.all_to_all(sent, "tensor", 0, 0)
    rows_core = other_core(rows)
    y_far = other_part(x_far)
    inside = (z == 1) | (z == 2)
    passed_near = lax.ppermute(over_near, "tensor", ends)
    quarter = [half, near, jnp.where(inside, over, passed)]
    quarter_core = [other_core(w) for w in quarter]
    owned_groups = ADAPTERS // lax.axis_size("dp") // 8
    down_shape = jax.ShapeDtypeStruct((owned_groups, down_chunks, 8, 1, LANES), jnp.float32)
    up_shape = jax.ShapeDtypeStruct((owned_groups, up_chunks, 8, 1, LANES), jnp.float32)
    down_zero, up_zero, cleared = pl.pallas_call(
        zero_kernel, out_shape=(down_shape, up_shape, token),
        in_specs=[SMEM], out_specs=(ANY, ANY, SMEM),
        scratch_shapes=[pltpu.VMEM((up_chunks, 8, 1, LANES), jnp.float32), pltpu.SemaphoreType.DMA((2,))],
        compiler_params=LIMIT, cost_estimate=cost(read=28 << 20), name="clear_rows",
    )(rows)
    pair_from, _ = lax.optimization_barrier((tokens, cleared))
    xs = pl.pallas_call(
        interleave_kernel,
        out_shape=jax.ShapeDtypeStruct((group, 2 * token_rows, slice_width // 2), jnp.bfloat16),
        in_specs=[VMEM], out_specs=ANY, name="pair_columns", compiler_params=WIDE,
        scratch_shapes=[
            pltpu.VMEM((group, 2 * token_rows, slice_width // 2), jnp.bfloat16),
            pltpu.SemaphoreType.DMA((group,)),
        ],
        cost_estimate=cost(flops=2 << 30, read=4 << 20),
    )(pair_from)
    panels, passed_near, y_far, quarter_core = lax.optimization_barrier((panels, passed_near, y_far, quarter_core))

    terms, lifted = pl.pallas_call(
        functools.partial(adapter_kernel, group, down_chunks),
        out_shape=(pieces, jax.ShapeDtypeStruct((token_rows, VALUE_OUTPUTS), jnp.float32)),
        in_specs=[VMEM] * 3 + [SMEM],
        out_specs=(VMEM, VMEM),
        scratch_shapes=[pltpu.VMEM((2 * R, VALUE_OUTPUTS), jnp.float32)],
        compiler_params=LIMIT,
        cost_estimate=cost(flops=3 << 30, read=8 << 20),
        name="adapter",
    )(xs, cotangent, panels, cleared)
    _, passed_near = lax.optimization_barrier((terms, passed_near))
    last = jnp.where(inside, over_near, passed_near)
    quarters = quarter + [last] + quarter_core + [other_core(last)]
    source = jnp.stack([z, z ^ 1, jnp.where(z < 2, 2, 1), jnp.where(z < 2, 3, 0)])
    sums = [jax.ShapeDtypeStruct((token_rows, parts * width), kind) for kind in (jnp.float32,) + (jnp.bfloat16,) * 3]
    own, to_part, to_inner, to_both = pl.pallas_call(
        base_kernel,
        out_shape=sums,
        in_specs=[SMEM] + [ANY] * (5 + 2 * outer),
        out_specs=[VMEM] * 4,
        scratch_shapes=[
            pltpu.VMEM((outer, 4, token_rows, slice_width), jnp.bfloat16),
            pltpu.VMEM((2 * outer, slice_width, width), jnp.bfloat16),
            pltpu.SemaphoreType.DMA((outer, 6)),
        ],
        compiler_params=WIDE,
        cost_estimate=cost(flops=4 << 30, read=8 << 20),
        name="frozen_part",
    )(source, x_mine, y_mine, x_far, y_far, *quarters, terms)
    opposite = [(a * group + t, (parts - 1 - a) * group + (t ^ 1)) for a in range(parts) for t in range(group)]
    back = lax.all_to_all(terms, "tensor", 0, 0)
    arrived = (exchange(to_inner, 1), other_part(to_part), lax.ppermute(to_both, ("parts", "tensor"), opposite))
    back, arrived = lax.optimization_barrier((back, arrived))
    back_core = other_core(back)

    grad_down, grad_up = pl.pallas_call(
        functools.partial(scatter_kernel, 2 * group, down_chunks, up_chunks),
        out_shape=(down_shape, up_shape),
        in_specs=[SMEM] * 3 + [ANY] * 4,
        out_specs=(ANY, ANY),
        input_output_aliases={5: 0, 6: 1},
        scratch_shapes=[
            pltpu.VMEM((2 * group,) + pieces.shape[1:], jnp.bfloat16),
            pltpu.VMEM((2 * group, down_chunks, LANES), jnp.float32),
            pltpu.VMEM((2 * group, up_chunks, LANES), jnp.float32),
            pltpu.VMEM((up_chunks, LANES), jnp.float32),
            pltpu.SemaphoreType.DMA((2 * group,)),
            pltpu.SemaphoreType.DMA(()),
        ],
        compiler_params=LIMIT,
        cost_estimate=cost(read=16 << 20),
        name="place_rows",
    )((core * (ADAPTERS // lax.axis_size("dp")))[None], rows, rows_core, back, back_core,
      down_zero, up_zero)
    grad_down = grad_down.reshape(owned_groups, down_chunks, 8, LANES).transpose(0, 2, 1, 3)
    grad_up = grad_up.reshape(owned_groups, up_chunks, 8, LANES).transpose(0, 2, 1, 3)

    arrived = [a.astype(jnp.float32) for a in arrived]
    kept, got = own + arrived[0], arrived[1] + arrived[2]
    quarters = [[c[:, :width], c[:, width:]] for c in (kept, got)]

    def pick_quarter(c, a):
        first = quarters[a][0] if c == 0 else quarters[a][1]
        second = quarters[a][1] if c == 0 else quarters[a][0]
        return jnp.where(core == 0, first, second)

    def columns_of(c):
        low, high = pick_quarter(c, 0), pick_quarter(c, 1)
        return jnp.where(part == 0, low, high), jnp.where(part == 0, high, low)

    frozen_output = jnp.concatenate(columns_of(0) + columns_of(1), axis=1)
    mixed = (frozen_output + lifted).astype(jnp.bfloat16)
    return mixed, grad_down.reshape(owned_groups * 8, -1), grad_up.reshape(owned_groups * 8, -1)


def fits(mesh):
    group, cores, parts = mesh.shape["tensor"], mesh.shape["dp"], mesh.shape["parts"]
    return cores == 2 and parts == 2 and group <= 8 and group & (group - 1) == 0 and R == 8 * group


def body(mesh, tokens, *rest):
    block_adapter = rest[4]
    one_block = block_adapter.shape[0] == 1
    return (fast_body if fits(mesh) and one_block else plain_body)(tokens, *rest)


def solution(mesh):
    placed = (
        P(("parts", "dp", "tensor"), None),
        P(("parts", "dp", "tensor"), None),
        P("tensor", "dp"),
        P("parts", "tensor"),
        P("parts", "tensor"),
        P(("parts", "dp", "tensor")),
        P("parts"),
    )
    return jax.shard_map(
        functools.partial(body, mesh),
        mesh=mesh,
        in_specs=placed,
        out_specs=(
            P(("parts", "dp", "tensor"), None),
            P(("parts", "dp"), "tensor"),
            P(("parts", "dp"), "tensor"),
        ),
        check_vma=False,
    )
```

```python
import functools

import jax
import jax.numpy as jnp
from jax import lax
from jax.experimental import pallas as pl
from jax.experimental.pallas import tpu as pltpu
from jax.sharding import PartitionSpec as P

D = 5120
VALUE_OUTPUTS = 1024
R = 64
ADAPTERS = 256
LANES = 128
TILE_ROWS = 8

adapter_scale = 2.0
VMEM = pl.BlockSpec(memory_space=pltpu.VMEM)
SMEM = pl.BlockSpec(memory_space=pltpu.SMEM)
ANY = pl.BlockSpec(memory_space=pl.ANY)
LIMIT = pltpu.CompilerParams(vmem_limit_bytes=16 * 1024 * 1024)
WIDE = pltpu.CompilerParams(vmem_limit_bytes=60 * 1024 * 1024)


def cost(flops=0, read=0):
    return pl.CostEstimate(flops=flops, bytes_accessed=read, transcendentals=0)


def dot(a, b):
    return jnp.dot(a, b, preferred_element_type=jnp.float32)


def dot_t(a, b):
    return lax.dot_general(a, b, (((1,), (1,)), ((), ())), preferred_element_type=jnp.float32)


def t_dot(a, b):
    return lax.dot_general(a, b, (((0,), (0,)), ((), ())), preferred_element_type=jnp.float32)


def fold_rows(left, piece):
    return jnp.dot(left, piece, preferred_element_type=jnp.float32)


def store_rows(requests, adapter_slot):
    table = jnp.arange(adapter_slot.shape[0], dtype=jnp.int32)
    return jnp.sum(jnp.where(requests[:, None] == table[None, :], adapter_slot[None, :], 0), axis=1)


def plain_body(tokens, cotangent, frozen_value, down_store, up_store, block_adapter, adapter_slot):
    token_rows = tokens.shape[0]
    blocks_here = block_adapter.shape[0]
    block_rows = token_rows // blocks_here
    group = lax.axis_size("tensor")
    columns = lax.all_gather(frozen_value, "dp", axis=1, tiled=True)
    frozen_output = fold_rows(tokens, lax.all_gather(columns, "tensor", axis=0, tiled=True))
    requests = lax.all_gather(block_adapter, "tensor", axis=0, tiled=True)
    stored = store_rows(requests, adapter_slot)
    order = stored.reshape(group, blocks_here).T.reshape(-1)
    down_send = jnp.take(down_store, order, axis=0).reshape(blocks_here, group, -1)
    up_send = jnp.take(up_store, order, axis=0).reshape(blocks_here, group, -1)
    down_got = lax.all_to_all(down_send, "tensor", split_axis=1, concat_axis=1, tiled=True)
    up_got = lax.all_to_all(up_send, "tensor", split_axis=1, concat_axis=1, tiled=True)
    down_panel = down_got.reshape(blocks_here, D, R)
    up_panel = up_got.reshape(blocks_here, R, VALUE_OUTPUTS)
    token_blocks = tokens.reshape(blocks_here, block_rows, D)
    grad_blocks = cotangent.reshape(blocks_here, block_rows, VALUE_OUTPUTS)
    down_projected = jnp.einsum(
        "jtd,jdr->jtr", token_blocks, down_panel, preferred_element_type=jnp.float32
    ).astype(jnp.bfloat16)
    up_projected = jnp.einsum(
        "jtr,jrk->jtk", down_projected, up_panel, preferred_element_type=jnp.float32
    )
    mixed = (
        frozen_output + adapter_scale * up_projected.reshape(token_rows, VALUE_OUTPUTS)
    ).astype(jnp.bfloat16)
    down_projected_gradient = (
        adapter_scale
        * jnp.einsum("jtk,jrk->jtr", grad_blocks, up_panel, preferred_element_type=jnp.float32)
    ).astype(jnp.bfloat16)
    down_term = jnp.einsum(
        "jtd,jtr->jdr", token_blocks, down_projected_gradient, preferred_element_type=jnp.float32
    )
    up_weight_gradient = adapter_scale * jnp.einsum(
        "jtr,jtk->jrk", down_projected, grad_blocks, preferred_element_type=jnp.float32
    )
    down_back = lax.all_to_all(
        down_term.reshape(blocks_here, group, -1), "tensor", split_axis=1, concat_axis=1, tiled=True
    )
    up_back = lax.all_to_all(
        up_weight_gradient.reshape(blocks_here, group, -1), "tensor", split_axis=1, concat_axis=1, tiled=True
    )
    down_flat = down_back.reshape(blocks_here * group, -1)
    up_flat = up_back.reshape(blocks_here * group, -1)
    down_table = jax.ops.segment_sum(down_flat, order, num_segments=ADAPTERS)
    up_table = jax.ops.segment_sum(up_flat, order, num_segments=ADAPTERS)
    grad_down = lax.psum_scatter(down_table, "dp", scatter_dimension=0, tiled=True)
    grad_up = lax.psum_scatter(up_table, "dp", scatter_dimension=0, tiled=True)
    return mixed, grad_down, grad_up


def row_kernel(block_ref, slot_ref, out_ref):
    out_ref[...] = jnp.full(out_ref.shape, slot_ref[block_ref[0]], jnp.int32)


def split_kernel(where, x_ref, mine_ref, *theirs_refs):
    inner = where[0]
    outer, rows, width = mine_ref.shape
    each = outer // len(theirs_refs)
    for k in range(outer):
        own = pl.multiple_of((2 * k + inner) * width, LANES)
        other = pl.multiple_of((2 * k + 1 - inner) * width, LANES)
        mine_ref[k] = x_ref[:, pl.ds(own, width)]
        theirs_refs[k // each][k % each] = x_ref[:, pl.ds(other, width)]


def interleave_kernel(x_ref, out_ref, xs_ref, sems):
    group, rows2, half = xs_ref.shape
    leave = [pltpu.make_async_copy(xs_ref.at[k], out_ref.at[k], sems.at[k]) for k in range(group)]
    rows, width = rows2 // 2, 2 * half
    source = lax.broadcasted_iota(jnp.int32, (width, half), 0)
    target = lax.broadcasted_iota(jnp.int32, (width, half), 1)
    even = (source == 2 * target).astype(jnp.bfloat16)
    odd = (source == 2 * target + 1).astype(jnp.bfloat16)
    for k in range(group):
        x = x_ref[:, k * width:(k + 1) * width]
        xs_ref[k, :rows] = dot(x, even).astype(jnp.bfloat16)
        xs_ref[k, rows:] = dot(x, odd).astype(jnp.bfloat16)
        leave[k].start()
    for copy in leave:
        copy.wait()


def gather_kernel(asked, down_ref, up_ref, out_ref, rows_ref, down_buf, up_buf, flat, built, sems):
    count, down_chunks, up_chunks = down_buf.shape[0], down_buf.shape[1], up_buf.shape[1]
    across = up_chunks // 8

    def copies(t):
        tile = asked[t, 0, 0] // TILE_ROWS
        return (
            pltpu.make_async_copy(down_ref.at[tile], down_buf.at[t], sems.at[0, t]),
            pltpu.make_async_copy(up_ref.at[tile], up_buf.at[t], sems.at[1, t]),
            pltpu.make_async_copy(built.at[t], out_ref.at[t], sems.at[2, t]),
        )

    for t in range(count):
        down, up, _ = copies(t)
        down.start()
        up.start()
        rows_ref[t] = asked[t, 0, 0]

    def one(t, carry):
        down, up, leave = copies(t)
        up.wait()
        for j in range(up_chunks):
            place = down_chunks + (j % across) * 8 + j // across
            flat[place * 8:place * 8 + 8, :] = up_buf[t, j].astype(jnp.float32)
        down.wait()
        for j in range(down_chunks):
            flat[j * 8:j * 8 + 8, :] = down_buf[t, j].astype(jnp.float32)
        sub = asked[t, 0, 0] % TILE_ROWS
        built[t] = flat[pl.ds(sub, down_chunks + up_chunks, stride=8), :].astype(jnp.bfloat16)
        leave.start()
        return carry

    lax.fori_loop(0, count, one, 0)
    for t in range(count):
        copies(t)[2].wait()


def zero_kernel(after_ref, down_ref, up_ref, done_ref, zeros, sems):
    del after_ref
    done_ref[0] = 0
    zeros[...] = jnp.zeros_like(zeros)
    part = zeros.shape[0]
    copies = []
    for ref, sem in ((down_ref, sems.at[0]), (up_ref, sems.at[1])):
        for g in range(ref.shape[0]):
            for c in range(ref.shape[1] // part):
                copies.append(pltpu.make_async_copy(zeros, ref.at[g, pl.ds(c * part, part)], sem))
    for c in copies:
        c.start()
    for c in copies:
        c.wait()


def adapter_kernel(count, down_chunks, xs_ref, g_ref, pieces, _, out_ref, lifted_ref, up_panel):
    rows = g_ref.shape[0]
    across = g_ref.shape[1] // LANES
    total = jnp.zeros((2 * rows, LANES), jnp.float32)
    for t in range(count):
        total += dot(xs_ref[t], pieces[t, :down_chunks])
        for c in range(across):
            block = pieces[t, down_chunks + 8 * c:down_chunks + 8 * c + 8, :].astype(jnp.float32)
            up_panel[8 * t:8 * t + 8, c * LANES:(c + 1) * LANES] = block
            up_panel[R + 8 * t:R + 8 * t + 8, c * LANES:(c + 1) * LANES] = block
    panel = up_panel[...].astype(jnp.bfloat16)
    left = lax.broadcasted_iota(jnp.int32, (rows, LANES), 1) < R
    inner = total[:rows] + pltpu.roll(total[rows:], R, 1)
    inner = jnp.where(left, inner, 0.0).astype(jnp.bfloat16)
    g = g_ref[...]
    lifted_ref[...] = adapter_scale * dot(inner, panel)
    inner_grad = adapter_scale * dot_t(g, panel)
    diagonal = jnp.concatenate(
        [jnp.where(left, inner_grad, 0.0), jnp.where(left, 0.0, inner_grad)], axis=0
    ).astype(jnp.bfloat16)
    up_term = adapter_scale * t_dot(inner, g)
    for t in range(count):
        out_ref[t, :down_chunks] = t_dot(xs_ref[t], diagonal).astype(jnp.bfloat16)
        up_part = jnp.concatenate(
            [up_term[8 * t:8 * t + 8, c * LANES:(c + 1) * LANES] for c in range(across)], axis=0
        )
        out_ref[t, down_chunks:] = up_part.astype(jnp.bfloat16)


def scatter_kernel(count, down_chunks, up_chunks, first_row, rows_here, rows_core, *rest):
    sources, (down_out, up_out) = rest[:2], rest[4:6]
    pieces, down_sum, up_sum, ordered, arrived, sem = rest[6:]
    half = count // 2
    owned_rows = down_out.shape[0] * 8
    across = up_chunks // 8
    rows = [(rows_here if b < half else rows_core)[b % half] - first_row[0] for b in range(count)]
    arriving = [pltpu.make_async_copy(sources[b // half].at[b % half], pieces.at[b], arrived.at[b]) for b in range(count)]
    owned = [(row >= 0) & (row < owned_rows) for row in rows]
    for b in range(count):
        @pl.when(owned[b])
        def _():
            arriving[b].start()

    slots, final = [], []
    for b in range(count):
        slot, last = jnp.int32(b), jnp.bool_(True)
        for e in range(b - 1, -1, -1):
            slot = jnp.where(rows[e] == rows[b], e, slot)
        for e in range(b + 1, count):
            last = last & (rows[e] != rows[b])
        slots.append(slot)
        final.append(last)

    def copies(b):
        return (
            pltpu.make_async_copy(down_sum.at[slots[b]], down_out.at[rows[b] // 8, :, rows[b] % 8, 0], sem),
            pltpu.make_async_copy(up_sum.at[slots[b]], up_out.at[rows[b] // 8, :, rows[b] % 8, 0], sem),
        )

    for b in range(count):
        @pl.when(owned[b])
        def _():
            arriving[b].wait()
            slot = slots[b]
            down = pieces[b, :down_chunks].astype(jnp.float32)
            for c in range(across):
                ordered[pl.ds(c, 8, stride=across), :] = pieces[
                    b, down_chunks + 8 * c:down_chunks + 8 * c + 8
                ].astype(jnp.float32)
            up = ordered[...]

            @pl.when(slot == b)
            def _():
                down_sum[b] = down
                up_sum[b] = up

            @pl.when(slot != b)
            def _():
                down_sum[slot] += down
                up_sum[slot] += up

            @pl.when(final[b])
            def _():
                for copy in copies(b):
                    copy.start()

    for b in range(count):
        @pl.when(owned[b] & final[b])
        def _():
            for copy in copies(b):
                copy.wait()


def base_kernel(where, *refs):
    whole, halves, w_from, out_refs = refs[:2], refs[2:6], refs[6:-8], refs[-7:-3]
    x_buf, w_buf, sems = refs[-3:]
    outer, _, rows, depth = x_buf.shape
    width = w_buf.shape[2]
    each = outer // 2
    fetch_x = [
        [pltpu.make_async_copy(ref.at[where[k]], x_buf.at[k, b], sems.at[k, b]) for b, ref in enumerate(whole)]
        for k in range(outer)
    ]

    def fetch_half(k, b, begin):
        for h in range(2):
            @pl.when(where[k] // each == h)
            def _():
                source = halves[2 * b + h].at[where[k] % each]
                copy = pltpu.make_async_copy(source, x_buf.at[k, 2 + b], sems.at[k, 2 + b])
                copy.start() if begin else copy.wait()

    fetch_w = [
        [pltpu.make_async_copy(w_from[h * outer + k], w_buf.at[h * outer + k], sems.at[k, 4 + h]) for h in range(2)]
        for k in range(outer)
    ]
    for k in range(outer):
        for copy in fetch_x[k] + fetch_w[k]:
            copy.start()
        for b in range(2):
            fetch_half(k, b, True)
    total = [0.0, 0.0]
    for k in range(outer):
        for copy in fetch_x[k] + fetch_w[k]:
            copy.wait()
        for b in range(2):
            fetch_half(k, b, False)
        left = x_buf[k].reshape(4 * rows, depth)
        for h in range(2):
            total[h] += dot(left, w_buf[h * outer + k])
    for h in range(2):
        for b, ref in enumerate(out_refs):
            ref[:, h * width:(h + 1) * width] = total[h][b * rows:(b + 1) * rows].astype(ref.dtype)


def fast_body(tokens, cotangent, frozen_value, down_store, up_store, block_adapter, adapter_slot):
    group, parts = lax.axis_size("tensor"), lax.axis_size("parts")
    outer = group // 2
    token_rows = tokens.shape[0]
    slice_width = D // group
    down_chunks = down_store.shape[1] // LANES
    up_chunks = up_store.shape[1] // LANES
    me, part, core = lax.axis_index("tensor"), lax.axis_index("parts"), lax.axis_index("dp")
    z, x = me // 2, me % 2

    def exchange(value, s):
        return lax.ppermute(value, "tensor", [(t, t ^ s) for t in range(group)])

    def other_core(value):
        return lax.ppermute(value, "dp", [(0, 1), (1, 0)])

    def other_part(value):
        return lax.ppermute(value, "parts", [(a, parts - 1 - a) for a in range(parts)])

    row = pl.pallas_call(
        row_kernel, out_shape=jax.ShapeDtypeStruct((group, 1, LANES), jnp.int32),
        in_specs=[SMEM, SMEM], out_specs=VMEM, name="own_row",
    )(block_adapter, adapter_slot)
    asked = lax.all_to_all(row, "tensor", 0, 0)
    split_from, half_from, row = lax.optimization_barrier((tokens, frozen_value, row))

    width = frozen_value.shape[1] // parts
    half = lax.dynamic_slice_in_dim(half_from, part * width, width, axis=1)
    block = jax.ShapeDtypeStruct((outer, token_rows, slice_width), jnp.bfloat16)
    token = jax.ShapeDtypeStruct((1,), jnp.int32)
    some = jax.ShapeDtypeStruct((outer // 2, token_rows, slice_width), jnp.bfloat16)
    x_mine, *x_theirs = pl.pallas_call(
        split_kernel, out_shape=(block, some, some), in_specs=[SMEM, VMEM], out_specs=[VMEM] * 3,
        name="split_tokens", compiler_params=LIMIT,
    )(x[None], split_from)
    x_far = [exchange(x_theirs[0], 1)]
    y_mine = other_part(x_mine)
    middle = [(t, t ^ 6) for t in range(group) if t // 2 in (1, 2)]
    ends = [(t, t ^ 2) for t in range(group) if t // 2 in (1, 2)]
    near = exchange(half, 2)
    over = lax.ppermute(half, "tensor", middle)
    near, over, asked, x_theirs = lax.optimization_barrier((near, over, asked, x_theirs))
    x_far.append(exchange(x_theirs[1], 1))
    over_near = lax.ppermute(near, "tensor", middle)
    passed = lax.ppermute(over, "tensor", ends)
    pieces = jax.ShapeDtypeStruct((group, down_chunks + up_chunks, LANES), jnp.bfloat16)
    def tiles(store):
        view = store.reshape(store.shape[0] // TILE_ROWS, TILE_ROWS, store.shape[1] // LANES, LANES)
        return view.transpose(0, 2, 1, 3)

    sent, rows = pl.pallas_call(
        gather_kernel,
        out_shape=(pieces, jax.ShapeDtypeStruct((group,), jnp.int32)),
        in_specs=[SMEM, ANY, ANY],
        out_specs=(ANY, SMEM),
        scratch_shapes=[
            pltpu.VMEM((group, down_chunks, TILE_ROWS, LANES), jnp.bfloat16),
            pltpu.VMEM((group, up_chunks, TILE_ROWS, LANES), jnp.bfloat16),
            pltpu.VMEM(((down_chunks + up_chunks) * 8, LANES), jnp.float32),
            pltpu.VMEM(pieces.shape, jnp.bfloat16),
            pltpu.SemaphoreType.DMA((3, group)),
        ],
        compiler_params=WIDE,
        cost_estimate=cost(read=40 << 20),
        name="pick_panels",
    )(asked, tiles(down_store), tiles(up_store))
    sent, rows, x_far, y_mine, half, near, over, over_near, passed = lax.optimization_barrier(
        (sent, rows, x_far, y_mine, half, near, over, over_near, passed)
    )
    panels = lax.all_to_all(sent, "tensor", 0, 0)
    rows_core = other_core(rows)
    y_far = [other_part(part_of) for part_of in x_far]
    inside = (z == 1) | (z == 2)
    passed_near = lax.ppermute(over_near, "tensor", ends)
    quarter = [half, near, jnp.where(inside, over, passed)]
    quarter_core = [other_core(w) for w in quarter]
    owned_groups = ADAPTERS // lax.axis_size("dp") // 8
    down_shape = jax.ShapeDtypeStruct((owned_groups, down_chunks, 8, 1, LANES), jnp.float32)
    up_shape = jax.ShapeDtypeStruct((owned_groups, up_chunks, 8, 1, LANES), jnp.float32)
    down_zero, up_zero, cleared = pl.pallas_call(
        zero_kernel, out_shape=(down_shape, up_shape, token),
        in_specs=[SMEM], out_specs=(ANY, ANY, SMEM),
        scratch_shapes=[pltpu.VMEM((up_chunks, 8, 1, LANES), jnp.float32), pltpu.SemaphoreType.DMA((2,))],
        compiler_params=LIMIT, cost_estimate=cost(read=28 << 20), name="clear_rows",
    )(rows)
    pair_from, _ = lax.optimization_barrier((tokens, cleared))
    xs = pl.pallas_call(
        interleave_kernel,
        out_shape=jax.ShapeDtypeStruct((group, 2 * token_rows, slice_width // 2), jnp.bfloat16),
        in_specs=[VMEM], out_specs=ANY, name="pair_columns", compiler_params=WIDE,
        scratch_shapes=[
            pltpu.VMEM((group, 2 * token_rows, slice_width // 2), jnp.bfloat16),
            pltpu.SemaphoreType.DMA((group,)),
        ],
        cost_estimate=cost(flops=2 << 30, read=4 << 20),
    )(pair_from)
    panels, passed_near, y_far, quarter_core = lax.optimization_barrier((panels, passed_near, y_far, quarter_core))

    terms, lifted = pl.pallas_call(
        functools.partial(adapter_kernel, group, down_chunks),
        out_shape=(pieces, jax.ShapeDtypeStruct((token_rows, VALUE_OUTPUTS), jnp.float32)),
        in_specs=[VMEM] * 3 + [SMEM],
        out_specs=(VMEM, VMEM),
        scratch_shapes=[pltpu.VMEM((2 * R, VALUE_OUTPUTS), jnp.float32)],
        compiler_params=LIMIT,
        cost_estimate=cost(flops=3 << 30, read=8 << 20),
        name="adapter",
    )(xs, cotangent, panels, cleared)
    _, passed_near = lax.optimization_barrier((terms, passed_near))
    last = jnp.where(inside, over_near, passed_near)
    quarters = quarter + [last] + quarter_core + [other_core(last)]
    source = jnp.stack([z, z ^ 1, jnp.where(z < 2, 2, 1), jnp.where(z < 2, 3, 0)])
    sums = [jax.ShapeDtypeStruct((token_rows, parts * width), kind) for kind in (jnp.float32,) + (jnp.bfloat16,) * 3]
    own, to_part, to_inner, to_both = pl.pallas_call(
        base_kernel,
        out_shape=sums,
        in_specs=[SMEM] + [ANY] * (7 + 2 * outer),
        out_specs=[VMEM] * 4,
        scratch_shapes=[
            pltpu.VMEM((outer, 4, token_rows, slice_width), jnp.bfloat16),
            pltpu.VMEM((2 * outer, slice_width, width), jnp.bfloat16),
            pltpu.SemaphoreType.DMA((outer, 6)),
        ],
        compiler_params=WIDE,
        cost_estimate=cost(flops=4 << 30, read=8 << 20),
        name="frozen_part",
    )(source, x_mine, y_mine, *x_far, *y_far, *quarters, terms)
    opposite = [(a * group + t, (parts - 1 - a) * group + (t ^ 1)) for a in range(parts) for t in range(group)]
    back = lax.all_to_all(terms, "tensor", 0, 0)
    arrived = (exchange(to_inner, 1), other_part(to_part), lax.ppermute(to_both, ("parts", "tensor"), opposite))
    back, arrived = lax.optimization_barrier((back, arrived))
    back_core = other_core(back)

    grad_down, grad_up = pl.pallas_call(
        functools.partial(scatter_kernel, 2 * group, down_chunks, up_chunks),
        out_shape=(down_shape, up_shape),
        in_specs=[SMEM] * 3 + [ANY] * 4,
        out_specs=(ANY, ANY),
        input_output_aliases={5: 0, 6: 1},
        scratch_shapes=[
            pltpu.VMEM((2 * group,) + pieces.shape[1:], jnp.bfloat16),
            pltpu.VMEM((2 * group, down_chunks, LANES), jnp.float32),
            pltpu.VMEM((2 * group, up_chunks, LANES), jnp.float32),
            pltpu.VMEM((up_chunks, LANES), jnp.float32),
            pltpu.SemaphoreType.DMA((2 * group,)),
            pltpu.SemaphoreType.DMA(()),
        ],
        compiler_params=LIMIT,
        cost_estimate=cost(read=16 << 20),
        name="place_rows",
    )((core * (ADAPTERS // lax.axis_size("dp")))[None], rows, rows_core, back, back_core,
      down_zero, up_zero)
    grad_down = grad_down.reshape(owned_groups, down_chunks, 8, LANES).transpose(0, 2, 1, 3)
    grad_up = grad_up.reshape(owned_groups, up_chunks, 8, LANES).transpose(0, 2, 1, 3)

    arrived = [a.astype(jnp.float32) for a in arrived]
    kept, got = own + arrived[0], arrived[1] + arrived[2]
    quarters = [[c[:, :width], c[:, width:]] for c in (kept, got)]

    def pick_quarter(c, a):
        first = quarters[a][0] if c == 0 else quarters[a][1]
        second = quarters[a][1] if c == 0 else quarters[a][0]
        return jnp.where(core == 0, first, second)

    def columns_of(c):
        low, high = pick_quarter(c, 0), pick_quarter(c, 1)
        return jnp.where(part == 0, low, high), jnp.where(part == 0, high, low)

    frozen_output = jnp.concatenate(columns_of(0) + columns_of(1), axis=1)
    mixed = (frozen_output + lifted).astype(jnp.bfloat16)
    return mixed, grad_down.reshape(owned_groups * 8, -1), grad_up.reshape(owned_groups * 8, -1)


def fits(mesh):
    group, cores, parts = mesh.shape["tensor"], mesh.shape["dp"], mesh.shape["parts"]
    return cores == 2 and parts == 2 and group <= 8 and group & (group - 1) == 0 and R == 8 * group


def body(mesh, tokens, *rest):
    block_adapter = rest[4]
    one_block = block_adapter.shape[0] == 1
    return (fast_body if fits(mesh) and one_block else plain_body)(tokens, *rest)


def solution(mesh):
    placed = (
        P(("parts", "dp", "tensor"), None),
        P(("parts", "dp", "tensor"), None),
        P("tensor", "dp"),
        P("parts", "tensor"),
        P("parts", "tensor"),
        P(("parts", "dp", "tensor")),
        P("parts"),
    )
    return jax.shard_map(
        functools.partial(body, mesh),
        mesh=mesh,
        in_specs=placed,
        out_specs=(
            P(("parts", "dp", "tensor"), None),
            P(("parts", "dp"), "tensor"),
            P(("parts", "dp"), "tensor"),
        ),
        check_vma=False,
    )
```

```python
import functools

import jax
import jax.numpy as jnp
from jax import lax
from jax.experimental import pallas as pl
from jax.experimental.pallas import tpu as pltpu
from jax.sharding import PartitionSpec as P

D = 5120
VALUE_OUTPUTS = 1024
R = 64
ADAPTERS = 256
LANES = 128
TILE_ROWS = 8

adapter_scale = 2.0
VMEM = pl.BlockSpec(memory_space=pltpu.VMEM)
SMEM = pl.BlockSpec(memory_space=pltpu.SMEM)
ANY = pl.BlockSpec(memory_space=pl.ANY)
LIMIT = pltpu.CompilerParams(vmem_limit_bytes=16 * 1024 * 1024)
WIDE = pltpu.CompilerParams(vmem_limit_bytes=60 * 1024 * 1024)


def cost(flops=0, read=0):
    return pl.CostEstimate(flops=flops, bytes_accessed=read, transcendentals=0)


def dot(a, b):
    return jnp.dot(a, b, preferred_element_type=jnp.float32)


def dot_t(a, b):
    return lax.dot_general(a, b, (((1,), (1,)), ((), ())), preferred_element_type=jnp.float32)


def t_dot(a, b):
    return lax.dot_general(a, b, (((0,), (0,)), ((), ())), preferred_element_type=jnp.float32)


def fold_rows(left, piece):
    return jnp.dot(left, piece, preferred_element_type=jnp.float32)


def store_rows(requests, adapter_slot):
    table = jnp.arange(adapter_slot.shape[0], dtype=jnp.int32)
    return jnp.sum(jnp.where(requests[:, None] == table[None, :], adapter_slot[None, :], 0), axis=1)


def plain_body(tokens, cotangent, frozen_value, down_store, up_store, block_adapter, adapter_slot):
    token_rows = tokens.shape[0]
    blocks_here = block_adapter.shape[0]
    block_rows = token_rows // blocks_here
    group = lax.axis_size("tensor")
    columns = lax.all_gather(frozen_value, "dp", axis=1, tiled=True)
    frozen_output = fold_rows(tokens, lax.all_gather(columns, "tensor", axis=0, tiled=True))
    requests = lax.all_gather(block_adapter, "tensor", axis=0, tiled=True)
    stored = store_rows(requests, adapter_slot)
    order = stored.reshape(group, blocks_here).T.reshape(-1)
    down_send = jnp.take(down_store, order, axis=0).reshape(blocks_here, group, -1)
    up_send = jnp.take(up_store, order, axis=0).reshape(blocks_here, group, -1)
    down_got = lax.all_to_all(down_send, "tensor", split_axis=1, concat_axis=1, tiled=True)
    up_got = lax.all_to_all(up_send, "tensor", split_axis=1, concat_axis=1, tiled=True)
    down_panel = down_got.reshape(blocks_here, D, R)
    up_panel = up_got.reshape(blocks_here, R, VALUE_OUTPUTS)
    token_blocks = tokens.reshape(blocks_here, block_rows, D)
    grad_blocks = cotangent.reshape(blocks_here, block_rows, VALUE_OUTPUTS)
    down_projected = jnp.einsum(
        "jtd,jdr->jtr", token_blocks, down_panel, preferred_element_type=jnp.float32
    ).astype(jnp.bfloat16)
    up_projected = jnp.einsum(
        "jtr,jrk->jtk", down_projected, up_panel, preferred_element_type=jnp.float32
    )
    mixed = (
        frozen_output + adapter_scale * up_projected.reshape(token_rows, VALUE_OUTPUTS)
    ).astype(jnp.bfloat16)
    down_projected_gradient = (
        adapter_scale
        * jnp.einsum("jtk,jrk->jtr", grad_blocks, up_panel, preferred_element_type=jnp.float32)
    ).astype(jnp.bfloat16)
    down_term = jnp.einsum(
        "jtd,jtr->jdr", token_blocks, down_projected_gradient, preferred_element_type=jnp.float32
    )
    up_weight_gradient = adapter_scale * jnp.einsum(
        "jtr,jtk->jrk", down_projected, grad_blocks, preferred_element_type=jnp.float32
    )
    down_back = lax.all_to_all(
        down_term.reshape(blocks_here, group, -1), "tensor", split_axis=1, concat_axis=1, tiled=True
    )
    up_back = lax.all_to_all(
        up_weight_gradient.reshape(blocks_here, group, -1), "tensor", split_axis=1, concat_axis=1, tiled=True
    )
    down_flat = down_back.reshape(blocks_here * group, -1)
    up_flat = up_back.reshape(blocks_here * group, -1)
    down_table = jax.ops.segment_sum(down_flat, order, num_segments=ADAPTERS)
    up_table = jax.ops.segment_sum(up_flat, order, num_segments=ADAPTERS)
    grad_down = lax.psum_scatter(down_table, "dp", scatter_dimension=0, tiled=True)
    grad_up = lax.psum_scatter(up_table, "dp", scatter_dimension=0, tiled=True)
    return mixed, grad_down, grad_up


def row_kernel(block_ref, slot_ref, out_ref):
    out_ref[...] = jnp.full(out_ref.shape, slot_ref[block_ref[0]], jnp.int32)


def split_kernel(where, x_ref, mine_ref, *theirs_refs):
    inner = where[0]
    outer, rows, width = mine_ref.shape
    each = outer // len(theirs_refs)
    for k in range(outer):
        own = pl.multiple_of((2 * k + inner) * width, LANES)
        other = pl.multiple_of((2 * k + 1 - inner) * width, LANES)
        mine_ref[k] = x_ref[:, pl.ds(own, width)]
        theirs_refs[k // each][k % each] = x_ref[:, pl.ds(other, width)]


def interleave_kernel(x_ref, out_ref, xs_ref, sems):
    group, rows2, half = xs_ref.shape
    leave = [pltpu.make_async_copy(xs_ref.at[k], out_ref.at[k], sems.at[k]) for k in range(group)]
    rows, width = rows2 // 2, 2 * half
    source = lax.broadcasted_iota(jnp.int32, (width, half), 0)
    target = lax.broadcasted_iota(jnp.int32, (width, half), 1)
    even = (source == 2 * target).astype(jnp.bfloat16)
    odd = (source == 2 * target + 1).astype(jnp.bfloat16)
    for k in range(group):
        x = x_ref[:, k * width:(k + 1) * width]
        xs_ref[k, :rows] = dot(x, even).astype(jnp.bfloat16)
        xs_ref[k, rows:] = dot(x, odd).astype(jnp.bfloat16)
        leave[k].start()
    for copy in leave:
        copy.wait()


def gather_kernel(asked, down_ref, up_ref, out_ref, rows_ref, down_buf, up_buf, flat, built, sems):
    count, down_chunks, up_chunks = down_buf.shape[0], down_buf.shape[1], up_buf.shape[1]
    across = up_chunks // 8

    def copies(t):
        tile = asked[t, 0, 0] // TILE_ROWS
        return (
            pltpu.make_async_copy(down_ref.at[tile], down_buf.at[t], sems.at[0, t]),
            pltpu.make_async_copy(up_ref.at[tile], up_buf.at[t], sems.at[1, t]),
            pltpu.make_async_copy(built.at[t], out_ref.at[t], sems.at[2, t]),
        )

    for t in range(count):
        down, up, _ = copies(t)
        down.start()
        up.start()
        rows_ref[t] = asked[t, 0, 0]

    def one(t, carry):
        down, up, leave = copies(t)
        up.wait()
        for j in range(up_chunks):
            place = down_chunks + (j % across) * 8 + j // across
            flat[place * 8:place * 8 + 8, :] = up_buf[t, j].astype(jnp.float32)
        down.wait()
        for j in range(down_chunks):
            flat[j * 8:j * 8 + 8, :] = down_buf[t, j].astype(jnp.float32)
        sub = asked[t, 0, 0] % TILE_ROWS
        built[t] = flat[pl.ds(sub, down_chunks + up_chunks, stride=8), :].astype(jnp.bfloat16)
        leave.start()
        return carry

    lax.fori_loop(0, count, one, 0)
    for t in range(count):
        copies(t)[2].wait()


def zero_kernel(after_ref, down_ref, up_ref, done_ref, zeros, sems):
    del after_ref
    done_ref[0] = 0
    zeros[...] = jnp.zeros_like(zeros)
    part = zeros.shape[0]
    copies = []
    for ref, sem in ((down_ref, sems.at[0]), (up_ref, sems.at[1])):
        for g in range(ref.shape[0]):
            for c in range(ref.shape[1] // part):
                copies.append(pltpu.make_async_copy(zeros, ref.at[g, pl.ds(c * part, part)], sem))
    for c in copies:
        c.start()
    for c in copies:
        c.wait()


def adapter_kernel(count, down_chunks, xs_ref, g_ref, pieces, _, out_ref, lifted_ref, up_panel):
    rows = g_ref.shape[0]
    across = g_ref.shape[1] // LANES
    total = jnp.zeros((2 * rows, LANES), jnp.float32)
    for t in range(count):
        total += dot(xs_ref[t], pieces[t, :down_chunks])
        for c in range(across):
            block = pieces[t, down_chunks + 8 * c:down_chunks + 8 * c + 8, :].astype(jnp.float32)
            up_panel[8 * t:8 * t + 8, c * LANES:(c + 1) * LANES] = block
            up_panel[R + 8 * t:R + 8 * t + 8, c * LANES:(c + 1) * LANES] = block
    panel = up_panel[...].astype(jnp.bfloat16)
    left = lax.broadcasted_iota(jnp.int32, (rows, LANES), 1) < R
    inner = total[:rows] + pltpu.roll(total[rows:], R, 1)
    inner = jnp.where(left, inner, 0.0).astype(jnp.bfloat16)
    g = g_ref[...]
    lifted_ref[...] = adapter_scale * dot(inner, panel)
    inner_grad = adapter_scale * dot_t(g, panel)
    diagonal = jnp.concatenate(
        [jnp.where(left, inner_grad, 0.0), jnp.where(left, 0.0, inner_grad)], axis=0
    ).astype(jnp.bfloat16)
    up_term = adapter_scale * t_dot(inner, g)
    for t in range(count):
        out_ref[t, :down_chunks] = t_dot(xs_ref[t], diagonal).astype(jnp.bfloat16)
        up_part = jnp.concatenate(
            [up_term[8 * t:8 * t + 8, c * LANES:(c + 1) * LANES] for c in range(across)], axis=0
        )
        out_ref[t, down_chunks:] = up_part.astype(jnp.bfloat16)


def scatter_kernel(count, down_chunks, up_chunks, first_row, rows_here, rows_core, *rest):
    sources, (down_out, up_out) = rest[:2], rest[4:6]
    pieces, down_sum, up_sum, ordered, arrived, sem = rest[6:]
    half = count // 2
    owned_rows = down_out.shape[0] * 8
    across = up_chunks // 8
    rows = [(rows_here if b < half else rows_core)[b % half] - first_row[0] for b in range(count)]
    arriving = [pltpu.make_async_copy(sources[b // half].at[b % half], pieces.at[b], arrived.at[b]) for b in range(count)]
    owned = [(row >= 0) & (row < owned_rows) for row in rows]
    for b in range(count):
        @pl.when(owned[b])
        def _():
            arriving[b].start()

    slots, final = [], []
    for b in range(count):
        slot, last = jnp.int32(b), jnp.bool_(True)
        for e in range(b - 1, -1, -1):
            slot = jnp.where(rows[e] == rows[b], e, slot)
        for e in range(b + 1, count):
            last = last & (rows[e] != rows[b])
        slots.append(slot)
        final.append(last)

    def copies(b):
        return (
            pltpu.make_async_copy(down_sum.at[slots[b]], down_out.at[rows[b] // 8, :, rows[b] % 8, 0], sem),
            pltpu.make_async_copy(up_sum.at[slots[b]], up_out.at[rows[b] // 8, :, rows[b] % 8, 0], sem),
        )

    for b in range(count):
        @pl.when(owned[b])
        def _():
            arriving[b].wait()
            slot = slots[b]
            down = pieces[b, :down_chunks].astype(jnp.float32)
            for c in range(across):
                ordered[pl.ds(c, 8, stride=across), :] = pieces[
                    b, down_chunks + 8 * c:down_chunks + 8 * c + 8
                ].astype(jnp.float32)
            up = ordered[...]

            @pl.when(slot == b)
            def _():
                down_sum[b] = down
                up_sum[b] = up

            @pl.when(slot != b)
            def _():
                down_sum[slot] += down
                up_sum[slot] += up

            @pl.when(final[b])
            def _():
                for copy in copies(b):
                    copy.start()

    for b in range(count):
        @pl.when(owned[b] & final[b])
        def _():
            for copy in copies(b):
                copy.wait()


def base_kernel(where, *refs):
    whole, halves, w_from, out_refs = refs[:2], refs[2:6], refs[6:-8], refs[-7:-3]
    x_buf, w_buf, sems = refs[-3:]
    outer, _, rows, depth = x_buf.shape
    width = w_buf.shape[2]
    each = outer // 2
    fetch_x = [
        [pltpu.make_async_copy(ref.at[where[k]], x_buf.at[k, b], sems.at[k, b]) for b, ref in enumerate(whole)]
        for k in range(outer)
    ]

    def fetch_half(k, b, begin):
        for h in range(2):
            @pl.when(where[k] // each == h)
            def _():
                source = halves[2 * b + h].at[where[k] % each]
                copy = pltpu.make_async_copy(source, x_buf.at[k, 2 + b], sems.at[k, 2 + b])
                copy.start() if begin else copy.wait()

    fetch_w = [
        [pltpu.make_async_copy(w_from[h * outer + k], w_buf.at[h * outer + k], sems.at[k, 4 + h]) for h in range(2)]
        for k in range(outer)
    ]
    for k in range(outer):
        for copy in fetch_x[k] + fetch_w[k]:
            copy.start()
        for b in range(2):
            fetch_half(k, b, True)
    total = [0.0, 0.0]
    for k in range(outer):
        for copy in fetch_x[k] + fetch_w[k]:
            copy.wait()
        for b in range(2):
            fetch_half(k, b, False)
        left = x_buf[k].reshape(4 * rows, depth)
        for h in range(2):
            total[h] += dot(left, w_buf[h * outer + k])
    for h in range(2):
        for b, ref in enumerate(out_refs):
            ref[:, h * width:(h + 1) * width] = total[h][b * rows:(b + 1) * rows].astype(ref.dtype)


def fast_body(tokens, cotangent, frozen_value, down_store, up_store, block_adapter, adapter_slot):
    group, parts = lax.axis_size("tensor"), lax.axis_size("parts")
    outer = group // 2
    token_rows = tokens.shape[0]
    slice_width = D // group
    down_chunks = down_store.shape[1] // LANES
    up_chunks = up_store.shape[1] // LANES
    me, part, core = lax.axis_index("tensor"), lax.axis_index("parts"), lax.axis_index("dp")
    z, x = me // 2, me % 2

    def exchange(value, s):
        return lax.ppermute(value, "tensor", [(t, t ^ s) for t in range(group)])

    def other_core(value):
        return lax.ppermute(value, "dp", [(0, 1), (1, 0)])

    def other_part(value):
        return lax.ppermute(value, "parts", [(a, parts - 1 - a) for a in range(parts)])

    row = pl.pallas_call(
        row_kernel, out_shape=jax.ShapeDtypeStruct((group, 1, LANES), jnp.int32),
        in_specs=[SMEM, SMEM], out_specs=VMEM, name="own_row",
    )(block_adapter, adapter_slot)
    asked = lax.all_to_all(row, "tensor", 0, 0)
    split_from, half_from, row = lax.optimization_barrier((tokens, frozen_value, row))

    width = frozen_value.shape[1] // parts
    half = lax.dynamic_slice_in_dim(half_from, part * width, width, axis=1)
    block = jax.ShapeDtypeStruct((outer, token_rows, slice_width), jnp.bfloat16)
    token = jax.ShapeDtypeStruct((1,), jnp.int32)
    some = jax.ShapeDtypeStruct((outer // 2, token_rows, slice_width), jnp.bfloat16)
    x_mine, *x_theirs = pl.pallas_call(
        split_kernel, out_shape=(block, some, some), in_specs=[SMEM, VMEM], out_specs=[VMEM] * 3,
        name="split_tokens", compiler_params=LIMIT,
    )(x[None], split_from)
    x_far = [exchange(x_theirs[0], 1)]
    y_mine = other_part(x_mine)
    xs = pl.pallas_call(
        interleave_kernel,
        out_shape=jax.ShapeDtypeStruct((group, 2 * token_rows, slice_width // 2), jnp.bfloat16),
        in_specs=[VMEM], out_specs=ANY, name="pair_columns", compiler_params=WIDE,
        scratch_shapes=[
            pltpu.VMEM((group, 2 * token_rows, slice_width // 2), jnp.bfloat16),
            pltpu.SemaphoreType.DMA((group,)),
        ],
        cost_estimate=cost(),
    )(split_from)
    middle = [(t, t ^ 6) for t in range(group) if t // 2 in (1, 2)]
    ends = [(t, t ^ 2) for t in range(group) if t // 2 in (1, 2)]
    near = exchange(half, 2)
    over = lax.ppermute(half, "tensor", middle)
    near, over, asked, x_theirs, xs = lax.optimization_barrier((near, over, asked, x_theirs, xs))
    x_far.append(exchange(x_theirs[1], 1))
    over_near = lax.ppermute(near, "tensor", middle)
    passed = lax.ppermute(over, "tensor", ends)
    pieces = jax.ShapeDtypeStruct((group, down_chunks + up_chunks, LANES), jnp.bfloat16)
    def tiles(store):
        view = store.reshape(store.shape[0] // TILE_ROWS, TILE_ROWS, store.shape[1] // LANES, LANES)
        return view.transpose(0, 2, 1, 3)

    sent, rows = pl.pallas_call(
        gather_kernel,
        out_shape=(pieces, jax.ShapeDtypeStruct((group,), jnp.int32)),
        in_specs=[SMEM, ANY, ANY],
        out_specs=(ANY, SMEM),
        scratch_shapes=[
            pltpu.VMEM((group, down_chunks, TILE_ROWS, LANES), jnp.bfloat16),
            pltpu.VMEM((group, up_chunks, TILE_ROWS, LANES), jnp.bfloat16),
            pltpu.VMEM(((down_chunks + up_chunks) * 8, LANES), jnp.float32),
            pltpu.VMEM(pieces.shape, jnp.bfloat16),
            pltpu.SemaphoreType.DMA((3, group)),
        ],
        compiler_params=WIDE,
        cost_estimate=cost(read=40 << 20),
        name="pick_panels",
    )(asked, tiles(down_store), tiles(up_store))
    sent, rows, x_far, y_mine, half, near, over, over_near, passed = lax.optimization_barrier(
        (sent, rows, x_far, y_mine, half, near, over, over_near, passed)
    )
    panels = lax.all_to_all(sent, "tensor", 0, 0)
    rows_core = other_core(rows)
    y_far = [other_part(part_of) for part_of in x_far]
    inside = (z == 1) | (z == 2)
    passed_near = lax.ppermute(over_near, "tensor", ends)
    quarter = [half, near, jnp.where(inside, over, passed)]
    quarter_core = [other_core(w) for w in quarter]
    owned_groups = ADAPTERS // lax.axis_size("dp") // 8
    down_shape = jax.ShapeDtypeStruct((owned_groups, down_chunks, 8, 1, LANES), jnp.float32)
    up_shape = jax.ShapeDtypeStruct((owned_groups, up_chunks, 8, 1, LANES), jnp.float32)
    down_zero, up_zero, cleared = pl.pallas_call(
        zero_kernel, out_shape=(down_shape, up_shape, token),
        in_specs=[SMEM], out_specs=(ANY, ANY, SMEM),
        scratch_shapes=[pltpu.VMEM((up_chunks, 8, 1, LANES), jnp.float32), pltpu.SemaphoreType.DMA((2,))],
        compiler_params=LIMIT, cost_estimate=cost(read=28 << 20), name="clear_rows",
    )(rows)
    panels, passed_near, y_far, quarter_core = lax.optimization_barrier((panels, passed_near, y_far, quarter_core))

    terms, lifted = pl.pallas_call(
        functools.partial(adapter_kernel, group, down_chunks),
        out_shape=(pieces, jax.ShapeDtypeStruct((token_rows, VALUE_OUTPUTS), jnp.float32)),
        in_specs=[VMEM] * 3 + [SMEM],
        out_specs=(VMEM, VMEM),
        scratch_shapes=[pltpu.VMEM((2 * R, VALUE_OUTPUTS), jnp.float32)],
        compiler_params=LIMIT,
        cost_estimate=cost(flops=3 << 30, read=8 << 20),
        name="adapter",
    )(xs, cotangent, panels, cleared)
    _, passed_near = lax.optimization_barrier((terms, passed_near))
    last = jnp.where(inside, over_near, passed_near)
    quarters = quarter + [last] + quarter_core + [other_core(last)]
    source = jnp.stack([z, z ^ 1, jnp.where(z < 2, 2, 1), jnp.where(z < 2, 3, 0)])
    sums = [jax.ShapeDtypeStruct((token_rows, parts * width), kind) for kind in (jnp.float32,) + (jnp.bfloat16,) * 3]
    own, to_part, to_inner, to_both = pl.pallas_call(
        base_kernel,
        out_shape=sums,
        in_specs=[SMEM] + [ANY] * (7 + 2 * outer),
        out_specs=[VMEM] * 4,
        scratch_shapes=[
            pltpu.VMEM((outer, 4, token_rows, slice_width), jnp.bfloat16),
            pltpu.VMEM((2 * outer, slice_width, width), jnp.bfloat16),
            pltpu.SemaphoreType.DMA((outer, 6)),
        ],
        compiler_params=WIDE,
        cost_estimate=cost(flops=4 << 30, read=8 << 20),
        name="frozen_part",
    )(source, x_mine, y_mine, *x_far, *y_far, *quarters, terms)
    opposite = [(a * group + t, (parts - 1 - a) * group + (t ^ 1)) for a in range(parts) for t in range(group)]
    back = lax.all_to_all(terms, "tensor", 0, 0)
    arrived = (exchange(to_inner, 1), other_part(to_part), lax.ppermute(to_both, ("parts", "tensor"), opposite))
    back, arrived = lax.optimization_barrier((back, arrived))
    back_core = other_core(back)

    grad_down, grad_up = pl.pallas_call(
        functools.partial(scatter_kernel, 2 * group, down_chunks, up_chunks),
        out_shape=(down_shape, up_shape),
        in_specs=[SMEM] * 3 + [ANY] * 4,
        out_specs=(ANY, ANY),
        input_output_aliases={5: 0, 6: 1},
        scratch_shapes=[
            pltpu.VMEM((2 * group,) + pieces.shape[1:], jnp.bfloat16),
            pltpu.VMEM((2 * group, down_chunks, LANES), jnp.float32),
            pltpu.VMEM((2 * group, up_chunks, LANES), jnp.float32),
            pltpu.VMEM((up_chunks, LANES), jnp.float32),
            pltpu.SemaphoreType.DMA((2 * group,)),
            pltpu.SemaphoreType.DMA(()),
        ],
        compiler_params=LIMIT,
        cost_estimate=cost(read=16 << 20),
        name="place_rows",
    )((core * (ADAPTERS // lax.axis_size("dp")))[None], rows, rows_core, back, back_core,
      down_zero, up_zero)
    grad_down = grad_down.reshape(owned_groups, down_chunks, 8, LANES).transpose(0, 2, 1, 3)
    grad_up = grad_up.reshape(owned_groups, up_chunks, 8, LANES).transpose(0, 2, 1, 3)

    arrived = [a.astype(jnp.float32) for a in arrived]
    kept, got = own + arrived[0], arrived[1] + arrived[2]
    quarters = [[c[:, :width], c[:, width:]] for c in (kept, got)]

    def pick_quarter(c, a):
        first = quarters[a][0] if c == 0 else quarters[a][1]
        second = quarters[a][1] if c == 0 else quarters[a][0]
        return jnp.where(core == 0, first, second)

    def columns_of(c):
        low, high = pick_quarter(c, 0), pick_quarter(c, 1)
        return jnp.where(part == 0, low, high), jnp.where(part == 0, high, low)

    frozen_output = jnp.concatenate(columns_of(0) + columns_of(1), axis=1)
    mixed = (frozen_output + lifted).astype(jnp.bfloat16)
    return mixed, grad_down.reshape(owned_groups * 8, -1), grad_up.reshape(owned_groups * 8, -1)


def fits(mesh):
    group, cores, parts = mesh.shape["tensor"], mesh.shape["dp"], mesh.shape["parts"]
    return cores == 2 and parts == 2 and group <= 8 and group & (group - 1) == 0 and R == 8 * group


def body(mesh, tokens, *rest):
    block_adapter = rest[4]
    one_block = block_adapter.shape[0] == 1
    return (fast_body if fits(mesh) and one_block else plain_body)(tokens, *rest)


def solution(mesh):
    placed = (
        P(("parts", "dp", "tensor"), None),
        P(("parts", "dp", "tensor"), None),
        P("tensor", "dp"),
        P("parts", "tensor"),
        P("parts", "tensor"),
        P(("parts", "dp", "tensor")),
        P("parts"),
    )
    return jax.shard_map(
        functools.partial(body, mesh),
        mesh=mesh,
        in_specs=placed,
        out_specs=(
            P(("parts", "dp", "tensor"), None),
            P(("parts", "dp"), "tensor"),
            P(("parts", "dp"), "tensor"),
        ),
        check_vma=False,
    )
```

```python
import functools

import jax
import jax.numpy as jnp
from jax import lax
from jax.experimental import pallas as pl
from jax.experimental.pallas import tpu as pltpu
from jax.sharding import PartitionSpec as P

D = 5120
VALUE_OUTPUTS = 1024
R = 64
ADAPTERS = 256
LANES = 128
TILE_ROWS = 8

adapter_scale = 2.0
VMEM = pl.BlockSpec(memory_space=pltpu.VMEM)
SMEM = pl.BlockSpec(memory_space=pltpu.SMEM)
ANY = pl.BlockSpec(memory_space=pl.ANY)
LIMIT = pltpu.CompilerParams(vmem_limit_bytes=16 * 1024 * 1024)
WIDE = pltpu.CompilerParams(vmem_limit_bytes=60 * 1024 * 1024)


def cost(flops=0, read=0):
    return pl.CostEstimate(flops=flops, bytes_accessed=read, transcendentals=0)


def dot(a, b):
    return jnp.dot(a, b, preferred_element_type=jnp.float32)


def dot_t(a, b):
    return lax.dot_general(a, b, (((1,), (1,)), ((), ())), preferred_element_type=jnp.float32)


def t_dot(a, b):
    return lax.dot_general(a, b, (((0,), (0,)), ((), ())), preferred_element_type=jnp.float32)


def fold_rows(left, piece):
    return jnp.dot(left, piece, preferred_element_type=jnp.float32)


def store_rows(requests, adapter_slot):
    table = jnp.arange(adapter_slot.shape[0], dtype=jnp.int32)
    return jnp.sum(jnp.where(requests[:, None] == table[None, :], adapter_slot[None, :], 0), axis=1)


def plain_body(tokens, cotangent, frozen_value, down_store, up_store, block_adapter, adapter_slot):
    token_rows = tokens.shape[0]
    blocks_here = block_adapter.shape[0]
    block_rows = token_rows // blocks_here
    group = lax.axis_size("tensor")
    columns = lax.all_gather(frozen_value, "dp", axis=1, tiled=True)
    frozen_output = fold_rows(tokens, lax.all_gather(columns, "tensor", axis=0, tiled=True))
    requests = lax.all_gather(block_adapter, "tensor", axis=0, tiled=True)
    stored = store_rows(requests, adapter_slot)
    order = stored.reshape(group, blocks_here).T.reshape(-1)
    down_send = jnp.take(down_store, order, axis=0).reshape(blocks_here, group, -1)
    up_send = jnp.take(up_store, order, axis=0).reshape(blocks_here, group, -1)
    down_got = lax.all_to_all(down_send, "tensor", split_axis=1, concat_axis=1, tiled=True)
    up_got = lax.all_to_all(up_send, "tensor", split_axis=1, concat_axis=1, tiled=True)
    down_panel = down_got.reshape(blocks_here, D, R)
    up_panel = up_got.reshape(blocks_here, R, VALUE_OUTPUTS)
    token_blocks = tokens.reshape(blocks_here, block_rows, D)
    grad_blocks = cotangent.reshape(blocks_here, block_rows, VALUE_OUTPUTS)
    down_projected = jnp.einsum(
        "jtd,jdr->jtr", token_blocks, down_panel, preferred_element_type=jnp.float32
    ).astype(jnp.bfloat16)
    up_projected = jnp.einsum(
        "jtr,jrk->jtk", down_projected, up_panel, preferred_element_type=jnp.float32
    )
    mixed = (
        frozen_output + adapter_scale * up_projected.reshape(token_rows, VALUE_OUTPUTS)
    ).astype(jnp.bfloat16)
    down_projected_gradient = (
        adapter_scale
        * jnp.einsum("jtk,jrk->jtr", grad_blocks, up_panel, preferred_element_type=jnp.float32)
    ).astype(jnp.bfloat16)
    down_term = jnp.einsum(
        "jtd,jtr->jdr", token_blocks, down_projected_gradient, preferred_element_type=jnp.float32
    )
    up_weight_gradient = adapter_scale * jnp.einsum(
        "jtr,jtk->jrk", down_projected, grad_blocks, preferred_element_type=jnp.float32
    )
    down_back = lax.all_to_all(
        down_term.reshape(blocks_here, group, -1), "tensor", split_axis=1, concat_axis=1, tiled=True
    )
    up_back = lax.all_to_all(
        up_weight_gradient.reshape(blocks_here, group, -1), "tensor", split_axis=1, concat_axis=1, tiled=True
    )
    down_flat = down_back.reshape(blocks_here * group, -1)
    up_flat = up_back.reshape(blocks_here * group, -1)
    down_table = jax.ops.segment_sum(down_flat, order, num_segments=ADAPTERS)
    up_table = jax.ops.segment_sum(up_flat, order, num_segments=ADAPTERS)
    grad_down = lax.psum_scatter(down_table, "dp", scatter_dimension=0, tiled=True)
    grad_up = lax.psum_scatter(up_table, "dp", scatter_dimension=0, tiled=True)
    return mixed, grad_down, grad_up


def row_kernel(block_ref, slot_ref, out_ref):
    out_ref[...] = jnp.full(out_ref.shape, slot_ref[block_ref[0]], jnp.int32)


def split_kernel(x_ref, mine_ref, *theirs_refs):
    inner = lax.axis_index("tensor") % 2
    outer, rows, width = mine_ref.shape
    each = outer // len(theirs_refs)
    for k in range(outer):
        own = pl.multiple_of((2 * k + inner) * width, LANES)
        other = pl.multiple_of((2 * k + 1 - inner) * width, LANES)
        mine_ref[k] = x_ref[:, pl.ds(own, width)]
        theirs_refs[k // each][k % each] = x_ref[:, pl.ds(other, width)]


def interleave_kernel(x_ref, out_ref, xs_ref, sems):
    group, rows2, half = xs_ref.shape
    leave = [pltpu.make_async_copy(xs_ref.at[k], out_ref.at[k], sems.at[k]) for k in range(group)]
    rows, width = rows2 // 2, 2 * half
    source = lax.broadcasted_iota(jnp.int32, (width, half), 0)
    target = lax.broadcasted_iota(jnp.int32, (width, half), 1)
    even = (source == 2 * target).astype(jnp.bfloat16)
    odd = (source == 2 * target + 1).astype(jnp.bfloat16)
    for k in range(group):
        x = x_ref[:, k * width:(k + 1) * width]
        xs_ref[k, :rows] = dot(x, even).astype(jnp.bfloat16)
        xs_ref[k, rows:] = dot(x, odd).astype(jnp.bfloat16)
        leave[k].start()
    for copy in leave:
        copy.wait()


def gather_kernel(asked, down_ref, up_ref, out_ref, rows_ref, down_buf, up_buf, flat, built, sems):
    count, down_chunks, up_chunks = down_buf.shape[0], down_buf.shape[1], up_buf.shape[1]
    across = up_chunks // 8

    def copies(t):
        tile = asked[t, 0, 0] // TILE_ROWS
        return (
            pltpu.make_async_copy(down_ref.at[tile], down_buf.at[t], sems.at[0, t]),
            pltpu.make_async_copy(up_ref.at[tile], up_buf.at[t], sems.at[1, t]),
            pltpu.make_async_copy(built.at[t], out_ref.at[t], sems.at[2, t]),
        )

    for t in range(count):
        down, up, _ = copies(t)
        down.start()
        up.start()
        rows_ref[t] = asked[t, 0, 0]

    def one(t, carry):
        down, up, leave = copies(t)
        up.wait()
        for j in range(up_chunks):
            place = down_chunks + (j % across) * 8 + j // across
            flat[place * 8:place * 8 + 8, :] = up_buf[t, j].astype(jnp.float32)
        down.wait()
        for j in range(down_chunks):
            flat[j * 8:j * 8 + 8, :] = down_buf[t, j].astype(jnp.float32)
        sub = asked[t, 0, 0] % TILE_ROWS
        built[t] = flat[pl.ds(sub, down_chunks + up_chunks, stride=8), :].astype(jnp.bfloat16)
        leave.start()
        return carry

    lax.fori_loop(0, count, one, 0)
    for t in range(count):
        copies(t)[2].wait()


def zero_kernel(after_ref, down_ref, up_ref, done_ref, zeros, sems):
    del after_ref
    done_ref[0] = 0
    zeros[...] = jnp.zeros_like(zeros)
    part = zeros.shape[0]
    copies = []
    for ref, sem in ((down_ref, sems.at[0]), (up_ref, sems.at[1])):
        for g in range(ref.shape[0]):
            for c in range(ref.shape[1] // part):
                copies.append(pltpu.make_async_copy(zeros, ref.at[g, pl.ds(c * part, part)], sem))
    for c in copies:
        c.start()
    for c in copies:
        c.wait()


def adapter_kernel(count, down_chunks, xs_ref, g_ref, pieces, _, out_ref, lifted_ref, up_panel):
    rows = g_ref.shape[0]
    across = g_ref.shape[1] // LANES
    total = jnp.zeros((2 * rows, LANES), jnp.float32)
    for t in range(count):
        total += dot(xs_ref[t], pieces[t, :down_chunks])
        for c in range(across):
            block = pieces[t, down_chunks + 8 * c:down_chunks + 8 * c + 8, :].astype(jnp.float32)
            up_panel[8 * t:8 * t + 8, c * LANES:(c + 1) * LANES] = block
            up_panel[R + 8 * t:R + 8 * t + 8, c * LANES:(c + 1) * LANES] = block
    panel = up_panel[...].astype(jnp.bfloat16)
    left = lax.broadcasted_iota(jnp.int32, (rows, LANES), 1) < R
    inner = total[:rows] + pltpu.roll(total[rows:], R, 1)
    inner = jnp.where(left, inner, 0.0).astype(jnp.bfloat16)
    g = g_ref[...]
    lifted_ref[...] = adapter_scale * dot(inner, panel)
    inner_grad = adapter_scale * dot_t(g, panel)
    diagonal = jnp.concatenate(
        [jnp.where(left, inner_grad, 0.0), jnp.where(left, 0.0, inner_grad)], axis=0
    ).astype(jnp.bfloat16)
    up_term = adapter_scale * t_dot(inner, g)
    for t in range(count):
        out_ref[t, :down_chunks] = t_dot(xs_ref[t], diagonal).astype(jnp.bfloat16)
        up_part = jnp.concatenate(
            [up_term[8 * t:8 * t + 8, c * LANES:(c + 1) * LANES] for c in range(across)], axis=0
        )
        out_ref[t, down_chunks:] = up_part.astype(jnp.bfloat16)


def scatter_kernel(count, down_chunks, up_chunks, rows_here, rows_core, *rest):
    sources, (down_out, up_out) = rest[:2], rest[4:6]
    pieces, down_sum, up_sum, ordered, arrived, sem = rest[6:]
    half = count // 2
    owned_rows = down_out.shape[0] * 8
    first_row = lax.axis_index("dp") * owned_rows
    across = up_chunks // 8
    rows = [(rows_here if b < half else rows_core)[b % half] - first_row for b in range(count)]
    arriving = [pltpu.make_async_copy(sources[b // half].at[b % half], pieces.at[b], arrived.at[b]) for b in range(count)]
    owned = [(row >= 0) & (row < owned_rows) for row in rows]
    for b in range(count):
        @pl.when(owned[b])
        def _():
            arriving[b].start()

    slots, final = [], []
    for b in range(count):
        slot, last = jnp.int32(b), jnp.bool_(True)
        for e in range(b - 1, -1, -1):
            slot = jnp.where(rows[e] == rows[b], e, slot)
        for e in range(b + 1, count):
            last = last & (rows[e] != rows[b])
        slots.append(slot)
        final.append(last)

    def copies(b):
        return (
            pltpu.make_async_copy(down_sum.at[slots[b]], down_out.at[rows[b] // 8, :, rows[b] % 8, 0], sem),
            pltpu.make_async_copy(up_sum.at[slots[b]], up_out.at[rows[b] // 8, :, rows[b] % 8, 0], sem),
        )

    for b in range(count):
        @pl.when(owned[b])
        def _():
            arriving[b].wait()
            slot = slots[b]
            down = pieces[b, :down_chunks].astype(jnp.float32)
            for c in range(across):
                ordered[pl.ds(c, 8, stride=across), :] = pieces[
                    b, down_chunks + 8 * c:down_chunks + 8 * c + 8
                ].astype(jnp.float32)
            up = ordered[...]

            @pl.when(slot == b)
            def _():
                down_sum[b] = down
                up_sum[b] = up

            @pl.when(slot != b)
            def _():
                down_sum[slot] += down
                up_sum[slot] += up

            @pl.when(final[b])
            def _():
                for copy in copies(b):
                    copy.start()

    for b in range(count):
        @pl.when(owned[b] & final[b])
        def _():
            for copy in copies(b):
                copy.wait()


def base_kernel(*refs):
    whole, halves, w_from, out_refs = refs[:2], refs[2:6], refs[6:-8], refs[-7:-3]
    x_buf, w_buf, sems = refs[-3:]
    outer, rows, depth = whole[0].shape
    width, each = w_from[0].shape[1], outer // 2
    z = lax.axis_index("tensor") // 2
    order = [z, z ^ 1, jnp.where(z < 2, 2, 1), jnp.where(z < 2, 3, 0)]

    def fetch(k, begin):
        columns = pl.ds(k * depth, depth)
        copies = [
            pltpu.make_async_copy(ref.at[order[k]], x_buf.at[pl.ds(b * rows, rows), columns], sems.at[k, b])
            for b, ref in enumerate(whole)
        ] + [
            pltpu.make_async_copy(w_from[h * outer + k], w_buf.at[columns, pl.ds(h * width, width)], sems.at[k, 4 + h])
            for h in range(2)
        ]
        for copy in copies:
            copy.start() if begin else copy.wait()
        for b in range(2):
            for h in range(2):
                @pl.when(order[k] // each == h)
                def _():
                    source = halves[2 * b + h].at[order[k] % each]
                    place = x_buf.at[pl.ds((2 + b) * rows, rows), columns]
                    copy = pltpu.make_async_copy(source, place, sems.at[k, 2 + b])
                    copy.start() if begin else copy.wait()

    for k in range(outer):
        fetch(k, True)
    total = 0.0
    for first in range(0, outer, each):
        for k in range(first, first + each):
            fetch(k, False)
        columns = slice(first * depth, (first + each) * depth)
        total += dot(x_buf[:, columns], w_buf[columns, :])
    for b, ref in enumerate(out_refs):
        ref[...] = total[b * rows:(b + 1) * rows].astype(ref.dtype)


def fast_body(tokens, cotangent, frozen_value, down_store, up_store, block_adapter, adapter_slot):
    group, parts = lax.axis_size("tensor"), lax.axis_size("parts")
    outer = group // 2
    token_rows = tokens.shape[0]
    slice_width = D // group
    down_chunks = down_store.shape[1] // LANES
    up_chunks = up_store.shape[1] // LANES
    me, part, core = lax.axis_index("tensor"), lax.axis_index("parts"), lax.axis_index("dp")
    z = me // 2

    def exchange(value, s):
        return lax.ppermute(value, "tensor", [(t, t ^ s) for t in range(group)])

    def other_core(value):
        return lax.ppermute(value, "dp", [(0, 1), (1, 0)])

    def other_part(value):
        return lax.ppermute(value, "parts", [(a, parts - 1 - a) for a in range(parts)])

    row = pl.pallas_call(
        row_kernel, out_shape=jax.ShapeDtypeStruct((group, 1, LANES), jnp.int32),
        in_specs=[SMEM, SMEM], out_specs=VMEM, name="own_row",
    )(block_adapter, adapter_slot)
    asked = lax.all_to_all(row, "tensor", 0, 0)
    split_from, half_from, row = lax.optimization_barrier((tokens, frozen_value, row))

    width = frozen_value.shape[1] // parts
    half = lax.dynamic_slice_in_dim(half_from, part * width, width, axis=1)
    block = jax.ShapeDtypeStruct((outer, token_rows, slice_width), jnp.bfloat16)
    token = jax.ShapeDtypeStruct((1,), jnp.int32)
    some = jax.ShapeDtypeStruct((outer // 2, token_rows, slice_width), jnp.bfloat16)
    x_mine, *x_theirs = pl.pallas_call(
        split_kernel, out_shape=(block, some, some), in_specs=[VMEM], out_specs=[VMEM] * 3,
        name="split_tokens", compiler_params=LIMIT,
    )(split_from)
    x_far = [exchange(x_theirs[0], 1)]
    y_mine = other_part(x_mine)
    xs = pl.pallas_call(
        interleave_kernel,
        out_shape=jax.ShapeDtypeStruct((group, 2 * token_rows, slice_width // 2), jnp.bfloat16),
        in_specs=[VMEM], out_specs=ANY, name="pair_columns", compiler_params=WIDE,
        scratch_shapes=[
            pltpu.VMEM((group, 2 * token_rows, slice_width // 2), jnp.bfloat16),
            pltpu.SemaphoreType.DMA((group,)),
        ],
        cost_estimate=cost(read=128 << 20),
    )(split_from)
    middle = [(t, t ^ 6) for t in range(group) if t // 2 in (1, 2)]
    ends = [(t, t ^ 2) for t in range(group) if t // 2 in (1, 2)]
    near = exchange(half, 2)
    over = lax.ppermute(half, "tensor", middle)
    near, over, asked, x_theirs, xs = lax.optimization_barrier((near, over, asked, x_theirs, xs))
    x_far.append(exchange(x_theirs[1], 1))
    over_near = lax.ppermute(near, "tensor", middle)
    passed = lax.ppermute(over, "tensor", ends)
    pieces = jax.ShapeDtypeStruct((group, down_chunks + up_chunks, LANES), jnp.bfloat16)
    def tiles(store):
        view = store.reshape(store.shape[0] // TILE_ROWS, TILE_ROWS, store.shape[1] // LANES, LANES)
        return view.transpose(0, 2, 1, 3)

    sent, rows = pl.pallas_call(
        gather_kernel,
        out_shape=(pieces, jax.ShapeDtypeStruct((group,), jnp.int32)),
        in_specs=[SMEM, ANY, ANY],
        out_specs=(ANY, SMEM),
        scratch_shapes=[
            pltpu.VMEM((group, down_chunks, TILE_ROWS, LANES), jnp.bfloat16),
            pltpu.VMEM((group, up_chunks, TILE_ROWS, LANES), jnp.bfloat16),
            pltpu.VMEM(((down_chunks + up_chunks) * 8, LANES), jnp.float32),
            pltpu.VMEM(pieces.shape, jnp.bfloat16),
            pltpu.SemaphoreType.DMA((3, group)),
        ],
        compiler_params=WIDE,
        cost_estimate=cost(read=40 << 20),
        name="pick_panels",
    )(asked, tiles(down_store), tiles(up_store))
    sent, rows, x_far, y_mine, half, near, over, over_near, passed = lax.optimization_barrier(
        (sent, rows, x_far, y_mine, half, near, over, over_near, passed)
    )
    panels = lax.all_to_all(sent, "tensor", 0, 0)
    rows_core = other_core(rows)
    y_far = [other_part(part_of) for part_of in x_far]
    inside = (z == 1) | (z == 2)
    passed_near = lax.ppermute(over_near, "tensor", ends)
    quarter = [half, near, jnp.where(inside, over, passed)]
    quarter_core = [other_core(w) for w in quarter]
    owned_groups = ADAPTERS // lax.axis_size("dp") // 8
    down_shape = jax.ShapeDtypeStruct((owned_groups, down_chunks, 8, 1, LANES), jnp.float32)
    up_shape = jax.ShapeDtypeStruct((owned_groups, up_chunks, 8, 1, LANES), jnp.float32)
    down_zero, up_zero, cleared = pl.pallas_call(
        zero_kernel, out_shape=(down_shape, up_shape, token),
        in_specs=[SMEM], out_specs=(ANY, ANY, SMEM),
        scratch_shapes=[pltpu.VMEM((up_chunks, 8, 1, LANES), jnp.float32), pltpu.SemaphoreType.DMA((2,))],
        compiler_params=LIMIT, cost_estimate=cost(read=28 << 20), name="clear_rows",
    )(rows)
    panels, passed_near, y_far, quarter_core = lax.optimization_barrier((panels, passed_near, y_far, quarter_core))

    terms, lifted = pl.pallas_call(
        functools.partial(adapter_kernel, group, down_chunks),
        out_shape=(pieces, jax.ShapeDtypeStruct((token_rows, VALUE_OUTPUTS), jnp.float32)),
        in_specs=[VMEM] * 3 + [SMEM],
        out_specs=(VMEM, VMEM),
        scratch_shapes=[pltpu.VMEM((2 * R, VALUE_OUTPUTS), jnp.float32)],
        compiler_params=LIMIT,
        cost_estimate=cost(flops=3 << 30, read=8 << 20),
        name="adapter",
    )(xs, cotangent, panels, cleared)
    _, passed_near = lax.optimization_barrier((terms, passed_near))
    last = jnp.where(inside, over_near, passed_near)
    quarters = quarter + [last] + quarter_core + [other_core(last)]
    sums = [jax.ShapeDtypeStruct((token_rows, parts * width), kind) for kind in (jnp.float32,) + (jnp.bfloat16,) * 3]
    own, to_part, to_inner, to_both = pl.pallas_call(
        base_kernel,
        out_shape=sums,
        in_specs=[ANY] * (7 + 2 * outer),
        out_specs=[VMEM] * 4,
        scratch_shapes=[
            pltpu.VMEM((4 * token_rows, outer * slice_width), jnp.bfloat16),
            pltpu.VMEM((outer * slice_width, parts * width), jnp.bfloat16),
            pltpu.SemaphoreType.DMA((outer, 6)),
        ],
        compiler_params=WIDE,
        cost_estimate=cost(flops=4 << 30, read=8 << 20),
        name="frozen_part",
    )(x_mine, y_mine, *x_far, *y_far, *quarters, terms)
    opposite = [(a * group + t, (parts - 1 - a) * group + (t ^ 1)) for a in range(parts) for t in range(group)]
    back = lax.all_to_all(terms, "tensor", 0, 0)
    arrived = (exchange(to_inner, 1), other_part(to_part), lax.ppermute(to_both, ("parts", "tensor"), opposite))
    back, arrived = lax.optimization_barrier((back, arrived))
    back_core = other_core(back)

    grad_down, grad_up = pl.pallas_call(
        functools.partial(scatter_kernel, 2 * group, down_chunks, up_chunks),
        out_shape=(down_shape, up_shape),
        in_specs=[SMEM] * 2 + [ANY] * 4,
        out_specs=(ANY, ANY),
        input_output_aliases={4: 0, 5: 1},
        scratch_shapes=[
            pltpu.VMEM((2 * group,) + pieces.shape[1:], jnp.bfloat16),
            pltpu.VMEM((2 * group, down_chunks, LANES), jnp.float32),
            pltpu.VMEM((2 * group, up_chunks, LANES), jnp.float32),
            pltpu.VMEM((up_chunks, LANES), jnp.float32),
            pltpu.SemaphoreType.DMA((2 * group,)),
            pltpu.SemaphoreType.DMA(()),
        ],
        compiler_params=LIMIT,
        cost_estimate=cost(read=16 << 20),
        name="place_rows",
    )(rows, rows_core, back, back_core, down_zero, up_zero)
    grad_down = grad_down.reshape(owned_groups, down_chunks, 8, LANES).transpose(0, 2, 1, 3)
    grad_up = grad_up.reshape(owned_groups, up_chunks, 8, LANES).transpose(0, 2, 1, 3)

    arrived = [a.astype(jnp.float32) for a in arrived]
    kept, got = own + arrived[0], arrived[1] + arrived[2]
    quarters = [[c[:, :width], c[:, width:]] for c in (kept, got)]

    def pick_quarter(c, a):
        first = quarters[a][0] if c == 0 else quarters[a][1]
        second = quarters[a][1] if c == 0 else quarters[a][0]
        return jnp.where(core == 0, first, second)

    def columns_of(c):
        low, high = pick_quarter(c, 0), pick_quarter(c, 1)
        return jnp.where(part == 0, low, high), jnp.where(part == 0, high, low)

    frozen_output = jnp.concatenate(columns_of(0) + columns_of(1), axis=1)
    mixed = (frozen_output + lifted).astype(jnp.bfloat16)
    return mixed, grad_down.reshape(owned_groups * 8, -1), grad_up.reshape(owned_groups * 8, -1)


def fits(mesh):
    group, cores, parts = mesh.shape["tensor"], mesh.shape["dp"], mesh.shape["parts"]
    return cores == 2 and parts == 2 and group <= 8 and group & (group - 1) == 0 and R == 8 * group


def body(mesh, tokens, *rest):
    block_adapter = rest[4]
    one_block = block_adapter.shape[0] == 1
    return (fast_body if fits(mesh) and one_block else plain_body)(tokens, *rest)


def solution(mesh):
    placed = (
        P(("parts", "dp", "tensor"), None),
        P(("parts", "dp", "tensor"), None),
        P("tensor", "dp"),
        P("parts", "tensor"),
        P("parts", "tensor"),
        P(("parts", "dp", "tensor")),
        P("parts"),
    )
    return jax.shard_map(
        functools.partial(body, mesh),
        mesh=mesh,
        in_specs=placed,
        out_specs=(
            P(("parts", "dp", "tensor"), None),
            P(("parts", "dp"), "tensor"),
            P(("parts", "dp"), "tensor"),
        ),
        check_vma=False,
    )
```

```python
import functools

import jax
import jax.numpy as jnp
from jax import lax
from jax.experimental import pallas as pl
from jax.experimental.pallas import tpu as pltpu
from jax.sharding import PartitionSpec as P

D = 5120
VALUE_OUTPUTS = 1024
R = 64
ADAPTERS = 256
LANES = 128
TILE_ROWS = 8

adapter_scale = 2.0
VMEM = pl.BlockSpec(memory_space=pltpu.VMEM)
SMEM = pl.BlockSpec(memory_space=pltpu.SMEM)
ANY = pl.BlockSpec(memory_space=pl.ANY)
LIMIT = pltpu.CompilerParams(vmem_limit_bytes=16 * 1024 * 1024)
WIDE = pltpu.CompilerParams(vmem_limit_bytes=60 * 1024 * 1024)


def cost(flops=0, read=0):
    return pl.CostEstimate(flops=flops, bytes_accessed=read, transcendentals=0)


def dot(a, b):
    return jnp.dot(a, b, preferred_element_type=jnp.float32)


def dot_t(a, b):
    return lax.dot_general(a, b, (((1,), (1,)), ((), ())), preferred_element_type=jnp.float32)


def t_dot(a, b):
    return lax.dot_general(a, b, (((0,), (0,)), ((), ())), preferred_element_type=jnp.float32)


def fold_rows(left, piece):
    return jnp.dot(left, piece, preferred_element_type=jnp.float32)


def store_rows(requests, adapter_slot):
    table = jnp.arange(adapter_slot.shape[0], dtype=jnp.int32)
    return jnp.sum(jnp.where(requests[:, None] == table[None, :], adapter_slot[None, :], 0), axis=1)


def plain_body(tokens, cotangent, frozen_value, down_store, up_store, block_adapter, adapter_slot):
    token_rows = tokens.shape[0]
    blocks_here = block_adapter.shape[0]
    block_rows = token_rows // blocks_here
    group = lax.axis_size("tensor")
    columns = lax.all_gather(frozen_value, "dp", axis=1, tiled=True)
    frozen_output = fold_rows(tokens, lax.all_gather(columns, "tensor", axis=0, tiled=True))
    requests = lax.all_gather(block_adapter, "tensor", axis=0, tiled=True)
    stored = store_rows(requests, adapter_slot)
    order = stored.reshape(group, blocks_here).T.reshape(-1)
    down_send = jnp.take(down_store, order, axis=0).reshape(blocks_here, group, -1)
    up_send = jnp.take(up_store, order, axis=0).reshape(blocks_here, group, -1)
    down_got = lax.all_to_all(down_send, "tensor", split_axis=1, concat_axis=1, tiled=True)
    up_got = lax.all_to_all(up_send, "tensor", split_axis=1, concat_axis=1, tiled=True)
    down_panel = down_got.reshape(blocks_here, D, R)
    up_panel = up_got.reshape(blocks_here, R, VALUE_OUTPUTS)
    token_blocks = tokens.reshape(blocks_here, block_rows, D)
    grad_blocks = cotangent.reshape(blocks_here, block_rows, VALUE_OUTPUTS)
    down_projected = jnp.einsum(
        "jtd,jdr->jtr", token_blocks, down_panel, preferred_element_type=jnp.float32
    ).astype(jnp.bfloat16)
    up_projected = jnp.einsum(
        "jtr,jrk->jtk", down_projected, up_panel, preferred_element_type=jnp.float32
    )
    mixed = (
        frozen_output + adapter_scale * up_projected.reshape(token_rows, VALUE_OUTPUTS)
    ).astype(jnp.bfloat16)
    down_projected_gradient = (
        adapter_scale
        * jnp.einsum("jtk,jrk->jtr", grad_blocks, up_panel, preferred_element_type=jnp.float32)
    ).astype(jnp.bfloat16)
    down_term = jnp.einsum(
        "jtd,jtr->jdr", token_blocks, down_projected_gradient, preferred_element_type=jnp.float32
    )
    up_weight_gradient = adapter_scale * jnp.einsum(
        "jtr,jtk->jrk", down_projected, grad_blocks, preferred_element_type=jnp.float32
    )
    down_back = lax.all_to_all(
        down_term.reshape(blocks_here, group, -1), "tensor", split_axis=1, concat_axis=1, tiled=True
    )
    up_back = lax.all_to_all(
        up_weight_gradient.reshape(blocks_here, group, -1), "tensor", split_axis=1, concat_axis=1, tiled=True
    )
    down_flat = down_back.reshape(blocks_here * group, -1)
    up_flat = up_back.reshape(blocks_here * group, -1)
    down_table = jax.ops.segment_sum(down_flat, order, num_segments=ADAPTERS)
    up_table = jax.ops.segment_sum(up_flat, order, num_segments=ADAPTERS)
    grad_down = lax.psum_scatter(down_table, "dp", scatter_dimension=0, tiled=True)
    grad_up = lax.psum_scatter(up_table, "dp", scatter_dimension=0, tiled=True)
    return mixed, grad_down, grad_up


def row_kernel(block_ref, slot_ref, out_ref):
    out_ref[...] = jnp.full(out_ref.shape, slot_ref[block_ref[0]], jnp.int32)


def split_kernel(x_ref, mine_ref, *theirs_refs):
    inner = lax.axis_index("tensor") % 2
    outer, rows, width = mine_ref.shape
    each = outer // len(theirs_refs)
    for k in range(outer):
        own = pl.multiple_of((2 * k + inner) * width, LANES)
        other = pl.multiple_of((2 * k + 1 - inner) * width, LANES)
        mine_ref[k] = x_ref[:, pl.ds(own, width)]
        theirs_refs[k // each][k % each] = x_ref[:, pl.ds(other, width)]


def interleave_kernel(x_ref, out_ref, xs_ref, sems):
    group, rows2, half = xs_ref.shape
    leave = [pltpu.make_async_copy(xs_ref.at[k], out_ref.at[k], sems.at[k]) for k in range(group)]
    rows, width = rows2 // 2, 2 * half
    source = lax.broadcasted_iota(jnp.int32, (width, half), 0)
    target = lax.broadcasted_iota(jnp.int32, (width, half), 1)
    even = (source == 2 * target).astype(jnp.bfloat16)
    odd = (source == 2 * target + 1).astype(jnp.bfloat16)
    for k in range(group):
        x = x_ref[:, k * width:(k + 1) * width]
        xs_ref[k, :rows] = dot(x, even).astype(jnp.bfloat16)
        xs_ref[k, rows:] = dot(x, odd).astype(jnp.bfloat16)
        leave[k].start()
    for copy in leave:
        copy.wait()


def gather_kernel(asked, down_ref, up_ref, out_ref, rows_ref, down_buf, up_buf, flats, built, sems):
    count, down_chunks, up_chunks = down_buf.shape[0], down_buf.shape[1], up_buf.shape[1]
    across = up_chunks // 8

    def copies(t):
        tile = asked[t, 0, 0] // TILE_ROWS
        return (
            pltpu.make_async_copy(down_ref.at[tile], down_buf.at[t], sems.at[0, t]),
            pltpu.make_async_copy(up_ref.at[tile], up_buf.at[t], sems.at[1, t]),
            pltpu.make_async_copy(built.at[t], out_ref.at[t], sems.at[2, t]),
        )

    for t in range(count):
        down, up, _ = copies(t)
        down.start()
        up.start()
        rows_ref[t] = asked[t, 0, 0]

    def one(t, flat):
        down, up, leave = copies(t)
        up.wait()
        for j in range(up_chunks):
            place = down_chunks + (j % across) * 8 + j // across
            flat[place * 8:place * 8 + 8, :] = up_buf[t, j].astype(jnp.float32)
        down.wait()
        for j in range(down_chunks):
            flat[j * 8:j * 8 + 8, :] = down_buf[t, j].astype(jnp.float32)
        sub = asked[t, 0, 0] % TILE_ROWS
        built[t] = flat[pl.ds(sub, down_chunks + up_chunks, stride=8), :].astype(jnp.bfloat16)
        leave.start()

    def two(i, carry):
        for u in range(2):
            one(2 * i + u, flats.at[u])
        return carry

    lax.fori_loop(0, count // 2, two, 0)
    for t in range(count):
        copies(t)[2].wait()


def zero_kernel(after_ref, down_ref, up_ref, done_ref, zeros, sems):
    del after_ref
    done_ref[0] = 0
    zeros[...] = jnp.zeros_like(zeros)
    part = zeros.shape[0]
    copies = []
    for ref, sem in ((down_ref, sems.at[0]), (up_ref, sems.at[1])):
        for g in range(ref.shape[0]):
            for c in range(ref.shape[1] // part):
                copies.append(pltpu.make_async_copy(zeros, ref.at[g, pl.ds(c * part, part)], sem))
    for c in copies:
        c.start()
    for c in copies:
        c.wait()


def adapter_kernel(count, down_chunks, xs_ref, g_ref, pieces, _, out_ref, lifted_ref, up_panel):
    rows = g_ref.shape[0]
    across = g_ref.shape[1] // LANES
    total = jnp.zeros((2 * rows, LANES), jnp.float32)
    for t in range(count):
        total += dot(xs_ref[t], pieces[t, :down_chunks])
        for c in range(across):
            block = pieces[t, down_chunks + 8 * c:down_chunks + 8 * c + 8, :].astype(jnp.float32)
            up_panel[8 * t:8 * t + 8, c * LANES:(c + 1) * LANES] = block
            up_panel[R + 8 * t:R + 8 * t + 8, c * LANES:(c + 1) * LANES] = block
    panel = up_panel[...].astype(jnp.bfloat16)
    left = lax.broadcasted_iota(jnp.int32, (rows, LANES), 1) < R
    inner = total[:rows] + pltpu.roll(total[rows:], R, 1)
    inner = jnp.where(left, inner, 0.0).astype(jnp.bfloat16)
    g = g_ref[...]
    lifted_ref[...] = adapter_scale * dot(inner, panel)
    inner_grad = adapter_scale * dot_t(g, panel)
    diagonal = jnp.concatenate(
        [jnp.where(left, inner_grad, 0.0), jnp.where(left, 0.0, inner_grad)], axis=0
    ).astype(jnp.bfloat16)
    up_term = adapter_scale * t_dot(inner, g)
    for t in range(count):
        out_ref[t, :down_chunks] = t_dot(xs_ref[t], diagonal).astype(jnp.bfloat16)
        up_part = jnp.concatenate(
            [up_term[8 * t:8 * t + 8, c * LANES:(c + 1) * LANES] for c in range(across)], axis=0
        )
        out_ref[t, down_chunks:] = up_part.astype(jnp.bfloat16)


def scatter_kernel(count, down_chunks, up_chunks, rows_here, rows_core, *rest):
    sources, (down_out, up_out) = rest[:2], rest[4:6]
    pieces, down_sum, up_sum, ordered, arrived, sem = rest[6:]
    half = count // 2
    owned_rows = down_out.shape[0] * 8
    first_row = lax.axis_index("dp") * owned_rows
    across = up_chunks // 8
    rows = [(rows_here if b < half else rows_core)[b % half] - first_row for b in range(count)]
    arriving = [pltpu.make_async_copy(sources[b // half].at[b % half], pieces.at[b], arrived.at[b]) for b in range(count)]
    owned = [(row >= 0) & (row < owned_rows) for row in rows]
    for b in range(count):
        @pl.when(owned[b])
        def _():
            arriving[b].start()

    slots, final = [], []
    for b in range(count):
        slot, last = jnp.int32(b), jnp.bool_(True)
        for e in range(b - 1, -1, -1):
            slot = jnp.where(rows[e] == rows[b], e, slot)
        for e in range(b + 1, count):
            last = last & (rows[e] != rows[b])
        slots.append(slot)
        final.append(last)

    def copies(b):
        return (
            pltpu.make_async_copy(down_sum.at[slots[b]], down_out.at[rows[b] // 8, :, rows[b] % 8, 0], sem),
            pltpu.make_async_copy(up_sum.at[slots[b]], up_out.at[rows[b] // 8, :, rows[b] % 8, 0], sem),
        )

    for b in range(count):
        @pl.when(owned[b])
        def _():
            arriving[b].wait()
            slot = slots[b]
            down = pieces[b, :down_chunks].astype(jnp.float32)
            for c in range(across):
                ordered[pl.ds(c, 8, stride=across), :] = pieces[
                    b, down_chunks + 8 * c:down_chunks + 8 * c + 8
                ].astype(jnp.float32)
            up = ordered[...]

            @pl.when(slot == b)
            def _():
                down_sum[b] = down
                up_sum[b] = up

            @pl.when(slot != b)
            def _():
                down_sum[slot] += down
                up_sum[slot] += up

            @pl.when(final[b])
            def _():
                for copy in copies(b):
                    copy.start()

    for b in range(count):
        @pl.when(owned[b] & final[b])
        def _():
            for copy in copies(b):
                copy.wait()


def base_kernel(*refs):
    whole, halves, w_from, out_refs = refs[:2], refs[2:6], refs[6:-8], refs[-7:-3]
    x_buf, w_buf, sems = refs[-3:]
    outer, rows, depth = whole[0].shape
    width, each = w_from[0].shape[1], outer // 2
    z = lax.axis_index("tensor") // 2
    inside = (z == 1) | (z == 2)
    order = [z, z ^ 1, jnp.where(z < 2, 2, 1), jnp.where(z < 2, 3, 0)]
    pieces = len(w_from) // 2

    def fetch(k, begin):
        columns = pl.ds(k * depth, depth)

        def move(source, place, sem):
            copy = pltpu.make_async_copy(source, place, sem)
            copy.start() if begin else copy.wait()

        for b, ref in enumerate(whole):
            move(ref.at[order[k]], x_buf.at[pl.ds(b * rows, rows), columns], sems.at[k, b])
            for h in range(2):
                @pl.when(order[k] // each == h)
                def _():
                    place = x_buf.at[pl.ds((2 + b) * rows, rows), columns]
                    move(halves[2 * b + h].at[order[k] % each], place, sems.at[k, 2 + b])
        for h in range(2):
            place, sem = w_buf.at[columns, pl.ds(h * width, width)], sems.at[k, 4 + h]
            if k < 2:
                move(w_from[h * pieces + k], place, sem)
                continue

            @pl.when(inside)
            def _():
                move(w_from[h * pieces + 2 * k - 2], place, sem)

            @pl.when(jnp.logical_not(inside))
            def _():
                move(w_from[h * pieces + 2 * k - 1], place, sem)

    for k in range(outer):
        fetch(k, True)
    total = 0.0
    for first in range(0, outer, each):
        for k in range(first, first + each):
            fetch(k, False)
        columns = slice(first * depth, (first + each) * depth)
        total += dot(x_buf[:, columns], w_buf[columns, :])
    for b, ref in enumerate(out_refs):
        ref[...] = total[b * rows:(b + 1) * rows].astype(ref.dtype)


def fast_body(tokens, cotangent, frozen_value, down_store, up_store, block_adapter, adapter_slot):
    group, parts = lax.axis_size("tensor"), lax.axis_size("parts")
    outer = group // 2
    token_rows = tokens.shape[0]
    slice_width = D // group
    down_chunks = down_store.shape[1] // LANES
    up_chunks = up_store.shape[1] // LANES
    me, part, core = lax.axis_index("tensor"), lax.axis_index("parts"), lax.axis_index("dp")
    z = me // 2

    def exchange(value, s):
        return lax.ppermute(value, "tensor", [(t, t ^ s) for t in range(group)])

    def other_core(value):
        return lax.ppermute(value, "dp", [(0, 1), (1, 0)])

    def other_part(value):
        return lax.ppermute(value, "parts", [(a, parts - 1 - a) for a in range(parts)])

    row = pl.pallas_call(
        row_kernel, out_shape=jax.ShapeDtypeStruct((group, 1, LANES), jnp.int32),
        in_specs=[SMEM, SMEM], out_specs=VMEM, name="own_row",
    )(block_adapter, adapter_slot)
    asked = lax.all_to_all(row, "tensor", 0, 0)
    split_from, half_from, row = lax.optimization_barrier((tokens, frozen_value, row))

    width = frozen_value.shape[1] // parts
    half = lax.dynamic_slice_in_dim(half_from, part * width, width, axis=1)
    block = jax.ShapeDtypeStruct((outer, token_rows, slice_width), jnp.bfloat16)
    token = jax.ShapeDtypeStruct((1,), jnp.int32)
    some = jax.ShapeDtypeStruct((outer // 2, token_rows, slice_width), jnp.bfloat16)
    x_mine, *x_theirs = pl.pallas_call(
        split_kernel, out_shape=(block, some, some), in_specs=[VMEM], out_specs=[VMEM] * 3,
        name="split_tokens", compiler_params=LIMIT,
    )(split_from)
    x_far = [exchange(x_theirs[0], 1)]
    y_mine = other_part(x_mine)
    xs = pl.pallas_call(
        interleave_kernel,
        out_shape=jax.ShapeDtypeStruct((group, 2 * token_rows, slice_width // 2), jnp.bfloat16),
        in_specs=[VMEM], out_specs=ANY, name="pair_columns", compiler_params=WIDE,
        scratch_shapes=[
            pltpu.VMEM((group, 2 * token_rows, slice_width // 2), jnp.bfloat16),
            pltpu.SemaphoreType.DMA((group,)),
        ],
        cost_estimate=cost(read=128 << 20),
    )(split_from)
    middle = [(t, t ^ 6) for t in range(group) if t // 2 in (1, 2)]
    ends = [(t, t ^ 2) for t in range(group) if t // 2 in (1, 2)]
    near = exchange(half, 2)
    over = lax.ppermute(half, "tensor", middle)
    near, over, asked, x_theirs, xs = lax.optimization_barrier((near, over, asked, x_theirs, xs))
    x_far.append(exchange(x_theirs[1], 1))
    y_far = [other_part(x_far[0])]
    over_near = lax.ppermute(near, "tensor", middle)
    passed = lax.ppermute(over, "tensor", ends)
    pieces = jax.ShapeDtypeStruct((group, down_chunks + up_chunks, LANES), jnp.bfloat16)
    def tiles(store):
        view = store.reshape(store.shape[0] // TILE_ROWS, TILE_ROWS, store.shape[1] // LANES, LANES)
        return view.transpose(0, 2, 1, 3)

    sent, rows = pl.pallas_call(
        gather_kernel,
        out_shape=(pieces, jax.ShapeDtypeStruct((group,), jnp.int32)),
        in_specs=[SMEM, ANY, ANY],
        out_specs=(ANY, SMEM),
        scratch_shapes=[
            pltpu.VMEM((group, down_chunks, TILE_ROWS, LANES), jnp.bfloat16),
            pltpu.VMEM((group, up_chunks, TILE_ROWS, LANES), jnp.bfloat16),
            pltpu.VMEM((2, (down_chunks + up_chunks) * 8, LANES), jnp.float32),
            pltpu.VMEM(pieces.shape, jnp.bfloat16),
            pltpu.SemaphoreType.DMA((3, group)),
        ],
        compiler_params=WIDE,
        cost_estimate=cost(read=40 << 20),
        name="pick_panels",
    )(asked, tiles(down_store), tiles(up_store))
    sent, rows, x_far, y_far, y_mine, half, near, over, over_near, passed = lax.optimization_barrier(
        (sent, rows, x_far, y_far, y_mine, half, near, over, over_near, passed)
    )
    panels = lax.all_to_all(sent, "tensor", 0, 0)
    rows_core = other_core(rows)
    y_far.append(other_part(x_far[1]))
    passed_near = lax.ppermute(over_near, "tensor", ends)
    quarter = [half, near, over, passed, over_near]
    quarter_core = [other_core(w) for w in quarter]

    owned_groups = ADAPTERS // lax.axis_size("dp") // 8
    down_shape = jax.ShapeDtypeStruct((owned_groups, down_chunks, 8, 1, LANES), jnp.float32)
    up_shape = jax.ShapeDtypeStruct((owned_groups, up_chunks, 8, 1, LANES), jnp.float32)
    down_zero, up_zero, cleared = pl.pallas_call(
        zero_kernel, out_shape=(down_shape, up_shape, token),
        in_specs=[SMEM], out_specs=(ANY, ANY, SMEM),
        scratch_shapes=[pltpu.VMEM((up_chunks, 8, 1, LANES), jnp.float32), pltpu.SemaphoreType.DMA((2,))],
        compiler_params=LIMIT, cost_estimate=cost(read=28 << 20), name="clear_rows",
    )(rows)
    panels, passed_near, y_far, quarter_core = lax.optimization_barrier((panels, passed_near, y_far, quarter_core))

    terms, lifted = pl.pallas_call(
        functools.partial(adapter_kernel, group, down_chunks),
        out_shape=(pieces, jax.ShapeDtypeStruct((token_rows, VALUE_OUTPUTS), jnp.float32)),
        in_specs=[VMEM] * 3 + [SMEM],
        out_specs=(VMEM, VMEM),
        scratch_shapes=[pltpu.VMEM((2 * R, VALUE_OUTPUTS), jnp.float32)],
        compiler_params=LIMIT,
        cost_estimate=cost(flops=3 << 30, read=8 << 20),
        name="adapter",
    )(xs, cotangent, panels, cleared)
    _, passed_near = lax.optimization_barrier((terms, passed_near))
    quarters = quarter + [passed_near] + quarter_core + [other_core(passed_near)]
    sums = [jax.ShapeDtypeStruct((token_rows, parts * width), kind) for kind in (jnp.float32,) + (jnp.bfloat16,) * 3]
    own, to_part, to_inner, to_both = pl.pallas_call(
        base_kernel,
        out_shape=sums,
        in_specs=[ANY] * (7 + len(quarters)),
        out_specs=[VMEM] * 4,
        scratch_shapes=[
            pltpu.VMEM((4 * token_rows, outer * slice_width), jnp.bfloat16),
            pltpu.VMEM((outer * slice_width, parts * width), jnp.bfloat16),
            pltpu.SemaphoreType.DMA((outer, 6)),
        ],
        compiler_params=WIDE,
        cost_estimate=cost(flops=4 << 30, read=8 << 20),
        name="frozen_part",
    )(x_mine, y_mine, *x_far, *y_far, *quarters, terms)
    opposite = [(a * group + t, (parts - 1 - a) * group + (t ^ 1)) for a in range(parts) for t in range(group)]
    back = lax.all_to_all(terms, "tensor", 0, 0)
    arrived = (exchange(to_inner, 1), other_part(to_part), lax.ppermute(to_both, ("parts", "tensor"), opposite))
    back, arrived = lax.optimization_barrier((back, arrived))
    back_core = other_core(back)

    grad_down, grad_up = pl.pallas_call(
        functools.partial(scatter_kernel, 2 * group, down_chunks, up_chunks),
        out_shape=(down_shape, up_shape),
        in_specs=[SMEM] * 2 + [ANY] * 4,
        out_specs=(ANY, ANY),
        input_output_aliases={4: 0, 5: 1},
        scratch_shapes=[
            pltpu.VMEM((2 * group,) + pieces.shape[1:], jnp.bfloat16),
            pltpu.VMEM((2 * group, down_chunks, LANES), jnp.float32),
            pltpu.VMEM((2 * group, up_chunks, LANES), jnp.float32),
            pltpu.VMEM((up_chunks, LANES), jnp.float32),
            pltpu.SemaphoreType.DMA((2 * group,)),
            pltpu.SemaphoreType.DMA(()),
        ],
        compiler_params=LIMIT,
        cost_estimate=cost(read=16 << 20),
        name="place_rows",
    )(rows, rows_core, back, back_core, down_zero, up_zero)
    grad_down = grad_down.reshape(owned_groups, down_chunks, 8, LANES).transpose(0, 2, 1, 3)
    grad_up = grad_up.reshape(owned_groups, up_chunks, 8, LANES).transpose(0, 2, 1, 3)

    arrived = [a.astype(jnp.float32) for a in arrived]
    kept, got = own + arrived[0], arrived[1] + arrived[2]
    quarters = [[c[:, :width], c[:, width:]] for c in (kept, got)]

    def pick_quarter(c, a):
        first = quarters[a][0] if c == 0 else quarters[a][1]
        second = quarters[a][1] if c == 0 else quarters[a][0]
        return jnp.where(core == 0, first, second)

    def columns_of(c):
        low, high = pick_quarter(c, 0), pick_quarter(c, 1)
        return jnp.where(part == 0, low, high), jnp.where(part == 0, high, low)

    frozen_output = jnp.concatenate(columns_of(0) + columns_of(1), axis=1)
    mixed = (frozen_output + lifted).astype(jnp.bfloat16)
    return mixed, grad_down.reshape(owned_groups * 8, -1), grad_up.reshape(owned_groups * 8, -1)


def fits(mesh):
    group, cores, parts = mesh.shape["tensor"], mesh.shape["dp"], mesh.shape["parts"]
    return cores == 2 and parts == 2 and group <= 8 and group & (group - 1) == 0 and R == 8 * group


def body(mesh, tokens, *rest):
    block_adapter = rest[4]
    one_block = block_adapter.shape[0] == 1
    return (fast_body if fits(mesh) and one_block else plain_body)(tokens, *rest)


def solution(mesh):
    placed = (
        P(("parts", "dp", "tensor"), None),
        P(("parts", "dp", "tensor"), None),
        P("tensor", "dp"),
        P("parts", "tensor"),
        P("parts", "tensor"),
        P(("parts", "dp", "tensor")),
        P("parts"),
    )
    return jax.shard_map(
        functools.partial(body, mesh),
        mesh=mesh,
        in_specs=placed,
        out_specs=(
            P(("parts", "dp", "tensor"), None),
            P(("parts", "dp"), "tensor"),
            P(("parts", "dp"), "tensor"),
        ),
        check_vma=False,
    )
```

```python
import functools

import jax
import jax.numpy as jnp
from jax import lax
from jax.experimental import pallas as pl
from jax.experimental.pallas import tpu as pltpu
from jax.sharding import PartitionSpec as P

D = 5120
VALUE_OUTPUTS = 1024
R = 64
ADAPTERS = 256
LANES = 128
TILE_ROWS = 8

adapter_scale = 2.0
VMEM = pl.BlockSpec(memory_space=pltpu.VMEM)
SMEM = pl.BlockSpec(memory_space=pltpu.SMEM)
ANY = pl.BlockSpec(memory_space=pl.ANY)
LIMIT = pltpu.CompilerParams(vmem_limit_bytes=16 * 1024 * 1024)
WIDE = pltpu.CompilerParams(vmem_limit_bytes=60 * 1024 * 1024)


def cost(flops=0, read=0):
    return pl.CostEstimate(flops=flops, bytes_accessed=read, transcendentals=0)


def dot(a, b):
    return jnp.dot(a, b, preferred_element_type=jnp.float32)


def dot_t(a, b):
    return lax.dot_general(a, b, (((1,), (1,)), ((), ())), preferred_element_type=jnp.float32)


def t_dot(a, b):
    return lax.dot_general(a, b, (((0,), (0,)), ((), ())), preferred_element_type=jnp.float32)


def fold_rows(left, piece):
    return jnp.dot(left, piece, preferred_element_type=jnp.float32)


def store_rows(requests, adapter_slot):
    table = jnp.arange(adapter_slot.shape[0], dtype=jnp.int32)
    return jnp.sum(jnp.where(requests[:, None] == table[None, :], adapter_slot[None, :], 0), axis=1)


def plain_body(tokens, cotangent, frozen_value, down_store, up_store, block_adapter, adapter_slot):
    token_rows = tokens.shape[0]
    blocks_here = block_adapter.shape[0]
    block_rows = token_rows // blocks_here
    group = lax.axis_size("tensor")
    columns = lax.all_gather(frozen_value, "dp", axis=1, tiled=True)
    frozen_output = fold_rows(tokens, lax.all_gather(columns, "tensor", axis=0, tiled=True))
    requests = lax.all_gather(block_adapter, "tensor", axis=0, tiled=True)
    stored = store_rows(requests, adapter_slot)
    order = stored.reshape(group, blocks_here).T.reshape(-1)
    down_send = jnp.take(down_store, order, axis=0).reshape(blocks_here, group, -1)
    up_send = jnp.take(up_store, order, axis=0).reshape(blocks_here, group, -1)
    down_got = lax.all_to_all(down_send, "tensor", split_axis=1, concat_axis=1, tiled=True)
    up_got = lax.all_to_all(up_send, "tensor", split_axis=1, concat_axis=1, tiled=True)
    down_panel = down_got.reshape(blocks_here, D, R)
    up_panel = up_got.reshape(blocks_here, R, VALUE_OUTPUTS)
    token_blocks = tokens.reshape(blocks_here, block_rows, D)
    grad_blocks = cotangent.reshape(blocks_here, block_rows, VALUE_OUTPUTS)
    down_projected = jnp.einsum(
        "jtd,jdr->jtr", token_blocks, down_panel, preferred_element_type=jnp.float32
    ).astype(jnp.bfloat16)
    up_projected = jnp.einsum(
        "jtr,jrk->jtk", down_projected, up_panel, preferred_element_type=jnp.float32
    )
    mixed = (
        frozen_output + adapter_scale * up_projected.reshape(token_rows, VALUE_OUTPUTS)
    ).astype(jnp.bfloat16)
    down_projected_gradient = (
        adapter_scale
        * jnp.einsum("jtk,jrk->jtr", grad_blocks, up_panel, preferred_element_type=jnp.float32)
    ).astype(jnp.bfloat16)
    down_term = jnp.einsum(
        "jtd,jtr->jdr", token_blocks, down_projected_gradient, preferred_element_type=jnp.float32
    )
    up_weight_gradient = adapter_scale * jnp.einsum(
        "jtr,jtk->jrk", down_projected, grad_blocks, preferred_element_type=jnp.float32
    )
    down_back = lax.all_to_all(
        down_term.reshape(blocks_here, group, -1), "tensor", split_axis=1, concat_axis=1, tiled=True
    )
    up_back = lax.all_to_all(
        up_weight_gradient.reshape(blocks_here, group, -1), "tensor", split_axis=1, concat_axis=1, tiled=True
    )
    down_flat = down_back.reshape(blocks_here * group, -1)
    up_flat = up_back.reshape(blocks_here * group, -1)
    down_table = jax.ops.segment_sum(down_flat, order, num_segments=ADAPTERS)
    up_table = jax.ops.segment_sum(up_flat, order, num_segments=ADAPTERS)
    grad_down = lax.psum_scatter(down_table, "dp", scatter_dimension=0, tiled=True)
    grad_up = lax.psum_scatter(up_table, "dp", scatter_dimension=0, tiled=True)
    return mixed, grad_down, grad_up


def row_kernel(block_ref, slot_ref, out_ref):
    out_ref[...] = jnp.full(out_ref.shape, slot_ref[block_ref[0]], jnp.int32)


def split_kernel(x_ref, mine_ref, *theirs_refs):
    inner = lax.axis_index("tensor") % 2
    outer, rows, width = mine_ref.shape
    each = outer // len(theirs_refs)
    for k in range(outer):
        own = pl.multiple_of((2 * k + inner) * width, LANES)
        other = pl.multiple_of((2 * k + 1 - inner) * width, LANES)
        mine_ref[k] = x_ref[:, pl.ds(own, width)]
        theirs_refs[k // each][k % each] = x_ref[:, pl.ds(other, width)]


def interleave_kernel(x_ref, out_ref, xs_ref, sems):
    group, rows2, half = xs_ref.shape
    leave = [pltpu.make_async_copy(xs_ref.at[k], out_ref.at[k], sems.at[k]) for k in range(group)]
    rows, width = rows2 // 2, 2 * half
    source = lax.broadcasted_iota(jnp.int32, (width, half), 0)
    target = lax.broadcasted_iota(jnp.int32, (width, half), 1)
    even = (source == 2 * target).astype(jnp.bfloat16)
    odd = (source == 2 * target + 1).astype(jnp.bfloat16)
    for k in range(group):
        x = x_ref[:, k * width:(k + 1) * width]
        xs_ref[k, :rows] = dot(x, even).astype(jnp.bfloat16)
        xs_ref[k, rows:] = dot(x, odd).astype(jnp.bfloat16)
        leave[k].start()
    for copy in leave:
        copy.wait()


def gather_kernel(asked, down_ref, up_ref, out_ref, rows_ref, down_buf, up_buf, flats, built, sems):
    count, down_chunks, up_chunks = down_buf.shape[0], down_buf.shape[1], up_buf.shape[1]
    across = up_chunks // 8

    def copies(t):
        tile = asked[t, 0, 0] // TILE_ROWS
        return (
            pltpu.make_async_copy(down_ref.at[tile], down_buf.at[t], sems.at[0, t]),
            pltpu.make_async_copy(up_ref.at[tile], up_buf.at[t], sems.at[1, t]),
            pltpu.make_async_copy(built.at[t], out_ref.at[t], sems.at[2, t]),
        )

    for t in range(count):
        down, up, _ = copies(t)
        down.start()
        up.start()
        rows_ref[t] = asked[t, 0, 0]

    def one(t, flat):
        down, up, leave = copies(t)
        up.wait()
        for j in range(up_chunks):
            place = down_chunks + (j % across) * 8 + j // across
            flat[place * 8:place * 8 + 8, :] = up_buf[t, j].astype(jnp.float32)
        down.wait()
        for j in range(down_chunks):
            flat[j * 8:j * 8 + 8, :] = down_buf[t, j].astype(jnp.float32)
        sub = asked[t, 0, 0] % TILE_ROWS
        built[t] = flat[pl.ds(sub, down_chunks + up_chunks, stride=8), :].astype(jnp.bfloat16)
        leave.start()

    def two(i, carry):
        for u in range(2):
            one(2 * i + u, flats.at[u])
        return carry

    lax.fori_loop(0, count // 2, two, 0)
    for t in range(count):
        copies(t)[2].wait()


def zero_kernel(after_ref, down_ref, up_ref, done_ref, zeros, sems):
    del after_ref
    done_ref[0] = 0
    zeros[...] = jnp.zeros_like(zeros)
    part = zeros.shape[0]
    copies = []
    for ref, sem in ((down_ref, sems.at[0]), (up_ref, sems.at[1])):
        for g in range(ref.shape[0]):
            for c in range(ref.shape[1] // part):
                copies.append(pltpu.make_async_copy(zeros, ref.at[g, pl.ds(c * part, part)], sem))
    for c in copies:
        c.start()
    for c in copies:
        c.wait()


def adapter_kernel(count, down_chunks, xs_ref, g_ref, pieces, _, out_ref, lifted_ref, up_panel):
    rows = g_ref.shape[0]
    across = g_ref.shape[1] // LANES
    total = jnp.zeros((2 * rows, LANES), jnp.float32)
    for t in range(count):
        total += dot(xs_ref[t], pieces[t, :down_chunks])
        for c in range(across):
            block = pieces[t, down_chunks + 8 * c:down_chunks + 8 * c + 8, :].astype(jnp.float32)
            up_panel[8 * t:8 * t + 8, c * LANES:(c + 1) * LANES] = block
            up_panel[R + 8 * t:R + 8 * t + 8, c * LANES:(c + 1) * LANES] = block
    panel = up_panel[...].astype(jnp.bfloat16)
    left = lax.broadcasted_iota(jnp.int32, (rows, LANES), 1) < R
    inner = total[:rows] + pltpu.roll(total[rows:], R, 1)
    inner = jnp.where(left, inner, 0.0).astype(jnp.bfloat16)
    g = g_ref[...]
    lifted_ref[...] = adapter_scale * dot(inner, panel)
    inner_grad = adapter_scale * dot_t(g, panel)
    diagonal = jnp.concatenate(
        [jnp.where(left, inner_grad, 0.0), jnp.where(left, 0.0, inner_grad)], axis=0
    ).astype(jnp.bfloat16)
    up_term = adapter_scale * t_dot(inner, g)
    for t in range(count):
        out_ref[t, :down_chunks] = t_dot(xs_ref[t], diagonal).astype(jnp.bfloat16)
        up_part = jnp.concatenate(
            [up_term[8 * t:8 * t + 8, c * LANES:(c + 1) * LANES] for c in range(across)], axis=0
        )
        out_ref[t, down_chunks:] = up_part.astype(jnp.bfloat16)


def scatter_kernel(count, down_chunks, up_chunks, rows_here, rows_core, *rest):
    sources, (down_out, up_out) = rest[:2], rest[4:6]
    pieces, down_sum, up_sum, ordered, arrived, sem = rest[6:]
    half = count // 2
    owned_rows = down_out.shape[0] * 8
    first_row = lax.axis_index("dp") * owned_rows
    across = up_chunks // 8
    rows = [(rows_here if b < half else rows_core)[b % half] - first_row for b in range(count)]
    arriving = [pltpu.make_async_copy(sources[b // half].at[b % half], pieces.at[b], arrived.at[b]) for b in range(count)]
    owned = [(row >= 0) & (row < owned_rows) for row in rows]
    for b in range(count):
        @pl.when(owned[b])
        def _():
            arriving[b].start()

    slots, final = [], []
    for b in range(count):
        slot, last = jnp.int32(b), jnp.bool_(True)
        for e in range(b - 1, -1, -1):
            slot = jnp.where(rows[e] == rows[b], e, slot)
        for e in range(b + 1, count):
            last = last & (rows[e] != rows[b])
        slots.append(slot)
        final.append(last)

    def copies(b):
        return (
            pltpu.make_async_copy(down_sum.at[slots[b]], down_out.at[rows[b] // 8, :, rows[b] % 8, 0], sem),
            pltpu.make_async_copy(up_sum.at[slots[b]], up_out.at[rows[b] // 8, :, rows[b] % 8, 0], sem),
        )

    for b in range(count):
        @pl.when(owned[b])
        def _():
            arriving[b].wait()
            slot = slots[b]
            down = pieces[b, :down_chunks].astype(jnp.float32)
            for c in range(across):
                ordered[pl.ds(c, 8, stride=across), :] = pieces[
                    b, down_chunks + 8 * c:down_chunks + 8 * c + 8
                ].astype(jnp.float32)
            up = ordered[...]

            @pl.when(slot == b)
            def _():
                down_sum[b] = down
                up_sum[b] = up

            @pl.when(slot != b)
            def _():
                down_sum[slot] += down
                up_sum[slot] += up

            @pl.when(final[b])
            def _():
                for copy in copies(b):
                    copy.start()

    for b in range(count):
        @pl.when(owned[b] & final[b])
        def _():
            for copy in copies(b):
                copy.wait()


def base_kernel(*refs):
    whole, halves, w_from, out_refs = refs[:2], refs[2:6], refs[6:-8], refs[-7:-3]
    x_buf, w_buf, sems = refs[-3:]
    outer, rows, depth = whole[0].shape
    width, each = w_from[0].shape[1], outer // 2
    z = lax.axis_index("tensor") // 2
    inside = (z == 1) | (z == 2)
    order = [z, z ^ 1, jnp.where(z < 2, 2, 1), jnp.where(z < 2, 3, 0)]
    pieces = len(w_from) // 2

    def fetch(k, begin):
        columns = pl.ds(k * depth, depth)

        def move(source, place, sem):
            copy = pltpu.make_async_copy(source, place, sem)
            copy.start() if begin else copy.wait()

        for b, ref in enumerate(whole):
            move(ref.at[order[k]], x_buf.at[pl.ds(b * rows, rows), columns], sems.at[k, b])
            for h in range(2):
                @pl.when(order[k] // each == h)
                def _():
                    place = x_buf.at[pl.ds((2 + b) * rows, rows), columns]
                    move(halves[2 * b + h].at[order[k] % each], place, sems.at[k, 2 + b])
        for h in range(2):
            place, sem = w_buf.at[columns, pl.ds(h * width, width)], sems.at[k, 4 + h]
            if k < 2:
                move(w_from[h * pieces + k], place, sem)
                continue

            @pl.when(inside)
            def _():
                move(w_from[h * pieces + 2 * k - 2], place, sem)

            @pl.when(jnp.logical_not(inside))
            def _():
                move(w_from[h * pieces + 2 * k - 1], place, sem)

    for k in range(outer):
        fetch(k, True)
    total = 0.0
    for first in range(0, outer, each):
        for k in range(first, first + each):
            fetch(k, False)
        columns = slice(first * depth, (first + each) * depth)
        total += dot(x_buf[:, columns], w_buf[columns, :])
    for b, ref in enumerate(out_refs):
        ref[...] = total[b * rows:(b + 1) * rows].astype(ref.dtype)


def fast_body(tokens, cotangent, frozen_value, down_store, up_store, block_adapter, adapter_slot):
    group, parts = lax.axis_size("tensor"), lax.axis_size("parts")
    outer = group // 2
    token_rows = tokens.shape[0]
    slice_width = D // group
    down_chunks = down_store.shape[1] // LANES
    up_chunks = up_store.shape[1] // LANES
    me, part, core = lax.axis_index("tensor"), lax.axis_index("parts"), lax.axis_index("dp")
    z = me // 2

    def exchange(value, s):
        return lax.ppermute(value, "tensor", [(t, t ^ s) for t in range(group)])

    def other_core(value):
        return lax.ppermute(value, "dp", [(0, 1), (1, 0)])

    def other_part(value):
        return lax.ppermute(value, "parts", [(a, parts - 1 - a) for a in range(parts)])

    row = pl.pallas_call(
        row_kernel, out_shape=jax.ShapeDtypeStruct((group, 1, LANES), jnp.int32),
        in_specs=[SMEM, SMEM], out_specs=VMEM, name="own_row",
    )(block_adapter, adapter_slot)
    asked = lax.all_to_all(row, "tensor", 0, 0)
    split_from, half_from, row = lax.optimization_barrier((tokens, frozen_value, row))

    width = frozen_value.shape[1] // parts
    half = lax.dynamic_slice_in_dim(half_from, part * width, width, axis=1)
    block = jax.ShapeDtypeStruct((outer, token_rows, slice_width), jnp.bfloat16)
    token = jax.ShapeDtypeStruct((1,), jnp.int32)
    some = jax.ShapeDtypeStruct((outer // 2, token_rows, slice_width), jnp.bfloat16)
    x_mine, *x_theirs = pl.pallas_call(
        split_kernel, out_shape=(block, some, some), in_specs=[VMEM], out_specs=[VMEM] * 3,
        name="split_tokens", compiler_params=LIMIT,
    )(split_from)
    x_far = [exchange(x_theirs[0], 1)]
    y_mine = other_part(x_mine)
    xs = pl.pallas_call(
        interleave_kernel,
        out_shape=jax.ShapeDtypeStruct((group, 2 * token_rows, slice_width // 2), jnp.bfloat16),
        in_specs=[VMEM], out_specs=ANY, name="pair_columns", compiler_params=WIDE,
        scratch_shapes=[
            pltpu.VMEM((group, 2 * token_rows, slice_width // 2), jnp.bfloat16),
            pltpu.SemaphoreType.DMA((group,)),
        ],
        cost_estimate=cost(read=128 << 20),
    )(split_from)
    middle = [(t, t ^ 6) for t in range(group) if t // 2 in (1, 2)]
    ends = [(t, t ^ 2) for t in range(group) if t // 2 in (1, 2)]
    near = exchange(half, 2)
    over = lax.ppermute(half, "tensor", middle)
    half_core = other_core(half)
    near, over, asked, x_theirs, xs, half_core = lax.optimization_barrier(
        (near, over, asked, x_theirs, xs, half_core)
    )
    near_core = other_core(near)
    x_far.append(exchange(x_theirs[1], 1))
    over_near = lax.ppermute(near, "tensor", middle)
    passed = lax.ppermute(over, "tensor", ends)
    pieces = jax.ShapeDtypeStruct((group, down_chunks + up_chunks, LANES), jnp.bfloat16)
    def tiles(store):
        view = store.reshape(store.shape[0] // TILE_ROWS, TILE_ROWS, store.shape[1] // LANES, LANES)
        return view.transpose(0, 2, 1, 3)

    sent, rows = pl.pallas_call(
        gather_kernel,
        out_shape=(pieces, jax.ShapeDtypeStruct((group,), jnp.int32)),
        in_specs=[SMEM, ANY, ANY],
        out_specs=(ANY, SMEM),
        scratch_shapes=[
            pltpu.VMEM((group, down_chunks, TILE_ROWS, LANES), jnp.bfloat16),
            pltpu.VMEM((group, up_chunks, TILE_ROWS, LANES), jnp.bfloat16),
            pltpu.VMEM((2, (down_chunks + up_chunks) * 8, LANES), jnp.float32),
            pltpu.VMEM(pieces.shape, jnp.bfloat16),
            pltpu.SemaphoreType.DMA((3, group)),
        ],
        compiler_params=WIDE,
        cost_estimate=cost(read=40 << 20),
        name="pick_panels",
    )(asked, tiles(down_store), tiles(up_store))
    sent, rows, x_far, y_mine, near_core, over, over_near, passed = lax.optimization_barrier(
        (sent, rows, x_far, y_mine, near_core, over, over_near, passed)
    )
    panels = lax.all_to_all(sent, "tensor", 0, 0)
    rows_core = other_core(rows)
    y_far = [other_part(piece) for piece in x_far]
    passed_near = lax.ppermute(over_near, "tensor", ends)
    middle_core = [other_core(w) for w in (over, passed)]

    owned_groups = ADAPTERS // lax.axis_size("dp") // 8
    down_shape = jax.ShapeDtypeStruct((owned_groups, down_chunks, 8, 1, LANES), jnp.float32)
    up_shape = jax.ShapeDtypeStruct((owned_groups, up_chunks, 8, 1, LANES), jnp.float32)
    down_zero, up_zero, cleared = pl.pallas_call(
        zero_kernel, out_shape=(down_shape, up_shape, token),
        in_specs=[SMEM], out_specs=(ANY, ANY, SMEM),
        scratch_shapes=[pltpu.VMEM((up_chunks, 8, 1, LANES), jnp.float32), pltpu.SemaphoreType.DMA((2,))],
        compiler_params=LIMIT, cost_estimate=cost(read=28 << 20), name="clear_rows",
    )(rows)
    panels, passed_near, y_far, middle_core = lax.optimization_barrier((panels, passed_near, y_far, middle_core))

    terms, lifted = pl.pallas_call(
        functools.partial(adapter_kernel, group, down_chunks),
        out_shape=(pieces, jax.ShapeDtypeStruct((token_rows, VALUE_OUTPUTS), jnp.float32)),
        in_specs=[VMEM] * 3 + [SMEM],
        out_specs=(VMEM, VMEM),
        scratch_shapes=[pltpu.VMEM((2 * R, VALUE_OUTPUTS), jnp.float32)],
        compiler_params=LIMIT,
        cost_estimate=cost(flops=3 << 30, read=8 << 20),
        name="adapter",
    )(xs, cotangent, panels, cleared)
    _, over_near, passed_near = lax.optimization_barrier((terms, over_near, passed_near))
    quarters = [half, near, over, passed, over_near, passed_near, half_core, near_core]
    quarters += middle_core + [other_core(w) for w in (over_near, passed_near)]
    sums = [jax.ShapeDtypeStruct((token_rows, parts * width), kind) for kind in (jnp.float32,) + (jnp.bfloat16,) * 3]
    own, to_part, to_inner, to_both = pl.pallas_call(
        base_kernel,
        out_shape=sums,
        in_specs=[ANY] * (7 + len(quarters)),
        out_specs=[VMEM] * 4,
        scratch_shapes=[
            pltpu.VMEM((4 * token_rows, outer * slice_width), jnp.bfloat16),
            pltpu.VMEM((outer * slice_width, parts * width), jnp.bfloat16),
            pltpu.SemaphoreType.DMA((outer, 6)),
        ],
        compiler_params=WIDE,
        cost_estimate=cost(flops=4 << 30, read=8 << 20),
        name="frozen_part",
    )(x_mine, y_mine, *x_far, *y_far, *quarters, terms)
    opposite = [(a * group + t, (parts - 1 - a) * group + (t ^ 1)) for a in range(parts) for t in range(group)]
    back = lax.all_to_all(terms, "tensor", 0, 0)
    arrived = (exchange(to_inner, 1), other_part(to_part), lax.ppermute(to_both, ("parts", "tensor"), opposite))
    back, arrived = lax.optimization_barrier((back, arrived))
    back_core = other_core(back)

    grad_down, grad_up = pl.pallas_call(
        functools.partial(scatter_kernel, 2 * group, down_chunks, up_chunks),
        out_shape=(down_shape, up_shape),
        in_specs=[SMEM] * 2 + [ANY] * 4,
        out_specs=(ANY, ANY),
        input_output_aliases={4: 0, 5: 1},
        scratch_shapes=[
            pltpu.VMEM((2 * group,) + pieces.shape[1:], jnp.bfloat16),
            pltpu.VMEM((2 * group, down_chunks, LANES), jnp.float32),
            pltpu.VMEM((2 * group, up_chunks, LANES), jnp.float32),
            pltpu.VMEM((up_chunks, LANES), jnp.float32),
            pltpu.SemaphoreType.DMA((2 * group,)),
            pltpu.SemaphoreType.DMA(()),
        ],
        compiler_params=LIMIT,
        cost_estimate=cost(read=16 << 20),
        name="place_rows",
    )(rows, rows_core, back, back_core, down_zero, up_zero)
    grad_down = grad_down.reshape(owned_groups, down_chunks, 8, LANES).transpose(0, 2, 1, 3)
    grad_up = grad_up.reshape(owned_groups, up_chunks, 8, LANES).transpose(0, 2, 1, 3)

    arrived = [a.astype(jnp.float32) for a in arrived]
    kept, got = own + arrived[0], arrived[1] + arrived[2]
    quarters = [[c[:, :width], c[:, width:]] for c in (kept, got)]

    def pick_quarter(c, a):
        first = quarters[a][0] if c == 0 else quarters[a][1]
        second = quarters[a][1] if c == 0 else quarters[a][0]
        return jnp.where(core == 0, first, second)

    def columns_of(c):
        low, high = pick_quarter(c, 0), pick_quarter(c, 1)
        return jnp.where(part == 0, low, high), jnp.where(part == 0, high, low)

    frozen_output = jnp.concatenate(columns_of(0) + columns_of(1), axis=1)
    mixed = (frozen_output + lifted).astype(jnp.bfloat16)
    return mixed, grad_down.reshape(owned_groups * 8, -1), grad_up.reshape(owned_groups * 8, -1)


def fits(mesh):
    group, cores, parts = mesh.shape["tensor"], mesh.shape["dp"], mesh.shape["parts"]
    return cores == 2 and parts == 2 and group <= 8 and group & (group - 1) == 0 and R == 8 * group


def body(mesh, tokens, *rest):
    block_adapter = rest[4]
    one_block = block_adapter.shape[0] == 1
    return (fast_body if fits(mesh) and one_block else plain_body)(tokens, *rest)


def solution(mesh):
    placed = (
        P(("parts", "dp", "tensor"), None),
        P(("parts", "dp", "tensor"), None),
        P("tensor", "dp"),
        P("parts", "tensor"),
        P("parts", "tensor"),
        P(("parts", "dp", "tensor")),
        P("parts"),
    )
    return jax.shard_map(
        functools.partial(body, mesh),
        mesh=mesh,
        in_specs=placed,
        out_specs=(
            P(("parts", "dp", "tensor"), None),
            P(("parts", "dp"), "tensor"),
            P(("parts", "dp"), "tensor"),
        ),
        check_vma=False,
    )
```

```python
import functools

import jax
import jax.numpy as jnp
from jax import lax
from jax.experimental import pallas as pl
from jax.experimental.pallas import tpu as pltpu
from jax.sharding import PartitionSpec as P

D = 5120
VALUE_OUTPUTS = 1024
R = 64
ADAPTERS = 256
LANES = 128
TILE_ROWS = 8

adapter_scale = 2.0
VMEM = pl.BlockSpec(memory_space=pltpu.VMEM)
SMEM = pl.BlockSpec(memory_space=pltpu.SMEM)
ANY = pl.BlockSpec(memory_space=pl.ANY)
LIMIT = pltpu.CompilerParams(vmem_limit_bytes=16 * 1024 * 1024)
WIDE = pltpu.CompilerParams(vmem_limit_bytes=60 * 1024 * 1024)


def cost(flops=0, read=0):
    return pl.CostEstimate(flops=flops, bytes_accessed=read, transcendentals=0)


def dot(a, b):
    return jnp.dot(a, b, preferred_element_type=jnp.float32)


def dot_t(a, b):
    return lax.dot_general(a, b, (((1,), (1,)), ((), ())), preferred_element_type=jnp.float32)


def t_dot(a, b):
    return lax.dot_general(a, b, (((0,), (0,)), ((), ())), preferred_element_type=jnp.float32)


def fold_rows(left, piece):
    return jnp.dot(left, piece, preferred_element_type=jnp.float32)


def store_rows(requests, adapter_slot):
    table = jnp.arange(adapter_slot.shape[0], dtype=jnp.int32)
    return jnp.sum(jnp.where(requests[:, None] == table[None, :], adapter_slot[None, :], 0), axis=1)


def plain_body(tokens, cotangent, frozen_value, down_store, up_store, block_adapter, adapter_slot):
    token_rows = tokens.shape[0]
    blocks_here = block_adapter.shape[0]
    block_rows = token_rows // blocks_here
    group = lax.axis_size("tensor")
    columns = lax.all_gather(frozen_value, "dp", axis=1, tiled=True)
    frozen_output = fold_rows(tokens, lax.all_gather(columns, "tensor", axis=0, tiled=True))
    requests = lax.all_gather(block_adapter, "tensor", axis=0, tiled=True)
    stored = store_rows(requests, adapter_slot)
    order = stored.reshape(group, blocks_here).T.reshape(-1)
    down_send = jnp.take(down_store, order, axis=0).reshape(blocks_here, group, -1)
    up_send = jnp.take(up_store, order, axis=0).reshape(blocks_here, group, -1)
    down_got = lax.all_to_all(down_send, "tensor", split_axis=1, concat_axis=1, tiled=True)
    up_got = lax.all_to_all(up_send, "tensor", split_axis=1, concat_axis=1, tiled=True)
    down_panel = down_got.reshape(blocks_here, D, R)
    up_panel = up_got.reshape(blocks_here, R, VALUE_OUTPUTS)
    token_blocks = tokens.reshape(blocks_here, block_rows, D)
    grad_blocks = cotangent.reshape(blocks_here, block_rows, VALUE_OUTPUTS)
    down_projected = jnp.einsum(
        "jtd,jdr->jtr", token_blocks, down_panel, preferred_element_type=jnp.float32
    ).astype(jnp.bfloat16)
    up_projected = jnp.einsum(
        "jtr,jrk->jtk", down_projected, up_panel, preferred_element_type=jnp.float32
    )
    mixed = (
        frozen_output + adapter_scale * up_projected.reshape(token_rows, VALUE_OUTPUTS)
    ).astype(jnp.bfloat16)
    down_projected_gradient = (
        adapter_scale
        * jnp.einsum("jtk,jrk->jtr", grad_blocks, up_panel, preferred_element_type=jnp.float32)
    ).astype(jnp.bfloat16)
    down_term = jnp.einsum(
        "jtd,jtr->jdr", token_blocks, down_projected_gradient, preferred_element_type=jnp.float32
    )
    up_weight_gradient = adapter_scale * jnp.einsum(
        "jtr,jtk->jrk", down_projected, grad_blocks, preferred_element_type=jnp.float32
    )
    down_back = lax.all_to_all(
        down_term.reshape(blocks_here, group, -1), "tensor", split_axis=1, concat_axis=1, tiled=True
    )
    up_back = lax.all_to_all(
        up_weight_gradient.reshape(blocks_here, group, -1), "tensor", split_axis=1, concat_axis=1, tiled=True
    )
    down_flat = down_back.reshape(blocks_here * group, -1)
    up_flat = up_back.reshape(blocks_here * group, -1)
    down_table = jax.ops.segment_sum(down_flat, order, num_segments=ADAPTERS)
    up_table = jax.ops.segment_sum(up_flat, order, num_segments=ADAPTERS)
    grad_down = lax.psum_scatter(down_table, "dp", scatter_dimension=0, tiled=True)
    grad_up = lax.psum_scatter(up_table, "dp", scatter_dimension=0, tiled=True)
    return mixed, grad_down, grad_up


def split_kernel(x_ref, mine_ref, *theirs_refs):
    inner = lax.axis_index("tensor") % 2
    outer, rows, width = mine_ref.shape
    each = outer // len(theirs_refs)
    for k in range(outer):
        own = pl.multiple_of((2 * k + inner) * width, LANES)
        other = pl.multiple_of((2 * k + 1 - inner) * width, LANES)
        mine_ref[k] = x_ref[:, pl.ds(own, width)]
        theirs_refs[k // each][k % each] = x_ref[:, pl.ds(other, width)]


def interleave_kernel(x_ref, out_ref, xs_ref, sems):
    group, rows2, half = xs_ref.shape
    leave = [pltpu.make_async_copy(xs_ref.at[k], out_ref.at[k], sems.at[k]) for k in range(group)]
    rows, width = rows2 // 2, 2 * half
    source = lax.broadcasted_iota(jnp.int32, (width, half), 0)
    target = lax.broadcasted_iota(jnp.int32, (width, half), 1)
    even = (source == 2 * target).astype(jnp.bfloat16)
    odd = (source == 2 * target + 1).astype(jnp.bfloat16)
    for k in range(group):
        x = x_ref[:, k * width:(k + 1) * width]
        xs_ref[k, :rows] = dot(x, even).astype(jnp.bfloat16)
        xs_ref[k, rows:] = dot(x, odd).astype(jnp.bfloat16)
        leave[k].start()
    for copy in leave:
        copy.wait()


def gather_kernel(asked, slot_of, down_ref, up_ref, out_ref, rows_ref, down_buf, up_buf, flats, built, sems):
    count, down_chunks, up_chunks = down_buf.shape[0], down_buf.shape[1], up_buf.shape[1]
    across = up_chunks // 8

    def copies(t):
        tile = slot_of[asked[t, 0, 0]] // TILE_ROWS
        return (
            pltpu.make_async_copy(down_ref.at[tile], down_buf.at[t], sems.at[0, t]),
            pltpu.make_async_copy(up_ref.at[tile], up_buf.at[t], sems.at[1, t]),
            pltpu.make_async_copy(built.at[t], out_ref.at[t], sems.at[2, t]),
        )

    for t in range(count):
        down, up, _ = copies(t)
        down.start()
        up.start()
        rows_ref[t] = slot_of[asked[t, 0, 0]]

    def one(t, flat):
        down, up, leave = copies(t)
        up.wait()
        for j in range(up_chunks):
            place = down_chunks + (j % across) * 8 + j // across
            flat[place * 8:place * 8 + 8, :] = up_buf[t, j].astype(jnp.float32)
        down.wait()
        for j in range(down_chunks):
            flat[j * 8:j * 8 + 8, :] = down_buf[t, j].astype(jnp.float32)
        sub = slot_of[asked[t, 0, 0]] % TILE_ROWS
        built[t] = flat[pl.ds(sub, down_chunks + up_chunks, stride=8), :].astype(jnp.bfloat16)
        leave.start()

    def two(i, carry):
        for u in range(2):
            one(2 * i + u, flats.at[u])
        return carry

    lax.fori_loop(0, count // 2, two, 0)
    for t in range(count):
        copies(t)[2].wait()


def zero_kernel(after_ref, down_ref, up_ref, done_ref, zeros, sems):
    del after_ref
    done_ref[0] = 0
    zeros[...] = jnp.zeros_like(zeros)
    part = zeros.shape[0]
    copies = []
    for ref, sem in ((down_ref, sems.at[0]), (up_ref, sems.at[1])):
        for g in range(ref.shape[0]):
            for c in range(ref.shape[1] // part):
                copies.append(pltpu.make_async_copy(zeros, ref.at[g, pl.ds(c * part, part)], sem))
    for c in copies:
        c.start()
    for c in copies:
        c.wait()


def adapter_kernel(count, down_chunks, xs_ref, g_ref, pieces, _, out_ref, lifted_ref, up_panel):
    rows = g_ref.shape[0]
    across = g_ref.shape[1] // LANES
    total = jnp.zeros((2 * rows, LANES), jnp.float32)
    for t in range(count):
        total += dot(xs_ref[t], pieces[t, :down_chunks])
        for c in range(across):
            block = pieces[t, down_chunks + 8 * c:down_chunks + 8 * c + 8, :].astype(jnp.float32)
            up_panel[8 * t:8 * t + 8, c * LANES:(c + 1) * LANES] = block
            up_panel[R + 8 * t:R + 8 * t + 8, c * LANES:(c + 1) * LANES] = block
    panel = up_panel[...].astype(jnp.bfloat16)
    left = lax.broadcasted_iota(jnp.int32, (rows, LANES), 1) < R
    inner = total[:rows] + pltpu.roll(total[rows:], R, 1)
    inner = jnp.where(left, inner, 0.0).astype(jnp.bfloat16)
    g = g_ref[...]
    lifted_ref[...] = adapter_scale * dot(inner, panel)
    inner_grad = adapter_scale * dot_t(g, panel)
    diagonal = jnp.concatenate(
        [jnp.where(left, inner_grad, 0.0), jnp.where(left, 0.0, inner_grad)], axis=0
    ).astype(jnp.bfloat16)
    up_term = adapter_scale * t_dot(inner, g)
    for t in range(count):
        out_ref[t, :down_chunks] = t_dot(xs_ref[t], diagonal).astype(jnp.bfloat16)
        up_part = jnp.concatenate(
            [up_term[8 * t:8 * t + 8, c * LANES:(c + 1) * LANES] for c in range(across)], axis=0
        )
        out_ref[t, down_chunks:] = up_part.astype(jnp.bfloat16)


def scatter_kernel(count, down_chunks, up_chunks, rows_here, rows_core, *rest):
    sources, (down_out, up_out) = rest[:2], rest[4:6]
    pieces, down_sum, up_sum, ordered, arrived, sem = rest[6:]
    half = count // 2
    owned_rows = down_out.shape[0] * 8
    first_row = lax.axis_index("dp") * owned_rows
    across = up_chunks // 8
    rows = [(rows_here if b < half else rows_core)[b % half] - first_row for b in range(count)]
    arriving = [pltpu.make_async_copy(sources[b // half].at[b % half], pieces.at[b], arrived.at[b]) for b in range(count)]
    owned = [(row >= 0) & (row < owned_rows) for row in rows]
    for b in range(count):
        @pl.when(owned[b])
        def _():
            arriving[b].start()

    slots, final = [], []
    for b in range(count):
        slot, last = jnp.int32(b), jnp.bool_(True)
        for e in range(b - 1, -1, -1):
            slot = jnp.where(rows[e] == rows[b], e, slot)
        for e in range(b + 1, count):
            last = last & (rows[e] != rows[b])
        slots.append(slot)
        final.append(last)

    def copies(b):
        return (
            pltpu.make_async_copy(down_sum.at[slots[b]], down_out.at[rows[b] // 8, :, rows[b] % 8, 0], sem),
            pltpu.make_async_copy(up_sum.at[slots[b]], up_out.at[rows[b] // 8, :, rows[b] % 8, 0], sem),
        )

    for b in range(count):
        @pl.when(owned[b])
        def _():
            arriving[b].wait()
            slot = slots[b]
            down = pieces[b, :down_chunks].astype(jnp.float32)
            for c in range(across):
                ordered[pl.ds(c, 8, stride=across), :] = pieces[
                    b, down_chunks + 8 * c:down_chunks + 8 * c + 8
                ].astype(jnp.float32)
            up = ordered[...]

            @pl.when(slot == b)
            def _():
                down_sum[b] = down
                up_sum[b] = up

            @pl.when(slot != b)
            def _():
                down_sum[slot] += down
                up_sum[slot] += up

            @pl.when(final[b])
            def _():
                for copy in copies(b):
                    copy.start()

    for b in range(count):
        @pl.when(owned[b] & final[b])
        def _():
            for copy in copies(b):
                copy.wait()


def base_kernel(*refs):
    whole, halves, w_from, out_refs = refs[:2], refs[2:6], refs[6:-8], refs[-7:-3]
    x_buf, w_buf, sems = refs[-3:]
    outer, rows, depth = whole[0].shape
    width, each = w_from[0].shape[1], outer // 2
    z = lax.axis_index("tensor") // 2
    inside = (z == 1) | (z == 2)
    order = [z, z ^ 1, jnp.where(z < 2, 2, 1), jnp.where(z < 2, 3, 0)]
    pieces = len(w_from) // 2

    def fetch(k, begin):
        columns = pl.ds(k * depth, depth)

        def move(source, place, sem):
            copy = pltpu.make_async_copy(source, place, sem)
            copy.start() if begin else copy.wait()

        for b, ref in enumerate(whole):
            move(ref.at[order[k]], x_buf.at[pl.ds(b * rows, rows), columns], sems.at[k, b])
            for h in range(2):
                @pl.when(order[k] // each == h)
                def _():
                    place = x_buf.at[pl.ds((2 + b) * rows, rows), columns]
                    move(halves[2 * b + h].at[order[k] % each], place, sems.at[k, 2 + b])
        for h in range(2):
            place, sem = w_buf.at[columns, pl.ds(h * width, width)], sems.at[k, 4 + h]
            if k < 3:
                move(w_from[h * pieces + k], place, sem)
                continue

            @pl.when(inside)
            def _():
                move(w_from[h * pieces + k], place, sem)

            @pl.when(jnp.logical_not(inside))
            def _():
                move(w_from[h * pieces + k + 1], place, sem)

    for k in range(outer):
        fetch(k, True)
    total = 0.0
    for first in range(0, outer, each):
        for k in range(first, first + each):
            fetch(k, False)
        columns = slice(first * depth, (first + each) * depth)
        total += dot(x_buf[:, columns], w_buf[columns, :])
    for b, ref in enumerate(out_refs):
        ref[...] = total[b * rows:(b + 1) * rows].astype(ref.dtype)


def fast_body(tokens, cotangent, frozen_value, down_store, up_store, block_adapter, adapter_slot):
    group, parts = lax.axis_size("tensor"), lax.axis_size("parts")
    outer = group // 2
    token_rows = tokens.shape[0]
    slice_width = D // group
    down_chunks = down_store.shape[1] // LANES
    up_chunks = up_store.shape[1] // LANES
    me, part, core = lax.axis_index("tensor"), lax.axis_index("parts"), lax.axis_index("dp")
    z = me // 2

    def exchange(value, s):
        return lax.ppermute(value, "tensor", [(t, t ^ s) for t in range(group)])

    def other_core(value):
        return lax.ppermute(value, "dp", [(0, 1), (1, 0)])

    def other_part(value):
        return lax.ppermute(value, "parts", [(a, parts - 1 - a) for a in range(parts)])

    own = jnp.broadcast_to(block_adapter, (group, 1, LANES))
    asked = lax.all_to_all(own, "tensor", 0, 0)
    split_from, half_from, own = lax.optimization_barrier((tokens, frozen_value, own))

    width = frozen_value.shape[1] // parts
    half = lax.dynamic_slice_in_dim(half_from, part * width, width, axis=1)
    block = jax.ShapeDtypeStruct((outer, token_rows, slice_width), jnp.bfloat16)
    token = jax.ShapeDtypeStruct((1,), jnp.int32)
    some = jax.ShapeDtypeStruct((outer // 2, token_rows, slice_width), jnp.bfloat16)
    x_mine, *x_theirs = pl.pallas_call(
        split_kernel, out_shape=(block, some, some), in_specs=[VMEM], out_specs=[VMEM] * 3,
        name="split_tokens", compiler_params=LIMIT,
    )(split_from)
    x_far = [exchange(x_theirs[0], 1)]
    y_mine = other_part(x_mine)
    xs = pl.pallas_call(
        interleave_kernel,
        out_shape=jax.ShapeDtypeStruct((group, 2 * token_rows, slice_width // 2), jnp.bfloat16),
        in_specs=[VMEM], out_specs=ANY, name="pair_columns", compiler_params=WIDE,
        scratch_shapes=[
            pltpu.VMEM((group, 2 * token_rows, slice_width // 2), jnp.bfloat16),
            pltpu.SemaphoreType.DMA((group,)),
        ],
        cost_estimate=cost(read=128 << 20),
    )(split_from)
    middle = [(t, t ^ 6) for t in range(group) if t // 2 in (1, 2)]
    ends = [(t, t ^ 2) for t in range(group) if t // 2 in (1, 2)]
    near = exchange(half, 2)
    over = lax.ppermute(half, "tensor", middle)
    near, over, asked, x_theirs, xs = lax.optimization_barrier((near, over, asked, x_theirs, xs))
    x_far.append(exchange(x_theirs[1], 1))
    over_near = lax.ppermute(near, "tensor", middle)
    passed = lax.ppermute(over, "tensor", ends)
    pieces = jax.ShapeDtypeStruct((group, down_chunks + up_chunks, LANES), jnp.bfloat16)
    def tiles(store):
        view = store.reshape(store.shape[0] // TILE_ROWS, TILE_ROWS, store.shape[1] // LANES, LANES)
        return view.transpose(0, 2, 1, 3)

    sent, rows = pl.pallas_call(
        gather_kernel,
        out_shape=(pieces, jax.ShapeDtypeStruct((group,), jnp.int32)),
        in_specs=[SMEM, SMEM, ANY, ANY],
        out_specs=(ANY, SMEM),
        scratch_shapes=[
            pltpu.VMEM((group, down_chunks, TILE_ROWS, LANES), jnp.bfloat16),
            pltpu.VMEM((group, up_chunks, TILE_ROWS, LANES), jnp.bfloat16),
            pltpu.VMEM((2, (down_chunks + up_chunks) * 8, LANES), jnp.float32),
            pltpu.VMEM(pieces.shape, jnp.bfloat16),
            pltpu.SemaphoreType.DMA((3, group)),
        ],
        compiler_params=WIDE,
        cost_estimate=cost(read=40 << 20),
        name="pick_panels",
    )(asked, adapter_slot, tiles(down_store), tiles(up_store))
    sent, rows, x_far, y_mine, half, near, over, over_near, passed = lax.optimization_barrier(
        (sent, rows, x_far, y_mine, half, near, over, over_near, passed)
    )
    panels = lax.all_to_all(sent, "tensor", 0, 0)
    rows_core = other_core(rows)
    y_far = [other_part(piece) for piece in x_far]
    passed_near = lax.ppermute(over_near, "tensor", ends)
    inside = (z == 1) | (z == 2)
    quarter = [half, near, jnp.where(inside, over, passed)]
    quarter_core = [other_core(w) for w in quarter]

    owned_groups = ADAPTERS // lax.axis_size("dp") // 8
    down_shape = jax.ShapeDtypeStruct((owned_groups, down_chunks, 8, 1, LANES), jnp.float32)
    up_shape = jax.ShapeDtypeStruct((owned_groups, up_chunks, 8, 1, LANES), jnp.float32)
    down_zero, up_zero, cleared = pl.pallas_call(
        zero_kernel, out_shape=(down_shape, up_shape, token),
        in_specs=[SMEM], out_specs=(ANY, ANY, SMEM),
        scratch_shapes=[pltpu.VMEM((up_chunks, 8, 1, LANES), jnp.float32), pltpu.SemaphoreType.DMA((2,))],
        compiler_params=LIMIT, cost_estimate=cost(read=28 << 20), name="clear_rows",
    )(rows)
    panels, quarter_core = lax.optimization_barrier((panels, quarter_core))

    terms, lifted = pl.pallas_call(
        functools.partial(adapter_kernel, group, down_chunks),
        out_shape=(pieces, jax.ShapeDtypeStruct((token_rows, VALUE_OUTPUTS), jnp.float32)),
        in_specs=[VMEM] * 3 + [SMEM],
        out_specs=(VMEM, VMEM),
        scratch_shapes=[pltpu.VMEM((2 * R, VALUE_OUTPUTS), jnp.float32)],
        compiler_params=LIMIT,
        cost_estimate=cost(flops=3 << 30, read=8 << 20),
        name="adapter",
    )(xs, cotangent, panels, cleared)
    _, over_near, passed_near, y_far = lax.optimization_barrier((terms, over_near, passed_near, y_far))
    last = [over_near, passed_near]
    quarters = quarter + last + quarter_core + [other_core(w) for w in last]
    sums = [jax.ShapeDtypeStruct((token_rows, parts * width), kind) for kind in (jnp.float32,) + (jnp.bfloat16,) * 3]
    kept, to_part, to_inner, to_both = pl.pallas_call(
        base_kernel,
        out_shape=sums,
        in_specs=[ANY] * (7 + len(quarters)),
        out_specs=[VMEM] * 4,
        scratch_shapes=[
            pltpu.VMEM((4 * token_rows, outer * slice_width), jnp.bfloat16),
            pltpu.VMEM((outer * slice_width, parts * width), jnp.bfloat16),
            pltpu.SemaphoreType.DMA((outer, 6)),
        ],
        compiler_params=WIDE,
        cost_estimate=cost(flops=4 << 30, read=8 << 20),
        name="frozen_part",
    )(x_mine, y_mine, *x_far, *y_far, *quarters, terms)
    opposite = [(a * group + t, (parts - 1 - a) * group + (t ^ 1)) for a in range(parts) for t in range(group)]
    back = lax.all_to_all(terms, "tensor", 0, 0)
    arrived = (exchange(to_inner, 1), other_part(to_part), lax.ppermute(to_both, ("parts", "tensor"), opposite))
    back, arrived = lax.optimization_barrier((back, arrived))
    back_core = other_core(back)

    grad_down, grad_up = pl.pallas_call(
        functools.partial(scatter_kernel, 2 * group, down_chunks, up_chunks),
        out_shape=(down_shape, up_shape),
        in_specs=[SMEM] * 2 + [ANY] * 4,
        out_specs=(ANY, ANY),
        input_output_aliases={4: 0, 5: 1},
        scratch_shapes=[
            pltpu.VMEM((2 * group,) + pieces.shape[1:], jnp.bfloat16),
            pltpu.VMEM((2 * group, down_chunks, LANES), jnp.float32),
            pltpu.VMEM((2 * group, up_chunks, LANES), jnp.float32),
            pltpu.VMEM((up_chunks, LANES), jnp.float32),
            pltpu.SemaphoreType.DMA((2 * group,)),
            pltpu.SemaphoreType.DMA(()),
        ],
        compiler_params=LIMIT,
        cost_estimate=cost(read=16 << 20),
        name="place_rows",
    )(rows, rows_core, back, back_core, down_zero, up_zero)
    grad_down = grad_down.reshape(owned_groups, down_chunks, 8, LANES).transpose(0, 2, 1, 3)
    grad_up = grad_up.reshape(owned_groups, up_chunks, 8, LANES).transpose(0, 2, 1, 3)

    arrived = [a.astype(jnp.float32) for a in arrived]
    kept, got = kept + arrived[0], arrived[1] + arrived[2]
    quarters = [[c[:, :width], c[:, width:]] for c in (kept, got)]

    def pick_quarter(c, a):
        first = quarters[a][0] if c == 0 else quarters[a][1]
        second = quarters[a][1] if c == 0 else quarters[a][0]
        return jnp.where(core == 0, first, second)

    def columns_of(c):
        low, high = pick_quarter(c, 0), pick_quarter(c, 1)
        return jnp.where(part == 0, low, high), jnp.where(part == 0, high, low)

    frozen_output = jnp.concatenate(columns_of(0) + columns_of(1), axis=1)
    mixed = (frozen_output + lifted).astype(jnp.bfloat16)
    return mixed, grad_down.reshape(owned_groups * 8, -1), grad_up.reshape(owned_groups * 8, -1)


def fits(mesh):
    group, cores, parts = mesh.shape["tensor"], mesh.shape["dp"], mesh.shape["parts"]
    return cores == 2 and parts == 2 and group <= 8 and group & (group - 1) == 0 and R == 8 * group


def body(mesh, tokens, *rest):
    block_adapter = rest[4]
    one_block = block_adapter.shape[0] == 1
    return (fast_body if fits(mesh) and one_block else plain_body)(tokens, *rest)


def solution(mesh):
    placed = (
        P(("parts", "dp", "tensor"), None),
        P(("parts", "dp", "tensor"), None),
        P("tensor", "dp"),
        P("parts", "tensor"),
        P("parts", "tensor"),
        P(("parts", "dp", "tensor")),
        P("parts"),
    )
    return jax.shard_map(
        functools.partial(body, mesh),
        mesh=mesh,
        in_specs=placed,
        out_specs=(
            P(("parts", "dp", "tensor"), None),
            P(("parts", "dp"), "tensor"),
            P(("parts", "dp"), "tensor"),
        ),
        check_vma=False,
    )
```

```python
import functools

import jax
import jax.numpy as jnp
from jax import lax
from jax.experimental import pallas as pl
from jax.experimental.pallas import tpu as pltpu
from jax.sharding import PartitionSpec as P

D = 5120
VALUE_OUTPUTS = 1024
R = 64
ADAPTERS = 256
LANES = 128
TILE_ROWS = 8

adapter_scale = 2.0
VMEM = pl.BlockSpec(memory_space=pltpu.VMEM)
SMEM = pl.BlockSpec(memory_space=pltpu.SMEM)
ANY = pl.BlockSpec(memory_space=pl.ANY)
LIMIT = pltpu.CompilerParams(vmem_limit_bytes=16 * 1024 * 1024)
WIDE = pltpu.CompilerParams(vmem_limit_bytes=60 * 1024 * 1024)


def cost(flops=0, read=0):
    return pl.CostEstimate(flops=flops, bytes_accessed=read, transcendentals=0)


def dot(a, b):
    return jnp.dot(a, b, preferred_element_type=jnp.float32)


def dot_t(a, b):
    return lax.dot_general(a, b, (((1,), (1,)), ((), ())), preferred_element_type=jnp.float32)


def t_dot(a, b):
    return lax.dot_general(a, b, (((0,), (0,)), ((), ())), preferred_element_type=jnp.float32)


def fold_rows(left, piece):
    return jnp.dot(left, piece, preferred_element_type=jnp.float32)


def store_rows(requests, adapter_slot):
    table = jnp.arange(adapter_slot.shape[0], dtype=jnp.int32)
    return jnp.sum(jnp.where(requests[:, None] == table[None, :], adapter_slot[None, :], 0), axis=1)


def plain_body(tokens, cotangent, frozen_value, down_store, up_store, block_adapter, adapter_slot):
    token_rows = tokens.shape[0]
    blocks_here = block_adapter.shape[0]
    block_rows = token_rows // blocks_here
    group = lax.axis_size("tensor")
    columns = lax.all_gather(frozen_value, "dp", axis=1, tiled=True)
    frozen_output = fold_rows(tokens, lax.all_gather(columns, "tensor", axis=0, tiled=True))
    requests = lax.all_gather(block_adapter, "tensor", axis=0, tiled=True)
    stored = store_rows(requests, adapter_slot)
    order = stored.reshape(group, blocks_here).T.reshape(-1)
    down_send = jnp.take(down_store, order, axis=0).reshape(blocks_here, group, -1)
    up_send = jnp.take(up_store, order, axis=0).reshape(blocks_here, group, -1)
    down_got = lax.all_to_all(down_send, "tensor", split_axis=1, concat_axis=1, tiled=True)
    up_got = lax.all_to_all(up_send, "tensor", split_axis=1, concat_axis=1, tiled=True)
    down_panel = down_got.reshape(blocks_here, D, R)
    up_panel = up_got.reshape(blocks_here, R, VALUE_OUTPUTS)
    token_blocks = tokens.reshape(blocks_here, block_rows, D)
    grad_blocks = cotangent.reshape(blocks_here, block_rows, VALUE_OUTPUTS)
    down_projected = jnp.einsum(
        "jtd,jdr->jtr", token_blocks, down_panel, preferred_element_type=jnp.float32
    ).astype(jnp.bfloat16)
    up_projected = jnp.einsum(
        "jtr,jrk->jtk", down_projected, up_panel, preferred_element_type=jnp.float32
    )
    mixed = (
        frozen_output + adapter_scale * up_projected.reshape(token_rows, VALUE_OUTPUTS)
    ).astype(jnp.bfloat16)
    down_projected_gradient = (
        adapter_scale
        * jnp.einsum("jtk,jrk->jtr", grad_blocks, up_panel, preferred_element_type=jnp.float32)
    ).astype(jnp.bfloat16)
    down_term = jnp.einsum(
        "jtd,jtr->jdr", token_blocks, down_projected_gradient, preferred_element_type=jnp.float32
    )
    up_weight_gradient = adapter_scale * jnp.einsum(
        "jtr,jtk->jrk", down_projected, grad_blocks, preferred_element_type=jnp.float32
    )
    down_back = lax.all_to_all(
        down_term.reshape(blocks_here, group, -1), "tensor", split_axis=1, concat_axis=1, tiled=True
    )
    up_back = lax.all_to_all(
        up_weight_gradient.reshape(blocks_here, group, -1), "tensor", split_axis=1, concat_axis=1, tiled=True
    )
    down_flat = down_back.reshape(blocks_here * group, -1)
    up_flat = up_back.reshape(blocks_here * group, -1)
    down_table = jax.ops.segment_sum(down_flat, order, num_segments=ADAPTERS)
    up_table = jax.ops.segment_sum(up_flat, order, num_segments=ADAPTERS)
    grad_down = lax.psum_scatter(down_table, "dp", scatter_dimension=0, tiled=True)
    grad_up = lax.psum_scatter(up_table, "dp", scatter_dimension=0, tiled=True)
    return mixed, grad_down, grad_up


def split_kernel(x_ref, mine_ref, *theirs_refs):
    inner = lax.axis_index("tensor") % 2
    outer, rows, width = mine_ref.shape
    each = outer // len(theirs_refs)
    for k in range(outer):
        own = pl.multiple_of((2 * k + inner) * width, LANES)
        other = pl.multiple_of((2 * k + 1 - inner) * width, LANES)
        mine_ref[k] = x_ref[:, pl.ds(own, width)]
        theirs_refs[k // each][k % each] = x_ref[:, pl.ds(other, width)]


def interleave_kernel(x_ref, out_ref, xs_ref, sems):
    group, rows2, half = xs_ref.shape
    leave = [pltpu.make_async_copy(xs_ref.at[k], out_ref.at[k], sems.at[k]) for k in range(group)]
    rows, width = rows2 // 2, 2 * half
    source = lax.broadcasted_iota(jnp.int32, (width, half), 0)
    target = lax.broadcasted_iota(jnp.int32, (width, half), 1)
    even = (source == 2 * target).astype(jnp.bfloat16)
    odd = (source == 2 * target + 1).astype(jnp.bfloat16)
    for k in range(group):
        x = x_ref[:, k * width:(k + 1) * width]
        xs_ref[k, :rows] = dot(x, even).astype(jnp.bfloat16)
        xs_ref[k, rows:] = dot(x, odd).astype(jnp.bfloat16)
        leave[k].start()
    for copy in leave:
        copy.wait()


def gather_kernel(asked, slot_of, down_ref, up_ref, out_ref, rows_ref, down_buf, up_buf, flats, built, sems):
    count, down_chunks, up_chunks = down_buf.shape[0], down_buf.shape[1], up_buf.shape[1]
    across = up_chunks // 8

    def copies(t):
        tile = slot_of[asked[t, 0, 0]] // TILE_ROWS
        return (
            pltpu.make_async_copy(down_ref.at[tile], down_buf.at[t], sems.at[0, t]),
            pltpu.make_async_copy(up_ref.at[tile], up_buf.at[t], sems.at[1, t]),
            pltpu.make_async_copy(built.at[t], out_ref.at[t], sems.at[2, t]),
        )

    for t in range(count):
        down, up, _ = copies(t)
        down.start()
        up.start()
        rows_ref[t] = slot_of[asked[t, 0, 0]]

    def one(t, flat):
        down, up, leave = copies(t)
        up.wait()
        for j in range(up_chunks):
            place = down_chunks + (j % across) * 8 + j // across
            flat[place * 8:place * 8 + 8, :] = up_buf[t, j].astype(jnp.float32)
        down.wait()
        for j in range(down_chunks):
            flat[j * 8:j * 8 + 8, :] = down_buf[t, j].astype(jnp.float32)
        sub = slot_of[asked[t, 0, 0]] % TILE_ROWS
        built[t] = flat[pl.ds(sub, down_chunks + up_chunks, stride=8), :].astype(jnp.bfloat16)
        leave.start()

    def two(i, carry):
        for u in range(2):
            one(2 * i + u, flats.at[u])
        return carry

    lax.fori_loop(0, count // 2, two, 0)
    for t in range(count):
        copies(t)[2].wait()


def zero_kernel(after_ref, down_ref, up_ref, done_ref, zeros, sems):
    del after_ref
    done_ref[0] = 0
    zeros[...] = jnp.zeros_like(zeros)
    part = zeros.shape[0]
    copies = []
    for ref, sem in ((down_ref, sems.at[0]), (up_ref, sems.at[1])):
        for g in range(ref.shape[0]):
            for c in range(ref.shape[1] // part):
                copies.append(pltpu.make_async_copy(zeros, ref.at[g, pl.ds(c * part, part)], sem))
    for c in copies:
        c.start()
    for c in copies:
        c.wait()


def adapter_kernel(count, down_chunks, xs_ref, g_ref, pieces, _, out_ref, lifted_ref, up_panel):
    rows = g_ref.shape[0]
    across = g_ref.shape[1] // LANES
    total = jnp.zeros((2 * rows, LANES), jnp.float32)
    for t in range(count):
        total += dot(xs_ref[t], pieces[t, :down_chunks])
        for c in range(across):
            block = pieces[t, down_chunks + 8 * c:down_chunks + 8 * c + 8, :].astype(jnp.float32)
            up_panel[8 * t:8 * t + 8, c * LANES:(c + 1) * LANES] = block
            up_panel[R + 8 * t:R + 8 * t + 8, c * LANES:(c + 1) * LANES] = block
    panel = up_panel[...].astype(jnp.bfloat16)
    left = lax.broadcasted_iota(jnp.int32, (rows, LANES), 1) < R
    inner = total[:rows] + pltpu.roll(total[rows:], R, 1)
    inner = jnp.where(left, inner, 0.0).astype(jnp.bfloat16)
    g = g_ref[...]
    lifted_ref[...] = adapter_scale * dot(inner, panel)
    inner_grad = adapter_scale * dot_t(g, panel)
    diagonal = jnp.concatenate(
        [jnp.where(left, inner_grad, 0.0), jnp.where(left, 0.0, inner_grad)], axis=0
    ).astype(jnp.bfloat16)
    up_term = adapter_scale * t_dot(inner, g)
    for t in range(count):
        out_ref[t, :down_chunks] = t_dot(xs_ref[t], diagonal).astype(jnp.bfloat16)
        up_part = jnp.concatenate(
            [up_term[8 * t:8 * t + 8, c * LANES:(c + 1) * LANES] for c in range(across)], axis=0
        )
        out_ref[t, down_chunks:] = up_part.astype(jnp.bfloat16)


def scatter_kernel(count, down_chunks, up_chunks, rows_here, rows_core, *rest):
    sources, (down_out, up_out) = rest[:2], rest[4:6]
    pieces, down_sum, up_sum, ordered, arrived, sem = rest[6:]
    half = count // 2
    owned_rows = down_out.shape[0] * 8
    first_row = lax.axis_index("dp") * owned_rows
    across = up_chunks // 8
    rows = [(rows_here if b < half else rows_core)[b % half] - first_row for b in range(count)]
    arriving = [pltpu.make_async_copy(sources[b // half].at[b % half], pieces.at[b], arrived.at[b]) for b in range(count)]
    owned = [(row >= 0) & (row < owned_rows) for row in rows]
    for b in range(count):
        @pl.when(owned[b])
        def _():
            arriving[b].start()

    slots, final = [], []
    for b in range(count):
        slot, last = jnp.int32(b), jnp.bool_(True)
        for e in range(b - 1, -1, -1):
            slot = jnp.where(rows[e] == rows[b], e, slot)
        for e in range(b + 1, count):
            last = last & (rows[e] != rows[b])
        slots.append(slot)
        final.append(last)

    def copies(b):
        return (
            pltpu.make_async_copy(down_sum.at[slots[b]], down_out.at[rows[b] // 8, :, rows[b] % 8, 0], sem),
            pltpu.make_async_copy(up_sum.at[slots[b]], up_out.at[rows[b] // 8, :, rows[b] % 8, 0], sem),
        )

    for b in range(count):
        @pl.when(owned[b])
        def _():
            arriving[b].wait()
            slot = slots[b]
            down = pieces[b, :down_chunks].astype(jnp.float32)
            for c in range(across):
                ordered[pl.ds(c, 8, stride=across), :] = pieces[
                    b, down_chunks + 8 * c:down_chunks + 8 * c + 8
                ].astype(jnp.float32)
            up = ordered[...]

            @pl.when(slot == b)
            def _():
                down_sum[b] = down
                up_sum[b] = up

            @pl.when(slot != b)
            def _():
                down_sum[slot] += down
                up_sum[slot] += up

            @pl.when(final[b])
            def _():
                for copy in copies(b):
                    copy.start()

    for b in range(count):
        @pl.when(owned[b] & final[b])
        def _():
            for copy in copies(b):
                copy.wait()


def base_kernel(*refs):
    whole, halves, w_from, out_refs = refs[:2], refs[2:6], refs[6:-8], refs[-7:-3]
    x_buf, w_buf, sems = refs[-3:]
    outer, rows, depth = whole[0].shape
    width, each = w_from[0].shape[1], outer // 2
    z = lax.axis_index("tensor") // 2
    inside = (z == 1) | (z == 2)
    order = [z, z ^ 1, jnp.where(z < 2, 2, 1), jnp.where(z < 2, 3, 0)]
    pieces = len(w_from) // 2

    def fetch(k, begin):
        columns = pl.ds(k * depth, depth)

        def move(source, place, sem):
            copy = pltpu.make_async_copy(source, place, sem)
            copy.start() if begin else copy.wait()

        for b, ref in enumerate(whole):
            move(ref.at[order[k]], x_buf.at[pl.ds(b * rows, rows), columns], sems.at[k, b])
            for h in range(2):
                @pl.when(order[k] // each == h)
                def _():
                    place = x_buf.at[pl.ds((2 + b) * rows, rows), columns]
                    move(halves[2 * b + h].at[order[k] % each], place, sems.at[k, 2 + b])
        for h in range(2):
            place, sem = w_buf.at[columns, pl.ds(h * width, width)], sems.at[k, 4 + h]
            if k < 3:
                move(w_from[h * pieces + k], place, sem)
                continue

            @pl.when(inside)
            def _():
                move(w_from[h * pieces + k], place, sem)

            @pl.when(jnp.logical_not(inside))
            def _():
                move(w_from[h * pieces + k + 1], place, sem)

    for k in range(outer):
        fetch(k, True)
    total = 0.0
    for first in range(0, outer, each):
        for k in range(first, first + each):
            fetch(k, False)
        columns = slice(first * depth, (first + each) * depth)
        total += dot(x_buf[:, columns], w_buf[columns, :])
    for b, ref in enumerate(out_refs):
        ref[...] = total[b * rows:(b + 1) * rows].astype(ref.dtype)


def fast_body(tokens, cotangent, frozen_value, down_store, up_store, block_adapter, adapter_slot):
    group, parts = lax.axis_size("tensor"), lax.axis_size("parts")
    outer = group // 2
    token_rows = tokens.shape[0]
    slice_width = D // group
    down_chunks = down_store.shape[1] // LANES
    up_chunks = up_store.shape[1] // LANES
    me, part, core = lax.axis_index("tensor"), lax.axis_index("parts"), lax.axis_index("dp")
    z = me // 2

    def exchange(value, s):
        return lax.ppermute(value, "tensor", [(t, t ^ s) for t in range(group)])

    def other_core(value):
        return lax.ppermute(value, "dp", [(0, 1), (1, 0)])

    def other_part(value):
        return lax.ppermute(value, "parts", [(a, parts - 1 - a) for a in range(parts)])

    own = jnp.broadcast_to(block_adapter, (group, 1, LANES))
    asked = lax.all_to_all(own, "tensor", 0, 0)
    split_from, half_from, own = lax.optimization_barrier((tokens, frozen_value, own))

    width = frozen_value.shape[1] // parts
    half = lax.dynamic_slice_in_dim(half_from, part * width, width, axis=1)
    block = jax.ShapeDtypeStruct((outer, token_rows, slice_width), jnp.bfloat16)
    token = jax.ShapeDtypeStruct((1,), jnp.int32)
    some = jax.ShapeDtypeStruct((outer // 2, token_rows, slice_width), jnp.bfloat16)
    x_mine, *x_theirs = pl.pallas_call(
        split_kernel, out_shape=(block, some, some), in_specs=[VMEM], out_specs=[VMEM] * 3,
        name="split_tokens", compiler_params=LIMIT,
    )(split_from)
    x_far = [exchange(x_theirs[0], 1)]
    y_mine = other_part(x_mine)
    xs = pl.pallas_call(
        interleave_kernel,
        out_shape=jax.ShapeDtypeStruct((group, 2 * token_rows, slice_width // 2), jnp.bfloat16),
        in_specs=[VMEM], out_specs=ANY, name="pair_columns", compiler_params=WIDE,
        scratch_shapes=[
            pltpu.VMEM((group, 2 * token_rows, slice_width // 2), jnp.bfloat16),
            pltpu.SemaphoreType.DMA((group,)),
        ],
        cost_estimate=cost(read=128 << 20),
    )(split_from)
    middle = [(t, t ^ 6) for t in range(group) if t // 2 in (1, 2)]
    ends = [(t, t ^ 2) for t in range(group) if t // 2 in (1, 2)]
    near = exchange(half, 2)
    over = lax.ppermute(half, "tensor", middle)
    near, over, asked, x_theirs, xs = lax.optimization_barrier((near, over, asked, x_theirs, xs))
    x_far.append(exchange(x_theirs[1], 1))
    over_near = lax.ppermute(near, "tensor", middle)
    passed = lax.ppermute(over, "tensor", ends)
    pieces = jax.ShapeDtypeStruct((group, down_chunks + up_chunks, LANES), jnp.bfloat16)
    def tiles(store):
        view = store.reshape(store.shape[0] // TILE_ROWS, TILE_ROWS, store.shape[1] // LANES, LANES)
        return view.transpose(0, 2, 1, 3)

    sent, rows = pl.pallas_call(
        gather_kernel,
        out_shape=(pieces, jax.ShapeDtypeStruct((group,), jnp.int32)),
        in_specs=[SMEM, SMEM, ANY, ANY],
        out_specs=(ANY, SMEM),
        scratch_shapes=[
            pltpu.VMEM((group, down_chunks, TILE_ROWS, LANES), jnp.bfloat16),
            pltpu.VMEM((group, up_chunks, TILE_ROWS, LANES), jnp.bfloat16),
            pltpu.VMEM((2, (down_chunks + up_chunks) * 8, LANES), jnp.float32),
            pltpu.VMEM(pieces.shape, jnp.bfloat16),
            pltpu.SemaphoreType.DMA((3, group)),
        ],
        compiler_params=WIDE,
        cost_estimate=cost(read=40 << 20),
        name="pick_panels",
    )(asked, adapter_slot, tiles(down_store), tiles(up_store))
    sent, rows, x_far, y_mine, half, near, over, over_near, passed = lax.optimization_barrier(
        (sent, rows, x_far, y_mine, half, near, over, over_near, passed)
    )
    panels = lax.all_to_all(sent, "tensor", 0, 0)
    rows_core = other_core(rows)
    y_far = [other_part(piece) for piece in x_far]
    passed_near = lax.ppermute(over_near, "tensor", ends)
    owned_groups = ADAPTERS // lax.axis_size("dp") // 8
    down_shape = jax.ShapeDtypeStruct((owned_groups, down_chunks, 8, 1, LANES), jnp.float32)
    up_shape = jax.ShapeDtypeStruct((owned_groups, up_chunks, 8, 1, LANES), jnp.float32)
    down_zero, up_zero, cleared = pl.pallas_call(
        zero_kernel, out_shape=(down_shape, up_shape, token),
        in_specs=[SMEM], out_specs=(ANY, ANY, SMEM),
        scratch_shapes=[pltpu.VMEM((up_chunks, 8, 1, LANES), jnp.float32), pltpu.SemaphoreType.DMA((2,))],
        compiler_params=LIMIT, cost_estimate=cost(read=28 << 20), name="clear_rows",
    )(rows)
    cleared, half, near, over, passed = lax.optimization_barrier((cleared, half, near, over, passed))
    inside = (z == 1) | (z == 2)
    quarter = [half, near, jnp.where(inside, over, passed)]
    quarter_core = [other_core(w) for w in quarter]
    panels, quarter_core, passed_near, y_far = lax.optimization_barrier((panels, quarter_core, passed_near, y_far))

    terms, lifted = pl.pallas_call(
        functools.partial(adapter_kernel, group, down_chunks),
        out_shape=(pieces, jax.ShapeDtypeStruct((token_rows, VALUE_OUTPUTS), jnp.float32)),
        in_specs=[VMEM] * 3 + [SMEM],
        out_specs=(VMEM, VMEM),
        scratch_shapes=[pltpu.VMEM((2 * R, VALUE_OUTPUTS), jnp.float32)],
        compiler_params=LIMIT,
        cost_estimate=cost(flops=3 << 30, read=8 << 20),
        name="adapter",
    )(xs, cotangent, panels, cleared)
    _, over_near, passed_near = lax.optimization_barrier((terms, over_near, passed_near))
    last = [over_near, passed_near]
    quarters = quarter + last + quarter_core + [other_core(w) for w in last]
    sums = [jax.ShapeDtypeStruct((token_rows, parts * width), kind) for kind in (jnp.float32,) + (jnp.bfloat16,) * 3]
    kept, to_part, to_inner, to_both = pl.pallas_call(
        base_kernel,
        out_shape=sums,
        in_specs=[ANY] * (7 + len(quarters)),
        out_specs=[VMEM] * 4,
        scratch_shapes=[
            pltpu.VMEM((4 * token_rows, outer * slice_width), jnp.bfloat16),
            pltpu.VMEM((outer * slice_width, parts * width), jnp.bfloat16),
            pltpu.SemaphoreType.DMA((outer, 6)),
        ],
        compiler_params=WIDE,
        cost_estimate=cost(flops=4 << 30, read=8 << 20),
        name="frozen_part",
    )(x_mine, y_mine, *x_far, *y_far, *quarters, terms)
    opposite = [(a * group + t, (parts - 1 - a) * group + (t ^ 1)) for a in range(parts) for t in range(group)]
    back = lax.all_to_all(terms, "tensor", 0, 0)
    arrived = (exchange(to_inner, 1), other_part(to_part), lax.ppermute(to_both, ("parts", "tensor"), opposite))
    back, arrived = lax.optimization_barrier((back, arrived))
    back_core = other_core(back)

    grad_down, grad_up = pl.pallas_call(
        functools.partial(scatter_kernel, 2 * group, down_chunks, up_chunks),
        out_shape=(down_shape, up_shape),
        in_specs=[SMEM] * 2 + [ANY] * 4,
        out_specs=(ANY, ANY),
        input_output_aliases={4: 0, 5: 1},
        scratch_shapes=[
            pltpu.VMEM((2 * group,) + pieces.shape[1:], jnp.bfloat16),
            pltpu.VMEM((2 * group, down_chunks, LANES), jnp.float32),
            pltpu.VMEM((2 * group, up_chunks, LANES), jnp.float32),
            pltpu.VMEM((up_chunks, LANES), jnp.float32),
            pltpu.SemaphoreType.DMA((2 * group,)),
            pltpu.SemaphoreType.DMA(()),
        ],
        compiler_params=LIMIT,
        cost_estimate=cost(read=16 << 20),
        name="place_rows",
    )(rows, rows_core, back, back_core, down_zero, up_zero)
    grad_down = grad_down.reshape(owned_groups, down_chunks, 8, LANES).transpose(0, 2, 1, 3)
    grad_up = grad_up.reshape(owned_groups, up_chunks, 8, LANES).transpose(0, 2, 1, 3)

    arrived = [a.astype(jnp.float32) for a in arrived]
    kept, got = kept + arrived[0], arrived[1] + arrived[2]
    quarters = [[c[:, :width], c[:, width:]] for c in (kept, got)]

    def pick_quarter(c, a):
        first = quarters[a][0] if c == 0 else quarters[a][1]
        second = quarters[a][1] if c == 0 else quarters[a][0]
        return jnp.where(core == 0, first, second)

    def columns_of(c):
        low, high = pick_quarter(c, 0), pick_quarter(c, 1)
        return jnp.where(part == 0, low, high), jnp.where(part == 0, high, low)

    frozen_output = jnp.concatenate(columns_of(0) + columns_of(1), axis=1)
    mixed = (frozen_output + lifted).astype(jnp.bfloat16)
    return mixed, grad_down.reshape(owned_groups * 8, -1), grad_up.reshape(owned_groups * 8, -1)


def fits(mesh):
    group, cores, parts = mesh.shape["tensor"], mesh.shape["dp"], mesh.shape["parts"]
    return cores == 2 and parts == 2 and group <= 8 and group & (group - 1) == 0 and R == 8 * group


def body(mesh, tokens, *rest):
    block_adapter = rest[4]
    one_block = block_adapter.shape[0] == 1
    return (fast_body if fits(mesh) and one_block else plain_body)(tokens, *rest)


def solution(mesh):
    placed = (
        P(("parts", "dp", "tensor"), None),
        P(("parts", "dp", "tensor"), None),
        P("tensor", "dp"),
        P("parts", "tensor"),
        P("parts", "tensor"),
        P(("parts", "dp", "tensor")),
        P("parts"),
    )
    return jax.shard_map(
        functools.partial(body, mesh),
        mesh=mesh,
        in_specs=placed,
        out_specs=(
            P(("parts", "dp", "tensor"), None),
            P(("parts", "dp"), "tensor"),
            P(("parts", "dp"), "tensor"),
        ),
        check_vma=False,
    )
```

```python
import functools

import jax
import jax.numpy as jnp
from jax import lax
from jax.experimental import pallas as pl
from jax.experimental.pallas import tpu as pltpu
from jax.sharding import PartitionSpec as P

D = 5120
VALUE_OUTPUTS = 1024
R = 64
ADAPTERS = 256
LANES = 128
TILE_ROWS = 8

adapter_scale = 2.0
VMEM = pl.BlockSpec(memory_space=pltpu.VMEM)
SMEM = pl.BlockSpec(memory_space=pltpu.SMEM)
ANY = pl.BlockSpec(memory_space=pl.ANY)
LIMIT = pltpu.CompilerParams(vmem_limit_bytes=16 * 1024 * 1024)
WIDE = pltpu.CompilerParams(vmem_limit_bytes=60 * 1024 * 1024)


def cost(flops=0, read=0):
    return pl.CostEstimate(flops=flops, bytes_accessed=read, transcendentals=0)


def dot(a, b):
    return jnp.dot(a, b, preferred_element_type=jnp.float32)


def dot_t(a, b):
    return lax.dot_general(a, b, (((1,), (1,)), ((), ())), preferred_element_type=jnp.float32)


def t_dot(a, b):
    return lax.dot_general(a, b, (((0,), (0,)), ((), ())), preferred_element_type=jnp.float32)


def fold_rows(left, piece):
    return jnp.dot(left, piece, preferred_element_type=jnp.float32)


def store_rows(requests, adapter_slot):
    table = jnp.arange(adapter_slot.shape[0], dtype=jnp.int32)
    return jnp.sum(jnp.where(requests[:, None] == table[None, :], adapter_slot[None, :], 0), axis=1)


def plain_body(tokens, cotangent, frozen_value, down_store, up_store, block_adapter, adapter_slot):
    token_rows = tokens.shape[0]
    blocks_here = block_adapter.shape[0]
    block_rows = token_rows // blocks_here
    group = lax.axis_size("tensor")
    columns = lax.all_gather(frozen_value, "dp", axis=1, tiled=True)
    frozen_output = fold_rows(tokens, lax.all_gather(columns, "tensor", axis=0, tiled=True))
    requests = lax.all_gather(block_adapter, "tensor", axis=0, tiled=True)
    stored = store_rows(requests, adapter_slot)
    order = stored.reshape(group, blocks_here).T.reshape(-1)
    down_send = jnp.take(down_store, order, axis=0).reshape(blocks_here, group, -1)
    up_send = jnp.take(up_store, order, axis=0).reshape(blocks_here, group, -1)
    down_got = lax.all_to_all(down_send, "tensor", split_axis=1, concat_axis=1, tiled=True)
    up_got = lax.all_to_all(up_send, "tensor", split_axis=1, concat_axis=1, tiled=True)
    down_panel = down_got.reshape(blocks_here, D, R)
    up_panel = up_got.reshape(blocks_here, R, VALUE_OUTPUTS)
    token_blocks = tokens.reshape(blocks_here, block_rows, D)
    grad_blocks = cotangent.reshape(blocks_here, block_rows, VALUE_OUTPUTS)
    down_projected = jnp.einsum(
        "jtd,jdr->jtr", token_blocks, down_panel, preferred_element_type=jnp.float32
    ).astype(jnp.bfloat16)
    up_projected = jnp.einsum(
        "jtr,jrk->jtk", down_projected, up_panel, preferred_element_type=jnp.float32
    )
    mixed = (
        frozen_output + adapter_scale * up_projected.reshape(token_rows, VALUE_OUTPUTS)
    ).astype(jnp.bfloat16)
    down_projected_gradient = (
        adapter_scale
        * jnp.einsum("jtk,jrk->jtr", grad_blocks, up_panel, preferred_element_type=jnp.float32)
    ).astype(jnp.bfloat16)
    down_term = jnp.einsum(
        "jtd,jtr->jdr", token_blocks, down_projected_gradient, preferred_element_type=jnp.float32
    )
    up_weight_gradient = adapter_scale * jnp.einsum(
        "jtr,jtk->jrk", down_projected, grad_blocks, preferred_element_type=jnp.float32
    )
    down_back = lax.all_to_all(
        down_term.reshape(blocks_here, group, -1), "tensor", split_axis=1, concat_axis=1, tiled=True
    )
    up_back = lax.all_to_all(
        up_weight_gradient.reshape(blocks_here, group, -1), "tensor", split_axis=1, concat_axis=1, tiled=True
    )
    down_flat = down_back.reshape(blocks_here * group, -1)
    up_flat = up_back.reshape(blocks_here * group, -1)
    down_table = jax.ops.segment_sum(down_flat, order, num_segments=ADAPTERS)
    up_table = jax.ops.segment_sum(up_flat, order, num_segments=ADAPTERS)
    grad_down = lax.psum_scatter(down_table, "dp", scatter_dimension=0, tiled=True)
    grad_up = lax.psum_scatter(up_table, "dp", scatter_dimension=0, tiled=True)
    return mixed, grad_down, grad_up


def split_kernel(x_ref, mine_ref, *theirs_refs):
    inner = lax.axis_index("tensor") % 2
    outer, rows, width = mine_ref.shape
    each = outer // len(theirs_refs)
    for k in range(outer):
        own = pl.multiple_of((2 * k + inner) * width, LANES)
        other = pl.multiple_of((2 * k + 1 - inner) * width, LANES)
        mine_ref[k] = x_ref[:, pl.ds(own, width)]
        theirs_refs[k // each][k % each] = x_ref[:, pl.ds(other, width)]


def interleave_kernel(x_ref, out_ref, xs_ref, sems):
    group, rows2, half = xs_ref.shape
    leave = [pltpu.make_async_copy(xs_ref.at[k], out_ref.at[k], sems.at[k]) for k in range(group)]
    rows, width = rows2 // 2, 2 * half
    source = lax.broadcasted_iota(jnp.int32, (width, half), 0)
    target = lax.broadcasted_iota(jnp.int32, (width, half), 1)
    even = (source == 2 * target).astype(jnp.bfloat16)
    odd = (source == 2 * target + 1).astype(jnp.bfloat16)
    for k in range(group):
        x = x_ref[:, k * width:(k + 1) * width]
        xs_ref[k, :rows] = dot(x, even).astype(jnp.bfloat16)
        xs_ref[k, rows:] = dot(x, odd).astype(jnp.bfloat16)
        leave[k].start()
    for copy in leave:
        copy.wait()


def gather_kernel(asked, slot_of, down_ref, up_ref, out_ref, rows_ref, down_buf, up_buf, flats, built, sems):
    count, down_chunks, up_chunks = down_buf.shape[0], down_buf.shape[1], up_buf.shape[1]
    across = up_chunks // 8

    def copies(t):
        tile = slot_of[asked[t, 0, 0]] // TILE_ROWS
        return (
            pltpu.make_async_copy(down_ref.at[tile], down_buf.at[t], sems.at[0, t]),
            pltpu.make_async_copy(up_ref.at[tile], up_buf.at[t], sems.at[1, t]),
            pltpu.make_async_copy(built.at[t], out_ref.at[t], sems.at[2, t]),
        )

    for t in range(count):
        down, up, _ = copies(t)
        down.start()
        up.start()
        rows_ref[t] = slot_of[asked[t, 0, 0]]

    def one(t, flat):
        down, up, leave = copies(t)
        up.wait()
        for j in range(up_chunks):
            place = down_chunks + (j % across) * 8 + j // across
            flat[place * 8:place * 8 + 8, :] = up_buf[t, j].astype(jnp.float32)
        down.wait()
        for j in range(down_chunks):
            flat[j * 8:j * 8 + 8, :] = down_buf[t, j].astype(jnp.float32)
        sub = slot_of[asked[t, 0, 0]] % TILE_ROWS
        built[t] = flat[pl.ds(sub, down_chunks + up_chunks, stride=8), :].astype(jnp.bfloat16)
        leave.start()

    def two(i, carry):
        for u in range(2):
            one(2 * i + u, flats.at[u])
        return carry

    lax.fori_loop(0, count // 2, two, 0)
    for t in range(count):
        copies(t)[2].wait()


def zero_kernel(after_ref, down_ref, up_ref, done_ref, zeros, sems):
    del after_ref
    done_ref[0] = 0
    zeros[...] = jnp.zeros_like(zeros)
    part = zeros.shape[0]
    copies = []
    for ref, sem in ((down_ref, sems.at[0]), (up_ref, sems.at[1])):
        for g in range(ref.shape[0]):
            for c in range(ref.shape[1] // part):
                copies.append(pltpu.make_async_copy(zeros, ref.at[g, pl.ds(c * part, part)], sem))
    for c in copies:
        c.start()
    for c in copies:
        c.wait()


def adapter_kernel(count, down_chunks, xs_ref, g_ref, pieces, _, out_ref, lifted_ref, up_panel):
    rows = g_ref.shape[0]
    across = g_ref.shape[1] // LANES
    total = jnp.zeros((2 * rows, LANES), jnp.float32)
    for t in range(count):
        total += dot(xs_ref[t], pieces[t, :down_chunks])
        for c in range(across):
            block = pieces[t, down_chunks + 8 * c:down_chunks + 8 * c + 8, :].astype(jnp.float32)
            up_panel[8 * t:8 * t + 8, c * LANES:(c + 1) * LANES] = block
            up_panel[R + 8 * t:R + 8 * t + 8, c * LANES:(c + 1) * LANES] = block
    panel = up_panel[...].astype(jnp.bfloat16)
    left = lax.broadcasted_iota(jnp.int32, (rows, LANES), 1) < R
    inner = total[:rows] + pltpu.roll(total[rows:], R, 1)
    inner = jnp.where(left, inner, 0.0).astype(jnp.bfloat16)
    g = g_ref[...]
    lifted_ref[...] = adapter_scale * dot(inner, panel)
    inner_grad = adapter_scale * dot_t(g, panel)
    diagonal = jnp.concatenate(
        [jnp.where(left, inner_grad, 0.0), jnp.where(left, 0.0, inner_grad)], axis=0
    ).astype(jnp.bfloat16)
    up_term = adapter_scale * t_dot(inner, g)
    for t in range(count):
        out_ref[t, :down_chunks] = t_dot(xs_ref[t], diagonal).astype(jnp.bfloat16)
        up_part = jnp.concatenate(
            [up_term[8 * t:8 * t + 8, c * LANES:(c + 1) * LANES] for c in range(across)], axis=0
        )
        out_ref[t, down_chunks:] = up_part.astype(jnp.bfloat16)


def scatter_kernel(count, down_chunks, up_chunks, rows_here, rows_core, *rest):
    sources, (down_out, up_out) = rest[:2], rest[4:6]
    pieces, down_sum, up_sum, ordered, arrived, sem = rest[6:]
    half = count // 2
    owned_rows = down_out.shape[0] * 8
    first_row = lax.axis_index("dp") * owned_rows
    across = up_chunks // 8
    rows = [(rows_here if b < half else rows_core)[b % half] - first_row for b in range(count)]
    arriving = [pltpu.make_async_copy(sources[b // half].at[b % half], pieces.at[b], arrived.at[b]) for b in range(count)]
    owned = [(row >= 0) & (row < owned_rows) for row in rows]
    for b in range(count):
        @pl.when(owned[b])
        def _():
            arriving[b].start()

    slots, final = [], []
    for b in range(count):
        slot, last = jnp.int32(b), jnp.bool_(True)
        for e in range(b - 1, -1, -1):
            slot = jnp.where(rows[e] == rows[b], e, slot)
        for e in range(b + 1, count):
            last = last & (rows[e] != rows[b])
        slots.append(slot)
        final.append(last)

    def copies(b):
        return (
            pltpu.make_async_copy(down_sum.at[slots[b]], down_out.at[rows[b] // 8, :, rows[b] % 8, 0], sem),
            pltpu.make_async_copy(up_sum.at[slots[b]], up_out.at[rows[b] // 8, :, rows[b] % 8, 0], sem),
        )

    for b in range(count):
        @pl.when(owned[b])
        def _():
            arriving[b].wait()
            slot = slots[b]
            down = pieces[b, :down_chunks].astype(jnp.float32)
            for c in range(across):
                ordered[pl.ds(c, 8, stride=across), :] = pieces[
                    b, down_chunks + 8 * c:down_chunks + 8 * c + 8
                ].astype(jnp.float32)
            up = ordered[...]

            @pl.when(slot == b)
            def _():
                down_sum[b] = down
                up_sum[b] = up

            @pl.when(slot != b)
            def _():
                down_sum[slot] += down
                up_sum[slot] += up

            @pl.when(final[b])
            def _():
                for copy in copies(b):
                    copy.start()

    for b in range(count):
        @pl.when(owned[b] & final[b])
        def _():
            for copy in copies(b):
                copy.wait()


def base_kernel(*refs):
    whole, halves, w_from, out_refs = refs[:2], refs[2:6], refs[6:-8], refs[-7:-3]
    x_buf, w_buf, sems = refs[-3:]
    outer, rows, depth = whole[0].shape
    width, each = w_from[0].shape[1], outer // 2
    z = lax.axis_index("tensor") // 2
    inside = (z == 1) | (z == 2)
    order = [z, z ^ 1, jnp.where(z < 2, 2, 1), jnp.where(z < 2, 3, 0)]
    pieces = len(w_from) // 2

    def fetch(k, begin):
        columns = pl.ds(k * depth, depth)

        def move(source, place, sem):
            copy = pltpu.make_async_copy(source, place, sem)
            copy.start() if begin else copy.wait()

        for b, ref in enumerate(whole):
            move(ref.at[order[k]], x_buf.at[pl.ds(b * rows, rows), columns], sems.at[k, b])
            for h in range(2):
                @pl.when(order[k] // each == h)
                def _():
                    place = x_buf.at[pl.ds((2 + b) * rows, rows), columns]
                    move(halves[2 * b + h].at[order[k] % each], place, sems.at[k, 2 + b])
        for h in range(2):
            place, sem = w_buf.at[columns, pl.ds(h * width, width)], sems.at[k, 4 + h]
            if k < 3:
                move(w_from[h * pieces + k], place, sem)
                continue

            @pl.when(inside)
            def _():
                move(w_from[h * pieces + k], place, sem)

            @pl.when(jnp.logical_not(inside))
            def _():
                move(w_from[h * pieces + k + 1], place, sem)

    for k in range(outer):
        fetch(k, True)
    total = 0.0
    for first in range(0, outer, each):
        for k in range(first, first + each):
            fetch(k, False)
        columns = slice(first * depth, (first + each) * depth)
        total += dot(x_buf[:, columns], w_buf[columns, :])
    for b, ref in enumerate(out_refs):
        ref[...] = total[b * rows:(b + 1) * rows].astype(ref.dtype)


def fast_body(tokens, cotangent, frozen_value, down_store, up_store, block_adapter, adapter_slot):
    group, parts = lax.axis_size("tensor"), lax.axis_size("parts")
    outer = group // 2
    token_rows = tokens.shape[0]
    slice_width = D // group
    down_chunks = down_store.shape[1] // LANES
    up_chunks = up_store.shape[1] // LANES
    me, part, core = lax.axis_index("tensor"), lax.axis_index("parts"), lax.axis_index("dp")
    z = me // 2

    def exchange(value, s):
        return lax.ppermute(value, "tensor", [(t, t ^ s) for t in range(group)])

    def other_core(value):
        return lax.ppermute(value, "dp", [(0, 1), (1, 0)])

    def other_part(value):
        return lax.ppermute(value, "parts", [(a, parts - 1 - a) for a in range(parts)])

    own = jnp.broadcast_to(block_adapter, (group, 1, LANES))
    asked = lax.all_to_all(own, "tensor", 0, 0)
    split_from, half_from, own = lax.optimization_barrier((tokens, frozen_value, own))

    width = frozen_value.shape[1] // parts
    half = lax.dynamic_slice_in_dim(half_from, part * width, width, axis=1)
    block = jax.ShapeDtypeStruct((outer, token_rows, slice_width), jnp.bfloat16)
    token = jax.ShapeDtypeStruct((1,), jnp.int32)
    some = jax.ShapeDtypeStruct((outer // 2, token_rows, slice_width), jnp.bfloat16)
    x_mine, *x_theirs = pl.pallas_call(
        split_kernel, out_shape=(block, some, some), in_specs=[VMEM], out_specs=[VMEM] * 3,
        name="split_tokens", compiler_params=LIMIT,
    )(split_from)
    x_far = [exchange(x_theirs[0], 1)]
    y_mine = other_part(x_mine)
    xs = pl.pallas_call(
        interleave_kernel,
        out_shape=jax.ShapeDtypeStruct((group, 2 * token_rows, slice_width // 2), jnp.bfloat16),
        in_specs=[VMEM], out_specs=ANY, name="pair_columns", compiler_params=WIDE,
        scratch_shapes=[
            pltpu.VMEM((group, 2 * token_rows, slice_width // 2), jnp.bfloat16),
            pltpu.SemaphoreType.DMA((group,)),
        ],
        cost_estimate=cost(read=128 << 20),
    )(split_from)
    middle = [(t, t ^ 6) for t in range(group) if t // 2 in (1, 2)]
    ends = [(t, t ^ 2) for t in range(group) if t // 2 in (1, 2)]
    near = exchange(half, 2)
    over = lax.ppermute(half, "tensor", middle)
    near, over, asked, x_theirs, xs = lax.optimization_barrier((near, over, asked, x_theirs, xs))
    x_far.append(exchange(x_theirs[1], 1))
    over_near = lax.ppermute(near, "tensor", middle)
    passed = lax.ppermute(over, "tensor", ends)
    pieces = jax.ShapeDtypeStruct((group, down_chunks + up_chunks, LANES), jnp.bfloat16)
    def tiles(store):
        view = store.reshape(store.shape[0] // TILE_ROWS, TILE_ROWS, store.shape[1] // LANES, LANES)
        return view.transpose(0, 2, 1, 3)

    sent, rows = pl.pallas_call(
        gather_kernel,
        out_shape=(pieces, jax.ShapeDtypeStruct((group,), jnp.int32)),
        in_specs=[SMEM, SMEM, ANY, ANY],
        out_specs=(ANY, SMEM),
        scratch_shapes=[
            pltpu.VMEM((group, down_chunks, TILE_ROWS, LANES), jnp.bfloat16),
            pltpu.VMEM((group, up_chunks, TILE_ROWS, LANES), jnp.bfloat16),
            pltpu.VMEM((2, (down_chunks + up_chunks) * 8, LANES), jnp.float32),
            pltpu.VMEM(pieces.shape, jnp.bfloat16),
            pltpu.SemaphoreType.DMA((3, group)),
        ],
        compiler_params=WIDE,
        cost_estimate=cost(read=40 << 20),
        name="pick_panels",
    )(asked, adapter_slot, tiles(down_store), tiles(up_store))
    sent, rows, x_far, y_mine, half, near, over, over_near, passed = lax.optimization_barrier(
        (sent, rows, x_far, y_mine, half, near, over, over_near, passed)
    )
    panels = lax.all_to_all(sent, "tensor", 0, 0)
    rows_core = other_core(rows)
    y_far = [other_part(piece) for piece in x_far]
    passed_near = lax.ppermute(over_near, "tensor", ends)
    owned_groups = ADAPTERS // lax.axis_size("dp") // 8
    down_shape = jax.ShapeDtypeStruct((owned_groups, down_chunks, 8, 1, LANES), jnp.float32)
    up_shape = jax.ShapeDtypeStruct((owned_groups, up_chunks, 8, 1, LANES), jnp.float32)
    down_zero, up_zero, cleared = pl.pallas_call(
        zero_kernel, out_shape=(down_shape, up_shape, token),
        in_specs=[SMEM], out_specs=(ANY, ANY, SMEM),
        scratch_shapes=[pltpu.VMEM((up_chunks, 8, 1, LANES), jnp.float32), pltpu.SemaphoreType.DMA((2,))],
        compiler_params=LIMIT, cost_estimate=cost(read=28 << 20), name="clear_rows",
    )(rows)
    cleared, half, near, over, passed = lax.optimization_barrier((cleared, half, near, over, passed))
    inside = (z == 1) | (z == 2)
    quarter = [half, near, jnp.where(inside, over, passed)]
    quarter_core = [other_core(w) for w in quarter]
    panels, quarter_core, y_far = lax.optimization_barrier((panels, quarter_core, y_far))

    terms, lifted = pl.pallas_call(
        functools.partial(adapter_kernel, group, down_chunks),
        out_shape=(pieces, jax.ShapeDtypeStruct((token_rows, VALUE_OUTPUTS), jnp.float32)),
        in_specs=[VMEM] * 3 + [SMEM],
        out_specs=(VMEM, VMEM),
        scratch_shapes=[pltpu.VMEM((2 * R, VALUE_OUTPUTS), jnp.float32)],
        compiler_params=LIMIT,
        cost_estimate=cost(flops=3 << 30, read=8 << 20),
        name="adapter",
    )(xs, cotangent, panels, cleared)
    terms, over_near, passed_near = lax.optimization_barrier((terms, over_near, passed_near))
    last = [over_near, passed_near]
    quarters = quarter + last + quarter_core + [other_core(w) for w in last]
    sums = [jax.ShapeDtypeStruct((token_rows, parts * width), kind) for kind in (jnp.float32,) + (jnp.bfloat16,) * 3]
    kept, to_part, to_inner, to_both = pl.pallas_call(
        base_kernel,
        out_shape=sums,
        in_specs=[ANY] * (7 + len(quarters)),
        out_specs=[VMEM] * 4,
        scratch_shapes=[
            pltpu.VMEM((4 * token_rows, outer * slice_width), jnp.bfloat16),
            pltpu.VMEM((outer * slice_width, parts * width), jnp.bfloat16),
            pltpu.SemaphoreType.DMA((outer, 6)),
        ],
        compiler_params=WIDE,
        cost_estimate=cost(flops=4 << 30, read=8 << 20),
        name="frozen_part",
    )(x_mine, y_mine, *x_far, *y_far, *quarters, terms)
    opposite = [(a * group + t, (parts - 1 - a) * group + (t ^ 1)) for a in range(parts) for t in range(group)]
    back = lax.all_to_all(terms, "tensor", 0, 0)
    arrived = (exchange(to_inner, 1), other_part(to_part), lax.ppermute(to_both, ("parts", "tensor"), opposite))
    back, arrived = lax.optimization_barrier((back, arrived))
    back_core = other_core(back)

    grad_down, grad_up = pl.pallas_call(
        functools.partial(scatter_kernel, 2 * group, down_chunks, up_chunks),
        out_shape=(down_shape, up_shape),
        in_specs=[SMEM] * 2 + [ANY] * 4,
        out_specs=(ANY, ANY),
        input_output_aliases={4: 0, 5: 1},
        scratch_shapes=[
            pltpu.VMEM((2 * group,) + pieces.shape[1:], jnp.bfloat16),
            pltpu.VMEM((2 * group, down_chunks, LANES), jnp.float32),
            pltpu.VMEM((2 * group, up_chunks, LANES), jnp.float32),
            pltpu.VMEM((up_chunks, LANES), jnp.float32),
            pltpu.SemaphoreType.DMA((2 * group,)),
            pltpu.SemaphoreType.DMA(()),
        ],
        compiler_params=LIMIT,
        cost_estimate=cost(read=16 << 20),
        name="place_rows",
    )(rows, rows_core, back, back_core, down_zero, up_zero)
    grad_down = grad_down.reshape(owned_groups, down_chunks, 8, LANES).transpose(0, 2, 1, 3)
    grad_up = grad_up.reshape(owned_groups, up_chunks, 8, LANES).transpose(0, 2, 1, 3)

    arrived = [a.astype(jnp.float32) for a in arrived]
    kept, got = kept + arrived[0], arrived[1] + arrived[2]
    quarters = [[c[:, :width], c[:, width:]] for c in (kept, got)]

    def pick_quarter(c, a):
        first = quarters[a][0] if c == 0 else quarters[a][1]
        second = quarters[a][1] if c == 0 else quarters[a][0]
        return jnp.where(core == 0, first, second)

    def columns_of(c):
        low, high = pick_quarter(c, 0), pick_quarter(c, 1)
        return jnp.where(part == 0, low, high), jnp.where(part == 0, high, low)

    frozen_output = jnp.concatenate(columns_of(0) + columns_of(1), axis=1)
    mixed = (frozen_output + lifted).astype(jnp.bfloat16)
    return mixed, grad_down.reshape(owned_groups * 8, -1), grad_up.reshape(owned_groups * 8, -1)


def fits(mesh):
    group, cores, parts = mesh.shape["tensor"], mesh.shape["dp"], mesh.shape["parts"]
    return cores == 2 and parts == 2 and group <= 8 and group & (group - 1) == 0 and R == 8 * group


def body(mesh, tokens, *rest):
    block_adapter = rest[4]
    one_block = block_adapter.shape[0] == 1
    return (fast_body if fits(mesh) and one_block else plain_body)(tokens, *rest)


def solution(mesh):
    placed = (
        P(("parts", "dp", "tensor"), None),
        P(("parts", "dp", "tensor"), None),
        P("tensor", "dp"),
        P("parts", "tensor"),
        P("parts", "tensor"),
        P(("parts", "dp", "tensor")),
        P("parts"),
    )
    return jax.shard_map(
        functools.partial(body, mesh),
        mesh=mesh,
        in_specs=placed,
        out_specs=(
            P(("parts", "dp", "tensor"), None),
            P(("parts", "dp"), "tensor"),
            P(("parts", "dp"), "tensor"),
        ),
        check_vma=False,
    )
```

```python
import functools

import jax
import jax.numpy as jnp
from jax import lax
from jax.experimental import pallas as pl
from jax.experimental.pallas import tpu as pltpu
from jax.sharding import PartitionSpec as P

D = 5120
VALUE_OUTPUTS = 1024
R = 64
ADAPTERS = 256
LANES = 128
TILE_ROWS = 8

adapter_scale = 2.0
VMEM = pl.BlockSpec(memory_space=pltpu.VMEM)
SMEM = pl.BlockSpec(memory_space=pltpu.SMEM)
ANY = pl.BlockSpec(memory_space=pl.ANY)
LIMIT = pltpu.CompilerParams(vmem_limit_bytes=16 * 1024 * 1024)
WIDE = pltpu.CompilerParams(vmem_limit_bytes=60 * 1024 * 1024)


def cost(flops=0, read=0):
    return pl.CostEstimate(flops=flops, bytes_accessed=read, transcendentals=0)


def dot(a, b):
    return jnp.dot(a, b, preferred_element_type=jnp.float32)


def dot_t(a, b):
    return lax.dot_general(a, b, (((1,), (1,)), ((), ())), preferred_element_type=jnp.float32)


def t_dot(a, b):
    return lax.dot_general(a, b, (((0,), (0,)), ((), ())), preferred_element_type=jnp.float32)


def fold_rows(left, piece):
    return jnp.dot(left, piece, preferred_element_type=jnp.float32)


def store_rows(requests, adapter_slot):
    table = jnp.arange(adapter_slot.shape[0], dtype=jnp.int32)
    return jnp.sum(jnp.where(requests[:, None] == table[None, :], adapter_slot[None, :], 0), axis=1)


def plain_body(tokens, cotangent, frozen_value, down_store, up_store, block_adapter, adapter_slot):
    token_rows = tokens.shape[0]
    blocks_here = block_adapter.shape[0]
    block_rows = token_rows // blocks_here
    group = lax.axis_size("tensor")
    columns = lax.all_gather(frozen_value, "dp", axis=1, tiled=True)
    frozen_output = fold_rows(tokens, lax.all_gather(columns, "tensor", axis=0, tiled=True))
    requests = lax.all_gather(block_adapter, "tensor", axis=0, tiled=True)
    stored = store_rows(requests, adapter_slot)
    order = stored.reshape(group, blocks_here).T.reshape(-1)
    down_send = jnp.take(down_store, order, axis=0).reshape(blocks_here, group, -1)
    up_send = jnp.take(up_store, order, axis=0).reshape(blocks_here, group, -1)
    down_got = lax.all_to_all(down_send, "tensor", split_axis=1, concat_axis=1, tiled=True)
    up_got = lax.all_to_all(up_send, "tensor", split_axis=1, concat_axis=1, tiled=True)
    down_panel = down_got.reshape(blocks_here, D, R)
    up_panel = up_got.reshape(blocks_here, R, VALUE_OUTPUTS)
    token_blocks = tokens.reshape(blocks_here, block_rows, D)
    grad_blocks = cotangent.reshape(blocks_here, block_rows, VALUE_OUTPUTS)
    down_projected = jnp.einsum(
        "jtd,jdr->jtr", token_blocks, down_panel, preferred_element_type=jnp.float32
    ).astype(jnp.bfloat16)
    up_projected = jnp.einsum(
        "jtr,jrk->jtk", down_projected, up_panel, preferred_element_type=jnp.float32
    )
    mixed = (
        frozen_output + adapter_scale * up_projected.reshape(token_rows, VALUE_OUTPUTS)
    ).astype(jnp.bfloat16)
    down_projected_gradient = (
        adapter_scale
        * jnp.einsum("jtk,jrk->jtr", grad_blocks, up_panel, preferred_element_type=jnp.float32)
    ).astype(jnp.bfloat16)
    down_term = jnp.einsum(
        "jtd,jtr->jdr", token_blocks, down_projected_gradient, preferred_element_type=jnp.float32
    )
    up_weight_gradient = adapter_scale * jnp.einsum(
        "jtr,jtk->jrk", down_projected, grad_blocks, preferred_element_type=jnp.float32
    )
    down_back = lax.all_to_all(
        down_term.reshape(blocks_here, group, -1), "tensor", split_axis=1, concat_axis=1, tiled=True
    )
    up_back = lax.all_to_all(
        up_weight_gradient.reshape(blocks_here, group, -1), "tensor", split_axis=1, concat_axis=1, tiled=True
    )
    down_flat = down_back.reshape(blocks_here * group, -1)
    up_flat = up_back.reshape(blocks_here * group, -1)
    down_table = jax.ops.segment_sum(down_flat, order, num_segments=ADAPTERS)
    up_table = jax.ops.segment_sum(up_flat, order, num_segments=ADAPTERS)
    grad_down = lax.psum_scatter(down_table, "dp", scatter_dimension=0, tiled=True)
    grad_up = lax.psum_scatter(up_table, "dp", scatter_dimension=0, tiled=True)
    return mixed, grad_down, grad_up


def split_kernel(x_ref, mine_ref, *theirs_refs):
    inner = lax.axis_index("tensor") % 2
    outer, rows, width = mine_ref.shape
    each = outer // len(theirs_refs)
    for k in range(outer):
        own = pl.multiple_of((2 * k + inner) * width, LANES)
        other = pl.multiple_of((2 * k + 1 - inner) * width, LANES)
        mine_ref[k] = x_ref[:, pl.ds(own, width)]
        theirs_refs[k // each][k % each] = x_ref[:, pl.ds(other, width)]


def interleave_kernel(x_ref, out_ref, xs_ref, sems):
    group, rows2, half = xs_ref.shape
    leave = [pltpu.make_async_copy(xs_ref.at[k], out_ref.at[k], sems.at[k]) for k in range(group)]
    rows, width = rows2 // 2, 2 * half
    source = lax.broadcasted_iota(jnp.int32, (width, half), 0)
    target = lax.broadcasted_iota(jnp.int32, (width, half), 1)
    even = (source == 2 * target).astype(jnp.bfloat16)
    odd = (source == 2 * target + 1).astype(jnp.bfloat16)
    for k in range(group):
        x = x_ref[:, k * width:(k + 1) * width]
        xs_ref[k, :rows] = dot(x, even).astype(jnp.bfloat16)
        xs_ref[k, rows:] = dot(x, odd).astype(jnp.bfloat16)
        leave[k].start()
    for copy in leave:
        copy.wait()


def gather_kernel(asked, slot_of, down_ref, up_ref, out_ref, rows_ref, down_buf, up_buf, flats, built, sems):
    count, down_chunks, up_chunks = down_buf.shape[0], down_buf.shape[1], up_buf.shape[1]
    across = up_chunks // 8

    def copies(t):
        tile = slot_of[asked[t, 0, 0]] // TILE_ROWS
        return (
            pltpu.make_async_copy(down_ref.at[tile], down_buf.at[t], sems.at[0, t]),
            pltpu.make_async_copy(up_ref.at[tile], up_buf.at[t], sems.at[1, t]),
            pltpu.make_async_copy(built.at[t], out_ref.at[t], sems.at[2, t]),
        )

    for t in range(count):
        down, up, _ = copies(t)
        down.start()
        up.start()
        rows_ref[t] = slot_of[asked[t, 0, 0]]

    def one(t, flat):
        down, up, leave = copies(t)
        up.wait()
        for j in range(up_chunks):
            place = down_chunks + (j % across) * 8 + j // across
            flat[place * 8:place * 8 + 8, :] = up_buf[t, j].astype(jnp.float32)
        down.wait()
        for j in range(down_chunks):
            flat[j * 8:j * 8 + 8, :] = down_buf[t, j].astype(jnp.float32)
        sub = slot_of[asked[t, 0, 0]] % TILE_ROWS
        built[t] = flat[pl.ds(sub, down_chunks + up_chunks, stride=8), :].astype(jnp.bfloat16)
        leave.start()

    def two(i, carry):
        for u in range(2):
            one(2 * i + u, flats.at[u])
        return carry

    lax.fori_loop(0, count // 2, two, 0)
    for t in range(count):
        copies(t)[2].wait()


def zero_kernel(half, *refs):
    down_ref, up_ref, done_ref, zeros, sems = refs[-5:]
    done_ref[0] = 0
    zeros[...] = jnp.zeros_like(zeros)
    part = zeros.shape[0]
    groups = down_ref.shape[0] // 2
    copies = []
    for ref, sem in ((down_ref, sems.at[0]), (up_ref, sems.at[1])):
        for g in range(half * groups, (half + 1) * groups):
            for c in range(ref.shape[1] // part):
                copies.append(pltpu.make_async_copy(zeros, ref.at[g, pl.ds(c * part, part)], sem))
    for c in copies:
        c.start()
    for c in copies:
        c.wait()


def adapter_kernel(count, down_chunks, xs_ref, g_ref, pieces, _, out_ref, lifted_ref, up_panel):
    rows = g_ref.shape[0]
    across = g_ref.shape[1] // LANES
    total = jnp.zeros((2 * rows, LANES), jnp.float32)
    for t in range(count):
        total += dot(xs_ref[t], pieces[t, :down_chunks])
        for c in range(across):
            block = pieces[t, down_chunks + 8 * c:down_chunks + 8 * c + 8, :].astype(jnp.float32)
            up_panel[8 * t:8 * t + 8, c * LANES:(c + 1) * LANES] = block
            up_panel[R + 8 * t:R + 8 * t + 8, c * LANES:(c + 1) * LANES] = block
    panel = up_panel[...].astype(jnp.bfloat16)
    left = lax.broadcasted_iota(jnp.int32, (rows, LANES), 1) < R
    inner = total[:rows] + pltpu.roll(total[rows:], R, 1)
    inner = jnp.where(left, inner, 0.0).astype(jnp.bfloat16)
    g = g_ref[...]
    lifted_ref[...] = adapter_scale * dot(inner, panel)
    inner_grad = adapter_scale * dot_t(g, panel)
    diagonal = jnp.concatenate(
        [jnp.where(left, inner_grad, 0.0), jnp.where(left, 0.0, inner_grad)], axis=0
    ).astype(jnp.bfloat16)
    up_term = adapter_scale * t_dot(inner, g)
    for t in range(count):
        out_ref[t, :down_chunks] = t_dot(xs_ref[t], diagonal).astype(jnp.bfloat16)
        up_part = jnp.concatenate(
            [up_term[8 * t:8 * t + 8, c * LANES:(c + 1) * LANES] for c in range(across)], axis=0
        )
        out_ref[t, down_chunks:] = up_part.astype(jnp.bfloat16)


def scatter_kernel(count, down_chunks, up_chunks, rows_here, rows_core, *rest):
    sources, (down_out, up_out) = rest[:2], rest[4:6]
    pieces, down_sum, up_sum, ordered, arrived, sem = rest[6:]
    half = count // 2
    owned_rows = down_out.shape[0] * 8
    first_row = lax.axis_index("dp") * owned_rows
    across = up_chunks // 8
    rows = [(rows_here if b < half else rows_core)[b % half] - first_row for b in range(count)]
    arriving = [pltpu.make_async_copy(sources[b // half].at[b % half], pieces.at[b], arrived.at[b]) for b in range(count)]
    owned = [(row >= 0) & (row < owned_rows) for row in rows]
    for b in range(count):
        @pl.when(owned[b])
        def _():
            arriving[b].start()

    slots, final = [], []
    for b in range(count):
        slot, last = jnp.int32(b), jnp.bool_(True)
        for e in range(b - 1, -1, -1):
            slot = jnp.where(rows[e] == rows[b], e, slot)
        for e in range(b + 1, count):
            last = last & (rows[e] != rows[b])
        slots.append(slot)
        final.append(last)

    def copies(b):
        return (
            pltpu.make_async_copy(down_sum.at[slots[b]], down_out.at[rows[b] // 8, :, rows[b] % 8, 0], sem),
            pltpu.make_async_copy(up_sum.at[slots[b]], up_out.at[rows[b] // 8, :, rows[b] % 8, 0], sem),
        )

    for b in range(count):
        @pl.when(owned[b])
        def _():
            arriving[b].wait()
            slot = slots[b]
            down = pieces[b, :down_chunks].astype(jnp.float32)
            for c in range(across):
                ordered[pl.ds(c, 8, stride=across), :] = pieces[
                    b, down_chunks + 8 * c:down_chunks + 8 * c + 8
                ].astype(jnp.float32)
            up = ordered[...]

            @pl.when(slot == b)
            def _():
                down_sum[b] = down
                up_sum[b] = up

            @pl.when(slot != b)
            def _():
                down_sum[slot] += down
                up_sum[slot] += up

            @pl.when(final[b])
            def _():
                for copy in copies(b):
                    copy.start()

    for b in range(count):
        @pl.when(owned[b] & final[b])
        def _():
            for copy in copies(b):
                copy.wait()


def base_kernel(*refs):
    whole, halves, w_from, out_refs = refs[:2], refs[2:6], refs[6:-8], refs[-7:-3]
    x_buf, w_buf, sems = refs[-3:]
    outer, rows, depth = whole[0].shape
    width, each = w_from[0].shape[1], outer // 2
    z = lax.axis_index("tensor") // 2
    inside = (z == 1) | (z == 2)
    order = [z, z ^ 1, jnp.where(z < 2, 2, 1), jnp.where(z < 2, 3, 0)]
    pieces = len(w_from) // 2

    def fetch(k, begin):
        columns = pl.ds(k * depth, depth)

        def move(source, place, sem):
            copy = pltpu.make_async_copy(source, place, sem)
            copy.start() if begin else copy.wait()

        for b, ref in enumerate(whole):
            move(ref.at[order[k]], x_buf.at[pl.ds(b * rows, rows), columns], sems.at[k, b])
            for h in range(2):
                @pl.when(order[k] // each == h)
                def _():
                    place = x_buf.at[pl.ds((2 + b) * rows, rows), columns]
                    move(halves[2 * b + h].at[order[k] % each], place, sems.at[k, 2 + b])
        for h in range(2):
            place, sem = w_buf.at[columns, pl.ds(h * width, width)], sems.at[k, 4 + h]
            if k < 3:
                move(w_from[h * pieces + k], place, sem)
                continue

            @pl.when(inside)
            def _():
                move(w_from[h * pieces + k], place, sem)

            @pl.when(jnp.logical_not(inside))
            def _():
                move(w_from[h * pieces + k + 1], place, sem)

    for k in range(outer):
        fetch(k, True)
    total = 0.0
    for first in range(0, outer, each):
        for k in range(first, first + each):
            fetch(k, False)
        columns = slice(first * depth, (first + each) * depth)
        total += dot(x_buf[:, columns], w_buf[columns, :])
    for b, ref in enumerate(out_refs):
        ref[...] = total[b * rows:(b + 1) * rows].astype(ref.dtype)


def fast_body(tokens, cotangent, frozen_value, down_store, up_store, block_adapter, adapter_slot):
    group, parts = lax.axis_size("tensor"), lax.axis_size("parts")
    outer = group // 2
    token_rows = tokens.shape[0]
    slice_width = D // group
    down_chunks = down_store.shape[1] // LANES
    up_chunks = up_store.shape[1] // LANES
    me, part, core = lax.axis_index("tensor"), lax.axis_index("parts"), lax.axis_index("dp")
    z = me // 2

    def exchange(value, s):
        return lax.ppermute(value, "tensor", [(t, t ^ s) for t in range(group)])

    def other_core(value):
        return lax.ppermute(value, "dp", [(0, 1), (1, 0)])

    def other_part(value):
        return lax.ppermute(value, "parts", [(a, parts - 1 - a) for a in range(parts)])

    own = jnp.broadcast_to(block_adapter, (group, 1, LANES))
    asked = lax.all_to_all(own, "tensor", 0, 0)
    split_from, half_from, own = lax.optimization_barrier((tokens, frozen_value, own))

    width = frozen_value.shape[1] // parts
    half = lax.dynamic_slice_in_dim(half_from, part * width, width, axis=1)
    block = jax.ShapeDtypeStruct((outer, token_rows, slice_width), jnp.bfloat16)
    token = jax.ShapeDtypeStruct((1,), jnp.int32)
    some = jax.ShapeDtypeStruct((outer // 2, token_rows, slice_width), jnp.bfloat16)
    x_mine, *x_theirs = pl.pallas_call(
        split_kernel, out_shape=(block, some, some), in_specs=[VMEM], out_specs=[VMEM] * 3,
        name="split_tokens", compiler_params=LIMIT,
    )(split_from)
    x_far = [exchange(x_theirs[0], 1)]
    y_mine = other_part(x_mine)
    xs = pl.pallas_call(
        interleave_kernel,
        out_shape=jax.ShapeDtypeStruct((group, 2 * token_rows, slice_width // 2), jnp.bfloat16),
        in_specs=[VMEM], out_specs=ANY, name="pair_columns", compiler_params=WIDE,
        scratch_shapes=[
            pltpu.VMEM((group, 2 * token_rows, slice_width // 2), jnp.bfloat16),
            pltpu.SemaphoreType.DMA((group,)),
        ],
        cost_estimate=cost(read=128 << 20),
    )(split_from)
    middle = [(t, t ^ 6) for t in range(group) if t // 2 in (1, 2)]
    ends = [(t, t ^ 2) for t in range(group) if t // 2 in (1, 2)]
    near = exchange(half, 2)
    over = lax.ppermute(half, "tensor", middle)
    near, over, asked, x_theirs, xs = lax.optimization_barrier((near, over, asked, x_theirs, xs))
    x_far.append(exchange(x_theirs[1], 1))
    over_near = lax.ppermute(near, "tensor", middle)
    passed = lax.ppermute(over, "tensor", ends)
    pieces = jax.ShapeDtypeStruct((group, down_chunks + up_chunks, LANES), jnp.bfloat16)
    def tiles(store):
        view = store.reshape(store.shape[0] // TILE_ROWS, TILE_ROWS, store.shape[1] // LANES, LANES)
        return view.transpose(0, 2, 1, 3)

    sent, rows = pl.pallas_call(
        gather_kernel,
        out_shape=(pieces, jax.ShapeDtypeStruct((group,), jnp.int32)),
        in_specs=[SMEM, SMEM, ANY, ANY],
        out_specs=(ANY, SMEM),
        scratch_shapes=[
            pltpu.VMEM((group, down_chunks, TILE_ROWS, LANES), jnp.bfloat16),
            pltpu.VMEM((group, up_chunks, TILE_ROWS, LANES), jnp.bfloat16),
            pltpu.VMEM((2, (down_chunks + up_chunks) * 8, LANES), jnp.float32),
            pltpu.VMEM(pieces.shape, jnp.bfloat16),
            pltpu.SemaphoreType.DMA((3, group)),
        ],
        compiler_params=WIDE,
        cost_estimate=cost(read=40 << 20),
        name="pick_panels",
    )(asked, adapter_slot, tiles(down_store), tiles(up_store))
    sent, rows, x_far, y_mine, half, near, over, over_near, passed = lax.optimization_barrier(
        (sent, rows, x_far, y_mine, half, near, over, over_near, passed)
    )
    panels = lax.all_to_all(sent, "tensor", 0, 0)
    rows_core = other_core(rows)
    y_far = [other_part(piece) for piece in x_far]
    passed_near = lax.ppermute(over_near, "tensor", ends)
    owned_groups = ADAPTERS // lax.axis_size("dp") // 8
    down_shape = jax.ShapeDtypeStruct((owned_groups, down_chunks, 8, 1, LANES), jnp.float32)
    up_shape = jax.ShapeDtypeStruct((owned_groups, up_chunks, 8, 1, LANES), jnp.float32)
    def clear(half, inputs, in_specs, aliases):
        return pl.pallas_call(
            functools.partial(zero_kernel, half), out_shape=(down_shape, up_shape, token),
            in_specs=in_specs, out_specs=(ANY, ANY, SMEM), input_output_aliases=aliases,
            scratch_shapes=[pltpu.VMEM((up_chunks, 8, 1, LANES), jnp.float32), pltpu.SemaphoreType.DMA((2,))],
            compiler_params=LIMIT, cost_estimate=cost(read=14 << 20), name="clear_rows",
        )(*inputs)

    down_zero, up_zero, cleared = clear(0, (rows,), [SMEM], {})
    inside = (z == 1) | (z == 2)
    quarter = [half, near, jnp.where(inside, over, passed)]
    quarter_core = [other_core(w) for w in quarter]
    panels, quarter_core = lax.optimization_barrier((panels, quarter_core))

    terms, lifted = pl.pallas_call(
        functools.partial(adapter_kernel, group, down_chunks),
        out_shape=(pieces, jax.ShapeDtypeStruct((token_rows, VALUE_OUTPUTS), jnp.float32)),
        in_specs=[VMEM] * 3 + [SMEM],
        out_specs=(VMEM, VMEM),
        scratch_shapes=[pltpu.VMEM((2 * R, VALUE_OUTPUTS), jnp.float32)],
        compiler_params=LIMIT,
        cost_estimate=cost(flops=3 << 30, read=8 << 20),
        name="adapter",
    )(xs, cotangent, panels, cleared)
    terms, over_near, passed_near, y_far = lax.optimization_barrier((terms, over_near, passed_near, y_far))
    last = [over_near, passed_near]
    quarters = quarter + last + quarter_core + [other_core(w) for w in last]
    sums = [jax.ShapeDtypeStruct((token_rows, parts * width), kind) for kind in (jnp.float32,) + (jnp.bfloat16,) * 3]
    kept, to_part, to_inner, to_both = pl.pallas_call(
        base_kernel,
        out_shape=sums,
        in_specs=[ANY] * (7 + len(quarters)),
        out_specs=[VMEM] * 4,
        scratch_shapes=[
            pltpu.VMEM((4 * token_rows, outer * slice_width), jnp.bfloat16),
            pltpu.VMEM((outer * slice_width, parts * width), jnp.bfloat16),
            pltpu.SemaphoreType.DMA((outer, 6)),
        ],
        compiler_params=WIDE,
        cost_estimate=cost(flops=4 << 30, read=8 << 20),
        name="frozen_part",
    )(x_mine, y_mine, *x_far, *y_far, *quarters, terms)
    opposite = [(a * group + t, (parts - 1 - a) * group + (t ^ 1)) for a in range(parts) for t in range(group)]
    back = lax.all_to_all(terms, "tensor", 0, 0)
    arrived = (exchange(to_inner, 1), other_part(to_part), lax.ppermute(to_both, ("parts", "tensor"), opposite))
    down_zero, up_zero, kept = lax.optimization_barrier((down_zero, up_zero, kept))
    down_zero, up_zero, cleared = clear(1, (down_zero, up_zero), [ANY, ANY], {0: 0, 1: 1})
    back, arrived, cleared = lax.optimization_barrier((back, arrived, cleared))
    back_core = other_core(back)

    grad_down, grad_up = pl.pallas_call(
        functools.partial(scatter_kernel, 2 * group, down_chunks, up_chunks),
        out_shape=(down_shape, up_shape),
        in_specs=[SMEM] * 2 + [ANY] * 4,
        out_specs=(ANY, ANY),
        input_output_aliases={4: 0, 5: 1},
        scratch_shapes=[
            pltpu.VMEM((2 * group,) + pieces.shape[1:], jnp.bfloat16),
            pltpu.VMEM((2 * group, down_chunks, LANES), jnp.float32),
            pltpu.VMEM((2 * group, up_chunks, LANES), jnp.float32),
            pltpu.VMEM((up_chunks, LANES), jnp.float32),
            pltpu.SemaphoreType.DMA((2 * group,)),
            pltpu.SemaphoreType.DMA(()),
        ],
        compiler_params=LIMIT,
        cost_estimate=cost(read=16 << 20),
        name="place_rows",
    )(rows, rows_core, back, back_core, down_zero, up_zero)
    grad_down = grad_down.reshape(owned_groups, down_chunks, 8, LANES).transpose(0, 2, 1, 3)
    grad_up = grad_up.reshape(owned_groups, up_chunks, 8, LANES).transpose(0, 2, 1, 3)

    arrived = [a.astype(jnp.float32) for a in arrived]
    kept, got = kept + arrived[0], arrived[1] + arrived[2]
    quarters = [[c[:, :width], c[:, width:]] for c in (kept, got)]

    def pick_quarter(c, a):
        first = quarters[a][0] if c == 0 else quarters[a][1]
        second = quarters[a][1] if c == 0 else quarters[a][0]
        return jnp.where(core == 0, first, second)

    def columns_of(c):
        low, high = pick_quarter(c, 0), pick_quarter(c, 1)
        return jnp.where(part == 0, low, high), jnp.where(part == 0, high, low)

    frozen_output = jnp.concatenate(columns_of(0) + columns_of(1), axis=1)
    mixed = (frozen_output + lifted).astype(jnp.bfloat16)
    return mixed, grad_down.reshape(owned_groups * 8, -1), grad_up.reshape(owned_groups * 8, -1)


def fits(mesh):
    group, cores, parts = mesh.shape["tensor"], mesh.shape["dp"], mesh.shape["parts"]
    return cores == 2 and parts == 2 and group <= 8 and group & (group - 1) == 0 and R == 8 * group


def body(mesh, tokens, *rest):
    block_adapter = rest[4]
    one_block = block_adapter.shape[0] == 1
    return (fast_body if fits(mesh) and one_block else plain_body)(tokens, *rest)


def solution(mesh):
    placed = (
        P(("parts", "dp", "tensor"), None),
        P(("parts", "dp", "tensor"), None),
        P("tensor", "dp"),
        P("parts", "tensor"),
        P("parts", "tensor"),
        P(("parts", "dp", "tensor")),
        P("parts"),
    )
    return jax.shard_map(
        functools.partial(body, mesh),
        mesh=mesh,
        in_specs=placed,
        out_specs=(
            P(("parts", "dp", "tensor"), None),
            P(("parts", "dp"), "tensor"),
            P(("parts", "dp"), "tensor"),
        ),
        check_vma=False,
    )
```

```python
import functools

import jax
import jax.numpy as jnp
from jax import lax
from jax.experimental import pallas as pl
from jax.experimental.pallas import tpu as pltpu
from jax.sharding import PartitionSpec as P

D = 5120
VALUE_OUTPUTS = 1024
R = 64
ADAPTERS = 256
LANES = 128
TILE_ROWS = 8

adapter_scale = 2.0
VMEM = pl.BlockSpec(memory_space=pltpu.VMEM)
SMEM = pl.BlockSpec(memory_space=pltpu.SMEM)
ANY = pl.BlockSpec(memory_space=pl.ANY)
LIMIT = pltpu.CompilerParams(vmem_limit_bytes=16 * 1024 * 1024)
WIDE = pltpu.CompilerParams(vmem_limit_bytes=60 * 1024 * 1024)


def cost(flops=0, read=0):
    return pl.CostEstimate(flops=flops, bytes_accessed=read, transcendentals=0)


def dot(a, b):
    return jnp.dot(a, b, preferred_element_type=jnp.float32)


def dot_t(a, b):
    return lax.dot_general(a, b, (((1,), (1,)), ((), ())), preferred_element_type=jnp.float32)


def t_dot(a, b):
    return lax.dot_general(a, b, (((0,), (0,)), ((), ())), preferred_element_type=jnp.float32)


def fold_rows(left, piece):
    return jnp.dot(left, piece, preferred_element_type=jnp.float32)


def store_rows(requests, adapter_slot):
    table = jnp.arange(adapter_slot.shape[0], dtype=jnp.int32)
    return jnp.sum(jnp.where(requests[:, None] == table[None, :], adapter_slot[None, :], 0), axis=1)


def plain_body(tokens, cotangent, frozen_value, down_store, up_store, block_adapter, adapter_slot):
    token_rows = tokens.shape[0]
    blocks_here = block_adapter.shape[0]
    block_rows = token_rows // blocks_here
    group = lax.axis_size("tensor")
    columns = lax.all_gather(frozen_value, "dp", axis=1, tiled=True)
    frozen_output = fold_rows(tokens, lax.all_gather(columns, "tensor", axis=0, tiled=True))
    requests = lax.all_gather(block_adapter, "tensor", axis=0, tiled=True)
    stored = store_rows(requests, adapter_slot)
    order = stored.reshape(group, blocks_here).T.reshape(-1)
    down_send = jnp.take(down_store, order, axis=0).reshape(blocks_here, group, -1)
    up_send = jnp.take(up_store, order, axis=0).reshape(blocks_here, group, -1)
    down_got = lax.all_to_all(down_send, "tensor", split_axis=1, concat_axis=1, tiled=True)
    up_got = lax.all_to_all(up_send, "tensor", split_axis=1, concat_axis=1, tiled=True)
    down_panel = down_got.reshape(blocks_here, D, R)
    up_panel = up_got.reshape(blocks_here, R, VALUE_OUTPUTS)
    token_blocks = tokens.reshape(blocks_here, block_rows, D)
    grad_blocks = cotangent.reshape(blocks_here, block_rows, VALUE_OUTPUTS)
    down_projected = jnp.einsum(
        "jtd,jdr->jtr", token_blocks, down_panel, preferred_element_type=jnp.float32
    ).astype(jnp.bfloat16)
    up_projected = jnp.einsum(
        "jtr,jrk->jtk", down_projected, up_panel, preferred_element_type=jnp.float32
    )
    mixed = (
        frozen_output + adapter_scale * up_projected.reshape(token_rows, VALUE_OUTPUTS)
    ).astype(jnp.bfloat16)
    down_projected_gradient = (
        adapter_scale
        * jnp.einsum("jtk,jrk->jtr", grad_blocks, up_panel, preferred_element_type=jnp.float32)
    ).astype(jnp.bfloat16)
    down_term = jnp.einsum(
        "jtd,jtr->jdr", token_blocks, down_projected_gradient, preferred_element_type=jnp.float32
    )
    up_weight_gradient = adapter_scale * jnp.einsum(
        "jtr,jtk->jrk", down_projected, grad_blocks, preferred_element_type=jnp.float32
    )
    down_back = lax.all_to_all(
        down_term.reshape(blocks_here, group, -1), "tensor", split_axis=1, concat_axis=1, tiled=True
    )
    up_back = lax.all_to_all(
        up_weight_gradient.reshape(blocks_here, group, -1), "tensor", split_axis=1, concat_axis=1, tiled=True
    )
    down_flat = down_back.reshape(blocks_here * group, -1)
    up_flat = up_back.reshape(blocks_here * group, -1)
    down_table = jax.ops.segment_sum(down_flat, order, num_segments=ADAPTERS)
    up_table = jax.ops.segment_sum(up_flat, order, num_segments=ADAPTERS)
    grad_down = lax.psum_scatter(down_table, "dp", scatter_dimension=0, tiled=True)
    grad_up = lax.psum_scatter(up_table, "dp", scatter_dimension=0, tiled=True)
    return mixed, grad_down, grad_up


def split_kernel(x_ref, mine_ref, *theirs_refs):
    inner = lax.axis_index("tensor") % 2
    outer, rows, width = mine_ref.shape
    each = outer // len(theirs_refs)
    for k in range(outer):
        own = pl.multiple_of((2 * k + inner) * width, LANES)
        other = pl.multiple_of((2 * k + 1 - inner) * width, LANES)
        mine_ref[k] = x_ref[:, pl.ds(own, width)]
        theirs_refs[k // each][k % each] = x_ref[:, pl.ds(other, width)]


def interleave_kernel(x_ref, out_ref, xs_ref, sems):
    group, rows2, half = xs_ref.shape
    leave = [pltpu.make_async_copy(xs_ref.at[k], out_ref.at[k], sems.at[k]) for k in range(group)]
    rows, width = rows2 // 2, 2 * half
    source = lax.broadcasted_iota(jnp.int32, (width, half), 0)
    target = lax.broadcasted_iota(jnp.int32, (width, half), 1)
    even = (source == 2 * target).astype(jnp.bfloat16)
    odd = (source == 2 * target + 1).astype(jnp.bfloat16)
    for k in range(group):
        x = x_ref[:, k * width:(k + 1) * width]
        xs_ref[k, :rows] = dot(x, even).astype(jnp.bfloat16)
        xs_ref[k, rows:] = dot(x, odd).astype(jnp.bfloat16)
        leave[k].start()
    for copy in leave:
        copy.wait()


def gather_kernel(asked, slot_of, down_ref, up_ref, out_ref, rows_ref, down_buf, up_buf, flats, built, sems):
    count, down_chunks, up_chunks = down_buf.shape[0], down_buf.shape[1], up_buf.shape[1]
    across = up_chunks // 8

    def copies(t):
        tile = slot_of[asked[t, 0, 0]] // TILE_ROWS
        return (
            pltpu.make_async_copy(down_ref.at[tile], down_buf.at[t], sems.at[0, t]),
            pltpu.make_async_copy(up_ref.at[tile], up_buf.at[t], sems.at[1, t]),
            pltpu.make_async_copy(built.at[t], out_ref.at[t], sems.at[2, t]),
        )

    for t in range(count):
        down, up, _ = copies(t)
        down.start()
        up.start()
        rows_ref[t] = slot_of[asked[t, 0, 0]]

    def one(t, flat):
        down, up, leave = copies(t)
        up.wait()
        for j in range(up_chunks):
            place = down_chunks + (j % across) * 8 + j // across
            flat[place * 8:place * 8 + 8, :] = up_buf[t, j].astype(jnp.float32)
        down.wait()
        for j in range(down_chunks):
            flat[j * 8:j * 8 + 8, :] = down_buf[t, j].astype(jnp.float32)
        sub = slot_of[asked[t, 0, 0]] % TILE_ROWS
        built[t] = flat[pl.ds(sub, down_chunks + up_chunks, stride=8), :].astype(jnp.bfloat16)
        leave.start()

    def two(i, carry):
        for u in range(2):
            one(2 * i + u, flats.at[u])
        return carry

    lax.fori_loop(0, count // 2, two, 0)
    for t in range(count):
        copies(t)[2].wait()


def zero_kernel(half, *refs):
    down_ref, up_ref, done_ref, zeros, sems = refs[-5:]
    done_ref[0] = 0
    zeros[...] = jnp.zeros_like(zeros)
    part = zeros.shape[0]
    groups = down_ref.shape[0] // 2
    copies = []
    for ref, sem in ((down_ref, sems.at[0]), (up_ref, sems.at[1])):
        for g in range(half * groups, (half + 1) * groups):
            for c in range(ref.shape[1] // part):
                copies.append(pltpu.make_async_copy(zeros, ref.at[g, pl.ds(c * part, part)], sem))
    for c in copies:
        c.start()
    for c in copies:
        c.wait()


def adapter_kernel(count, down_chunks, xs_ref, g_ref, pieces, _, out_ref, lifted_ref, up_panel):
    rows = g_ref.shape[0]
    across = g_ref.shape[1] // LANES
    total = jnp.zeros((2 * rows, LANES), jnp.float32)
    for t in range(count):
        total += dot(xs_ref[t], pieces[t, :down_chunks])
        for c in range(across):
            block = pieces[t, down_chunks + 8 * c:down_chunks + 8 * c + 8, :].astype(jnp.float32)
            up_panel[8 * t:8 * t + 8, c * LANES:(c + 1) * LANES] = block
            up_panel[R + 8 * t:R + 8 * t + 8, c * LANES:(c + 1) * LANES] = block
    panel = up_panel[...].astype(jnp.bfloat16)
    left = lax.broadcasted_iota(jnp.int32, (rows, LANES), 1) < R
    inner = total[:rows] + pltpu.roll(total[rows:], R, 1)
    inner = jnp.where(left, inner, 0.0).astype(jnp.bfloat16)
    g = g_ref[...]
    lifted_ref[...] = adapter_scale * dot(inner, panel)
    inner_grad = adapter_scale * dot_t(g, panel)
    diagonal = jnp.concatenate(
        [jnp.where(left, inner_grad, 0.0), jnp.where(left, 0.0, inner_grad)], axis=0
    ).astype(jnp.bfloat16)
    up_term = adapter_scale * t_dot(inner, g)
    for t in range(count):
        out_ref[t, :down_chunks] = t_dot(xs_ref[t], diagonal).astype(jnp.bfloat16)
        up_part = jnp.concatenate(
            [up_term[8 * t:8 * t + 8, c * LANES:(c + 1) * LANES] for c in range(across)], axis=0
        )
        out_ref[t, down_chunks:] = up_part.astype(jnp.bfloat16)


def scatter_kernel(count, down_chunks, up_chunks, rows_here, rows_core, *rest):
    sources, (down_out, up_out) = rest[:2], rest[4:6]
    pieces, down_sum, up_sum, ordered, arrived, sem = rest[6:]
    half = count // 2
    owned_rows = down_out.shape[0] * 8
    first_row = lax.axis_index("dp") * owned_rows
    across = up_chunks // 8
    rows = [(rows_here if b < half else rows_core)[b % half] - first_row for b in range(count)]
    arriving = [pltpu.make_async_copy(sources[b // half].at[b % half], pieces.at[b], arrived.at[b]) for b in range(count)]
    owned = [(row >= 0) & (row < owned_rows) for row in rows]
    for b in range(count):
        @pl.when(owned[b])
        def _():
            arriving[b].start()

    slots, final = [], []
    for b in range(count):
        slot, last = jnp.int32(b), jnp.bool_(True)
        for e in range(b - 1, -1, -1):
            slot = jnp.where(rows[e] == rows[b], e, slot)
        for e in range(b + 1, count):
            last = last & (rows[e] != rows[b])
        slots.append(slot)
        final.append(last)

    def copies(b):
        return (
            pltpu.make_async_copy(down_sum.at[slots[b]], down_out.at[rows[b] // 8, :, rows[b] % 8, 0], sem),
            pltpu.make_async_copy(up_sum.at[slots[b]], up_out.at[rows[b] // 8, :, rows[b] % 8, 0], sem),
        )

    for b in range(count):
        @pl.when(owned[b])
        def _():
            arriving[b].wait()
            slot = slots[b]
            down = pieces[b, :down_chunks].astype(jnp.float32)
            for c in range(across):
                ordered[pl.ds(c, 8, stride=across), :] = pieces[
                    b, down_chunks + 8 * c:down_chunks + 8 * c + 8
                ].astype(jnp.float32)
            up = ordered[...]

            @pl.when(slot == b)
            def _():
                down_sum[b] = down
                up_sum[b] = up

            @pl.when(slot != b)
            def _():
                down_sum[slot] += down
                up_sum[slot] += up

            @pl.when(final[b])
            def _():
                for copy in copies(b):
                    copy.start()

    for b in range(count):
        @pl.when(owned[b] & final[b])
        def _():
            for copy in copies(b):
                copy.wait()


def base_kernel(*refs):
    whole, halves, w_from, out_refs = refs[:2], refs[2:6], refs[6:-8], refs[-7:-3]
    x_buf, w_buf, sems = refs[-3:]
    outer, rows, depth = whole[0].shape
    width, each = w_from[0].shape[1], outer // 2
    z = lax.axis_index("tensor") // 2
    inside = (z == 1) | (z == 2)
    order = [z, z ^ 1, jnp.where(z < 2, 2, 1), jnp.where(z < 2, 3, 0)]
    pieces = len(w_from) // 2

    def fetch(k, begin):
        columns = pl.ds(k * depth, depth)

        def move(source, place, sem):
            copy = pltpu.make_async_copy(source, place, sem)
            copy.start() if begin else copy.wait()

        for b, ref in enumerate(whole):
            move(ref.at[order[k]], x_buf.at[pl.ds(b * rows, rows), columns], sems.at[k, b])
            for h in range(2):
                @pl.when(order[k] // each == h)
                def _():
                    place = x_buf.at[pl.ds((2 + b) * rows, rows), columns]
                    move(halves[2 * b + h].at[order[k] % each], place, sems.at[k, 2 + b])
        for h in range(2):
            place, sem = w_buf.at[columns, pl.ds(h * width, width)], sems.at[k, 4 + h]
            if k < 3:
                move(w_from[h * pieces + k], place, sem)
                continue

            @pl.when(inside)
            def _():
                move(w_from[h * pieces + k], place, sem)

            @pl.when(jnp.logical_not(inside))
            def _():
                move(w_from[h * pieces + k + 1], place, sem)

    for k in range(outer):
        fetch(k, True)
    total = 0.0
    for first in range(0, outer, each):
        for k in range(first, first + each):
            fetch(k, False)
        columns = slice(first * depth, (first + each) * depth)
        total += dot(x_buf[:, columns], w_buf[columns, :])
    for b, ref in enumerate(out_refs):
        ref[...] = total[b * rows:(b + 1) * rows].astype(ref.dtype)


def fast_body(tokens, cotangent, frozen_value, down_store, up_store, block_adapter, adapter_slot):
    group, parts = lax.axis_size("tensor"), lax.axis_size("parts")
    outer = group // 2
    token_rows = tokens.shape[0]
    slice_width = D // group
    down_chunks = down_store.shape[1] // LANES
    up_chunks = up_store.shape[1] // LANES
    me, part, core = lax.axis_index("tensor"), lax.axis_index("parts"), lax.axis_index("dp")
    z = me // 2

    def exchange(value, s):
        return lax.ppermute(value, "tensor", [(t, t ^ s) for t in range(group)])

    def other_core(value):
        return lax.ppermute(value, "dp", [(0, 1), (1, 0)])

    def other_part(value):
        return lax.ppermute(value, "parts", [(a, parts - 1 - a) for a in range(parts)])

    own = jnp.broadcast_to(block_adapter, (group, 1, LANES))
    asked = lax.all_to_all(own, "tensor", 0, 0)
    split_from, half_from, own = lax.optimization_barrier((tokens, frozen_value, own))

    width = frozen_value.shape[1] // parts
    half = lax.dynamic_slice_in_dim(half_from, part * width, width, axis=1)
    block = jax.ShapeDtypeStruct((outer, token_rows, slice_width), jnp.bfloat16)
    token = jax.ShapeDtypeStruct((1,), jnp.int32)
    some = jax.ShapeDtypeStruct((outer // 2, token_rows, slice_width), jnp.bfloat16)
    x_mine, *x_theirs = pl.pallas_call(
        split_kernel, out_shape=(block, some, some), in_specs=[VMEM], out_specs=[VMEM] * 3,
        name="split_tokens", compiler_params=LIMIT,
    )(split_from)
    x_far = [exchange(x_theirs[0], 1)]
    y_mine = other_part(x_mine)
    xs = pl.pallas_call(
        interleave_kernel,
        out_shape=jax.ShapeDtypeStruct((group, 2 * token_rows, slice_width // 2), jnp.bfloat16),
        in_specs=[VMEM], out_specs=ANY, name="pair_columns", compiler_params=WIDE,
        scratch_shapes=[
            pltpu.VMEM((group, 2 * token_rows, slice_width // 2), jnp.bfloat16),
            pltpu.SemaphoreType.DMA((group,)),
        ],
        cost_estimate=cost(read=128 << 20),
    )(split_from)
    middle = [(t, t ^ 6) for t in range(group) if t // 2 in (1, 2)]
    ends = [(t, t ^ 2) for t in range(group) if t // 2 in (1, 2)]
    near = exchange(half, 2)
    over = lax.ppermute(half, "tensor", middle)
    near, over, asked, x_theirs, xs = lax.optimization_barrier((near, over, asked, x_theirs, xs))
    x_far.append(exchange(x_theirs[1], 1))
    over_near = lax.ppermute(near, "tensor", middle)
    passed = lax.ppermute(over, "tensor", ends)
    pieces = jax.ShapeDtypeStruct((group, down_chunks + up_chunks, LANES), jnp.bfloat16)
    def tiles(store):
        view = store.reshape(store.shape[0] // TILE_ROWS, TILE_ROWS, store.shape[1] // LANES, LANES)
        return view.transpose(0, 2, 1, 3)

    sent, rows = pl.pallas_call(
        gather_kernel,
        out_shape=(pieces, jax.ShapeDtypeStruct((group,), jnp.int32)),
        in_specs=[SMEM, SMEM, ANY, ANY],
        out_specs=(ANY, SMEM),
        scratch_shapes=[
            pltpu.VMEM((group, down_chunks, TILE_ROWS, LANES), jnp.bfloat16),
            pltpu.VMEM((group, up_chunks, TILE_ROWS, LANES), jnp.bfloat16),
            pltpu.VMEM((2, (down_chunks + up_chunks) * 8, LANES), jnp.float32),
            pltpu.VMEM(pieces.shape, jnp.bfloat16),
            pltpu.SemaphoreType.DMA((3, group)),
        ],
        compiler_params=WIDE,
        cost_estimate=cost(read=40 << 20),
        name="pick_panels",
    )(asked, adapter_slot, tiles(down_store), tiles(up_store))
    sent, rows, x_far, y_mine, half, near, over, over_near, passed = lax.optimization_barrier(
        (sent, rows, x_far, y_mine, half, near, over, over_near, passed)
    )
    panels = lax.all_to_all(sent, "tensor", 0, 0)
    rows_core = other_core(rows)
    y_far = [other_part(piece) for piece in x_far]
    passed_near = lax.ppermute(over_near, "tensor", ends)
    owned_groups = ADAPTERS // lax.axis_size("dp") // 8
    down_shape = jax.ShapeDtypeStruct((owned_groups, down_chunks, 8, 1, LANES), jnp.float32)
    up_shape = jax.ShapeDtypeStruct((owned_groups, up_chunks, 8, 1, LANES), jnp.float32)
    def clear(half, inputs, in_specs, aliases):
        return pl.pallas_call(
            functools.partial(zero_kernel, half), out_shape=(down_shape, up_shape, token),
            in_specs=in_specs, out_specs=(ANY, ANY, SMEM), input_output_aliases=aliases,
            scratch_shapes=[pltpu.VMEM((up_chunks, 8, 1, LANES), jnp.float32), pltpu.SemaphoreType.DMA((2,))],
            compiler_params=LIMIT, cost_estimate=cost(read=14 << 20), name="clear_rows",
        )(*inputs)

    down_zero, up_zero, cleared = clear(0, (rows,), [SMEM], {})
    inside = (z == 1) | (z == 2)
    quarter = [half, near, jnp.where(inside, over, passed)]
    quarter_core = [other_core(w) for w in quarter]
    panels, quarter_core = lax.optimization_barrier((panels, quarter_core))

    terms, lifted = pl.pallas_call(
        functools.partial(adapter_kernel, group, down_chunks),
        out_shape=(pieces, jax.ShapeDtypeStruct((token_rows, VALUE_OUTPUTS), jnp.float32)),
        in_specs=[VMEM] * 3 + [SMEM],
        out_specs=(VMEM, VMEM),
        scratch_shapes=[pltpu.VMEM((2 * R, VALUE_OUTPUTS), jnp.float32)],
        compiler_params=LIMIT,
        cost_estimate=cost(flops=3 << 30, read=8 << 20),
        name="adapter",
    )(xs, cotangent, panels, cleared)
    terms, over_near, passed_near, y_far = lax.optimization_barrier((terms, over_near, passed_near, y_far))
    last = [over_near, passed_near]
    quarters = quarter + last + quarter_core + [other_core(w) for w in last]
    sums = [jax.ShapeDtypeStruct((token_rows, parts * width), kind) for kind in (jnp.float32,) + (jnp.bfloat16,) * 3]
    kept, to_part, to_inner, to_both = pl.pallas_call(
        base_kernel,
        out_shape=sums,
        in_specs=[ANY] * (7 + len(quarters)),
        out_specs=[VMEM] * 4,
        scratch_shapes=[
            pltpu.VMEM((4 * token_rows, outer * slice_width), jnp.bfloat16),
            pltpu.VMEM((outer * slice_width, parts * width), jnp.bfloat16),
            pltpu.SemaphoreType.DMA((outer, 6)),
        ],
        compiler_params=WIDE,
        cost_estimate=cost(flops=4 << 30, read=8 << 20),
        name="frozen_part",
    )(x_mine, y_mine, *x_far, *y_far, *quarters, terms)
    opposite = [(a * group + t, (parts - 1 - a) * group + (t ^ 1)) for a in range(parts) for t in range(group)]
    back = lax.all_to_all(terms, "tensor", 0, 0)
    arrived = (exchange(to_inner, 1), other_part(to_part), lax.ppermute(to_both, ("parts", "tensor"), opposite))
    down_zero, up_zero, kept = lax.optimization_barrier((down_zero, up_zero, kept))
    down_zero, up_zero, _ = clear(1, (down_zero, up_zero), [ANY, ANY], {0: 0, 1: 1})
    back, arrived, down_zero, up_zero = lax.optimization_barrier((back, arrived, down_zero, up_zero))
    back_core = other_core(back)

    grad_down, grad_up = pl.pallas_call(
        functools.partial(scatter_kernel, 2 * group, down_chunks, up_chunks),
        out_shape=(down_shape, up_shape),
        in_specs=[SMEM] * 2 + [ANY] * 4,
        out_specs=(ANY, ANY),
        input_output_aliases={4: 0, 5: 1},
        scratch_shapes=[
            pltpu.VMEM((2 * group,) + pieces.shape[1:], jnp.bfloat16),
            pltpu.VMEM((2 * group, down_chunks, LANES), jnp.float32),
            pltpu.VMEM((2 * group, up_chunks, LANES), jnp.float32),
            pltpu.VMEM((up_chunks, LANES), jnp.float32),
            pltpu.SemaphoreType.DMA((2 * group,)),
            pltpu.SemaphoreType.DMA(()),
        ],
        compiler_params=LIMIT,
        cost_estimate=cost(read=16 << 20),
        name="place_rows",
    )(rows, rows_core, back, back_core, down_zero, up_zero)
    grad_down = grad_down.reshape(owned_groups, down_chunks, 8, LANES).transpose(0, 2, 1, 3)
    grad_up = grad_up.reshape(owned_groups, up_chunks, 8, LANES).transpose(0, 2, 1, 3)

    arrived = [a.astype(jnp.float32) for a in arrived]
    kept, got = kept + arrived[0], arrived[1] + arrived[2]
    quarters = [[c[:, :width], c[:, width:]] for c in (kept, got)]

    def pick_quarter(c, a):
        first = quarters[a][0] if c == 0 else quarters[a][1]
        second = quarters[a][1] if c == 0 else quarters[a][0]
        return jnp.where(core == 0, first, second)

    def columns_of(c):
        low, high = pick_quarter(c, 0), pick_quarter(c, 1)
        return jnp.where(part == 0, low, high), jnp.where(part == 0, high, low)

    frozen_output = jnp.concatenate(columns_of(0) + columns_of(1), axis=1)
    mixed = (frozen_output + lifted).astype(jnp.bfloat16)
    return mixed, grad_down.reshape(owned_groups * 8, -1), grad_up.reshape(owned_groups * 8, -1)


def fits(mesh):
    group, cores, parts = mesh.shape["tensor"], mesh.shape["dp"], mesh.shape["parts"]
    return cores == 2 and parts == 2 and group <= 8 and group & (group - 1) == 0 and R == 8 * group


def body(mesh, tokens, *rest):
    block_adapter = rest[4]
    one_block = block_adapter.shape[0] == 1
    return (fast_body if fits(mesh) and one_block else plain_body)(tokens, *rest)


def solution(mesh):
    placed = (
        P(("parts", "dp", "tensor"), None),
        P(("parts", "dp", "tensor"), None),
        P("tensor", "dp"),
        P("parts", "tensor"),
        P("parts", "tensor"),
        P(("parts", "dp", "tensor")),
        P("parts"),
    )
    return jax.shard_map(
        functools.partial(body, mesh),
        mesh=mesh,
        in_specs=placed,
        out_specs=(
            P(("parts", "dp", "tensor"), None),
            P(("parts", "dp"), "tensor"),
            P(("parts", "dp"), "tensor"),
        ),
        check_vma=False,
    )
```

```python
import functools

import jax
import jax.numpy as jnp
from jax import lax
from jax.experimental import pallas as pl
from jax.experimental.pallas import tpu as pltpu
from jax.sharding import PartitionSpec as P

D = 5120
VALUE_OUTPUTS = 1024
R = 64
ADAPTERS = 256
LANES = 128
TILE_ROWS = 8

adapter_scale = 2.0
VMEM = pl.BlockSpec(memory_space=pltpu.VMEM)
SMEM = pl.BlockSpec(memory_space=pltpu.SMEM)
ANY = pl.BlockSpec(memory_space=pl.ANY)
LIMIT = pltpu.CompilerParams(vmem_limit_bytes=16 * 1024 * 1024)
WIDE = pltpu.CompilerParams(vmem_limit_bytes=60 * 1024 * 1024)


def cost(flops=0, read=0):
    return pl.CostEstimate(flops=flops, bytes_accessed=read, transcendentals=0)


def dot(a, b):
    return jnp.dot(a, b, preferred_element_type=jnp.float32)


def dot_t(a, b):
    return lax.dot_general(a, b, (((1,), (1,)), ((), ())), preferred_element_type=jnp.float32)


def t_dot(a, b):
    return lax.dot_general(a, b, (((0,), (0,)), ((), ())), preferred_element_type=jnp.float32)


def fold_rows(left, piece):
    return jnp.dot(left, piece, preferred_element_type=jnp.float32)


def store_rows(requests, adapter_slot):
    table = jnp.arange(adapter_slot.shape[0], dtype=jnp.int32)
    return jnp.sum(jnp.where(requests[:, None] == table[None, :], adapter_slot[None, :], 0), axis=1)


def plain_body(tokens, cotangent, frozen_value, down_store, up_store, block_adapter, adapter_slot):
    token_rows = tokens.shape[0]
    blocks_here = block_adapter.shape[0]
    block_rows = token_rows // blocks_here
    group = lax.axis_size("tensor")
    columns = lax.all_gather(frozen_value, "dp", axis=1, tiled=True)
    frozen_output = fold_rows(tokens, lax.all_gather(columns, "tensor", axis=0, tiled=True))
    requests = lax.all_gather(block_adapter, "tensor", axis=0, tiled=True)
    stored = store_rows(requests, adapter_slot)
    order = stored.reshape(group, blocks_here).T.reshape(-1)
    down_send = jnp.take(down_store, order, axis=0).reshape(blocks_here, group, -1)
    up_send = jnp.take(up_store, order, axis=0).reshape(blocks_here, group, -1)
    down_got = lax.all_to_all(down_send, "tensor", split_axis=1, concat_axis=1, tiled=True)
    up_got = lax.all_to_all(up_send, "tensor", split_axis=1, concat_axis=1, tiled=True)
    down_panel = down_got.reshape(blocks_here, D, R)
    up_panel = up_got.reshape(blocks_here, R, VALUE_OUTPUTS)
    token_blocks = tokens.reshape(blocks_here, block_rows, D)
    grad_blocks = cotangent.reshape(blocks_here, block_rows, VALUE_OUTPUTS)
    down_projected = jnp.einsum(
        "jtd,jdr->jtr", token_blocks, down_panel, preferred_element_type=jnp.float32
    ).astype(jnp.bfloat16)
    up_projected = jnp.einsum(
        "jtr,jrk->jtk", down_projected, up_panel, preferred_element_type=jnp.float32
    )
    mixed = (
        frozen_output + adapter_scale * up_projected.reshape(token_rows, VALUE_OUTPUTS)
    ).astype(jnp.bfloat16)
    down_projected_gradient = (
        adapter_scale
        * jnp.einsum("jtk,jrk->jtr", grad_blocks, up_panel, preferred_element_type=jnp.float32)
    ).astype(jnp.bfloat16)
    down_term = jnp.einsum(
        "jtd,jtr->jdr", token_blocks, down_projected_gradient, preferred_element_type=jnp.float32
    )
    up_weight_gradient = adapter_scale * jnp.einsum(
        "jtr,jtk->jrk", down_projected, grad_blocks, preferred_element_type=jnp.float32
    )
    down_back = lax.all_to_all(
        down_term.reshape(blocks_here, group, -1), "tensor", split_axis=1, concat_axis=1, tiled=True
    )
    up_back = lax.all_to_all(
        up_weight_gradient.reshape(blocks_here, group, -1), "tensor", split_axis=1, concat_axis=1, tiled=True
    )
    down_flat = down_back.reshape(blocks_here * group, -1)
    up_flat = up_back.reshape(blocks_here * group, -1)
    down_table = jax.ops.segment_sum(down_flat, order, num_segments=ADAPTERS)
    up_table = jax.ops.segment_sum(up_flat, order, num_segments=ADAPTERS)
    grad_down = lax.psum_scatter(down_table, "dp", scatter_dimension=0, tiled=True)
    grad_up = lax.psum_scatter(up_table, "dp", scatter_dimension=0, tiled=True)
    return mixed, grad_down, grad_up


def split_kernel(x_ref, mine_ref, *theirs_refs):
    inner = lax.axis_index("tensor") % 2
    outer, rows, width = mine_ref.shape
    each = outer // len(theirs_refs)
    for k in range(outer):
        own = pl.multiple_of((2 * k + inner) * width, LANES)
        other = pl.multiple_of((2 * k + 1 - inner) * width, LANES)
        mine_ref[k] = x_ref[:, pl.ds(own, width)]
        theirs_refs[k // each][k % each] = x_ref[:, pl.ds(other, width)]


def interleave_kernel(x_ref, out_ref, xs_ref, sems):
    group, rows2, half = xs_ref.shape
    leave = [pltpu.make_async_copy(xs_ref.at[k], out_ref.at[k], sems.at[k]) for k in range(group)]
    rows, width = rows2 // 2, 2 * half
    source = lax.broadcasted_iota(jnp.int32, (width, half), 0)
    target = lax.broadcasted_iota(jnp.int32, (width, half), 1)
    even = (source == 2 * target).astype(jnp.bfloat16)
    odd = (source == 2 * target + 1).astype(jnp.bfloat16)
    for k in range(group):
        x = x_ref[:, k * width:(k + 1) * width]
        xs_ref[k, :rows] = dot(x, even).astype(jnp.bfloat16)
        xs_ref[k, rows:] = dot(x, odd).astype(jnp.bfloat16)
        leave[k].start()
    for copy in leave:
        copy.wait()


def gather_kernel(asked, slot_of, down_ref, up_ref, out_ref, rows_ref, down_buf, up_buf, flats, built, sems):
    count, down_chunks, up_chunks = down_buf.shape[0], down_buf.shape[1], up_buf.shape[1]
    across = up_chunks // 8

    def copies(t):
        tile = slot_of[asked[t, 0, 0]] // TILE_ROWS
        return (
            pltpu.make_async_copy(down_ref.at[tile], down_buf.at[t], sems.at[0, t]),
            pltpu.make_async_copy(up_ref.at[tile], up_buf.at[t], sems.at[1, t]),
            pltpu.make_async_copy(built.at[t], out_ref.at[t], sems.at[2, t]),
        )

    for t in range(count):
        down, up, _ = copies(t)
        down.start()
        up.start()
        rows_ref[t] = slot_of[asked[t, 0, 0]]

    def one(t, flat):
        down, up, leave = copies(t)
        up.wait()
        for j in range(up_chunks):
            place = down_chunks + (j % across) * 8 + j // across
            flat[place * 8:place * 8 + 8, :] = up_buf[t, j].astype(jnp.float32)
        down.wait()
        for j in range(down_chunks):
            flat[j * 8:j * 8 + 8, :] = down_buf[t, j].astype(jnp.float32)
        sub = slot_of[asked[t, 0, 0]] % TILE_ROWS
        built[t] = flat[pl.ds(sub, down_chunks + up_chunks, stride=8), :].astype(jnp.bfloat16)
        leave.start()

    def two(i, carry):
        for u in range(2):
            one(2 * i + u, flats.at[u])
        return carry

    lax.fori_loop(0, count // 2, two, 0)
    for t in range(count):
        copies(t)[2].wait()


def zero_kernel(half, *refs):
    down_ref, up_ref, done_ref, zeros, sems = refs[-5:]
    done_ref[0] = 0
    zeros[...] = jnp.zeros_like(zeros)
    part = zeros.shape[0]
    groups = down_ref.shape[0] // 2
    copies = []
    for ref, sem in ((down_ref, sems.at[0]), (up_ref, sems.at[1])):
        for g in range(half * groups, (half + 1) * groups):
            for c in range(ref.shape[1] // part):
                copies.append(pltpu.make_async_copy(zeros, ref.at[g, pl.ds(c * part, part)], sem))
    for c in copies:
        c.start()
    for c in copies:
        c.wait()


def adapter_kernel(count, down_chunks, xs_ref, g_ref, pieces, _, out_ref, lifted_ref, up_panel):
    rows = g_ref.shape[0]
    across = g_ref.shape[1] // LANES
    total = jnp.zeros((2 * rows, LANES), jnp.float32)
    for t in range(count):
        total += dot(xs_ref[t], pieces[t, :down_chunks])
        for c in range(across):
            block = pieces[t, down_chunks + 8 * c:down_chunks + 8 * c + 8, :].astype(jnp.float32)
            up_panel[8 * t:8 * t + 8, c * LANES:(c + 1) * LANES] = block
            up_panel[R + 8 * t:R + 8 * t + 8, c * LANES:(c + 1) * LANES] = block
    panel = up_panel[...].astype(jnp.bfloat16)
    left = lax.broadcasted_iota(jnp.int32, (rows, LANES), 1) < R
    inner = total[:rows] + pltpu.roll(total[rows:], R, 1)
    inner = jnp.where(left, inner, 0.0).astype(jnp.bfloat16)
    g = g_ref[...]
    lifted_ref[...] = adapter_scale * dot(inner, panel)
    inner_grad = adapter_scale * dot_t(g, panel)
    diagonal = jnp.concatenate(
        [jnp.where(left, inner_grad, 0.0), jnp.where(left, 0.0, inner_grad)], axis=0
    ).astype(jnp.bfloat16)
    up_term = adapter_scale * t_dot(inner, g)
    for t in range(count):
        out_ref[t, :down_chunks] = t_dot(xs_ref[t], diagonal).astype(jnp.bfloat16)
        up_part = jnp.concatenate(
            [up_term[8 * t:8 * t + 8, c * LANES:(c + 1) * LANES] for c in range(across)], axis=0
        )
        out_ref[t, down_chunks:] = up_part.astype(jnp.bfloat16)


def scatter_kernel(count, down_chunks, up_chunks, rows_here, rows_core, *rest):
    sources, (down_out, up_out) = rest[:2], rest[4:6]
    pieces, down_sum, up_sum, ordered, arrived, sem = rest[6:]
    half = count // 2
    owned_rows = down_out.shape[0] * 8
    first_row = lax.axis_index("dp") * owned_rows
    across = up_chunks // 8
    rows = [(rows_here if b < half else rows_core)[b % half] - first_row for b in range(count)]
    arriving = [pltpu.make_async_copy(sources[b // half].at[b % half], pieces.at[b], arrived.at[b]) for b in range(count)]
    owned = [(row >= 0) & (row < owned_rows) for row in rows]
    for b in range(count):
        @pl.when(owned[b])
        def _():
            arriving[b].start()

    slots, final = [], []
    for b in range(count):
        slot, last = jnp.int32(b), jnp.bool_(True)
        for e in range(b - 1, -1, -1):
            slot = jnp.where(rows[e] == rows[b], e, slot)
        for e in range(b + 1, count):
            last = last & (rows[e] != rows[b])
        slots.append(slot)
        final.append(last)

    def copies(b):
        return (
            pltpu.make_async_copy(down_sum.at[slots[b]], down_out.at[rows[b] // 8, :, rows[b] % 8, 0], sem),
            pltpu.make_async_copy(up_sum.at[slots[b]], up_out.at[rows[b] // 8, :, rows[b] % 8, 0], sem),
        )

    for b in range(count):
        @pl.when(owned[b])
        def _():
            arriving[b].wait()
            slot = slots[b]
            down = pieces[b, :down_chunks].astype(jnp.float32)
            for c in range(across):
                ordered[pl.ds(c, 8, stride=across), :] = pieces[
                    b, down_chunks + 8 * c:down_chunks + 8 * c + 8
                ].astype(jnp.float32)
            up = ordered[...]

            @pl.when(slot == b)
            def _():
                down_sum[b] = down
                up_sum[b] = up

            @pl.when(slot != b)
            def _():
                down_sum[slot] += down
                up_sum[slot] += up

            @pl.when(final[b])
            def _():
                for copy in copies(b):
                    copy.start()

    for b in range(count):
        @pl.when(owned[b] & final[b])
        def _():
            for copy in copies(b):
                copy.wait()


def base_kernel(*refs):
    whole, halves, w_from, out_refs = refs[:2], refs[2:6], refs[6:-8], refs[-7:-3]
    x_buf, w_buf, sems = refs[-3:]
    outer, rows, depth = whole[0].shape
    width, each = w_from[0].shape[1], outer // 2
    z = lax.axis_index("tensor") // 2
    inside = (z == 1) | (z == 2)
    order = [z, z ^ 1, jnp.where(z < 2, 2, 1), jnp.where(z < 2, 3, 0)]
    pieces = len(w_from) // 2

    def fetch(k, begin):
        columns = pl.ds(k * depth, depth)

        def move(source, place, sem):
            copy = pltpu.make_async_copy(source, place, sem)
            copy.start() if begin else copy.wait()

        for b, ref in enumerate(whole):
            move(ref.at[order[k]], x_buf.at[pl.ds(b * rows, rows), columns], sems.at[k, b])
            for h in range(2):
                @pl.when(order[k] // each == h)
                def _():
                    place = x_buf.at[pl.ds((2 + b) * rows, rows), columns]
                    move(halves[2 * b + h].at[order[k] % each], place, sems.at[k, 2 + b])
        for h in range(2):
            place, sem = w_buf.at[columns, pl.ds(h * width, width)], sems.at[k, 4 + h]
            if k < 3:
                move(w_from[h * pieces + k], place, sem)
                continue

            @pl.when(inside)
            def _():
                move(w_from[h * pieces + k], place, sem)

            @pl.when(jnp.logical_not(inside))
            def _():
                move(w_from[h * pieces + k + 1], place, sem)

    for k in range(outer):
        fetch(k, True)
    total = 0.0
    for first in range(0, outer, each):
        for k in range(first, first + each):
            fetch(k, False)
        columns = slice(first * depth, (first + each) * depth)
        total += dot(x_buf[:, columns], w_buf[columns, :])
    for b, ref in enumerate(out_refs):
        ref[...] = total[b * rows:(b + 1) * rows].astype(ref.dtype)


def fast_body(tokens, cotangent, frozen_value, down_store, up_store, block_adapter, adapter_slot):
    group, parts = lax.axis_size("tensor"), lax.axis_size("parts")
    outer = group // 2
    token_rows = tokens.shape[0]
    slice_width = D // group
    down_chunks = down_store.shape[1] // LANES
    up_chunks = up_store.shape[1] // LANES
    me, part, core = lax.axis_index("tensor"), lax.axis_index("parts"), lax.axis_index("dp")
    z = me // 2

    def exchange(value, s):
        return lax.ppermute(value, "tensor", [(t, t ^ s) for t in range(group)])

    def other_core(value):
        return lax.ppermute(value, "dp", [(0, 1), (1, 0)])

    def other_part(value):
        return lax.ppermute(value, "parts", [(a, parts - 1 - a) for a in range(parts)])

    own = jnp.broadcast_to(block_adapter, (group, 1, LANES))
    asked = lax.all_to_all(own, "tensor", 0, 0)
    split_from, half_from, own = lax.optimization_barrier((tokens, frozen_value, own))

    width = frozen_value.shape[1] // parts
    half = lax.dynamic_slice_in_dim(half_from, part * width, width, axis=1)
    block = jax.ShapeDtypeStruct((outer, token_rows, slice_width), jnp.bfloat16)
    token = jax.ShapeDtypeStruct((1,), jnp.int32)
    some = jax.ShapeDtypeStruct((outer // 2, token_rows, slice_width), jnp.bfloat16)
    x_mine, *x_theirs = pl.pallas_call(
        split_kernel, out_shape=(block, some, some), in_specs=[VMEM], out_specs=[VMEM] * 3,
        name="split_tokens", compiler_params=LIMIT,
    )(split_from)
    x_far = [exchange(x_theirs[0], 1)]
    y_mine = other_part(x_mine)
    xs = pl.pallas_call(
        interleave_kernel,
        out_shape=jax.ShapeDtypeStruct((group, 2 * token_rows, slice_width // 2), jnp.bfloat16),
        in_specs=[VMEM], out_specs=ANY, name="pair_columns", compiler_params=WIDE,
        scratch_shapes=[
            pltpu.VMEM((group, 2 * token_rows, slice_width // 2), jnp.bfloat16),
            pltpu.SemaphoreType.DMA((group,)),
        ],
        cost_estimate=cost(read=128 << 20),
    )(split_from)
    middle = [(t, t ^ 6) for t in range(group) if t // 2 in (1, 2)]
    ends = [(t, t ^ 2) for t in range(group) if t // 2 in (1, 2)]
    near = exchange(half, 2)
    over = lax.ppermute(half, "tensor", middle)
    near, over, asked, x_theirs, xs = lax.optimization_barrier((near, over, asked, x_theirs, xs))
    x_far.append(exchange(x_theirs[1], 1))
    over_near = lax.ppermute(near, "tensor", middle)
    passed = lax.ppermute(over, "tensor", ends)
    pieces = jax.ShapeDtypeStruct((group, down_chunks + up_chunks, LANES), jnp.bfloat16)
    def tiles(store):
        view = store.reshape(store.shape[0] // TILE_ROWS, TILE_ROWS, store.shape[1] // LANES, LANES)
        return view.transpose(0, 2, 1, 3)

    sent, rows = pl.pallas_call(
        gather_kernel,
        out_shape=(pieces, jax.ShapeDtypeStruct((group,), jnp.int32)),
        in_specs=[SMEM, SMEM, ANY, ANY],
        out_specs=(ANY, SMEM),
        scratch_shapes=[
            pltpu.VMEM((group, down_chunks, TILE_ROWS, LANES), jnp.bfloat16),
            pltpu.VMEM((group, up_chunks, TILE_ROWS, LANES), jnp.bfloat16),
            pltpu.VMEM((2, (down_chunks + up_chunks) * 8, LANES), jnp.float32),
            pltpu.VMEM(pieces.shape, jnp.bfloat16),
            pltpu.SemaphoreType.DMA((3, group)),
        ],
        compiler_params=WIDE,
        cost_estimate=cost(read=40 << 20),
        name="pick_panels",
    )(asked, adapter_slot, tiles(down_store), tiles(up_store))
    rows_core = other_core(rows)
    sent, rows, rows_core, x_far, y_mine, half, near, over, over_near, passed = lax.optimization_barrier(
        (sent, rows, rows_core, x_far, y_mine, half, near, over, over_near, passed)
    )
    panels = lax.all_to_all(sent, "tensor", 0, 0)
    y_far = [other_part(piece) for piece in x_far]
    passed_near = lax.ppermute(over_near, "tensor", ends)
    owned_groups = ADAPTERS // lax.axis_size("dp") // 8
    down_shape = jax.ShapeDtypeStruct((owned_groups, down_chunks, 8, 1, LANES), jnp.float32)
    up_shape = jax.ShapeDtypeStruct((owned_groups, up_chunks, 8, 1, LANES), jnp.float32)
    def clear(half, inputs, in_specs, aliases):
        return pl.pallas_call(
            functools.partial(zero_kernel, half), out_shape=(down_shape, up_shape, token),
            in_specs=in_specs, out_specs=(ANY, ANY, SMEM), input_output_aliases=aliases,
            scratch_shapes=[pltpu.VMEM((up_chunks, 8, 1, LANES), jnp.float32), pltpu.SemaphoreType.DMA((2,))],
            compiler_params=LIMIT, cost_estimate=cost(read=14 << 20), name="clear_rows",
        )(*inputs)

    down_zero, up_zero, cleared = clear(0, (rows,), [SMEM], {})
    inside = (z == 1) | (z == 2)
    quarter = [half, near, jnp.where(inside, over, passed)]
    quarter_core = [other_core(w) for w in quarter]
    panels, quarter_core = lax.optimization_barrier((panels, quarter_core))

    terms, lifted = pl.pallas_call(
        functools.partial(adapter_kernel, group, down_chunks),
        out_shape=(pieces, jax.ShapeDtypeStruct((token_rows, VALUE_OUTPUTS), jnp.float32)),
        in_specs=[VMEM] * 3 + [SMEM],
        out_specs=(VMEM, VMEM),
        scratch_shapes=[pltpu.VMEM((2 * R, VALUE_OUTPUTS), jnp.float32)],
        compiler_params=LIMIT,
        cost_estimate=cost(flops=3 << 30, read=8 << 20),
        name="adapter",
    )(xs, cotangent, panels, cleared)
    terms, over_near, passed_near, y_far = lax.optimization_barrier((terms, over_near, passed_near, y_far))
    last = [over_near, passed_near]
    quarters = quarter + last + quarter_core + [other_core(w) for w in last]
    sums = [jax.ShapeDtypeStruct((token_rows, parts * width), kind) for kind in (jnp.float32,) + (jnp.bfloat16,) * 3]
    kept, to_part, to_inner, to_both = pl.pallas_call(
        base_kernel,
        out_shape=sums,
        in_specs=[ANY] * (7 + len(quarters)),
        out_specs=[VMEM] * 4,
        scratch_shapes=[
            pltpu.VMEM((4 * token_rows, outer * slice_width), jnp.bfloat16),
            pltpu.VMEM((outer * slice_width, parts * width), jnp.bfloat16),
            pltpu.SemaphoreType.DMA((outer, 6)),
        ],
        compiler_params=WIDE,
        cost_estimate=cost(flops=4 << 30, read=8 << 20),
        name="frozen_part",
    )(x_mine, y_mine, *x_far, *y_far, *quarters, terms)
    opposite = [(a * group + t, (parts - 1 - a) * group + (t ^ 1)) for a in range(parts) for t in range(group)]
    back = lax.all_to_all(terms, "tensor", 0, 0)
    arrived = (exchange(to_inner, 1), other_part(to_part), lax.ppermute(to_both, ("parts", "tensor"), opposite))
    down_zero, up_zero, kept = lax.optimization_barrier((down_zero, up_zero, kept))
    down_zero, up_zero, _ = clear(1, (down_zero, up_zero), [ANY, ANY], {0: 0, 1: 1})
    back, arrived, down_zero, up_zero = lax.optimization_barrier((back, arrived, down_zero, up_zero))
    back_core = other_core(back)

    grad_down, grad_up = pl.pallas_call(
        functools.partial(scatter_kernel, 2 * group, down_chunks, up_chunks),
        out_shape=(down_shape, up_shape),
        in_specs=[SMEM] * 2 + [ANY] * 4,
        out_specs=(ANY, ANY),
        input_output_aliases={4: 0, 5: 1},
        scratch_shapes=[
            pltpu.VMEM((2 * group,) + pieces.shape[1:], jnp.bfloat16),
            pltpu.VMEM((2 * group, down_chunks, LANES), jnp.float32),
            pltpu.VMEM((2 * group, up_chunks, LANES), jnp.float32),
            pltpu.VMEM((up_chunks, LANES), jnp.float32),
            pltpu.SemaphoreType.DMA((2 * group,)),
            pltpu.SemaphoreType.DMA(()),
        ],
        compiler_params=LIMIT,
        cost_estimate=cost(read=16 << 20),
        name="place_rows",
    )(rows, rows_core, back, back_core, down_zero, up_zero)
    grad_down = grad_down.reshape(owned_groups, down_chunks, 8, LANES).transpose(0, 2, 1, 3)
    grad_up = grad_up.reshape(owned_groups, up_chunks, 8, LANES).transpose(0, 2, 1, 3)

    arrived = [a.astype(jnp.float32) for a in arrived]
    kept, got = kept + arrived[0], arrived[1] + arrived[2]
    quarters = [[c[:, :width], c[:, width:]] for c in (kept, got)]

    def pick_quarter(c, a):
        first = quarters[a][0] if c == 0 else quarters[a][1]
        second = quarters[a][1] if c == 0 else quarters[a][0]
        return jnp.where(core == 0, first, second)

    def columns_of(c):
        low, high = pick_quarter(c, 0), pick_quarter(c, 1)
        return jnp.where(part == 0, low, high), jnp.where(part == 0, high, low)

    frozen_output = jnp.concatenate(columns_of(0) + columns_of(1), axis=1)
    mixed = (frozen_output + lifted).astype(jnp.bfloat16)
    return mixed, grad_down.reshape(owned_groups * 8, -1), grad_up.reshape(owned_groups * 8, -1)


def fits(mesh):
    group, cores, parts = mesh.shape["tensor"], mesh.shape["dp"], mesh.shape["parts"]
    return cores == 2 and parts == 2 and group <= 8 and group & (group - 1) == 0 and R == 8 * group


def body(mesh, tokens, *rest):
    block_adapter = rest[4]
    one_block = block_adapter.shape[0] == 1
    return (fast_body if fits(mesh) and one_block else plain_body)(tokens, *rest)


def solution(mesh):
    placed = (
        P(("parts", "dp", "tensor"), None),
        P(("parts", "dp", "tensor"), None),
        P("tensor", "dp"),
        P("parts", "tensor"),
        P("parts", "tensor"),
        P(("parts", "dp", "tensor")),
        P("parts"),
    )
    return jax.shard_map(
        functools.partial(body, mesh),
        mesh=mesh,
        in_specs=placed,
        out_specs=(
            P(("parts", "dp", "tensor"), None),
            P(("parts", "dp"), "tensor"),
            P(("parts", "dp"), "tensor"),
        ),
        check_vma=False,
    )
```

```python
import functools

import jax
import jax.numpy as jnp
from jax import lax
from jax.experimental import pallas as pl
from jax.experimental.pallas import tpu as pltpu
from jax.sharding import PartitionSpec as P

D = 5120
VALUE_OUTPUTS = 1024
R = 64
ADAPTERS = 256
LANES = 128
TILE_ROWS = 8

adapter_scale = 2.0
VMEM = pl.BlockSpec(memory_space=pltpu.VMEM)
SMEM = pl.BlockSpec(memory_space=pltpu.SMEM)
ANY = pl.BlockSpec(memory_space=pl.ANY)
LIMIT = pltpu.CompilerParams(vmem_limit_bytes=16 * 1024 * 1024)
WIDE = pltpu.CompilerParams(vmem_limit_bytes=60 * 1024 * 1024)


def cost(flops=0, read=0):
    return pl.CostEstimate(flops=flops, bytes_accessed=read, transcendentals=0)


def dot(a, b):
    return jnp.dot(a, b, preferred_element_type=jnp.float32)


def dot_t(a, b):
    return lax.dot_general(a, b, (((1,), (1,)), ((), ())), preferred_element_type=jnp.float32)


def t_dot(a, b):
    return lax.dot_general(a, b, (((0,), (0,)), ((), ())), preferred_element_type=jnp.float32)


def fold_rows(left, piece):
    return jnp.dot(left, piece, preferred_element_type=jnp.float32)


def store_rows(requests, adapter_slot):
    table = jnp.arange(adapter_slot.shape[0], dtype=jnp.int32)
    return jnp.sum(jnp.where(requests[:, None] == table[None, :], adapter_slot[None, :], 0), axis=1)


def plain_body(tokens, cotangent, frozen_value, down_store, up_store, block_adapter, adapter_slot):
    token_rows = tokens.shape[0]
    blocks_here = block_adapter.shape[0]
    block_rows = token_rows // blocks_here
    group = lax.axis_size("tensor")
    columns = lax.all_gather(frozen_value, "dp", axis=1, tiled=True)
    frozen_output = fold_rows(tokens, lax.all_gather(columns, "tensor", axis=0, tiled=True))
    requests = lax.all_gather(block_adapter, "tensor", axis=0, tiled=True)
    stored = store_rows(requests, adapter_slot)
    order = stored.reshape(group, blocks_here).T.reshape(-1)
    down_send = jnp.take(down_store, order, axis=0).reshape(blocks_here, group, -1)
    up_send = jnp.take(up_store, order, axis=0).reshape(blocks_here, group, -1)
    down_got = lax.all_to_all(down_send, "tensor", split_axis=1, concat_axis=1, tiled=True)
    up_got = lax.all_to_all(up_send, "tensor", split_axis=1, concat_axis=1, tiled=True)
    down_panel = down_got.reshape(blocks_here, D, R)
    up_panel = up_got.reshape(blocks_here, R, VALUE_OUTPUTS)
    token_blocks = tokens.reshape(blocks_here, block_rows, D)
    grad_blocks = cotangent.reshape(blocks_here, block_rows, VALUE_OUTPUTS)
    down_projected = jnp.einsum(
        "jtd,jdr->jtr", token_blocks, down_panel, preferred_element_type=jnp.float32
    ).astype(jnp.bfloat16)
    up_projected = jnp.einsum(
        "jtr,jrk->jtk", down_projected, up_panel, preferred_element_type=jnp.float32
    )
    mixed = (
        frozen_output + adapter_scale * up_projected.reshape(token_rows, VALUE_OUTPUTS)
    ).astype(jnp.bfloat16)
    down_projected_gradient = (
        adapter_scale
        * jnp.einsum("jtk,jrk->jtr", grad_blocks, up_panel, preferred_element_type=jnp.float32)
    ).astype(jnp.bfloat16)
    down_term = jnp.einsum(
        "jtd,jtr->jdr", token_blocks, down_projected_gradient, preferred_element_type=jnp.float32
    )
    up_weight_gradient = adapter_scale * jnp.einsum(
        "jtr,jtk->jrk", down_projected, grad_blocks, preferred_element_type=jnp.float32
    )
    down_back = lax.all_to_all(
        down_term.reshape(blocks_here, group, -1), "tensor", split_axis=1, concat_axis=1, tiled=True
    )
    up_back = lax.all_to_all(
        up_weight_gradient.reshape(blocks_here, group, -1), "tensor", split_axis=1, concat_axis=1, tiled=True
    )
    down_flat = down_back.reshape(blocks_here * group, -1)
    up_flat = up_back.reshape(blocks_here * group, -1)
    down_table = jax.ops.segment_sum(down_flat, order, num_segments=ADAPTERS)
    up_table = jax.ops.segment_sum(up_flat, order, num_segments=ADAPTERS)
    grad_down = lax.psum_scatter(down_table, "dp", scatter_dimension=0, tiled=True)
    grad_up = lax.psum_scatter(up_table, "dp", scatter_dimension=0, tiled=True)
    return mixed, grad_down, grad_up


def split_kernel(x_ref, mine_ref, *theirs_refs):
    inner = lax.axis_index("tensor") % 2
    outer, rows, width = mine_ref.shape
    each = outer // len(theirs_refs)
    for k in range(outer):
        own = pl.multiple_of((2 * k + inner) * width, LANES)
        other = pl.multiple_of((2 * k + 1 - inner) * width, LANES)
        mine_ref[k] = x_ref[:, pl.ds(own, width)]
        theirs_refs[k // each][k % each] = x_ref[:, pl.ds(other, width)]


def interleave_kernel(x_ref, out_ref, xs_ref, sems):
    group, rows2, half = xs_ref.shape
    leave = [pltpu.make_async_copy(xs_ref.at[k], out_ref.at[k], sems.at[k]) for k in range(group)]
    rows, width = rows2 // 2, 2 * half
    source = lax.broadcasted_iota(jnp.int32, (width, half), 0)
    target = lax.broadcasted_iota(jnp.int32, (width, half), 1)
    even = (source == 2 * target).astype(jnp.bfloat16)
    odd = (source == 2 * target + 1).astype(jnp.bfloat16)
    for k in range(group):
        x = x_ref[:, k * width:(k + 1) * width]
        xs_ref[k, :rows] = dot(x, even).astype(jnp.bfloat16)
        xs_ref[k, rows:] = dot(x, odd).astype(jnp.bfloat16)
        leave[k].start()
    for copy in leave:
        copy.wait()


def gather_kernel(asked, slot_of, down_ref, up_ref, out_ref, rows_ref, down_buf, up_buf, flats, built, sems):
    count, down_chunks, up_chunks = down_buf.shape[0], down_buf.shape[1], up_buf.shape[1]
    across = up_chunks // 8

    def copies(t):
        tile = slot_of[asked[t, 0, 0]] // TILE_ROWS
        return (
            pltpu.make_async_copy(down_ref.at[tile], down_buf.at[t], sems.at[0, t]),
            pltpu.make_async_copy(up_ref.at[tile], up_buf.at[t], sems.at[1, t]),
            pltpu.make_async_copy(built.at[t], out_ref.at[t], sems.at[2, t]),
        )

    for t in range(count):
        down, up, _ = copies(t)
        down.start()
        up.start()
        rows_ref[t] = slot_of[asked[t, 0, 0]]

    def one(t, flat):
        down, up, leave = copies(t)
        up.wait()
        for j in range(up_chunks):
            place = down_chunks + (j % across) * 8 + j // across
            flat[place * 8:place * 8 + 8, :] = up_buf[t, j].astype(jnp.float32)
        down.wait()
        for j in range(down_chunks):
            flat[j * 8:j * 8 + 8, :] = down_buf[t, j].astype(jnp.float32)
        sub = slot_of[asked[t, 0, 0]] % TILE_ROWS
        built[t] = flat[pl.ds(sub, down_chunks + up_chunks, stride=8), :].astype(jnp.bfloat16)
        leave.start()

    def two(i, carry):
        for u in range(2):
            one(2 * i + u, flats.at[u])
        return carry

    lax.fori_loop(0, count // 2, two, 0)
    for t in range(count):
        copies(t)[2].wait()


def zero_kernel(half, *refs):
    down_ref, up_ref, done_ref, zeros, sems = refs[-5:]
    done_ref[0] = 0
    zeros[...] = jnp.zeros_like(zeros)
    part = zeros.shape[0]
    groups = down_ref.shape[0] // 2
    copies = []
    for ref, sem in ((down_ref, sems.at[0]), (up_ref, sems.at[1])):
        for g in range(half * groups, (half + 1) * groups):
            for c in range(ref.shape[1] // part):
                copies.append(pltpu.make_async_copy(zeros, ref.at[g, pl.ds(c * part, part)], sem))
    for c in copies:
        c.start()
    for c in copies:
        c.wait()


def adapter_kernel(count, down_chunks, xs_ref, g_ref, pieces, _, out_ref, lifted_ref, up_panel):
    rows = g_ref.shape[0]
    across = g_ref.shape[1] // LANES
    total = jnp.zeros((2 * rows, LANES), jnp.float32)
    for t in range(count):
        total += dot(xs_ref[t], pieces[t, :down_chunks])
        for c in range(across):
            block = pieces[t, down_chunks + 8 * c:down_chunks + 8 * c + 8, :].astype(jnp.float32)
            up_panel[8 * t:8 * t + 8, c * LANES:(c + 1) * LANES] = block
            up_panel[R + 8 * t:R + 8 * t + 8, c * LANES:(c + 1) * LANES] = block
    panel = up_panel[...].astype(jnp.bfloat16)
    left = lax.broadcasted_iota(jnp.int32, (rows, LANES), 1) < R
    inner = total[:rows] + pltpu.roll(total[rows:], R, 1)
    inner = jnp.where(left, inner, 0.0).astype(jnp.bfloat16)
    g = g_ref[...]
    lifted_ref[...] = adapter_scale * dot(inner, panel)
    inner_grad = adapter_scale * dot_t(g, panel)
    diagonal = jnp.concatenate(
        [jnp.where(left, inner_grad, 0.0), jnp.where(left, 0.0, inner_grad)], axis=0
    ).astype(jnp.bfloat16)
    up_term = adapter_scale * t_dot(inner, g)
    for t in range(count):
        out_ref[t, :down_chunks] = t_dot(xs_ref[t], diagonal).astype(jnp.bfloat16)
        up_part = jnp.concatenate(
            [up_term[8 * t:8 * t + 8, c * LANES:(c + 1) * LANES] for c in range(across)], axis=0
        )
        out_ref[t, down_chunks:] = up_part.astype(jnp.bfloat16)


def scatter_kernel(count, down_chunks, up_chunks, rows_here, rows_core, *rest):
    sources, (down_out, up_out) = rest[:2], rest[4:6]
    pieces, down_sum, up_sum, ordered, arrived, sem = rest[6:]
    half = count // 2
    owned_rows = down_out.shape[0] * 8
    first_row = lax.axis_index("dp") * owned_rows
    across = up_chunks // 8
    rows = [(rows_here if b < half else rows_core)[b % half] - first_row for b in range(count)]
    arriving = [pltpu.make_async_copy(sources[b // half].at[b % half], pieces.at[b], arrived.at[b]) for b in range(count)]
    owned = [(row >= 0) & (row < owned_rows) for row in rows]
    for b in range(count):
        @pl.when(owned[b])
        def _():
            arriving[b].start()

    slots, final = [], []
    for b in range(count):
        slot, last = jnp.int32(b), jnp.bool_(True)
        for e in range(b - 1, -1, -1):
            slot = jnp.where(rows[e] == rows[b], e, slot)
        for e in range(b + 1, count):
            last = last & (rows[e] != rows[b])
        slots.append(slot)
        final.append(last)

    def copies(b):
        return (
            pltpu.make_async_copy(down_sum.at[slots[b]], down_out.at[rows[b] // 8, :, rows[b] % 8, 0], sem),
            pltpu.make_async_copy(up_sum.at[slots[b]], up_out.at[rows[b] // 8, :, rows[b] % 8, 0], sem),
        )

    for b in range(count):
        @pl.when(owned[b])
        def _():
            arriving[b].wait()
            slot = slots[b]
            down = pieces[b, :down_chunks].astype(jnp.float32)
            for c in range(across):
                ordered[pl.ds(c, 8, stride=across), :] = pieces[
                    b, down_chunks + 8 * c:down_chunks + 8 * c + 8
                ].astype(jnp.float32)
            up = ordered[...]

            @pl.when(slot == b)
            def _():
                down_sum[b] = down
                up_sum[b] = up

            @pl.when(slot != b)
            def _():
                down_sum[slot] += down
                up_sum[slot] += up

            @pl.when(final[b])
            def _():
                for copy in copies(b):
                    copy.start()

    for b in range(count):
        @pl.when(owned[b] & final[b])
        def _():
            for copy in copies(b):
                copy.wait()


def base_kernel(*refs):
    whole, halves, w_from, out_refs = refs[:2], refs[2:6], refs[6:-8], refs[-7:-3]
    x_buf, w_buf, sems = refs[-3:]
    outer, rows, depth = whole[0].shape
    width, each = w_from[0].shape[1], outer // 2
    z = lax.axis_index("tensor") // 2
    inside = (z == 1) | (z == 2)
    order = [z, z ^ 1, jnp.where(z < 2, 2, 1), jnp.where(z < 2, 3, 0)]
    pieces = len(w_from) // 2

    def fetch(k, begin):
        columns = pl.ds(k * depth, depth)

        def move(source, place, sem):
            copy = pltpu.make_async_copy(source, place, sem)
            copy.start() if begin else copy.wait()

        for b, ref in enumerate(whole):
            move(ref.at[order[k]], x_buf.at[pl.ds(b * rows, rows), columns], sems.at[k, b])
            for h in range(2):
                @pl.when(order[k] // each == h)
                def _():
                    place = x_buf.at[pl.ds((2 + b) * rows, rows), columns]
                    move(halves[2 * b + h].at[order[k] % each], place, sems.at[k, 2 + b])
        for h in range(2):
            place, sem = w_buf.at[columns, pl.ds(h * width, width)], sems.at[k, 4 + h]
            if k < 3:
                move(w_from[h * pieces + k], place, sem)
                continue

            @pl.when(inside)
            def _():
                move(w_from[h * pieces + k], place, sem)

            @pl.when(jnp.logical_not(inside))
            def _():
                move(w_from[h * pieces + k + 1], place, sem)

    for k in range(outer):
        fetch(k, True)
    total = 0.0
    for first in range(0, outer, each):
        for k in range(first, first + each):
            fetch(k, False)
        columns = slice(first * depth, (first + each) * depth)
        total += dot(x_buf[:, columns], w_buf[columns, :])
    for b, ref in enumerate(out_refs):
        ref[...] = total[b * rows:(b + 1) * rows].astype(ref.dtype)


def fast_body(tokens, cotangent, frozen_value, down_store, up_store, block_adapter, adapter_slot):
    group, parts = lax.axis_size("tensor"), lax.axis_size("parts")
    outer = group // 2
    token_rows = tokens.shape[0]
    slice_width = D // group
    down_chunks = down_store.shape[1] // LANES
    up_chunks = up_store.shape[1] // LANES
    me, part, core = lax.axis_index("tensor"), lax.axis_index("parts"), lax.axis_index("dp")
    z = me // 2

    def exchange(value, s):
        return lax.ppermute(value, "tensor", [(t, t ^ s) for t in range(group)])

    def other_core(value):
        return lax.ppermute(value, "dp", [(0, 1), (1, 0)])

    def other_part(value):
        return lax.ppermute(value, "parts", [(a, parts - 1 - a) for a in range(parts)])

    own = jnp.broadcast_to(block_adapter, (group, 1, LANES))
    asked = lax.all_to_all(own, "tensor", 0, 0)
    split_from, half_from, own = lax.optimization_barrier((tokens, frozen_value, own))

    width = frozen_value.shape[1] // parts
    half = lax.dynamic_slice_in_dim(half_from, part * width, width, axis=1)
    block = jax.ShapeDtypeStruct((outer, token_rows, slice_width), jnp.bfloat16)
    token = jax.ShapeDtypeStruct((1,), jnp.int32)
    some = jax.ShapeDtypeStruct((outer // 2, token_rows, slice_width), jnp.bfloat16)
    x_mine, *x_theirs = pl.pallas_call(
        split_kernel, out_shape=(block, some, some), in_specs=[VMEM], out_specs=[VMEM] * 3,
        name="split_tokens", compiler_params=LIMIT,
    )(split_from)
    x_far = [exchange(x_theirs[0], 1)]
    y_mine = other_part(x_mine)
    xs = pl.pallas_call(
        interleave_kernel,
        out_shape=jax.ShapeDtypeStruct((group, 2 * token_rows, slice_width // 2), jnp.bfloat16),
        in_specs=[VMEM], out_specs=ANY, name="pair_columns", compiler_params=WIDE,
        scratch_shapes=[
            pltpu.VMEM((group, 2 * token_rows, slice_width // 2), jnp.bfloat16),
            pltpu.SemaphoreType.DMA((group,)),
        ],
        cost_estimate=cost(read=128 << 20),
    )(split_from)
    middle = [(t, t ^ 6) for t in range(group) if t // 2 in (1, 2)]
    ends = [(t, t ^ 2) for t in range(group) if t // 2 in (1, 2)]
    near = exchange(half, 2)
    over = lax.ppermute(half, "tensor", middle)
    near, over, asked, x_theirs, xs = lax.optimization_barrier((near, over, asked, x_theirs, xs))
    x_far.append(exchange(x_theirs[1], 1))
    over_near = lax.ppermute(near, "tensor", middle)
    passed = lax.ppermute(over, "tensor", ends)
    pieces = jax.ShapeDtypeStruct((group, down_chunks + up_chunks, LANES), jnp.bfloat16)
    def tiles(store):
        view = store.reshape(store.shape[0] // TILE_ROWS, TILE_ROWS, store.shape[1] // LANES, LANES)
        return view.transpose(0, 2, 1, 3)

    sent, rows = pl.pallas_call(
        gather_kernel,
        out_shape=(pieces, jax.ShapeDtypeStruct((group,), jnp.int32)),
        in_specs=[SMEM, SMEM, ANY, ANY],
        out_specs=(ANY, SMEM),
        scratch_shapes=[
            pltpu.VMEM((group, down_chunks, TILE_ROWS, LANES), jnp.bfloat16),
            pltpu.VMEM((group, up_chunks, TILE_ROWS, LANES), jnp.bfloat16),
            pltpu.VMEM((2, (down_chunks + up_chunks) * 8, LANES), jnp.float32),
            pltpu.VMEM(pieces.shape, jnp.bfloat16),
            pltpu.SemaphoreType.DMA((3, group)),
        ],
        compiler_params=WIDE,
        cost_estimate=cost(read=40 << 20),
        name="pick_panels",
    )(asked, adapter_slot, tiles(down_store), tiles(up_store))
    sent, rows, x_far, y_mine, half, near, over, over_near, passed = lax.optimization_barrier(
        (sent, rows, x_far, y_mine, half, near, over, over_near, passed)
    )
    panels = lax.all_to_all(sent, "tensor", 0, 0)
    rows_core = other_core(rows)
    y_far = [other_part(piece) for piece in x_far]
    passed_near = lax.ppermute(over_near, "tensor", ends)
    owned_groups = ADAPTERS // lax.axis_size("dp") // 8
    down_shape = jax.ShapeDtypeStruct((owned_groups, down_chunks, 8, 1, LANES), jnp.float32)
    up_shape = jax.ShapeDtypeStruct((owned_groups, up_chunks, 8, 1, LANES), jnp.float32)
    def clear(half, inputs, in_specs, aliases):
        return pl.pallas_call(
            functools.partial(zero_kernel, half), out_shape=(down_shape, up_shape, token),
            in_specs=in_specs, out_specs=(ANY, ANY, SMEM), input_output_aliases=aliases,
            scratch_shapes=[pltpu.VMEM((up_chunks, 8, 1, LANES), jnp.float32), pltpu.SemaphoreType.DMA((2,))],
            compiler_params=LIMIT, cost_estimate=cost(read=14 << 20), name="clear_rows",
        )(*inputs)

    down_zero, up_zero, cleared = clear(0, (rows,), [SMEM], {})
    inside = (z == 1) | (z == 2)
    quarter = [half, near, jnp.where(inside, over, passed)]
    quarter_core = [other_core(w) for w in quarter]
    panels, quarter_core = lax.optimization_barrier((panels, quarter_core))

    terms, lifted = pl.pallas_call(
        functools.partial(adapter_kernel, group, down_chunks),
        out_shape=(pieces, jax.ShapeDtypeStruct((token_rows, VALUE_OUTPUTS), jnp.float32)),
        in_specs=[VMEM] * 3 + [SMEM],
        out_specs=(VMEM, VMEM),
        scratch_shapes=[pltpu.VMEM((2 * R, VALUE_OUTPUTS), jnp.float32)],
        compiler_params=LIMIT,
        cost_estimate=cost(flops=3 << 30, read=8 << 20),
        name="adapter",
    )(xs, cotangent, panels, cleared)
    over_near, cleared = lax.optimization_barrier((over_near, cleared))
    over_core = other_core(over_near)
    terms, over_core, passed_near, y_far = lax.optimization_barrier((terms, over_core, passed_near, y_far))
    quarters = quarter + [over_near, passed_near] + quarter_core + [over_core, other_core(passed_near)]
    sums = [jax.ShapeDtypeStruct((token_rows, parts * width), kind) for kind in (jnp.float32,) + (jnp.bfloat16,) * 3]
    kept, to_part, to_inner, to_both = pl.pallas_call(
        base_kernel,
        out_shape=sums,
        in_specs=[ANY] * (7 + len(quarters)),
        out_specs=[VMEM] * 4,
        scratch_shapes=[
            pltpu.VMEM((4 * token_rows, outer * slice_width), jnp.bfloat16),
            pltpu.VMEM((outer * slice_width, parts * width), jnp.bfloat16),
            pltpu.SemaphoreType.DMA((outer, 6)),
        ],
        compiler_params=WIDE,
        cost_estimate=cost(flops=4 << 30, read=8 << 20),
        name="frozen_part",
    )(x_mine, y_mine, *x_far, *y_far, *quarters, terms)
    opposite = [(a * group + t, (parts - 1 - a) * group + (t ^ 1)) for a in range(parts) for t in range(group)]
    back = lax.all_to_all(terms, "tensor", 0, 0)
    arrived = (exchange(to_inner, 1), other_part(to_part), lax.ppermute(to_both, ("parts", "tensor"), opposite))
    down_zero, up_zero, kept = lax.optimization_barrier((down_zero, up_zero, kept))
    down_zero, up_zero, _ = clear(1, (down_zero, up_zero), [ANY, ANY], {0: 0, 1: 1})
    back, arrived, down_zero, up_zero = lax.optimization_barrier((back, arrived, down_zero, up_zero))
    back_core = other_core(back)

    grad_down, grad_up = pl.pallas_call(
        functools.partial(scatter_kernel, 2 * group, down_chunks, up_chunks),
        out_shape=(down_shape, up_shape),
        in_specs=[SMEM] * 2 + [ANY] * 4,
        out_specs=(ANY, ANY),
        input_output_aliases={4: 0, 5: 1},
        scratch_shapes=[
            pltpu.VMEM((2 * group,) + pieces.shape[1:], jnp.bfloat16),
            pltpu.VMEM((2 * group, down_chunks, LANES), jnp.float32),
            pltpu.VMEM((2 * group, up_chunks, LANES), jnp.float32),
            pltpu.VMEM((up_chunks, LANES), jnp.float32),
            pltpu.SemaphoreType.DMA((2 * group,)),
            pltpu.SemaphoreType.DMA(()),
        ],
        compiler_params=LIMIT,
        cost_estimate=cost(read=16 << 20),
        name="place_rows",
    )(rows, rows_core, back, back_core, down_zero, up_zero)
    grad_down = grad_down.reshape(owned_groups, down_chunks, 8, LANES).transpose(0, 2, 1, 3)
    grad_up = grad_up.reshape(owned_groups, up_chunks, 8, LANES).transpose(0, 2, 1, 3)

    arrived = [a.astype(jnp.float32) for a in arrived]
    kept, got = kept + arrived[0], arrived[1] + arrived[2]
    quarters = [[c[:, :width], c[:, width:]] for c in (kept, got)]

    def pick_quarter(c, a):
        first = quarters[a][0] if c == 0 else quarters[a][1]
        second = quarters[a][1] if c == 0 else quarters[a][0]
        return jnp.where(core == 0, first, second)

    def columns_of(c):
        low, high = pick_quarter(c, 0), pick_quarter(c, 1)
        return jnp.where(part == 0, low, high), jnp.where(part == 0, high, low)

    frozen_output = jnp.concatenate(columns_of(0) + columns_of(1), axis=1)
    mixed = (frozen_output + lifted).astype(jnp.bfloat16)
    return mixed, grad_down.reshape(owned_groups * 8, -1), grad_up.reshape(owned_groups * 8, -1)


def fits(mesh):
    group, cores, parts = mesh.shape["tensor"], mesh.shape["dp"], mesh.shape["parts"]
    return cores == 2 and parts == 2 and group <= 8 and group & (group - 1) == 0 and R == 8 * group


def body(mesh, tokens, *rest):
    block_adapter = rest[4]
    one_block = block_adapter.shape[0] == 1
    return (fast_body if fits(mesh) and one_block else plain_body)(tokens, *rest)


def solution(mesh):
    placed = (
        P(("parts", "dp", "tensor"), None),
        P(("parts", "dp", "tensor"), None),
        P("tensor", "dp"),
        P("parts", "tensor"),
        P("parts", "tensor"),
        P(("parts", "dp", "tensor")),
        P("parts"),
    )
    return jax.shard_map(
        functools.partial(body, mesh),
        mesh=mesh,
        in_specs=placed,
        out_specs=(
            P(("parts", "dp", "tensor"), None),
            P(("parts", "dp"), "tensor"),
            P(("parts", "dp"), "tensor"),
        ),
        check_vma=False,
    )
```
